512 devices in a mesh: seq: 64 (over z, y_lo, core), head: 8 (over y_hi, x).
Axes of the slice: x: 4, y: 4 (y_hi: 2, y_lo: 2; y = y_hi * 2 + y_lo), z: 16, core: 2. Of those that a mesh axis runs over, the one named last changes fastest.
Arguments:
- queries: bfloat16 [64, 64, 1, 3072], P('seq', 'head'), may hold values from -150 to 150
- keys: bfloat16 [64, 64, 1, 3072], P('seq', 'head'), may hold values from -6.1 to 6.1
- values: bfloat16 [64, 64, 1, 3072], P('seq', 'head'), may hold values from -6 to 6
- text_keys: bfloat16 [256, 3072], P(None, 'head'), may hold values from -6 to 6
- text_values: bfloat16 [256, 3072], P(None, 'head'), may hold values from -6 to 6
- text_mask: int32 [256], replicated, may hold values from 0 to 1, as said below
- tokens: bfloat16 [64, 64, 1, 3072], P('seq', 'head'), may hold values from -6 to 6
- out_weight: bfloat16 [3072, 3072], P('head'), may hold values from -0.109375 to 0.109375
- out_bias: float32 [3072], replicated, may hold values from -3 to 3
- gate: float32 [3072], replicated, may hold values from -4 to 4
- shift: float32 [3072], replicated, may hold values from -4 to 4
- scale: float32 [3072], replicated, may hold values from -2.5 to 2.5
- final_weight: bfloat16 [3072, 64], replicated, may hold values from -0.109375 to 0.109375
- final_bias: float32 [64], replicated, may hold values from -3 to 3
- conv_weight: bfloat16 [3, 3, 3, 16, 512], replicated, may hold values from -0.3125 to 0.3125
- conv_bias: float32 [512], replicated, may hold values from -3 to 3
Outputs:
- block_out: bfloat16 [64, 64, 1, 3072], P('seq', 'head')
- decoded: bfloat16 [1, 128, 128, 512], P(None, 'seq', 'head')
The draws below stay inside these ranges and needn't reach their ends.
Inputs may be any that keep to these rules, and one draw needn't show every extreme that they name: text_mask is 1 on a leading run of real text tokens and 0 on the padding after it; the first entry is always 1 and the last always 0.
All inputs are finite; a program needn't handle non-finite values.
Results may differ from the reference program's by a relative error of at most 0.017.
Values may be sent and summed in bfloat16 or wider, within the bound.
A program may use at most 64 MiB of HBM per device.

```python
import math
import jax
import jax.numpy as jnp
from jax import lax

D = 3072
HEADS = 24
HEAD_DIM = 128
TXT = 256
LAT_CH = 16
VAE_CH = 512
FRAMES = 1
PH = 64
PW = 64
HEIGHT = 128
WIDTH = 128


def shared_keys(key):
    return jnp.clip(jax.random.normal(key, (PH, PW, FRAMES, D), jnp.float32), -6.0, 6.0)


def draw_keys(key, part):
    base = shared_keys(key)
    return base.astype(jnp.bfloat16)


def draw_queries(key, part):
    key = jax.random.fold_in(key, 5)
    number = PH * PW * FRAMES
    row_spread = jnp.exp(jax.random.uniform(jax.random.fold_in(key, 2), (number, 1), jnp.float32, math.log(3.0), math.log(6.0)))
    own = jnp.clip(jax.random.normal(key, (number, D), jnp.float32), -6.0, 6.0) * row_spread
    return own.reshape(PH, PW, FRAMES, D).astype(jnp.bfloat16)


def draw_text_mask(key, part):
    key = jax.random.fold_in(key, 7)
    real_count = jax.random.randint(key, (), max(1, TXT // 4), TXT, jnp.int32)
    places = jnp.arange(TXT, dtype=jnp.int32)
    return (places < real_count).astype(jnp.int32)


def block_scale(stream_key, extent, shards, least, top_value):
    factor_of = 1.0
    for axis_at, shards_of in shards:
        steps = jax.random.uniform(jax.random.fold_in(jax.random.fold_in(stream_key, 6), axis_at), (shards_of,), jnp.float32, least / len(shards), top_value / len(shards))
        factor_of = factor_of * jnp.repeat(jnp.exp(steps), extent[axis_at] // shards_of).reshape((-1,) + (1,) * (len(extent) - 1 - axis_at))
    return factor_of


def centred(stream_key, extent, width, reach, shards=(), held_as=jnp.bfloat16):
    values = width * jax.random.normal(stream_key, extent, jnp.float32)
    if shards:
        values = values * block_scale(stream_key, extent, shards, -0.22, 0.18)
    return jnp.clip(values, -reach, reach).astype(held_as)


def setup_inputs(seed: int = 0) -> dict:
    key_list = jax.random.split(jax.random.key(seed), 17)
    return {
        "queries": draw_queries(jax.random.fold_in(key_list[16], 71), 0),
        "keys": draw_keys(jax.random.fold_in(key_list[16], 71), 0),
        "values": centred(key_list[2], (PH, PW, FRAMES, D), 1.0, 6.0, ((0, 64), (1, 8))),
        "text_keys": centred(key_list[3], (TXT, D), 1.0, 6.0, ((1, 8),)),
        "text_values": centred(key_list[4], (TXT, D), 1.0, 6.0, ((1, 8),)),
        "text_mask": draw_text_mask(jax.random.fold_in(key_list[16], 71), 0),
        "tokens": centred(key_list[6], (PH, PW, FRAMES, D), 1.0, 6.0, ((0, 64), (1, 8))),
        "out_weight": centred(key_list[7], (D, D), D ** -0.5, 0.109375, ((0, 8),)),
        "out_bias": centred(key_list[8], (D,), 0.5, 3.0, (), jnp.float32),
        "gate": centred(key_list[9], (D,), 1.0, 4.0, (), jnp.float32),
        "shift": centred(key_list[10], (D,), 1.0, 4.0, (), jnp.float32),
        "scale": centred(key_list[11], (D,), 0.5, 2.5, (), jnp.float32),
        "final_weight": centred(key_list[12], (D, 4 * LAT_CH), D ** -0.5, 0.109375),
        "final_bias": centred(key_list[13], (4 * LAT_CH,), 0.5, 3.0, (), jnp.float32),
        "conv_weight": centred(key_list[14], (3, 3, 3, LAT_CH, VAE_CH), (27 * LAT_CH) ** -0.5, 0.3125),
        "conv_bias": centred(key_list[15], (VAE_CH,), 0.5, 3.0, (), jnp.float32),
    }


NEG = -1e+30
LATENT_SCALE = 0.476986

def reference(queries, keys, values, text_keys, text_values, text_mask, tokens, out_weight, out_bias, gate, shift, scale, final_weight, final_bias, conv_weight, conv_bias):
    count = PH * PW * FRAMES
    flat_q = queries.reshape(count, HEADS, HEAD_DIM)
    all_k = jnp.concatenate([text_keys.reshape(TXT, HEADS, HEAD_DIM), keys.reshape(count, HEADS, HEAD_DIM)], 0)
    all_v = jnp.concatenate([text_values.reshape(TXT, HEADS, HEAD_DIM), values.reshape(count, HEADS, HEAD_DIM)], 0)
    valid = jnp.concatenate([text_mask == 1, jnp.ones((count,), bool)], 0)
    block = math.gcd(count, 1024)

    def one_head(head):
        q_head = lax.dynamic_index_in_dim(flat_q, head, 1, keepdims=False)
        k_head = lax.dynamic_index_in_dim(all_k, head, 1, keepdims=False)
        v_head = lax.dynamic_index_in_dim(all_v, head, 1, keepdims=False)

        def one_block(q_block):
            scores = jnp.dot(q_block, k_head.T, preferred_element_type=jnp.float32) * HEAD_DIM ** (-0.5)
            scores = jnp.where(valid[None, :], scores, NEG)
            top = lax.optimization_barrier(jnp.max(scores, axis=1, keepdims=True))
            weights = jnp.where(valid[None, :], jnp.exp(scores - top), 0.0)
            total = lax.optimization_barrier(jnp.sum(weights, axis=1, keepdims=True))
            return jnp.dot(weights.astype(jnp.bfloat16), v_head, preferred_element_type=jnp.float32) / total
        result = lax.map(one_block, q_head.reshape(count // block, block, HEAD_DIM))
        return result.reshape(count, HEAD_DIM)
    attended = lax.map(one_head, jnp.arange(HEADS).astype(jnp.int32))
    attended = attended.astype(jnp.bfloat16).transpose(1, 0, 2).reshape(count, D)
    projected = jnp.dot(attended, out_weight, preferred_element_type=jnp.float32)
    stream = tokens.reshape(count, D).astype(jnp.float32) + gate * (projected + out_bias)
    block_out = stream.astype(jnp.bfloat16)
    normed_in = block_out.astype(jnp.float32)
    centered = normed_in - lax.optimization_barrier(jnp.mean(normed_in, axis=1, keepdims=True))
    spread = lax.optimization_barrier(jnp.mean(centered * centered, axis=1, keepdims=True))
    normed = centered * lax.rsqrt(spread + 1e-06)
    modulated = (normed * (1.0 + scale) + shift).astype(jnp.bfloat16)
    patches = (jnp.dot(modulated, final_weight, preferred_element_type=jnp.float32) + final_bias) / LATENT_SCALE
    latent = patches.reshape(PH, PW, FRAMES, LAT_CH, 2, 2).transpose(2, 0, 4, 1, 5, 3)
    latent = latent.reshape(FRAMES, HEIGHT, WIDTH, LAT_CH).astype(jnp.bfloat16)
    padded = jnp.pad(latent, ((0, 0), (1, 1), (1, 1), (0, 0)), mode='edge')
    padded = jnp.concatenate([padded[:1], padded[:1], padded], 0)
    accum = jnp.zeros((FRAMES * HEIGHT * WIDTH, VAE_CH), jnp.float32)
    for tap_t in range(3):
        for tap_i in range(3):
            for tap_j in range(3):
                window = padded[tap_t:tap_t + FRAMES, tap_i:tap_i + HEIGHT, tap_j:tap_j + WIDTH, :]
                accum = accum + jnp.dot(window.reshape(-1, LAT_CH), conv_weight[tap_t, tap_i, tap_j], preferred_element_type=jnp.float32)
    decoded = (accum + conv_bias).reshape(FRAMES, HEIGHT, WIDTH, VAE_CH).astype(jnp.bfloat16)
    return (block_out.reshape(PH, PW, FRAMES, D), decoded)
```

```python
import functools

import jax
import jax.numpy as jnp
from jax import lax
from jax.experimental import pallas as pl
from jax.experimental.pallas import tpu as pltpu
from jax.sharding import PartitionSpec as P

HEAD_DIM = 128
GROUP = 3
LAT_CH = 16
TOK = 8
LAYER = 4
LATENT_SCALE = 0.476986
NEG = -1e30
SCORE_SCALE = HEAD_DIM ** (-0.5)
LOG2E = 1.4426950408889634
BF16 = jnp.bfloat16
F32 = jnp.float32
MESH = pl.DeviceIdType.MESH


def dot(a, b):
    return jnp.dot(a, b, preferred_element_type=F32)


def dot_nt(a, b):
    return lax.dot_general(a, b, (((1,), (1,)), ((), ())), preferred_element_type=F32)


def kernel(
    seqs,
    heads,
    q_hbm,
    k_hbm,
    v_hbm,
    text_k_hbm,
    text_v_hbm,
    mask_hbm,
    tokens_hbm,
    out_w_hbm,
    out_bias_hbm,
    gate_hbm,
    shift_hbm,
    scale_hbm,
    final_w_hbm,
    final_bias_hbm,
    conv_w_hbm,
    conv_bias_hbm,
    block_hbm,
    decoded_hbm,
    queries,
    keys,
    values,
    text_k,
    text_v,
    mask,
    tokens,
    out_w,
    out_bias,
    gate,
    shift,
    scale,
    final_w,
    final_bias,
    conv_w,
    conv_bias,
    stage,
    landing,
    kv,
    qs,
    run_max,
    run_sum,
    run_acc,
    marks,
    o_stage,
    o_in,
    rs_stage,
    rs_in,
    lat,
    halo,
    w_sum,
    w_full,
    pixels,
    block_out,
    decoded,
    local_sem,
    out_sem,
    a2a_send,
    a2a_recv,
    ring_send,
    half_send,
    ring_recv,
    far_recv,
    q_send,
    q_recv,
    o_send,
    o_recv,
    rs_send,
    rs_recv,
    halo_send,
    halo_recv,
):
    s = lax.axis_index("seq")
    h = lax.axis_index("head")
    layers = seqs // LAYER
    far = layers // 2
    z = s // LAYER
    j = lax.rem(s, LAYER)
    width = GROUP * HEAD_DIM
    dim = heads * width
    rows = heads * TOK
    rs_parts = rs_stage.shape[0]
    part_cols = dim // rs_parts

    def shifted(index, by, count):
        return lax.rem(index + (by % count), count)

    def head_peer(i):
        return shifted(h, i, heads)

    def layer_peer(i):
        return (z * LAYER + shifted(j, i, LAYER), h)

    def slot_at(by):
        return lax.rem(z + by + layers, layers)

    right = (slot_at(1) * LAYER + j, h)
    left = (slot_at(-1) * LAYER + j, h)

    def remote(src, dst, send, recv, device):
        return pltpu.make_async_remote_copy(
            src_ref=src,
            dst_ref=dst,
            send_sem=send,
            recv_sem=recv,
            device_id=device,
            device_id_type=MESH,
        )

    pairs = (
        (k_hbm, keys),
        (v_hbm, values),
        (q_hbm, queries),
        (conv_w_hbm, conv_w),
        (text_k_hbm, text_k),
        (text_v_hbm, text_v),
        (mask_hbm, mask),
        (tokens_hbm, tokens),
        (out_w_hbm, out_w),
        (out_bias_hbm, out_bias),
        (gate_hbm, gate),
        (shift_hbm, shift),
        (scale_hbm, scale),
        (final_w_hbm, final_w),
        (final_bias_hbm, final_bias),
        (conv_bias_hbm, conv_bias),
    )
    loads = [
        pltpu.make_async_copy(src, dst, local_sem.at[i]) for i, (src, dst) in enumerate(pairs)
    ]

    halo_steps = [(dr, dc) for dr in (-1, 0, 1) for dc in (-1, 0, 1) if (dr, dc) != (0, 0)]
    halo_peers = [(shifted(s, dr, seqs), shifted(h, dc, heads)) for dr, dc in halo_steps]
    partners = [(s, head_peer(i)) for i in range(1, heads)]
    partners += [layer_peer(i) for i in range(1, LAYER)]
    partners += [right, left]
    partners += [peer for peer, (dr, dc) in zip(halo_peers, halo_steps) if dr != 0]
    for load in loads[:3]:
        load.start()
    barrier = pltpu.get_barrier_semaphore()
    for partner in partners:
        pl.semaphore_signal(barrier, inc=1, device_id=partner, device_id_type=MESH)
    for load in loads[3:]:
        load.start()
    for at, whole in enumerate((keys, values, queries)):
        loads[at].wait()
        for g in range(heads):
            stage[g, at] = whole[:, g * width : (g + 1) * width]
    pl.semaphore_wait(barrier, len(partners))

    for i in range(1, heads):
        g = head_peer(i)
        remote(stage.at[g], landing.at[h], a2a_send, a2a_recv, (s, g)).start()
    landing[h] = stage[h]

    loads[3].wait()
    conv_all = conv_w[...].astype(F32)
    taps = conv_all.shape[0] // 3
    w_sum[...] = (conv_all[:taps] + conv_all[taps : 2 * taps] + conv_all[2 * taps :]).astype(BF16)
    parities = w_full.shape[0]
    features = final_w.shape[0]

    def conv_weights(parity, carry):
        up = parity // 2
        side = lax.rem(parity, 2)
        depth = w_full.shape[1]
        row = lax.broadcasted_iota(jnp.int32, (depth, taps), 0)
        col = lax.broadcasted_iota(jnp.int32, (depth, taps), 1)
        tap_i = 2 * (row >> 7) + ((row >> 1) & 1) + up - 1
        tap_j = 2 * ((row >> 6) & 1) + (row & 1) + side - 1
        inside = (tap_i >= 0) & (tap_i <= 2) & (tap_j >= 0) & (tap_j <= 2)
        source = (tap_i * 3 + tap_j) * LAT_CH + ((row & 63) >> 2)
        pick = jnp.where(inside & (source == col), 1.0, 0.0).astype(BF16)
        w_full[parity] = dot(pick, w_sum[...]).astype(BF16)
        return carry

    lax.fori_loop(0, parities, conv_weights, 0)

    def rows_of(block):
        return block.astype(F32).reshape(rows, width).astype(BF16)

    others = landing.at[pl.ds(0, heads - 1)]
    peer = (s, head_peer(1))
    remote(others, others, a2a_send, a2a_recv, peer).wait_recv()
    own_k = rows_of(landing[:, 0])
    own_v = rows_of(landing[:, 1])
    for n in range(GROUP):
        cols = slice(n * HEAD_DIM, (n + 1) * HEAD_DIM)
        kv[z, n, 0] = own_k[:, cols]
        kv[z, n, 1] = own_v[:, cols]

    def to_right(ref, recv, send=0):
        return remote(ref, ref, ring_send.at[0] if send == 0 else half_send.at[0], recv, right)

    def to_left(ref, recv, send=0):
        return remote(ref, ref, ring_send.at[1] if send == 0 else half_send.at[1], recv, left)

    for n in range(GROUP):
        to_right(kv.at[z, n], ring_recv.at[z, n]).start()
        to_left(kv.at[z, n], ring_recv.at[z, n]).start()

    own_q = rows_of(landing[:, 2])
    for n in range(GROUP):
        qs[n, j] = own_q[:, n * HEAD_DIM : (n + 1) * HEAD_DIM]
    for i in range(1, LAYER):
        remote(qs.at[:, j], qs.at[:, j], q_send, q_recv, layer_peer(i)).start()

    def queries_of(n):
        return qs[n].reshape(LAYER * rows, HEAD_DIM)

    def attend_text(n, carry):
        cols = pl.ds(pl.multiple_of(n * HEAD_DIM, HEAD_DIM), HEAD_DIM)
        scores = dot_nt(queries_of(n), text_k[:, cols])
        count = scores.shape[1]
        lane = lax.broadcasted_iota(jnp.int32, (1, count), 1)
        share = count // LAYER
        mine = (lane >= j * share) & (lane < (j + 1) * share) & (mask[...] == 1)
        mine = jnp.broadcast_to(mine, scores.shape)
        scores = jnp.where(mine, scores, NEG)
        top = jnp.max(scores, axis=1, keepdims=True)
        weights = jnp.where(mine, jnp.exp2((scores - top) * (SCORE_SCALE * LOG2E)), 0.0)
        total = jnp.sum(weights, axis=1, keepdims=True)
        shape = run_max.shape[1:]
        run_max[n] = jnp.broadcast_to(top, shape)
        run_sum[n] = jnp.broadcast_to(total, shape)
        run_acc[n] = dot(weights.astype(BF16), text_v[:, cols])
        return carry

    def absorb(n, one, other):
        keys_now = jnp.concatenate([kv[one, n, 0], kv[other, n, 0]], axis=0)
        values_now = jnp.concatenate([kv[one, n, 1], kv[other, n, 1]], axis=0)
        scores = dot_nt(queries_of(n), keys_now)
        old = run_max[n]
        top = jnp.maximum(old, jnp.max(scores, axis=1, keepdims=True))
        factor = jnp.exp2((old - top) * (SCORE_SCALE * LOG2E))
        weights = jnp.exp2((scores - top[:, : scores.shape[1]]) * (SCORE_SCALE * LOG2E))
        total = run_sum[n] * factor + jnp.sum(weights, axis=1, keepdims=True)
        acc = run_acc[n] * factor + dot(weights.astype(BF16), values_now)
        return top, total, acc

    def pass_on(step, n):
        one = slot_at(-step)
        other = slot_at(step)
        to_right(kv.at[one, n], ring_recv.at[one, n]).wait_recv()

        @pl.when(step < far - 1)
        def _():
            to_right(kv.at[one, n], ring_recv.at[one, n]).start()

        @pl.when(step == far - 1)
        def _():
            to_right(kv.at[one, n, 0], ring_recv.at[one, n], 1).start()

        to_left(kv.at[other, n], ring_recv.at[other, n]).wait_recv()

        @pl.when(step < far - 1)
        def _():
            to_left(kv.at[other, n], ring_recv.at[other, n]).start()

        @pl.when(step == far - 1)
        def _():
            to_left(kv.at[other, n, 1], far_recv.at[n], 1).start()

    def first_step(n, carry):
        pass_on(1, n)
        return carry

    lax.fori_loop(0, GROUP, first_step, 0)
    three = qs.at[:, pl.ds(0, LAYER - 1)]
    remote(three, three, q_send, q_recv, layer_peer(1)).wait_recv()
    for load in loads[4:7]:
        load.wait()
    lax.fori_loop(0, GROUP, attend_text, 0)

    def ring_step(step, carry):
        def one_head(n, inner):
            @pl.when(step < far)
            def _():
                pass_on(step, n)

            top, total, acc = absorb(n, slot_at(1 - step), slot_at(step - 1))
            run_max[n] = top
            run_sum[n] = total
            run_acc[n] = acc
            return inner

        return lax.fori_loop(0, GROUP, one_head, carry)

    lax.fori_loop(2, far + 1, ring_step, 0)

    opposite = slot_at(far)
    lane = lax.broadcasted_iota(jnp.int32, (1, HEAD_DIM), 1)
    marks[...] = jnp.zeros_like(marks)

    def send_share(n):
        for i in range(1, LAYER):
            remote(
                o_stage.at[shifted(j, i, LAYER), n], o_in.at[j, n], o_send, o_recv, layer_peer(i)
            ).start()

    def last_step(n, carry):
        to_right(kv.at[opposite, n, 0], ring_recv.at[opposite, n]).wait_recv()
        to_left(kv.at[opposite, n, 1], far_recv.at[n]).wait_recv()
        top, total, acc = absorb(n, z, opposite)
        share = (acc / total).astype(BF16)
        for i in range(LAYER):
            o_stage[i, n] = share[i * rows : (i + 1) * rows]
        send_share(n)
        level = top * SCORE_SCALE + jnp.log(total)
        first = level.astype(BF16).astype(F32)
        second = (level - first).astype(BF16).astype(F32)
        third = level - first - second
        here = jnp.where(lane == 3 * n, first, marks[...])
        here = jnp.where(lane == 3 * n + 1, second, here)
        marks[...] = jnp.where(lane == 3 * n + 2, third, here)
        return carry

    lax.fori_loop(0, GROUP, last_step, 0)
    level_rows = marks[...].astype(BF16)
    for i in range(LAYER):
        o_stage[i, GROUP] = level_rows[i * rows : (i + 1) * rows]
    send_share(GROUP)
    o_in[j] = o_stage[j]

    for load in loads[7:]:
        load.wait()
    three = o_in.at[pl.ds(0, LAYER - 1)]
    remote(three, three, o_send, o_recv, layer_peer(1)).wait_recv()
    level_parts = [o_in[i, GROUP].astype(F32) for i in range(LAYER)]
    attended = []
    for n in range(GROUP):
        own_lanes = (lane >= 3 * n) & (lane < 3 * n + 3)
        levels = [
            jnp.sum(jnp.where(own_lanes, part, 0.0), axis=1, keepdims=True)
            for part in level_parts
        ]
        top = functools.reduce(jnp.maximum, levels)
        shares = [jnp.exp(level - top) for level in levels]
        total = functools.reduce(jnp.add, shares)
        mixed = functools.reduce(
            jnp.add, [share * o_in[i, n].astype(F32) for i, share in enumerate(shares)]
        )
        attended.append((mixed / total).astype(BF16))
    attended = jnp.concatenate(attended, axis=1)

    for part in range(rs_parts):
        product = dot(attended, out_w[:, part * part_cols : (part + 1) * part_cols])
        rs_stage[part] = product.reshape(heads, TOK, part_cols).astype(BF16)
        for i in range(1, heads):
            g = head_peer(i)
            remote(
                rs_stage.at[part, g],
                rs_in.at[part, h],
                rs_send.at[part],
                rs_recv.at[part],
                (s, g),
            ).start()
        rs_in[part, h] = rs_stage[part, h]
    pieces = []
    for part in range(rs_parts):
        cols = slice(part * part_cols, (part + 1) * part_cols)
        others = rs_in.at[part, pl.ds(0, heads - 1)]
        remote(others, others, rs_send.at[part], rs_recv.at[part], peer).wait_recv()
        projected = jnp.sum(rs_in[part].astype(F32), axis=0)
        stream = tokens[:, cols].astype(F32) + gate[:, cols] * (projected + out_bias[:, cols])
        rounded = stream.astype(BF16)
        block_out[:, cols] = rounded
        pieces.append(rounded.astype(F32))
    block_copy = pltpu.make_async_copy(block_out, block_hbm, out_sem.at[0])
    block_copy.start()

    normed_in = jnp.concatenate(pieces, axis=1)
    centered = normed_in - jnp.mean(normed_in, axis=1, keepdims=True)
    spread = jnp.mean(centered * centered, axis=1, keepdims=True)
    normed = centered * lax.rsqrt(spread + 1e-06)
    modulated = (normed * (1.0 + scale[...]) + shift[...]).astype(BF16)
    patches = (dot_nt(modulated, final_w[...]) + final_bias[...]) / LATENT_SCALE
    padded = jnp.concatenate([patches, jnp.zeros((TOK, HEAD_DIM - features), F32)], axis=1)
    lat[...] = padded.astype(BF16)

    for at, to in enumerate(halo_peers):
        remote(lat, halo.at[at], halo_send, halo_recv, to).start()
    tiles = {(0, 0): lat[...].astype(F32)}
    remote(halo, halo, halo_send, halo_recv, peer).wait_recv()
    for at, (dr, dc) in enumerate(halo_steps):
        tiles[(-dr, -dc)] = halo[at].astype(F32)

    def rolled(tile, by):
        return pltpu.roll(tile, by % HEAD_DIM, 1)

    top_edge, bottom_edge = s == 0, s == seqs - 1
    first_tile, last_tile = h == 0, h == heads - 1
    for dc in (-1, 0, 1):
        middle = tiles[(0, dc)]
        tiles[(-1, dc)] = jnp.where(top_edge, rolled(middle, 2), tiles[(-1, dc)])
        tiles[(1, dc)] = jnp.where(bottom_edge, rolled(middle, -2), tiles[(1, dc)])
    low = lane < features
    packed = {}
    for dr in (-1, 0, 1):
        middle = tiles[(dr, 0)]
        before = jnp.where(first_tile, rolled(middle, 1)[:1], tiles[(dr, -1)][TOK - 1 :])
        after = jnp.where(last_tile, rolled(middle, -1)[TOK - 1 :], tiles[(dr, 1)][:1])
        before = jnp.concatenate([before, middle[: TOK - 1]], axis=0)
        after = jnp.concatenate([middle[1:], after], axis=0)
        packed[(dr, 0)] = jnp.where(low, before, rolled(middle, features))
        packed[(dr, 1)] = jnp.where(low, middle, rolled(after, features))
    for parity in range(parities):
        up, side = parity // 2, parity % 2
        stacked = jnp.concatenate([packed[(up - 1, side)], packed[(up, side)]], axis=1)
        result = dot(stacked.astype(BF16), w_full[parity]) + conv_bias[...]
        for tile in range(pixels.shape[1]):
            pixels[up, tile, pl.ds(side, TOK, stride=2), :] = result[
                :, tile * HEAD_DIM : (tile + 1) * HEAD_DIM
            ]
    for tile in range(pixels.shape[1]):
        cols = slice(tile * HEAD_DIM, (tile + 1) * HEAD_DIM)
        decoded[:, :, cols] = pixels[:, tile].astype(BF16)
    decoded_copy = pltpu.make_async_copy(decoded, decoded_hbm, out_sem.at[1])
    decoded_copy.start()

    others = stage.at[pl.ds(0, heads - 1)]
    remote(others, others, a2a_send, a2a_recv, peer).wait_send()
    ring_all = kv.at[pl.ds(0, far - 1)]
    to_right(ring_all, far_recv.at[0]).wait_send()
    to_left(ring_all, far_recv.at[0]).wait_send()
    ring_half = kv.at[0, :, 0]
    to_right(ring_half, far_recv.at[0], 1).wait_send()
    to_left(ring_half, far_recv.at[0], 1).wait_send()
    three = qs.at[:, pl.ds(0, LAYER - 1)]
    remote(three, three, q_send, q_recv, peer).wait_send()
    three = o_stage.at[pl.ds(0, LAYER - 1)]
    remote(three, three, o_send, o_recv, peer).wait_send()
    for part in range(rs_parts):
        others = rs_stage.at[part, pl.ds(0, heads - 1)]
        remote(others, others, rs_send.at[part], rs_recv.at[part], peer).wait_send()
    remote(halo, halo, halo_send, halo_recv, peer).wait_send()
    block_copy.wait()
    decoded_copy.wait()


def hand_over(block_in, decoded_in, block_to, decoded_to, sem):
    copies = [
        pltpu.make_async_copy(block_in, block_to, sem.at[0]),
        pltpu.make_async_copy(decoded_in, decoded_to, sem.at[1]),
    ]
    for copy in copies:
        copy.start()
    for copy in copies:
        copy.wait()


def body(seqs, heads, *args):
    (
        queries,
        keys,
        values,
        text_keys,
        text_values,
        text_mask,
        tokens,
        out_weight,
        out_bias,
        gate,
        shift,
        scale,
        final_weight,
        final_bias,
        conv_weight,
        conv_bias,
    ) = args
    dim = queries.shape[3]
    width = GROUP * HEAD_DIM
    text = text_keys.shape[0]
    layers = seqs // LAYER
    far = layers // 2
    rows = heads * TOK
    features = final_weight.shape[1]
    taps = 9 * LAT_CH
    channels = conv_weight.shape[4]
    rs_parts = 2
    operands = (
        queries.reshape(TOK, dim),
        keys.reshape(TOK, dim),
        values.reshape(TOK, dim),
        text_keys,
        text_values,
        text_mask.reshape(1, text),
        tokens.reshape(TOK, dim),
        out_weight,
        out_bias.reshape(1, dim),
        gate.reshape(1, dim),
        shift.reshape(1, dim),
        scale.reshape(1, dim),
        final_weight.T,
        final_bias.reshape(1, features),
        conv_weight.reshape(3 * taps, channels),
        conv_bias.reshape(1, channels),
    )
    copied = [pltpu.VMEM(x.shape, x.dtype) for x in operands]
    dma = pltpu.SemaphoreType.DMA
    anywhere = pl.BlockSpec(memory_space=pl.ANY)
    results = (
        jax.ShapeDtypeStruct((TOK, dim), BF16),
        jax.ShapeDtypeStruct((2, 2 * TOK, channels), BF16),
    )
    block_out, decoded = pl.pallas_call(
        functools.partial(kernel, seqs, heads),
        out_shape=results,
        in_specs=[anywhere] * len(operands),
        out_specs=(anywhere, anywhere),
        scratch_shapes=copied
        + [
            pltpu.VMEM((heads, 3, TOK, width), BF16),
            pltpu.VMEM((heads, 3, TOK, width), BF16),
            pltpu.VMEM((layers, GROUP, 2, rows, HEAD_DIM), BF16),
            pltpu.VMEM((GROUP, LAYER, rows, HEAD_DIM), BF16),
            pltpu.VMEM((GROUP, LAYER * rows, HEAD_DIM), F32),
            pltpu.VMEM((GROUP, LAYER * rows, HEAD_DIM), F32),
            pltpu.VMEM((GROUP, LAYER * rows, HEAD_DIM), F32),
            pltpu.VMEM((LAYER * rows, HEAD_DIM), F32),
            pltpu.VMEM((LAYER, GROUP + 1, rows, HEAD_DIM), BF16),
            pltpu.VMEM((LAYER, GROUP + 1, rows, HEAD_DIM), BF16),
            pltpu.VMEM((rs_parts, heads, TOK, dim // rs_parts), BF16),
            pltpu.VMEM((rs_parts, heads, TOK, dim // rs_parts), BF16),
            pltpu.VMEM((TOK, HEAD_DIM), BF16),
            pltpu.VMEM((8, TOK, HEAD_DIM), BF16),
            pltpu.VMEM((taps, channels), BF16),
            pltpu.VMEM((4, 4 * features, channels), BF16),
            pltpu.VMEM((2, channels // HEAD_DIM, 2 * TOK, HEAD_DIM), F32),
            pltpu.VMEM((TOK, dim), BF16),
            pltpu.VMEM((2, 2 * TOK, channels), BF16),
            dma((len(operands),)),
            dma((2,)),
            dma,
            dma,
            dma((2,)),
            dma((2,)),
            dma((layers, GROUP)),
            dma((GROUP,)),
            dma,
            dma,
            dma,
            dma,
            dma((rs_parts,)),
            dma((rs_parts,)),
            dma,
            dma,
        ],
        compiler_params=pltpu.CompilerParams(
            collective_id=0, has_side_effects=True, vmem_limit_bytes=60 * 1024 * 1024
        ),
        cost_estimate=pl.CostEstimate(
            flops=1_200_000_000, bytes_accessed=5_000_000, transcendentals=1_000_000
        ),
    )(*operands)
    block_out, decoded = pl.pallas_call(
        hand_over,
        out_shape=results,
        in_specs=[anywhere] * 2,
        out_specs=(anywhere, anywhere),
        scratch_shapes=[dma((2,))],
        compiler_params=pltpu.CompilerParams(vmem_limit_bytes=60 * 1024 * 1024),
    )(block_out, decoded)
    return (
        block_out.reshape(1, TOK, 1, dim),
        decoded.reshape(1, 2, 2 * TOK, channels),
    )


def solution(mesh):
    seqs = mesh.shape["seq"]
    heads = mesh.shape["head"]
    spread = P("seq", "head", None, None)
    in_specs = (
        spread,
        spread,
        spread,
        P(None, "head"),
        P(None, "head"),
        P(),
        spread,
        P("head", None),
    ) + (P(),) * 8
    out_specs = (spread, P(None, "seq", "head", None))
    return jax.shard_map(
        functools.partial(body, seqs, heads),
        mesh=mesh,
        in_specs=in_specs,
        out_specs=out_specs,
        check_vma=False,
    )
```

```python
import functools

import jax
import jax.numpy as jnp
from jax import lax
from jax.experimental import pallas as pl
from jax.experimental.pallas import tpu as pltpu
from jax.sharding import PartitionSpec as P

HEAD_DIM = 128
GROUP = 3
LAT_CH = 16
TOK = 8
LAYER = 4
LATENT_SCALE = 0.476986
NEG = -1e30
SCORE_SCALE = HEAD_DIM ** (-0.5)
LOG2E = 1.4426950408889634
BF16 = jnp.bfloat16
F32 = jnp.float32
MESH = pl.DeviceIdType.MESH


def dot(a, b):
    return jnp.dot(a, b, preferred_element_type=F32)


def dot_nt(a, b):
    return lax.dot_general(a, b, (((1,), (1,)), ((), ())), preferred_element_type=F32)


def kernel(
    seqs,
    heads,
    q_hbm,
    k_hbm,
    v_hbm,
    text_k_hbm,
    text_v_hbm,
    mask_hbm,
    tokens_hbm,
    out_w_hbm,
    out_bias_hbm,
    gate_hbm,
    shift_hbm,
    scale_hbm,
    final_w_hbm,
    final_bias_hbm,
    conv_w_hbm,
    conv_bias_hbm,
    block_hbm,
    decoded_hbm,
    queries,
    keys,
    values,
    text_k,
    text_v,
    mask,
    tokens,
    out_w,
    out_bias,
    gate,
    shift,
    scale,
    final_w,
    final_bias,
    conv_w,
    conv_bias,
    stage,
    landing,
    kv,
    qs,
    run_max,
    run_sum,
    run_acc,
    marks,
    o_stage,
    o_in,
    rs_stage,
    rs_in,
    lat,
    halo,
    w_sum,
    w_full,
    pixels,
    block_out,
    decoded,
    local_sem,
    out_sem,
    a2a_send,
    a2a_recv,
    ring_send,
    half_send,
    ring_recv,
    far_recv,
    q_send,
    q_recv,
    o_send,
    o_recv,
    rs_send,
    rs_recv,
    halo_send,
    halo_recv,
):
    s = lax.axis_index("seq")
    h = lax.axis_index("head")
    layers = seqs // LAYER
    far = layers // 2
    z = s // LAYER
    j = lax.rem(s, LAYER)
    width = GROUP * HEAD_DIM
    dim = heads * width
    rows = heads * TOK
    rs_parts = rs_stage.shape[0]
    part_cols = dim // rs_parts

    def shifted(index, by, count):
        return lax.rem(index + (by % count), count)

    r = lax.rem(j + LAYER // 2, LAYER)

    def head_peer(i):
        return (z * LAYER + r, shifted(h, i, heads))

    def layer_peer(i):
        return (z * LAYER + shifted(j, i, LAYER), h)

    def slot_at(by):
        return lax.rem(z + by + layers, layers)

    right = (slot_at(1) * LAYER + j, h)
    left = (slot_at(-1) * LAYER + j, h)

    def remote(src, dst, send, recv, device):
        return pltpu.make_async_remote_copy(
            src_ref=src,
            dst_ref=dst,
            send_sem=send,
            recv_sem=recv,
            device_id=device,
            device_id_type=MESH,
        )

    pairs = (
        (k_hbm, keys),
        (v_hbm, values),
        (q_hbm, queries),
        (conv_w_hbm, conv_w),
        (text_k_hbm, text_k),
        (text_v_hbm, text_v),
        (mask_hbm, mask),
        (tokens_hbm, tokens),
        (out_w_hbm, out_w),
        (out_bias_hbm, out_bias),
        (gate_hbm, gate),
        (shift_hbm, shift),
        (scale_hbm, scale),
        (final_w_hbm, final_w),
        (final_bias_hbm, final_bias),
        (conv_bias_hbm, conv_bias),
    )
    loads = [
        pltpu.make_async_copy(src, dst, local_sem.at[i]) for i, (src, dst) in enumerate(pairs)
    ]

    halo_steps = [(dr, dc) for dr in (-1, 0, 1) for dc in (-1, 0, 1) if (dr, dc) != (0, 0)]
    halo_peers = [(shifted(s, dr, seqs), shifted(h, dc, heads)) for dr, dc in halo_steps]
    partners = [head_peer(i) for i in range(heads)]
    partners += [layer_peer(i) for i in range(1, LAYER)]
    partners += [right, left]
    partners += halo_peers
    for load in loads[:3]:
        load.start()
    barrier = pltpu.get_barrier_semaphore()
    for partner in partners:
        pl.semaphore_signal(barrier, inc=1, device_id=partner, device_id_type=MESH)
    for load in loads[3:]:
        load.start()
    for at, whole in enumerate((keys, values, queries)):
        loads[at].wait()
        for g in range(heads):
            stage[g, at] = whole[:, g * width : (g + 1) * width]
    pl.semaphore_wait(barrier, len(partners))

    for i in range(heads):
        peer = head_peer(i)
        remote(stage.at[peer[1]], landing.at[h], a2a_send, a2a_recv, peer).start()

    loads[3].wait()
    conv_all = conv_w[...].astype(F32)
    taps = conv_all.shape[0] // 3
    w_sum[...] = (conv_all[:taps] + conv_all[taps : 2 * taps] + conv_all[2 * taps :]).astype(BF16)
    parities = w_full.shape[0]
    features = final_w.shape[0]

    def conv_weights(parity, carry):
        up = parity // 2
        side = lax.rem(parity, 2)
        depth = w_full.shape[1]
        row = lax.broadcasted_iota(jnp.int32, (depth, taps), 0)
        col = lax.broadcasted_iota(jnp.int32, (depth, taps), 1)
        tap_i = 2 * (row >> 7) + ((row >> 1) & 1) + up - 1
        tap_j = 2 * ((row >> 6) & 1) + (row & 1) + side - 1
        inside = (tap_i >= 0) & (tap_i <= 2) & (tap_j >= 0) & (tap_j <= 2)
        source = (tap_i * 3 + tap_j) * LAT_CH + ((row & 63) >> 2)
        pick = jnp.where(inside & (source == col), 1.0, 0.0).astype(BF16)
        w_full[parity] = dot(pick, w_sum[...]).astype(BF16)
        return carry

    lax.fori_loop(0, parities, conv_weights, 0)

    def rows_of(block):
        return block.astype(F32).reshape(rows, width).astype(BF16)

    peer = head_peer(0)
    remote(landing, landing, a2a_send, a2a_recv, peer).wait_recv()
    own_k = rows_of(landing[:, 0])
    own_v = rows_of(landing[:, 1])
    for n in range(GROUP):
        cols = slice(n * HEAD_DIM, (n + 1) * HEAD_DIM)
        kv[z, n, 0] = own_k[:, cols]
        kv[z, n, 1] = own_v[:, cols]

    def to_right(ref, recv, send=0):
        return remote(ref, ref, ring_send.at[0] if send == 0 else half_send.at[0], recv, right)

    def to_left(ref, recv, send=0):
        return remote(ref, ref, ring_send.at[1] if send == 0 else half_send.at[1], recv, left)

    for n in range(GROUP):
        to_right(kv.at[z, n], ring_recv.at[z, n]).start()
        to_left(kv.at[z, n], ring_recv.at[z, n]).start()

    own_q = rows_of(landing[:, 2])
    for n in range(GROUP):
        qs[n, r] = own_q[:, n * HEAD_DIM : (n + 1) * HEAD_DIM]
    for i in range(1, LAYER):
        remote(qs.at[:, r], qs.at[:, r], q_send, q_recv, layer_peer(i)).start()

    def queries_of(n):
        return qs[n].reshape(LAYER * rows, HEAD_DIM)

    def attend_text(n, carry):
        cols = pl.ds(pl.multiple_of(n * HEAD_DIM, HEAD_DIM), HEAD_DIM)
        scores = dot_nt(queries_of(n), text_k[:, cols])
        count = scores.shape[1]
        lane = lax.broadcasted_iota(jnp.int32, (1, count), 1)
        share = count // LAYER
        mine = (lane >= j * share) & (lane < (j + 1) * share) & (mask[...] == 1)
        mine = jnp.broadcast_to(mine, scores.shape)
        scores = jnp.where(mine, scores, NEG)
        top = jnp.max(scores, axis=1, keepdims=True)
        weights = jnp.where(mine, jnp.exp2((scores - top) * (SCORE_SCALE * LOG2E)), 0.0)
        total = jnp.sum(weights, axis=1, keepdims=True)
        shape = run_max.shape[1:]
        run_max[n] = jnp.broadcast_to(top, shape)
        run_sum[n] = jnp.broadcast_to(total, shape)
        run_acc[n] = dot(weights.astype(BF16), text_v[:, cols])
        return carry

    def absorb(n, one, other):
        keys_now = jnp.concatenate([kv[one, n, 0], kv[other, n, 0]], axis=0)
        values_now = jnp.concatenate([kv[one, n, 1], kv[other, n, 1]], axis=0)
        scores = dot_nt(queries_of(n), keys_now)
        old = run_max[n]
        top = jnp.maximum(old, jnp.max(scores, axis=1, keepdims=True))
        factor = jnp.exp2((old - top) * (SCORE_SCALE * LOG2E))
        weights = jnp.exp2((scores - top[:, : scores.shape[1]]) * (SCORE_SCALE * LOG2E))
        total = run_sum[n] * factor + jnp.sum(weights, axis=1, keepdims=True)
        acc = run_acc[n] * factor + dot(weights.astype(BF16), values_now)
        return top, total, acc

    def pass_on(step, n):
        one = slot_at(-step)
        other = slot_at(step)
        to_right(kv.at[one, n], ring_recv.at[one, n]).wait_recv()

        @pl.when(step < far - 1)
        def _():
            to_right(kv.at[one, n], ring_recv.at[one, n]).start()

        @pl.when(step == far - 1)
        def _():
            to_right(kv.at[one, n, 0], ring_recv.at[one, n], 1).start()

        to_left(kv.at[other, n], ring_recv.at[other, n]).wait_recv()

        @pl.when(step < far - 1)
        def _():
            to_left(kv.at[other, n], ring_recv.at[other, n]).start()

        @pl.when(step == far - 1)
        def _():
            to_left(kv.at[other, n, 1], far_recv.at[n], 1).start()

    def first_step(n, carry):
        pass_on(1, n)
        return carry

    lax.fori_loop(0, GROUP, first_step, 0)
    three = qs.at[:, pl.ds(0, LAYER - 1)]
    remote(three, three, q_send, q_recv, layer_peer(1)).wait_recv()
    for load in loads[4:7]:
        load.wait()
    lax.fori_loop(0, GROUP, attend_text, 0)

    def ring_step(step, carry):
        def one_head(n, inner):
            pass_on(step, n)
            return inner

        @pl.when(step < far)
        def _():
            lax.fori_loop(0, GROUP, one_head, 0)

        news = [absorb(n, slot_at(1 - step), slot_at(step - 1)) for n in range(GROUP)]
        for n, (top, total, acc) in enumerate(news):
            run_max[n] = top
            run_sum[n] = total
            run_acc[n] = acc
        return carry

    lax.fori_loop(2, far + 1, ring_step, 0)

    opposite = slot_at(far)
    lane = lax.broadcasted_iota(jnp.int32, (1, HEAD_DIM), 1)
    marks[...] = jnp.zeros_like(marks)

    def send_share(n):
        for i in range(1, LAYER):
            remote(
                o_stage.at[shifted(r, i, LAYER), n], o_in.at[j, n], o_send, o_recv, layer_peer(i)
            ).start()

    def last_step(n, carry):
        to_right(kv.at[opposite, n, 0], ring_recv.at[opposite, n]).wait_recv()
        to_left(kv.at[opposite, n, 1], far_recv.at[n]).wait_recv()
        top, total, acc = absorb(n, z, opposite)
        share = (acc / total).astype(BF16)
        for i in range(LAYER):
            o_stage[i, n] = share[i * rows : (i + 1) * rows]
        send_share(n)
        level = top * SCORE_SCALE + jnp.log(total)
        first = level.astype(BF16).astype(F32)
        second = (level - first).astype(BF16).astype(F32)
        third = level - first - second
        here = jnp.where(lane == 3 * n, first, marks[...])
        here = jnp.where(lane == 3 * n + 1, second, here)
        marks[...] = jnp.where(lane == 3 * n + 2, third, here)
        return carry

    lax.fori_loop(0, GROUP, last_step, 0)
    level_rows = marks[...].astype(BF16)
    for i in range(LAYER):
        o_stage[i, GROUP] = level_rows[i * rows : (i + 1) * rows]
    send_share(GROUP)
    o_in[j] = o_stage[r]

    for load in loads[7:]:
        load.wait()
    three = o_in.at[pl.ds(0, LAYER - 1)]
    remote(three, three, o_send, o_recv, layer_peer(1)).wait_recv()
    level_parts = [o_in[i, GROUP].astype(F32) for i in range(LAYER)]
    attended = []
    for n in range(GROUP):
        own_lanes = (lane >= 3 * n) & (lane < 3 * n + 3)
        levels = [
            jnp.sum(jnp.where(own_lanes, part, 0.0), axis=1, keepdims=True)
            for part in level_parts
        ]
        top = functools.reduce(jnp.maximum, levels)
        shares = [jnp.exp(level - top) for level in levels]
        total = functools.reduce(jnp.add, shares)
        mixed = functools.reduce(
            jnp.add, [share * o_in[i, n].astype(F32) for i, share in enumerate(shares)]
        )
        attended.append((mixed / total).astype(BF16))
    attended = jnp.concatenate(attended, axis=1)

    for part in range(rs_parts):
        product = dot(attended, out_w[:, part * part_cols : (part + 1) * part_cols])
        rs_stage[part] = product.reshape(heads, TOK, part_cols).astype(BF16)
        for i in range(heads):
            to = head_peer(i)
            remote(
                rs_stage.at[part, to[1]],
                rs_in.at[part, h],
                rs_send.at[part],
                rs_recv.at[part],
                to,
            ).start()
    pieces = []
    for part in range(rs_parts):
        cols = slice(part * part_cols, (part + 1) * part_cols)
        whole = rs_in.at[part]
        remote(whole, whole, rs_send.at[part], rs_recv.at[part], peer).wait_recv()
        projected = jnp.sum(rs_in[part].astype(F32), axis=0)
        stream = tokens[:, cols].astype(F32) + gate[:, cols] * (projected + out_bias[:, cols])
        rounded = stream.astype(BF16)
        block_out[:, cols] = rounded
        pieces.append(rounded.astype(F32))
    block_copy = pltpu.make_async_copy(block_out, block_hbm, out_sem.at[0])
    block_copy.start()

    normed_in = jnp.concatenate(pieces, axis=1)
    centered = normed_in - jnp.mean(normed_in, axis=1, keepdims=True)
    spread = jnp.mean(centered * centered, axis=1, keepdims=True)
    normed = centered * lax.rsqrt(spread + 1e-06)
    modulated = (normed * (1.0 + scale[...]) + shift[...]).astype(BF16)
    patches = (dot_nt(modulated, final_w[...]) + final_bias[...]) / LATENT_SCALE
    padded = jnp.concatenate([patches, jnp.zeros((TOK, HEAD_DIM - features), F32)], axis=1)
    lat[...] = padded.astype(BF16)

    for at, to in enumerate(halo_peers):
        remote(lat, halo.at[at], halo_send, halo_recv, to).start()
    tiles = {(0, 0): lat[...].astype(F32)}
    remote(halo, halo, halo_send, halo_recv, peer).wait_recv()
    for at, (dr, dc) in enumerate(halo_steps):
        tiles[(-dr, -dc)] = halo[at].astype(F32)

    def rolled(tile, by):
        return pltpu.roll(tile, by % HEAD_DIM, 1)

    top_edge, bottom_edge = s == 0, s == seqs - 1
    first_tile, last_tile = h == 0, h == heads - 1
    for dc in (-1, 0, 1):
        middle = tiles[(0, dc)]
        tiles[(-1, dc)] = jnp.where(top_edge, rolled(middle, 2), tiles[(-1, dc)])
        tiles[(1, dc)] = jnp.where(bottom_edge, rolled(middle, -2), tiles[(1, dc)])
    low = lane < features
    packed = {}
    for dr in (-1, 0, 1):
        middle = tiles[(dr, 0)]
        before = jnp.where(first_tile, rolled(middle, 1)[:1], tiles[(dr, -1)][TOK - 1 :])
        after = jnp.where(last_tile, rolled(middle, -1)[TOK - 1 :], tiles[(dr, 1)][:1])
        before = jnp.concatenate([before, middle[: TOK - 1]], axis=0)
        after = jnp.concatenate([middle[1:], after], axis=0)
        packed[(dr, 0)] = jnp.where(low, before, rolled(middle, features))
        packed[(dr, 1)] = jnp.where(low, middle, rolled(after, features))
    for parity in range(parities):
        up, side = parity // 2, parity % 2
        stacked = jnp.concatenate([packed[(up - 1, side)], packed[(up, side)]], axis=1)
        result = dot(stacked.astype(BF16), w_full[parity]) + conv_bias[...]
        for tile in range(pixels.shape[1]):
            pixels[up, tile, pl.ds(side, TOK, stride=2), :] = result[
                :, tile * HEAD_DIM : (tile + 1) * HEAD_DIM
            ]
    for tile in range(pixels.shape[1]):
        cols = slice(tile * HEAD_DIM, (tile + 1) * HEAD_DIM)
        decoded[:, :, cols] = pixels[:, tile].astype(BF16)
    decoded_copy = pltpu.make_async_copy(decoded, decoded_hbm, out_sem.at[1])
    decoded_copy.start()

    remote(stage, stage, a2a_send, a2a_recv, peer).wait_send()
    ring_all = kv.at[pl.ds(0, far - 1)]
    to_right(ring_all, far_recv.at[0]).wait_send()
    to_left(ring_all, far_recv.at[0]).wait_send()
    ring_half = kv.at[0, :, 0]
    to_right(ring_half, far_recv.at[0], 1).wait_send()
    to_left(ring_half, far_recv.at[0], 1).wait_send()
    three = qs.at[:, pl.ds(0, LAYER - 1)]
    remote(three, three, q_send, q_recv, peer).wait_send()
    three = o_stage.at[pl.ds(0, LAYER - 1)]
    remote(three, three, o_send, o_recv, peer).wait_send()
    for part in range(rs_parts):
        whole = rs_stage.at[part]
        remote(whole, whole, rs_send.at[part], rs_recv.at[part], peer).wait_send()
    remote(halo, halo, halo_send, halo_recv, peer).wait_send()
    block_copy.wait()
    decoded_copy.wait()


def body(seqs, heads, *args):
    (
        queries,
        keys,
        values,
        text_keys,
        text_values,
        text_mask,
        tokens,
        out_weight,
        out_bias,
        gate,
        shift,
        scale,
        final_weight,
        final_bias,
        conv_weight,
        conv_bias,
    ) = args
    dim = queries.shape[3]
    width = GROUP * HEAD_DIM
    text = text_keys.shape[0]
    layers = seqs // LAYER
    far = layers // 2
    rows = heads * TOK
    features = final_weight.shape[1]
    taps = 9 * LAT_CH
    channels = conv_weight.shape[4]
    rs_parts = 2
    operands = (
        queries.reshape(TOK, dim),
        keys.reshape(TOK, dim),
        values.reshape(TOK, dim),
        text_keys,
        text_values,
        text_mask.reshape(1, text),
        tokens.reshape(TOK, dim),
        out_weight,
        out_bias.reshape(1, dim),
        gate.reshape(1, dim),
        shift.reshape(1, dim),
        scale.reshape(1, dim),
        final_weight.T,
        final_bias.reshape(1, features),
        conv_weight.reshape(3 * taps, channels),
        conv_bias.reshape(1, channels),
    )
    copied = [pltpu.VMEM(x.shape, x.dtype) for x in operands]
    dma = pltpu.SemaphoreType.DMA
    anywhere = pl.BlockSpec(memory_space=pl.ANY)
    results = (
        jax.ShapeDtypeStruct((TOK, dim), BF16),
        jax.ShapeDtypeStruct((2, 2 * TOK, channels), BF16),
    )
    block_out, decoded = pl.pallas_call(
        functools.partial(kernel, seqs, heads),
        out_shape=results,
        in_specs=[anywhere] * len(operands),
        out_specs=(anywhere, anywhere),
        scratch_shapes=copied
        + [
            pltpu.VMEM((heads, 3, TOK, width), BF16),
            pltpu.VMEM((heads, 3, TOK, width), BF16),
            pltpu.VMEM((layers, GROUP, 2, rows, HEAD_DIM), BF16),
            pltpu.VMEM((GROUP, LAYER, rows, HEAD_DIM), BF16),
            pltpu.VMEM((GROUP, LAYER * rows, HEAD_DIM), F32),
            pltpu.VMEM((GROUP, LAYER * rows, HEAD_DIM), F32),
            pltpu.VMEM((GROUP, LAYER * rows, HEAD_DIM), F32),
            pltpu.VMEM((LAYER * rows, HEAD_DIM), F32),
            pltpu.VMEM((LAYER, GROUP + 1, rows, HEAD_DIM), BF16),
            pltpu.VMEM((LAYER, GROUP + 1, rows, HEAD_DIM), BF16),
            pltpu.VMEM((rs_parts, heads, TOK, dim // rs_parts), BF16),
            pltpu.VMEM((rs_parts, heads, TOK, dim // rs_parts), BF16),
            pltpu.VMEM((TOK, HEAD_DIM), BF16),
            pltpu.VMEM((8, TOK, HEAD_DIM), BF16),
            pltpu.VMEM((taps, channels), BF16),
            pltpu.VMEM((4, 4 * features, channels), BF16),
            pltpu.VMEM((2, channels // HEAD_DIM, 2 * TOK, HEAD_DIM), F32),
            pltpu.VMEM((TOK, dim), BF16),
            pltpu.VMEM((2, 2 * TOK, channels), BF16),
            dma((len(operands),)),
            dma((2,)),
            dma,
            dma,
            dma((2,)),
            dma((2,)),
            dma((layers, GROUP)),
            dma((GROUP,)),
            dma,
            dma,
            dma,
            dma,
            dma((rs_parts,)),
            dma((rs_parts,)),
            dma,
            dma,
        ],
        compiler_params=pltpu.CompilerParams(
            collective_id=0, has_side_effects=True, vmem_limit_bytes=60 * 1024 * 1024
        ),
        cost_estimate=pl.CostEstimate(
            flops=1_200_000_000, bytes_accessed=5_000_000, transcendentals=1_000_000
        ),
    )(*operands)
    return (
        block_out.reshape(1, TOK, 1, dim),
        decoded.reshape(1, 2, 2 * TOK, channels),
    )


def solution(mesh):
    seqs = mesh.shape["seq"]
    heads = mesh.shape["head"]
    spread = P("seq", "head", None, None)
    in_specs = (
        spread,
        spread,
        spread,
        P(None, "head"),
        P(None, "head"),
        P(),
        spread,
        P("head", None),
    ) + (P(),) * 8
    out_specs = (spread, P(None, "seq", "head", None))
    return jax.shard_map(
        functools.partial(body, seqs, heads),
        mesh=mesh,
        in_specs=in_specs,
        out_specs=out_specs,
        check_vma=False,
    )
```

```python
import functools

import jax
import jax.numpy as jnp
from jax import lax
from jax.experimental import pallas as pl
from jax.experimental.pallas import tpu as pltpu
from jax.sharding import PartitionSpec as P

HEAD_DIM = 128
GROUP = 3
LAT_CH = 16
TOK = 8
LAYER = 4
LATENT_SCALE = 0.476986
NEG = -1e30
SCORE_SCALE = HEAD_DIM ** (-0.5)
LOG2E = 1.4426950408889634
BF16 = jnp.bfloat16
F32 = jnp.float32
MESH = pl.DeviceIdType.MESH


def dot(a, b):
    return jnp.dot(a, b, preferred_element_type=F32)


def dot_tn(a, b):
    return lax.dot_general(a, b, (((0,), (0,)), ((), ())), preferred_element_type=F32)


def dot_nt(a, b):
    return lax.dot_general(a, b, (((1,), (1,)), ((), ())), preferred_element_type=F32)


def kernel(
    seqs,
    heads,
    q_hbm,
    k_hbm,
    v_hbm,
    text_k_hbm,
    text_v_hbm,
    mask_hbm,
    tokens_hbm,
    out_w_hbm,
    out_bias_hbm,
    gate_hbm,
    shift_hbm,
    scale_hbm,
    final_w_hbm,
    final_bias_hbm,
    conv_w_hbm,
    conv_bias_hbm,
    block_hbm,
    decoded_hbm,
    queries,
    keys,
    values,
    text_k,
    text_v,
    mask,
    tokens,
    out_w,
    out_bias,
    gate,
    shift,
    scale,
    final_w,
    final_bias,
    conv_w,
    conv_bias,
    kv_stage,
    q_stage,
    kv_in,
    q_in,
    kv,
    qs,
    q_turned,
    mask_column,
    run_max,
    run_sum,
    run_acc,
    marks,
    mark_stage,
    mark_in,
    shares,
    o_stage,
    o_in,
    rs_stage,
    rs_in,
    lat,
    halo,
    w_sum,
    w_full,
    pixels,
    block_out,
    decoded,
    local_sem,
    out_sem,
    kv_send,
    kv_recv,
    q_a2a_send,
    q_a2a_recv,
    ring_send,
    half_send,
    ring_recv,
    far_recv,
    q_send,
    q_recv,
    o_send,
    o_recv,
    mark_send,
    mark_recv,
    rs_send,
    rs_recv,
    halo_send,
    halo_recv,
):
    s = lax.axis_index("seq")
    h = lax.axis_index("head")
    layers = seqs // LAYER
    far = layers // 2
    z = s // LAYER
    j = lax.rem(s, LAYER)
    width = GROUP * HEAD_DIM
    dim = heads * width
    rows = heads * TOK
    rs_parts = rs_stage.shape[0]
    part_cols = dim // rs_parts

    def shifted(index, by, count):
        return lax.rem(index + (by % count), count)

    r = lax.rem(j + LAYER // 2, LAYER)

    def head_peer(i):
        return (z * LAYER + r, shifted(h, i, heads))

    def layer_peer(i):
        return (z * LAYER + shifted(j, i, LAYER), h)

    def slot_at(by):
        return lax.rem(z + by + layers, layers)

    right = (slot_at(1) * LAYER + j, h)
    left = (slot_at(-1) * LAYER + j, h)

    def remote(src, dst, send, recv, device):
        return pltpu.make_async_remote_copy(
            src_ref=src,
            dst_ref=dst,
            send_sem=send,
            recv_sem=recv,
            device_id=device,
            device_id_type=MESH,
        )

    pairs = (
        (k_hbm, keys),
        (v_hbm, values),
        (q_hbm, queries),
        (conv_w_hbm, conv_w),
        (text_k_hbm, text_k),
        (text_v_hbm, text_v),
        (mask_hbm, mask),
        (tokens_hbm, tokens),
        (out_w_hbm, out_w),
        (out_bias_hbm, out_bias),
        (gate_hbm, gate),
        (shift_hbm, shift),
        (scale_hbm, scale),
        (final_w_hbm, final_w),
        (final_bias_hbm, final_bias),
        (conv_bias_hbm, conv_bias),
    )
    loads = [
        pltpu.make_async_copy(src, dst, local_sem.at[i]) for i, (src, dst) in enumerate(pairs)
    ]

    halo_steps = [(dr, dc) for dr in (-1, 0, 1) for dc in (-1, 0, 1) if (dr, dc) != (0, 0)]
    halo_peers = [(shifted(s, dr, seqs), shifted(h, dc, heads)) for dr, dc in halo_steps]
    partners = [head_peer(i) for i in range(heads)]
    partners += [layer_peer(i) for i in range(1, LAYER)]
    partners += [right, left]
    partners += halo_peers
    for load in loads[:3]:
        load.start()
    barrier = pltpu.get_barrier_semaphore()
    for partner in partners:
        pl.semaphore_signal(barrier, inc=1, device_id=partner, device_id_type=MESH)
    group_cols = [slice(g * width, (g + 1) * width) for g in range(heads)]
    for at, whole in enumerate((keys, values)):
        loads[at].wait()
        for g, cols in enumerate(group_cols):
            kv_stage[g, at] = whole[:, cols]
    pl.semaphore_wait(barrier, len(partners))

    for i in range(heads):
        peer = head_peer(i)
        remote(kv_stage.at[peer[1]], kv_in.at[h], kv_send, kv_recv, peer).start()
    loads[2].wait()
    for g, cols in enumerate(group_cols):
        q_stage[g] = queries[:, cols]
    for i in range(heads):
        peer = head_peer(i)
        remote(q_stage.at[peer[1]], q_in.at[h], q_a2a_send, q_a2a_recv, peer).start()
    for load in loads[3:7]:
        load.start()

    def rows_of(block):
        return block.astype(F32).reshape(rows, width).astype(BF16)

    peer = head_peer(0)
    remote(kv_in, kv_in, kv_send, kv_recv, peer).wait_recv()
    own_k = rows_of(kv_in[:, 0])
    own_v = rows_of(kv_in[:, 1])
    for n in range(GROUP):
        cols = slice(n * HEAD_DIM, (n + 1) * HEAD_DIM)
        kv[z, n, 0] = own_k[:, cols]
        kv[z, n, 1] = own_v[:, cols]

    def to_right(ref, recv, send=0):
        return remote(ref, ref, ring_send.at[0] if send == 0 else half_send.at[0], recv, right)

    def to_left(ref, recv, send=0):
        return remote(ref, ref, ring_send.at[1] if send == 0 else half_send.at[1], recv, left)

    for n in range(GROUP):
        to_right(kv.at[z, n], ring_recv.at[z, n]).start()
        to_left(kv.at[z, n], ring_recv.at[z, n]).start()

    for load in loads[7:]:
        load.start()

    remote(q_in, q_in, q_a2a_send, q_a2a_recv, peer).wait_recv()
    own_q = rows_of(q_in[...])
    for n in range(GROUP):
        qs[n, r] = own_q[:, n * HEAD_DIM : (n + 1) * HEAD_DIM]
    for i in range(1, LAYER):
        remote(qs.at[:, r], qs.at[:, r], q_send, q_recv, layer_peer(i)).start()

    def attend_text(n):
        share = text_k.shape[0] // LAYER
        mine = pl.ds(pl.multiple_of(j * share, share), share)
        cols = slice(n * HEAD_DIM, (n + 1) * HEAD_DIM)
        scores = dot(text_k[mine, cols], q_turned[n])
        real = jnp.broadcast_to(mask_column[mine, :1] == 1.0, scores.shape)
        scores = jnp.where(real, scores, NEG)
        top = jnp.max(scores, axis=0, keepdims=True)
        weights = jnp.where(real, jnp.exp2((scores - top) * (SCORE_SCALE * LOG2E)), 0.0)
        run_max[n, :1] = top
        run_sum[n, :1] = jnp.sum(weights, axis=0, keepdims=True)
        run_acc[n] = dot_tn(text_v[mine, cols], weights.astype(BF16))

    def absorb(n, one, other):
        keys_now = jnp.concatenate([kv[one, n, 0], kv[other, n, 0]], axis=0)
        values_now = jnp.concatenate([kv[one, n, 1], kv[other, n, 1]], axis=0)
        scores = dot(keys_now, q_turned[n])
        old = run_max[n, :1]
        top = jnp.maximum(old, jnp.max(scores, axis=0, keepdims=True))
        factor = jnp.exp2((old - top) * (SCORE_SCALE * LOG2E))
        weights = jnp.exp2((scores - top) * (SCORE_SCALE * LOG2E))
        total = run_sum[n, :1] * factor + jnp.sum(weights, axis=0, keepdims=True)
        acc = run_acc[n] * factor + dot_tn(values_now, weights.astype(BF16))
        return top, total, acc

    taps = w_sum.shape[0]
    parities = w_full.shape[0]
    features = final_w.shape[0]

    def sum_taps():
        conv_all = conv_w[...].astype(F32)
        total = conv_all[:taps] + conv_all[taps : 2 * taps] + conv_all[2 * taps :]
        w_sum[...] = total.astype(BF16)

    def conv_weights(parity):
        up = parity // 2
        side = lax.rem(parity, 2)
        depth = w_full.shape[1]
        row = lax.broadcasted_iota(jnp.int32, (depth, taps), 0)
        col = lax.broadcasted_iota(jnp.int32, (depth, taps), 1)
        tap_i = 2 * (row >> 7) + ((row >> 1) & 1) + up - 1
        tap_j = 2 * ((row >> 6) & 1) + (row & 1) + side - 1
        inside = (tap_i >= 0) & (tap_i <= 2) & (tap_j >= 0) & (tap_j <= 2)
        source = (tap_i * 3 + tap_j) * LAT_CH + ((row & 63) >> 2)
        pick = jnp.where(inside & (source == col), 1.0, 0.0).astype(BF16)
        w_full[parity] = dot(pick, w_sum[...]).astype(BF16)

    def pass_on(step):
        one = slot_at(-step)
        other = slot_at(step)
        for n in range(GROUP):
            to_right(kv.at[one, n], ring_recv.at[one, n]).wait_recv()
            to_right(kv.at[one, n], ring_recv.at[one, n]).start()
            to_left(kv.at[other, n], ring_recv.at[other, n]).wait_recv()
            to_left(kv.at[other, n], ring_recv.at[other, n]).start()

    def pass_on_halves(step):
        one = slot_at(-step)
        other = slot_at(step)
        for n in range(GROUP):
            to_right(kv.at[one, n], ring_recv.at[one, n]).wait_recv()
            to_right(kv.at[one, n, 0], ring_recv.at[one, n], 1).start()
            to_left(kv.at[other, n], ring_recv.at[other, n]).wait_recv()
            to_left(kv.at[other, n, 1], far_recv.at[n], 1).start()

    pass_on(1)
    three = qs.at[:, pl.ds(0, LAYER - 1)]
    remote(three, three, q_send, q_recv, layer_peer(1)).wait_recv()
    for n in range(GROUP):
        q_turned[n] = qs[n].reshape(LAYER * rows, HEAD_DIM).T
    for load in loads[3:7]:
        load.wait()
    mask_column[...] = jnp.broadcast_to(mask[...].astype(F32), (TOK, mask.shape[1])).T
    for n in range(GROUP):
        attend_text(n)
    sum_taps()
    in_loop = min(parities, max(0, far - 3))

    def ring_step(step, carry):
        @pl.when(step < far - 1)
        def _():
            pass_on(step)

        @pl.when(step == far - 1)
        def _():
            pass_on_halves(step)

        news = [absorb(n, slot_at(1 - step), slot_at(step - 1)) for n in range(GROUP)]
        for n, (top, total, acc) in enumerate(news):
            run_max[n, :1] = top
            run_sum[n, :1] = total
            run_acc[n] = acc

        @pl.when(step - 2 < in_loop)
        def _():
            conv_weights(step - 2)

        return carry

    lax.fori_loop(2, far + 1, ring_step, 0)
    for parity in range(in_loop, parities):
        conv_weights(jnp.int32(parity))

    opposite = slot_at(far)
    marks[...] = jnp.zeros_like(marks)

    def share_of(i):
        return shifted(r, i, LAYER)

    def last_step(n, carry):
        to_right(kv.at[opposite, n, 0], ring_recv.at[opposite, n]).wait_recv()
        to_left(kv.at[opposite, n, 1], far_recv.at[n]).wait_recv()
        top, total, acc = absorb(n, z, opposite)
        share = (acc / total).T.astype(BF16)
        for i in range(LAYER):
            o_stage[i, n] = share[i * rows : (i + 1) * rows]
        for i in range(1, LAYER):
            remote(
                o_stage.at[share_of(i), n], o_in.at[j, n], o_send, o_recv, layer_peer(i)
            ).start()
        level = top * SCORE_SCALE + jnp.log(total)
        first = level.astype(BF16).astype(F32)
        second = (level - first).astype(BF16).astype(F32)
        marks[pl.ds(3 * n, 1)] = first
        marks[pl.ds(3 * n + 1, 1)] = second
        marks[pl.ds(3 * n + 2, 1)] = level - first - second
        return carry

    lax.fori_loop(0, GROUP, last_step, 0)
    level_rows = marks[...]
    lanes = mark_stage.shape[2]
    for i in range(LAYER):
        turned = level_rows if i == 0 else pltpu.roll(level_rows, (LAYER - i) * rows, 1)
        mark_stage[i] = turned[:, :lanes].astype(BF16)
    for i in range(1, LAYER):
        remote(
            mark_stage.at[share_of(i)], mark_in.at[j], mark_send, mark_recv, layer_peer(i)
        ).start()
    o_in[j] = o_stage[r]
    mark_in[j] = mark_stage[r]

    for load in loads[7:]:
        load.wait()
    three = o_in.at[pl.ds(0, LAYER - 1)]
    remote(three, three, o_send, o_recv, layer_peer(1)).wait_recv()
    three = mark_in.at[pl.ds(0, LAYER - 1)]
    remote(three, three, mark_send, mark_recv, layer_peer(1)).wait_recv()
    level_parts = [mark_in[i].astype(F32) for i in range(LAYER)]
    shares[...] = jnp.zeros_like(shares)
    for n in range(GROUP):
        levels = [
            part[3 * n : 3 * n + 1] + part[3 * n + 1 : 3 * n + 2] + part[3 * n + 2 : 3 * n + 3]
            for part in level_parts
        ]
        top = functools.reduce(jnp.maximum, levels)
        parts = [jnp.exp(level - top) for level in levels]
        total = functools.reduce(jnp.add, parts)
        for i, part in enumerate(parts):
            shares[n * LAYER + i : n * LAYER + i + 1] = part / total
    columns = shares[...].T[:rows]
    attended = []
    for n in range(GROUP):
        mixed = functools.reduce(
            jnp.add,
            [
                columns[:, n * LAYER + i : n * LAYER + i + 1] * o_in[i, n].astype(F32)
                for i in range(LAYER)
            ],
        )
        attended.append(mixed.astype(BF16))
    attended = jnp.concatenate(attended, axis=1)

    for part in range(rs_parts):
        product = dot(attended, out_w[:, part * part_cols : (part + 1) * part_cols])
        rs_stage[part] = product.reshape(heads, TOK, part_cols).astype(BF16)
        for i in range(heads):
            to = head_peer(i)
            remote(
                rs_stage.at[part, to[1]],
                rs_in.at[part, h],
                rs_send.at[part],
                rs_recv.at[part],
                to,
            ).start()
    pieces = []
    for part in range(rs_parts):
        cols = slice(part * part_cols, (part + 1) * part_cols)
        whole = rs_in.at[part]
        remote(whole, whole, rs_send.at[part], rs_recv.at[part], peer).wait_recv()
        projected = jnp.sum(rs_in[part].astype(F32), axis=0)
        stream = tokens[:, cols].astype(F32) + gate[:, cols] * (projected + out_bias[:, cols])
        rounded = stream.astype(BF16)
        block_out[:, cols] = rounded
        pieces.append(rounded.astype(F32))
    block_copy = pltpu.make_async_copy(block_out, block_hbm, out_sem.at[0])
    block_copy.start()

    normed_in = jnp.concatenate(pieces, axis=1)
    centered = normed_in - jnp.mean(normed_in, axis=1, keepdims=True)
    spread = jnp.mean(centered * centered, axis=1, keepdims=True)
    normed = centered * lax.rsqrt(spread + 1e-06)
    modulated = (normed * (1.0 + scale[...]) + shift[...]).astype(BF16)
    patches = (dot_nt(modulated, final_w[...]) + final_bias[...]) / LATENT_SCALE
    padded = jnp.concatenate([patches, jnp.zeros((TOK, HEAD_DIM - features), F32)], axis=1)
    lat[...] = padded.astype(BF16)

    for at, to in enumerate(halo_peers):
        remote(lat, halo.at[at], halo_send, halo_recv, to).start()
    tiles = {(0, 0): lat[...].astype(F32)}
    remote(halo, halo, halo_send, halo_recv, peer).wait_recv()
    for at, (dr, dc) in enumerate(halo_steps):
        tiles[(-dr, -dc)] = halo[at].astype(F32)

    def rolled(tile, by):
        return pltpu.roll(tile, by % HEAD_DIM, 1)

    top_edge, bottom_edge = s == 0, s == seqs - 1
    first_tile, last_tile = h == 0, h == heads - 1
    for dc in (-1, 0, 1):
        middle = tiles[(0, dc)]
        tiles[(-1, dc)] = jnp.where(top_edge, rolled(middle, 2), tiles[(-1, dc)])
        tiles[(1, dc)] = jnp.where(bottom_edge, rolled(middle, -2), tiles[(1, dc)])
    low = lax.broadcasted_iota(jnp.int32, (1, HEAD_DIM), 1) < features
    packed = {}
    for dr in (-1, 0, 1):
        middle = tiles[(dr, 0)]
        before = jnp.where(first_tile, rolled(middle, 1)[:1], tiles[(dr, -1)][TOK - 1 :])
        after = jnp.where(last_tile, rolled(middle, -1)[TOK - 1 :], tiles[(dr, 1)][:1])
        before = jnp.concatenate([before, middle[: TOK - 1]], axis=0)
        after = jnp.concatenate([middle[1:], after], axis=0)
        packed[(dr, 0)] = jnp.where(low, before, rolled(middle, features))
        packed[(dr, 1)] = jnp.where(low, middle, rolled(after, features))
    for parity in range(parities):
        up, side = parity // 2, parity % 2
        stacked = jnp.concatenate([packed[(up - 1, side)], packed[(up, side)]], axis=1)
        result = dot(stacked.astype(BF16), w_full[parity]) + conv_bias[...]
        for tile in range(pixels.shape[1]):
            pixels[up, tile, pl.ds(side, TOK, stride=2), :] = result[
                :, tile * HEAD_DIM : (tile + 1) * HEAD_DIM
            ]
    for tile in range(pixels.shape[1]):
        cols = slice(tile * HEAD_DIM, (tile + 1) * HEAD_DIM)
        decoded[:, :, cols] = pixels[:, tile].astype(BF16)
    decoded_copy = pltpu.make_async_copy(decoded, decoded_hbm, out_sem.at[1])
    decoded_copy.start()

    remote(kv_stage, kv_stage, kv_send, kv_recv, peer).wait_send()
    remote(q_stage, q_stage, q_a2a_send, q_a2a_recv, peer).wait_send()
    ring_all = kv.at[pl.ds(0, far - 1)]
    to_right(ring_all, far_recv.at[0]).wait_send()
    to_left(ring_all, far_recv.at[0]).wait_send()
    ring_half = kv.at[0, :, 0]
    to_right(ring_half, far_recv.at[0], 1).wait_send()
    to_left(ring_half, far_recv.at[0], 1).wait_send()
    three = qs.at[:, pl.ds(0, LAYER - 1)]
    remote(three, three, q_send, q_recv, peer).wait_send()
    three = o_stage.at[pl.ds(0, LAYER - 1)]
    remote(three, three, o_send, o_recv, peer).wait_send()
    three = mark_stage.at[pl.ds(0, LAYER - 1)]
    remote(three, three, mark_send, mark_recv, peer).wait_send()
    for part in range(rs_parts):
        whole = rs_stage.at[part]
        remote(whole, whole, rs_send.at[part], rs_recv.at[part], peer).wait_send()
    remote(halo, halo, halo_send, halo_recv, peer).wait_send()
    block_copy.wait()
    decoded_copy.wait()


def body(seqs, heads, *args):
    (
        queries,
        keys,
        values,
        text_keys,
        text_values,
        text_mask,
        tokens,
        out_weight,
        out_bias,
        gate,
        shift,
        scale,
        final_weight,
        final_bias,
        conv_weight,
        conv_bias,
    ) = args
    dim = queries.shape[3]
    width = GROUP * HEAD_DIM
    text = text_keys.shape[0]
    layers = seqs // LAYER
    far = layers // 2
    rows = heads * TOK
    features = final_weight.shape[1]
    taps = 9 * LAT_CH
    channels = conv_weight.shape[4]
    rs_parts = 2
    operands = (
        queries.reshape(TOK, dim),
        keys.reshape(TOK, dim),
        values.reshape(TOK, dim),
        text_keys,
        text_values,
        text_mask.reshape(1, text),
        tokens.reshape(TOK, dim),
        out_weight,
        out_bias.reshape(1, dim),
        gate.reshape(1, dim),
        shift.reshape(1, dim),
        scale.reshape(1, dim),
        final_weight.T,
        final_bias.reshape(1, features),
        conv_weight.reshape(3 * taps, channels),
        conv_bias.reshape(1, channels),
    )
    copied = [pltpu.VMEM(x.shape, x.dtype) for x in operands]
    dma = pltpu.SemaphoreType.DMA
    anywhere = pl.BlockSpec(memory_space=pl.ANY)
    results = (
        jax.ShapeDtypeStruct((TOK, dim), BF16),
        jax.ShapeDtypeStruct((2, 2 * TOK, channels), BF16),
    )
    block_out, decoded = pl.pallas_call(
        functools.partial(kernel, seqs, heads),
        out_shape=results,
        in_specs=[anywhere] * len(operands),
        out_specs=(anywhere, anywhere),
        scratch_shapes=copied
        + [
            pltpu.VMEM((heads, 2, TOK, width), BF16),
            pltpu.VMEM((heads, TOK, width), BF16),
            pltpu.VMEM((heads, 2, TOK, width), BF16),
            pltpu.VMEM((heads, TOK, width), BF16),
            pltpu.VMEM((layers, GROUP, 2, rows, HEAD_DIM), BF16),
            pltpu.VMEM((GROUP, LAYER, rows, HEAD_DIM), BF16),
            pltpu.VMEM((GROUP, HEAD_DIM, LAYER * rows), BF16),
            pltpu.VMEM((text, TOK), F32),
            pltpu.VMEM((GROUP, TOK, LAYER * rows), F32),
            pltpu.VMEM((GROUP, TOK, LAYER * rows), F32),
            pltpu.VMEM((GROUP, HEAD_DIM, LAYER * rows), F32),
            pltpu.VMEM((16, LAYER * rows), F32),
            pltpu.VMEM((LAYER, 16, min(HEAD_DIM, LAYER * rows)), BF16),
            pltpu.VMEM((LAYER, 16, min(HEAD_DIM, LAYER * rows)), BF16),
            pltpu.VMEM((16, min(HEAD_DIM, LAYER * rows)), F32),
            pltpu.VMEM((LAYER, GROUP, rows, HEAD_DIM), BF16),
            pltpu.VMEM((LAYER, GROUP, rows, HEAD_DIM), BF16),
            pltpu.VMEM((rs_parts, heads, TOK, dim // rs_parts), BF16),
            pltpu.VMEM((rs_parts, heads, TOK, dim // rs_parts), BF16),
            pltpu.VMEM((TOK, HEAD_DIM), BF16),
            pltpu.VMEM((8, TOK, HEAD_DIM), BF16),
            pltpu.VMEM((taps, channels), BF16),
            pltpu.VMEM((4, 4 * features, channels), BF16),
            pltpu.VMEM((2, channels // HEAD_DIM, 2 * TOK, HEAD_DIM), F32),
            pltpu.VMEM((TOK, dim), BF16),
            pltpu.VMEM((2, 2 * TOK, channels), BF16),
            dma((len(operands),)),
            dma((2,)),
            dma,
            dma,
            dma,
            dma,
            dma((2,)),
            dma((2,)),
            dma((layers, GROUP)),
            dma((GROUP,)),
            dma,
            dma,
            dma,
            dma,
            dma,
            dma,
            dma((rs_parts,)),
            dma((rs_parts,)),
            dma,
            dma,
        ],
        compiler_params=pltpu.CompilerParams(
            collective_id=0, has_side_effects=True, vmem_limit_bytes=60 * 1024 * 1024
        ),
        cost_estimate=pl.CostEstimate(
            flops=1_200_000_000, bytes_accessed=5_000_000, transcendentals=1_000_000
        ),
    )(*operands)
    return (
        block_out.reshape(1, TOK, 1, dim),
        decoded.reshape(1, 2, 2 * TOK, channels),
    )


def solution(mesh):
    seqs = mesh.shape["seq"]
    heads = mesh.shape["head"]
    spread = P("seq", "head", None, None)
    in_specs = (
        spread,
        spread,
        spread,
        P(None, "head"),
        P(None, "head"),
        P(),
        spread,
        P("head", None),
    ) + (P(),) * 8
    out_specs = (spread, P(None, "seq", "head", None))
    return jax.shard_map(
        functools.partial(body, seqs, heads),
        mesh=mesh,
        in_specs=in_specs,
        out_specs=out_specs,
        check_vma=False,
    )
```

```python
import functools

import jax
import jax.numpy as jnp
from jax import lax
from jax.experimental import pallas as pl
from jax.experimental.pallas import tpu as pltpu
from jax.sharding import PartitionSpec as P

HEAD_DIM = 128
GROUP = 3
LAT_CH = 16
TOK = 8
LAYER = 4
LATENT_SCALE = 0.476986
NEG = -1e30
SCORE_SCALE = HEAD_DIM ** (-0.5)
LOG2E = 1.4426950408889634
BF16 = jnp.bfloat16
F32 = jnp.float32
MESH = pl.DeviceIdType.MESH


def dot(a, b):
    return jnp.dot(a, b, preferred_element_type=F32)


def dot_tn(a, b):
    return lax.dot_general(a, b, (((0,), (0,)), ((), ())), preferred_element_type=F32)


def dot_nt(a, b):
    return lax.dot_general(a, b, (((1,), (1,)), ((), ())), preferred_element_type=F32)


def kernel(
    seqs,
    heads,
    q_hbm,
    k_hbm,
    v_hbm,
    text_k_hbm,
    text_v_hbm,
    mask_hbm,
    tokens_hbm,
    out_w_hbm,
    out_bias_hbm,
    gate_hbm,
    shift_hbm,
    scale_hbm,
    final_w_hbm,
    final_bias_hbm,
    conv_w_hbm,
    conv_bias_hbm,
    block_hbm,
    decoded_hbm,
    queries,
    keys,
    values,
    text_k,
    text_v,
    mask,
    tokens,
    out_w,
    out_bias,
    gate,
    shift,
    scale,
    final_w,
    final_bias,
    conv_w,
    conv_bias,
    kv_stage,
    q_stage,
    kv_in,
    q_in,
    kv,
    qs,
    q_turned,
    mask_column,
    run_max,
    run_sum,
    run_acc,
    marks,
    mark_stage,
    mark_in,
    shares,
    o_stage,
    o_in,
    rs_stage,
    rs_in,
    lat,
    halo,
    w_sum,
    w_full,
    pixels,
    block_out,
    decoded,
    local_sem,
    out_sem,
    kv_send,
    kv_recv,
    q_a2a_send,
    q_a2a_recv,
    ring_send,
    half_send,
    ring_recv,
    q_send,
    q_recv,
    o_send,
    o_recv,
    mark_send,
    mark_recv,
    rs_send,
    rs_recv,
    halo_send,
    halo_recv,
):
    s = lax.axis_index("seq")
    h = lax.axis_index("head")
    layers = seqs // LAYER
    far = layers // 2
    z = s // LAYER
    j = lax.rem(s, LAYER)
    width = GROUP * HEAD_DIM
    dim = heads * width
    rows = heads * TOK
    rs_parts = rs_stage.shape[0]
    part_cols = dim // rs_parts

    def shifted(index, by, count):
        return lax.rem(index + (by % count), count)

    r = lax.rem(j + LAYER // 2, LAYER)

    def head_peer(i):
        return (z * LAYER + r, shifted(h, i, heads))

    def layer_peer(i):
        return (z * LAYER + shifted(j, i, LAYER), h)

    def slot_at(by):
        return lax.rem(z + by + layers, layers)

    right = (slot_at(1) * LAYER + j, h)
    left = (slot_at(-1) * LAYER + j, h)

    def remote(src, dst, send, recv, device):
        return pltpu.make_async_remote_copy(
            src_ref=src,
            dst_ref=dst,
            send_sem=send,
            recv_sem=recv,
            device_id=device,
            device_id_type=MESH,
        )

    pairs = (
        (k_hbm, keys),
        (v_hbm, values),
        (q_hbm, queries),
        (conv_w_hbm, conv_w),
        (text_k_hbm, text_k),
        (text_v_hbm, text_v),
        (mask_hbm, mask),
        (tokens_hbm, tokens),
        (out_w_hbm, out_w),
        (out_bias_hbm, out_bias),
        (gate_hbm, gate),
        (shift_hbm, shift),
        (scale_hbm, scale),
        (final_w_hbm, final_w),
        (final_bias_hbm, final_bias),
        (conv_bias_hbm, conv_bias),
    )
    loads = [
        pltpu.make_async_copy(src, dst, local_sem.at[i]) for i, (src, dst) in enumerate(pairs)
    ]

    halo_steps = [(dr, dc) for dr in (-1, 0, 1) for dc in (-1, 0, 1) if (dr, dc) != (0, 0)]
    halo_peers = [(shifted(s, dr, seqs), shifted(h, dc, heads)) for dr, dc in halo_steps]
    partners = [head_peer(i) for i in range(heads)]
    partners += [layer_peer(i) for i in range(1, LAYER)]
    partners += [right, left]
    partners += halo_peers
    for load in loads[:3]:
        load.start()
    barrier = pltpu.get_barrier_semaphore()
    for partner in partners:
        pl.semaphore_signal(barrier, inc=1, device_id=partner, device_id_type=MESH)
    group_cols = [slice(g * width, (g + 1) * width) for g in range(heads)]
    for at, whole in enumerate((keys, values)):
        loads[at].wait()
        for g, cols in enumerate(group_cols):
            kv_stage[g, at] = whole[:, cols]
    pl.semaphore_wait(barrier, len(partners))

    for i in range(heads):
        peer = head_peer(i)
        remote(kv_stage.at[peer[1]], kv_in.at[h], kv_send, kv_recv, peer).start()
    loads[2].wait()
    for g, cols in enumerate(group_cols):
        q_stage[g] = queries[:, cols]
    for i in range(heads):
        peer = head_peer(i)
        remote(q_stage.at[peer[1]], q_in.at[h], q_a2a_send, q_a2a_recv, peer).start()
    for load in loads[3:7]:
        load.start()

    def rows_of(block):
        return block.astype(F32).reshape(rows, width).astype(BF16)

    peer = head_peer(0)
    remote(kv_in, kv_in, kv_send, kv_recv, peer).wait_recv()
    own_k = rows_of(kv_in[:, 0])
    own_v = rows_of(kv_in[:, 1])
    for n in range(GROUP):
        cols = slice(n * HEAD_DIM, (n + 1) * HEAD_DIM)
        kv[z, n, 0] = own_k[:, cols]
        kv[z, n, 1] = own_v[:, cols]

    def to_right(ref, recv, send=0):
        return remote(ref, ref, ring_send.at[0] if send == 0 else half_send.at[0], recv, right)

    def to_left(ref, recv, send=0):
        return remote(ref, ref, ring_send.at[1] if send == 0 else half_send.at[1], recv, left)

    pieces_of = [(n, part) for n in range(GROUP) for part in range(2)]
    for n, part in pieces_of:
        to_right(kv.at[z, n, part], ring_recv.at[z, n, part]).start()
        to_left(kv.at[z, n, part], ring_recv.at[z, n, part]).start()

    for load in loads[7:]:
        load.start()

    remote(q_in, q_in, q_a2a_send, q_a2a_recv, peer).wait_recv()
    own_q = rows_of(q_in[...])
    for n in range(GROUP):
        qs[n, r] = own_q[:, n * HEAD_DIM : (n + 1) * HEAD_DIM]
    for i in range(1, LAYER):
        remote(qs.at[:, r], qs.at[:, r], q_send, q_recv, layer_peer(i)).start()

    def attend_text(n):
        share = text_k.shape[0] // LAYER
        mine = pl.ds(pl.multiple_of(j * share, share), share)
        cols = slice(n * HEAD_DIM, (n + 1) * HEAD_DIM)
        scores = dot(text_k[mine, cols], q_turned[n])
        real = jnp.broadcast_to(mask_column[mine, :1] == 1.0, scores.shape)
        scores = jnp.where(real, scores, NEG)
        top = jnp.max(scores, axis=0, keepdims=True)
        weights = jnp.where(real, jnp.exp2((scores - top) * (SCORE_SCALE * LOG2E)), 0.0)
        run_max[n, :1] = top
        run_sum[n, :1] = jnp.sum(weights, axis=0, keepdims=True)
        run_acc[n] = dot_tn(text_v[mine, cols], weights.astype(BF16))

    def absorb(n, one, other):
        keys_now = jnp.concatenate([kv[one, n, 0], kv[other, n, 0]], axis=0)
        values_now = jnp.concatenate([kv[one, n, 1], kv[other, n, 1]], axis=0)
        scores = dot(keys_now, q_turned[n])
        old = run_max[n, :1]
        top = jnp.maximum(old, jnp.max(scores, axis=0, keepdims=True))
        factor = jnp.exp2((old - top) * (SCORE_SCALE * LOG2E))
        weights = jnp.exp2((scores - top) * (SCORE_SCALE * LOG2E))
        total = run_sum[n, :1] * factor + jnp.sum(weights, axis=0, keepdims=True)
        acc = run_acc[n] * factor + dot_tn(values_now, weights.astype(BF16))
        return top, total, acc

    taps = w_sum.shape[0]
    parities = w_full.shape[0]
    features = final_w.shape[0]

    def sum_taps():
        conv_all = conv_w[...].astype(F32)
        total = conv_all[:taps] + conv_all[taps : 2 * taps] + conv_all[2 * taps :]
        w_sum[...] = total.astype(BF16)

    def conv_weights(parity):
        up = parity // 2
        side = lax.rem(parity, 2)
        depth = w_full.shape[1]
        row = lax.broadcasted_iota(jnp.int32, (depth, taps), 0)
        col = lax.broadcasted_iota(jnp.int32, (depth, taps), 1)
        tap_i = 2 * (row >> 7) + ((row >> 1) & 1) + up - 1
        tap_j = 2 * ((row >> 6) & 1) + (row & 1) + side - 1
        inside = (tap_i >= 0) & (tap_i <= 2) & (tap_j >= 0) & (tap_j <= 2)
        source = (tap_i * 3 + tap_j) * LAT_CH + ((row & 63) >> 2)
        pick = jnp.where(inside & (source == col), 1.0, 0.0).astype(BF16)
        w_full[parity] = dot(pick, w_sum[...]).astype(BF16)

    def pass_on(step):
        one = slot_at(-step)
        other = slot_at(step)
        for n, part in pieces_of:
            copy = to_right(kv.at[one, n, part], ring_recv.at[one, n, part])
            copy.wait_recv()
            copy.start()
            copy = to_left(kv.at[other, n, part], ring_recv.at[other, n, part])
            copy.wait_recv()
            copy.start()

    def pass_on_halves(step):
        one = slot_at(-step)
        other = slot_at(step)
        for n, part in pieces_of:
            copy = to_right(kv.at[one, n, part], ring_recv.at[one, n, part], 1)
            copy.wait_recv()
            if part == 0:
                copy.start()
            copy = to_left(kv.at[other, n, part], ring_recv.at[other, n, part], 1)
            copy.wait_recv()
            if part == 1:
                copy.start()

    pass_on(1)
    three = qs.at[:, pl.ds(0, LAYER - 1)]
    remote(three, three, q_send, q_recv, layer_peer(1)).wait_recv()
    for n in range(GROUP):
        q_turned[n] = qs[n].reshape(LAYER * rows, HEAD_DIM).T
    for load in loads[3:7]:
        load.wait()
    mask_column[...] = jnp.broadcast_to(mask[...].astype(F32), (TOK, mask.shape[1])).T
    for n in range(GROUP):
        attend_text(n)
    sum_taps()
    in_loop = min(parities, max(0, far - 3))

    def ring_step(step, carry):
        @pl.when(step < far - 1)
        def _():
            pass_on(step)

        @pl.when(step == far - 1)
        def _():
            pass_on_halves(step)

        news = [absorb(n, slot_at(1 - step), slot_at(step - 1)) for n in range(GROUP)]
        for n, (top, total, acc) in enumerate(news):
            run_max[n, :1] = top
            run_sum[n, :1] = total
            run_acc[n] = acc

        @pl.when(step - 2 < in_loop)
        def _():
            conv_weights(step - 2)

        return carry

    lax.fori_loop(2, far + 1, ring_step, 0)
    for parity in range(in_loop, parities):
        conv_weights(jnp.int32(parity))

    opposite = slot_at(far)
    marks[...] = jnp.zeros_like(marks)

    def share_of(i):
        return shifted(r, i, LAYER)

    def last_step(n, carry):
        to_right(kv.at[opposite, n, 0], ring_recv.at[opposite, n, 0]).wait_recv()
        to_left(kv.at[opposite, n, 1], ring_recv.at[opposite, n, 1]).wait_recv()
        top, total, acc = absorb(n, z, opposite)
        share = (acc / total).T.astype(BF16)
        for i in range(LAYER):
            o_stage[i, n] = share[i * rows : (i + 1) * rows]
        for i in range(1, LAYER):
            remote(
                o_stage.at[share_of(i), n], o_in.at[j, n], o_send, o_recv, layer_peer(i)
            ).start()
        level = top * SCORE_SCALE + jnp.log(total)
        first = level.astype(BF16).astype(F32)
        second = (level - first).astype(BF16).astype(F32)
        marks[pl.ds(3 * n, 1)] = first
        marks[pl.ds(3 * n + 1, 1)] = second
        marks[pl.ds(3 * n + 2, 1)] = level - first - second
        return carry

    lax.fori_loop(0, GROUP, last_step, 0)
    level_rows = marks[...]
    lanes = mark_stage.shape[2]
    for i in range(LAYER):
        turned = level_rows if i == 0 else pltpu.roll(level_rows, (LAYER - i) * rows, 1)
        mark_stage[i] = turned[:, :lanes].astype(BF16)
    for i in range(1, LAYER):
        remote(
            mark_stage.at[share_of(i)], mark_in.at[j], mark_send, mark_recv, layer_peer(i)
        ).start()
    o_in[j] = o_stage[r]
    mark_in[j] = mark_stage[r]

    for load in loads[7:]:
        load.wait()
    three = o_in.at[pl.ds(0, LAYER - 1)]
    remote(three, three, o_send, o_recv, layer_peer(1)).wait_recv()
    three = mark_in.at[pl.ds(0, LAYER - 1)]
    remote(three, three, mark_send, mark_recv, layer_peer(1)).wait_recv()
    level_parts = [mark_in[i].astype(F32) for i in range(LAYER)]
    shares[...] = jnp.zeros_like(shares)
    for n in range(GROUP):
        levels = [
            part[3 * n : 3 * n + 1] + part[3 * n + 1 : 3 * n + 2] + part[3 * n + 2 : 3 * n + 3]
            for part in level_parts
        ]
        top = functools.reduce(jnp.maximum, levels)
        parts = [jnp.exp(level - top) for level in levels]
        total = functools.reduce(jnp.add, parts)
        for i, part in enumerate(parts):
            shares[n * LAYER + i : n * LAYER + i + 1] = part / total
    columns = shares[...].T[:rows]
    attended = []
    for n in range(GROUP):
        mixed = functools.reduce(
            jnp.add,
            [
                columns[:, n * LAYER + i : n * LAYER + i + 1] * o_in[i, n].astype(F32)
                for i in range(LAYER)
            ],
        )
        attended.append(mixed.astype(BF16))
    attended = jnp.concatenate(attended, axis=1)

    for part in range(rs_parts):
        product = dot(attended, out_w[:, part * part_cols : (part + 1) * part_cols])
        rs_stage[part] = product.reshape(heads, TOK, part_cols).astype(BF16)
        for i in range(heads):
            to = head_peer(i)
            remote(
                rs_stage.at[part, to[1]],
                rs_in.at[part, h],
                rs_send.at[part],
                rs_recv.at[part],
                to,
            ).start()
    pieces = []
    for part in range(rs_parts):
        cols = slice(part * part_cols, (part + 1) * part_cols)
        whole = rs_in.at[part]
        remote(whole, whole, rs_send.at[part], rs_recv.at[part], peer).wait_recv()
        projected = jnp.sum(rs_in[part].astype(F32), axis=0)
        stream = tokens[:, cols].astype(F32) + gate[:, cols] * (projected + out_bias[:, cols])
        rounded = stream.astype(BF16)
        block_out[:, cols] = rounded
        pieces.append(rounded.astype(F32))
    block_copy = pltpu.make_async_copy(block_out, block_hbm, out_sem.at[0])
    block_copy.start()

    normed_in = jnp.concatenate(pieces, axis=1)
    centered = normed_in - jnp.mean(normed_in, axis=1, keepdims=True)
    spread = jnp.mean(centered * centered, axis=1, keepdims=True)
    normed = centered * lax.rsqrt(spread + 1e-06)
    modulated = (normed * (1.0 + scale[...]) + shift[...]).astype(BF16)
    patches = (dot_nt(modulated, final_w[...]) + final_bias[...]) / LATENT_SCALE
    padded = jnp.concatenate([patches, jnp.zeros((TOK, HEAD_DIM - features), F32)], axis=1)
    lat[...] = padded.astype(BF16)

    for at, to in enumerate(halo_peers):
        remote(lat, halo.at[at], halo_send, halo_recv, to).start()
    tiles = {(0, 0): lat[...].astype(F32)}
    remote(halo, halo, halo_send, halo_recv, peer).wait_recv()
    for at, (dr, dc) in enumerate(halo_steps):
        tiles[(-dr, -dc)] = halo[at].astype(F32)

    def rolled(tile, by):
        return pltpu.roll(tile, by % HEAD_DIM, 1)

    top_edge, bottom_edge = s == 0, s == seqs - 1
    first_tile, last_tile = h == 0, h == heads - 1
    for dc in (-1, 0, 1):
        middle = tiles[(0, dc)]
        tiles[(-1, dc)] = jnp.where(top_edge, rolled(middle, 2), tiles[(-1, dc)])
        tiles[(1, dc)] = jnp.where(bottom_edge, rolled(middle, -2), tiles[(1, dc)])
    low = lax.broadcasted_iota(jnp.int32, (1, HEAD_DIM), 1) < features
    packed = {}
    for dr in (-1, 0, 1):
        middle = tiles[(dr, 0)]
        before = jnp.where(first_tile, rolled(middle, 1)[:1], tiles[(dr, -1)][TOK - 1 :])
        after = jnp.where(last_tile, rolled(middle, -1)[TOK - 1 :], tiles[(dr, 1)][:1])
        before = jnp.concatenate([before, middle[: TOK - 1]], axis=0)
        after = jnp.concatenate([middle[1:], after], axis=0)
        packed[(dr, 0)] = jnp.where(low, before, rolled(middle, features))
        packed[(dr, 1)] = jnp.where(low, middle, rolled(after, features))
    for parity in range(parities):
        up, side = parity // 2, parity % 2
        stacked = jnp.concatenate([packed[(up - 1, side)], packed[(up, side)]], axis=1)
        result = dot(stacked.astype(BF16), w_full[parity]) + conv_bias[...]
        for tile in range(pixels.shape[1]):
            pixels[up, tile, pl.ds(side, TOK, stride=2), :] = result[
                :, tile * HEAD_DIM : (tile + 1) * HEAD_DIM
            ]
    for tile in range(pixels.shape[1]):
        cols = slice(tile * HEAD_DIM, (tile + 1) * HEAD_DIM)
        decoded[:, :, cols] = pixels[:, tile].astype(BF16)
    decoded_copy = pltpu.make_async_copy(decoded, decoded_hbm, out_sem.at[1])
    decoded_copy.start()

    remote(kv_stage, kv_stage, kv_send, kv_recv, peer).wait_send()
    remote(q_stage, q_stage, q_a2a_send, q_a2a_recv, peer).wait_send()
    ring_all = kv.at[pl.ds(0, far - 1)]
    to_right(ring_all, ring_recv.at[0, 0, 0]).wait_send()
    to_left(ring_all, ring_recv.at[0, 0, 0]).wait_send()
    ring_half = kv.at[0, :, 0]
    to_right(ring_half, ring_recv.at[0, 0, 0], 1).wait_send()
    to_left(ring_half, ring_recv.at[0, 0, 0], 1).wait_send()
    three = qs.at[:, pl.ds(0, LAYER - 1)]
    remote(three, three, q_send, q_recv, peer).wait_send()
    three = o_stage.at[pl.ds(0, LAYER - 1)]
    remote(three, three, o_send, o_recv, peer).wait_send()
    three = mark_stage.at[pl.ds(0, LAYER - 1)]
    remote(three, three, mark_send, mark_recv, peer).wait_send()
    for part in range(rs_parts):
        whole = rs_stage.at[part]
        remote(whole, whole, rs_send.at[part], rs_recv.at[part], peer).wait_send()
    remote(halo, halo, halo_send, halo_recv, peer).wait_send()
    block_copy.wait()
    decoded_copy.wait()


def hand_over(block_in, decoded_in, block_to, decoded_to, block, decoded, sem):
    rooms = ((block_in, block, block_to), (decoded_in, decoded, decoded_to))
    loads = [pltpu.make_async_copy(a, b, sem.at[i]) for i, (a, b, _) in enumerate(rooms)]
    stores = [pltpu.make_async_copy(b, c, sem.at[2 + i]) for i, (_, b, c) in enumerate(rooms)]
    for load in loads:
        load.start()
    for load, store in zip(loads, stores):
        load.wait()
        store.start()
    for store in stores:
        store.wait()


def body(seqs, heads, *args):
    (
        queries,
        keys,
        values,
        text_keys,
        text_values,
        text_mask,
        tokens,
        out_weight,
        out_bias,
        gate,
        shift,
        scale,
        final_weight,
        final_bias,
        conv_weight,
        conv_bias,
    ) = args
    dim = queries.shape[3]
    width = GROUP * HEAD_DIM
    text = text_keys.shape[0]
    layers = seqs // LAYER
    far = layers // 2
    rows = heads * TOK
    features = final_weight.shape[1]
    taps = 9 * LAT_CH
    channels = conv_weight.shape[4]
    rs_parts = 2
    operands = (
        queries.reshape(TOK, dim),
        keys.reshape(TOK, dim),
        values.reshape(TOK, dim),
        text_keys,
        text_values,
        text_mask.reshape(1, text),
        tokens.reshape(TOK, dim),
        out_weight,
        out_bias.reshape(1, dim),
        gate.reshape(1, dim),
        shift.reshape(1, dim),
        scale.reshape(1, dim),
        final_weight.T,
        final_bias.reshape(1, features),
        conv_weight.reshape(3 * taps, channels),
        conv_bias.reshape(1, channels),
    )
    copied = [pltpu.VMEM(x.shape, x.dtype) for x in operands]
    dma = pltpu.SemaphoreType.DMA
    anywhere = pl.BlockSpec(memory_space=pl.ANY)
    results = (
        jax.ShapeDtypeStruct((TOK, dim), BF16),
        jax.ShapeDtypeStruct((2, 2 * TOK, channels), BF16),
    )
    block_out, decoded = pl.pallas_call(
        functools.partial(kernel, seqs, heads),
        out_shape=results,
        in_specs=[anywhere] * len(operands),
        out_specs=(anywhere, anywhere),
        scratch_shapes=copied
        + [
            pltpu.VMEM((heads, 2, TOK, width), BF16),
            pltpu.VMEM((heads, TOK, width), BF16),
            pltpu.VMEM((heads, 2, TOK, width), BF16),
            pltpu.VMEM((heads, TOK, width), BF16),
            pltpu.VMEM((layers, GROUP, 2, rows, HEAD_DIM), BF16),
            pltpu.VMEM((GROUP, LAYER, rows, HEAD_DIM), BF16),
            pltpu.VMEM((GROUP, HEAD_DIM, LAYER * rows), BF16),
            pltpu.VMEM((text, TOK), F32),
            pltpu.VMEM((GROUP, TOK, LAYER * rows), F32),
            pltpu.VMEM((GROUP, TOK, LAYER * rows), F32),
            pltpu.VMEM((GROUP, HEAD_DIM, LAYER * rows), F32),
            pltpu.VMEM((16, LAYER * rows), F32),
            pltpu.VMEM((LAYER, 16, min(HEAD_DIM, LAYER * rows)), BF16),
            pltpu.VMEM((LAYER, 16, min(HEAD_DIM, LAYER * rows)), BF16),
            pltpu.VMEM((16, min(HEAD_DIM, LAYER * rows)), F32),
            pltpu.VMEM((LAYER, GROUP, rows, HEAD_DIM), BF16),
            pltpu.VMEM((LAYER, GROUP, rows, HEAD_DIM), BF16),
            pltpu.VMEM((rs_parts, heads, TOK, dim // rs_parts), BF16),
            pltpu.VMEM((rs_parts, heads, TOK, dim // rs_parts), BF16),
            pltpu.VMEM((TOK, HEAD_DIM), BF16),
            pltpu.VMEM((8, TOK, HEAD_DIM), BF16),
            pltpu.VMEM((taps, channels), BF16),
            pltpu.VMEM((4, 4 * features, channels), BF16),
            pltpu.VMEM((2, channels // HEAD_DIM, 2 * TOK, HEAD_DIM), F32),
            pltpu.VMEM((TOK, dim), BF16),
            pltpu.VMEM((2, 2 * TOK, channels), BF16),
            dma((len(operands),)),
            dma((2,)),
            dma,
            dma,
            dma,
            dma,
            dma((2,)),
            dma((2,)),
            dma((layers, GROUP, 2)),
            dma,
            dma,
            dma,
            dma,
            dma,
            dma,
            dma((rs_parts,)),
            dma((rs_parts,)),
            dma,
            dma,
        ],
        compiler_params=pltpu.CompilerParams(
            collective_id=0, has_side_effects=True, vmem_limit_bytes=60 * 1024 * 1024
        ),
        cost_estimate=pl.CostEstimate(
            flops=1_200_000_000, bytes_accessed=5_000_000, transcendentals=1_000_000
        ),
    )(*operands)
    block_out, decoded = pl.pallas_call(
        hand_over,
        out_shape=results,
        in_specs=[anywhere] * 2,
        out_specs=(anywhere, anywhere),
        scratch_shapes=[pltpu.VMEM(x.shape, x.dtype) for x in results] + [dma((4,))],
        compiler_params=pltpu.CompilerParams(vmem_limit_bytes=60 * 1024 * 1024),
    )(block_out, decoded)
    return (
        block_out.reshape(1, TOK, 1, dim),
        decoded.reshape(1, 2, 2 * TOK, channels),
    )


def solution(mesh):
    seqs = mesh.shape["seq"]
    heads = mesh.shape["head"]
    spread = P("seq", "head", None, None)
    in_specs = (
        spread,
        spread,
        spread,
        P(None, "head"),
        P(None, "head"),
        P(),
        spread,
        P("head", None),
    ) + (P(),) * 8
    out_specs = (spread, P(None, "seq", "head", None))
    return jax.shard_map(
        functools.partial(body, seqs, heads),
        mesh=mesh,
        in_specs=in_specs,
        out_specs=out_specs,
        check_vma=False,
    )
```

```python
import functools

import jax
import jax.numpy as jnp
from jax import lax
from jax.experimental import pallas as pl
from jax.experimental.pallas import tpu as pltpu
from jax.sharding import PartitionSpec as P

HEAD_DIM = 128
GROUP = 3
LAT_CH = 16
TOK = 8
LAYER = 4
LATENT_SCALE = 0.476986
NEG = -1e30
SCORE_SCALE = HEAD_DIM ** (-0.5)
LOG2E = 1.4426950408889634
BF16 = jnp.bfloat16
F32 = jnp.float32
MESH = pl.DeviceIdType.MESH


def dot(a, b):
    return jnp.dot(a, b, preferred_element_type=F32)


def dot_tn(a, b):
    return lax.dot_general(a, b, (((0,), (0,)), ((), ())), preferred_element_type=F32)


def dot_nt(a, b):
    return lax.dot_general(a, b, (((1,), (1,)), ((), ())), preferred_element_type=F32)


def kernel(
    seqs,
    heads,
    q_hbm,
    k_hbm,
    v_hbm,
    text_k_hbm,
    text_v_hbm,
    mask_hbm,
    tokens_hbm,
    out_w_hbm,
    out_bias_hbm,
    gate_hbm,
    shift_hbm,
    scale_hbm,
    final_w_hbm,
    final_bias_hbm,
    conv_w_hbm,
    conv_bias_hbm,
    block_hbm,
    decoded_hbm,
    queries,
    keys,
    values,
    text_k,
    text_v,
    mask,
    tokens,
    out_w,
    out_bias,
    gate,
    shift,
    scale,
    final_w,
    final_bias,
    conv_w,
    conv_bias,
    kv_stage,
    q_stage,
    kv_in,
    q_in,
    kv,
    qs,
    q_turned,
    mask_column,
    run_max,
    run_sum,
    run_acc,
    marks,
    mark_stage,
    mark_in,
    shares,
    o_stage,
    o_in,
    rs_stage,
    rs_in,
    lat,
    halo,
    w_sum,
    w_full,
    pixels,
    block_out,
    decoded,
    local_sem,
    out_sem,
    kv_send,
    kv_recv,
    q_a2a_send,
    q_a2a_recv,
    ring_send,
    half_send,
    ring_recv,
    q_send,
    q_recv,
    o_send,
    o_recv,
    mark_send,
    mark_recv,
    rs_send,
    rs_recv,
    halo_send,
    halo_recv,
):
    s = lax.axis_index("seq")
    h = lax.axis_index("head")
    layers = seqs // LAYER
    far = layers // 2
    z = s // LAYER
    j = lax.rem(s, LAYER)
    width = GROUP * HEAD_DIM
    dim = heads * width
    rows = heads * TOK
    rs_parts = rs_stage.shape[0]
    part_cols = dim // rs_parts

    def shifted(index, by, count):
        return lax.rem(index + (by % count), count)

    r = lax.rem(j + LAYER // 2, LAYER)

    def head_peer(i):
        return (z * LAYER + r, shifted(h, i, heads))

    def layer_peer(i):
        return (z * LAYER + shifted(j, i, LAYER), h)

    def slot_at(by):
        return lax.rem(z + by + layers, layers)

    right = (slot_at(1) * LAYER + j, h)
    left = (slot_at(-1) * LAYER + j, h)

    def remote(src, dst, send, recv, device):
        return pltpu.make_async_remote_copy(
            src_ref=src,
            dst_ref=dst,
            send_sem=send,
            recv_sem=recv,
            device_id=device,
            device_id_type=MESH,
        )

    pairs = (
        (k_hbm, keys),
        (v_hbm, values),
        (q_hbm, queries),
        (conv_w_hbm, conv_w),
        (text_k_hbm, text_k),
        (text_v_hbm, text_v),
        (mask_hbm, mask),
        (tokens_hbm, tokens),
        (out_w_hbm, out_w),
        (out_bias_hbm, out_bias),
        (gate_hbm, gate),
        (shift_hbm, shift),
        (scale_hbm, scale),
        (final_w_hbm, final_w),
        (final_bias_hbm, final_bias),
        (conv_bias_hbm, conv_bias),
    )
    loads = [
        pltpu.make_async_copy(src, dst, local_sem.at[i]) for i, (src, dst) in enumerate(pairs)
    ]

    halo_steps = [(dr, dc) for dr in (-1, 0, 1) for dc in (-1, 0, 1) if (dr, dc) != (0, 0)]
    halo_peers = [(shifted(s, dr, seqs), shifted(h, dc, heads)) for dr, dc in halo_steps]
    partners = [head_peer(i) for i in range(heads)]
    partners += [layer_peer(i) for i in range(1, LAYER)]
    partners += [right, left]
    partners += halo_peers
    for load in loads[:3]:
        load.start()
    barrier = pltpu.get_barrier_semaphore()
    for partner in partners:
        pl.semaphore_signal(barrier, inc=1, device_id=partner, device_id_type=MESH)
    group_cols = [slice(g * width, (g + 1) * width) for g in range(heads)]
    for at, whole in enumerate((keys, values)):
        loads[at].wait()
        for g, cols in enumerate(group_cols):
            kv_stage[g, at] = whole[:, cols]
    pl.semaphore_wait(barrier, len(partners))

    for i in range(heads):
        peer = head_peer(i)
        remote(kv_stage.at[peer[1]], kv_in.at[h], kv_send, kv_recv, peer).start()
    loads[2].wait()
    for g, cols in enumerate(group_cols):
        q_stage[g] = queries[:, cols]
    for i in range(heads):
        peer = head_peer(i)
        remote(q_stage.at[peer[1]], q_in.at[h], q_a2a_send, q_a2a_recv, peer).start()
    for load in loads[3:7]:
        load.start()

    taps = w_sum.shape[0]
    parities = w_full.shape[0]
    features = final_w.shape[0]

    def sum_taps():
        conv_all = conv_w[...].astype(F32)
        total = conv_all[:taps] + conv_all[taps : 2 * taps] + conv_all[2 * taps :]
        w_sum[...] = total.astype(BF16)

    def conv_weights(parity):
        up = parity // 2
        side = lax.rem(parity, 2)
        depth = w_full.shape[1]
        row = lax.broadcasted_iota(jnp.int32, (depth, taps), 0)
        col = lax.broadcasted_iota(jnp.int32, (depth, taps), 1)
        tap_i = 2 * (row >> 7) + ((row >> 1) & 1) + up - 1
        tap_j = 2 * ((row >> 6) & 1) + (row & 1) + side - 1
        inside = (tap_i >= 0) & (tap_i <= 2) & (tap_j >= 0) & (tap_j <= 2)
        source = (tap_i * 3 + tap_j) * LAT_CH + ((row & 63) >> 2)
        pick = jnp.where(inside & (source == col), 1.0, 0.0).astype(BF16)
        w_full[parity] = dot(pick, w_sum[...]).astype(BF16)

    def rows_of(block):
        return block.astype(F32).reshape(rows, width).astype(BF16)

    peer = head_peer(0)
    remote(kv_in, kv_in, kv_send, kv_recv, peer).wait_recv()
    own_k = rows_of(kv_in[:, 0])
    own_v = rows_of(kv_in[:, 1])
    for n in range(GROUP):
        cols = slice(n * HEAD_DIM, (n + 1) * HEAD_DIM)
        kv[z, n, 0] = own_k[:, cols]
        kv[z, n, 1] = own_v[:, cols]

    def to_right(ref, recv, send=0):
        return remote(ref, ref, ring_send.at[0] if send == 0 else half_send.at[0], recv, right)

    def to_left(ref, recv, send=0):
        return remote(ref, ref, ring_send.at[1] if send == 0 else half_send.at[1], recv, left)

    pieces_of = [(n, part) for n in range(GROUP) for part in range(2)]

    def first_piece(at):
        n, part = pieces_of[at]
        to_right(kv.at[z, n, part], ring_recv.at[z, n, part]).start()
        to_left(kv.at[z, n, part], ring_recv.at[z, n, part]).start()

    first_piece(0)
    for load in loads[7:]:
        load.start()
    first_piece(1)

    remote(q_in, q_in, q_a2a_send, q_a2a_recv, peer).wait_recv()
    own_q = rows_of(q_in[...])
    for n in range(GROUP):
        qs[n, r] = own_q[:, n * HEAD_DIM : (n + 1) * HEAD_DIM]
    for i in range(1, LAYER):
        remote(qs.at[:, r], qs.at[:, r], q_send, q_recv, layer_peer(i)).start()
    first_piece(2)
    loads[3].wait()
    sum_taps()
    first_piece(3)
    conv_weights(jnp.int32(0))
    first_piece(4)
    conv_weights(jnp.int32(1))
    first_piece(5)
    made = 2

    def attend_text(n):
        share = text_k.shape[0] // LAYER
        mine = pl.ds(pl.multiple_of(j * share, share), share)
        cols = slice(n * HEAD_DIM, (n + 1) * HEAD_DIM)
        scores = dot(text_k[mine, cols], q_turned[n])
        real = jnp.broadcast_to(mask_column[mine, :1] == 1.0, scores.shape)
        scores = jnp.where(real, scores, NEG)
        top = jnp.max(scores, axis=0, keepdims=True)
        weights = jnp.where(real, jnp.exp2((scores - top) * (SCORE_SCALE * LOG2E)), 0.0)
        run_max[n, :1] = top
        run_sum[n, :1] = jnp.sum(weights, axis=0, keepdims=True)
        run_acc[n] = dot_tn(text_v[mine, cols], weights.astype(BF16))

    def absorb(n, one, other):
        keys_now = jnp.concatenate([kv[one, n, 0], kv[other, n, 0]], axis=0)
        values_now = jnp.concatenate([kv[one, n, 1], kv[other, n, 1]], axis=0)
        scores = dot(keys_now, q_turned[n])
        old = run_max[n, :1]
        top = jnp.maximum(old, jnp.max(scores, axis=0, keepdims=True))
        factor = jnp.exp2((old - top) * (SCORE_SCALE * LOG2E))
        weights = jnp.exp2((scores - top) * (SCORE_SCALE * LOG2E))
        total = run_sum[n, :1] * factor + jnp.sum(weights, axis=0, keepdims=True)
        acc = run_acc[n] * factor + dot_tn(values_now, weights.astype(BF16))
        return top, total, acc

    def pass_on(step, n):
        one = slot_at(-step)
        other = slot_at(step)
        for part in range(2):
            copy = to_right(kv.at[one, n, part], ring_recv.at[one, n, part])
            copy.wait_recv()
            copy.start()
            copy = to_left(kv.at[other, n, part], ring_recv.at[other, n, part])
            copy.wait_recv()
            copy.start()

    def pass_on_halves(step, n):
        one = slot_at(-step)
        other = slot_at(step)
        for part in range(2):
            copy = to_right(kv.at[one, n, part], ring_recv.at[one, n, part], 1)
            copy.wait_recv()
            if part == 0:
                copy.start()
            copy = to_left(kv.at[other, n, part], ring_recv.at[other, n, part], 1)
            copy.wait_recv()
            if part == 1:
                copy.start()

    pass_on(1, 0)
    three = qs.at[:, pl.ds(0, LAYER - 1)]
    remote(three, three, q_send, q_recv, layer_peer(1)).wait_recv()
    for n in range(GROUP):
        q_turned[n] = qs[n].reshape(LAYER * rows, HEAD_DIM).T
    pass_on(1, 1)
    for load in loads[4:7]:
        load.wait()
    mask_column[...] = jnp.broadcast_to(mask[...].astype(F32), (TOK, mask.shape[1])).T
    attend_text(0)
    pass_on(1, 2)
    for n in range(1, GROUP):
        attend_text(n)
    in_loop = min(parities - made, max(0, far - 3))

    def ring_step(step, carry):
        for n in range(GROUP):
            @pl.when(step < far - 1)
            def _():
                pass_on(step, n)

            @pl.when(step == far - 1)
            def _():
                pass_on_halves(step, n)

            top, total, acc = absorb(n, slot_at(1 - step), slot_at(step - 1))
            run_max[n, :1] = top
            run_sum[n, :1] = total
            run_acc[n] = acc

        @pl.when(step - 2 < in_loop)
        def _():
            conv_weights(step - 2 + made)

        return carry

    lax.fori_loop(2, far + 1, ring_step, 0)
    for parity in range(made + in_loop, parities):
        conv_weights(jnp.int32(parity))

    opposite = slot_at(far)
    marks[...] = jnp.zeros_like(marks)

    def share_of(i):
        return shifted(r, i, LAYER)

    def last_step(n, carry):
        to_right(kv.at[opposite, n, 0], ring_recv.at[opposite, n, 0]).wait_recv()
        to_left(kv.at[opposite, n, 1], ring_recv.at[opposite, n, 1]).wait_recv()
        top, total, acc = absorb(n, z, opposite)
        share = (acc / total).T.astype(BF16)
        for i in range(LAYER):
            o_stage[i, n] = share[i * rows : (i + 1) * rows]
        for i in range(1, LAYER):
            remote(
                o_stage.at[share_of(i), n], o_in.at[j, n], o_send, o_recv, layer_peer(i)
            ).start()
        level = top * SCORE_SCALE + jnp.log(total)
        first = level.astype(BF16).astype(F32)
        second = (level - first).astype(BF16).astype(F32)
        marks[pl.ds(3 * n, 1)] = first
        marks[pl.ds(3 * n + 1, 1)] = second
        marks[pl.ds(3 * n + 2, 1)] = level - first - second
        return carry

    lax.fori_loop(0, GROUP, last_step, 0)
    level_rows = marks[...]
    lanes = mark_stage.shape[2]
    for i in range(LAYER):
        turned = level_rows if i == 0 else pltpu.roll(level_rows, (LAYER - i) * rows, 1)
        mark_stage[i] = turned[:, :lanes].astype(BF16)
    for i in range(1, LAYER):
        remote(
            mark_stage.at[share_of(i)], mark_in.at[j], mark_send, mark_recv, layer_peer(i)
        ).start()
    o_in[j] = o_stage[r]
    mark_in[j] = mark_stage[r]

    for load in loads[7:]:
        load.wait()
    three = o_in.at[pl.ds(0, LAYER - 1)]
    remote(three, three, o_send, o_recv, layer_peer(1)).wait_recv()
    three = mark_in.at[pl.ds(0, LAYER - 1)]
    remote(three, three, mark_send, mark_recv, layer_peer(1)).wait_recv()
    level_parts = [mark_in[i].astype(F32) for i in range(LAYER)]
    shares[...] = jnp.zeros_like(shares)
    for n in range(GROUP):
        levels = [
            part[3 * n : 3 * n + 1] + part[3 * n + 1 : 3 * n + 2] + part[3 * n + 2 : 3 * n + 3]
            for part in level_parts
        ]
        top = functools.reduce(jnp.maximum, levels)
        parts = [jnp.exp(level - top) for level in levels]
        total = functools.reduce(jnp.add, parts)
        for i, part in enumerate(parts):
            shares[n * LAYER + i : n * LAYER + i + 1] = part / total
    columns = shares[...].T[:rows]
    attended = []
    for n in range(GROUP):
        mixed = functools.reduce(
            jnp.add,
            [
                columns[:, n * LAYER + i : n * LAYER + i + 1] * o_in[i, n].astype(F32)
                for i in range(LAYER)
            ],
        )
        attended.append(mixed.astype(BF16))
    attended = jnp.concatenate(attended, axis=1)

    for part in range(rs_parts):
        product = dot(attended, out_w[:, part * part_cols : (part + 1) * part_cols])
        rs_stage[part] = product.reshape(heads, TOK, part_cols).astype(BF16)
        for i in range(heads):
            to = head_peer(i)
            remote(
                rs_stage.at[part, to[1]],
                rs_in.at[part, h],
                rs_send.at[part],
                rs_recv.at[part],
                to,
            ).start()
    pieces = []
    for part in range(rs_parts):
        cols = slice(part * part_cols, (part + 1) * part_cols)
        whole = rs_in.at[part]
        remote(whole, whole, rs_send.at[part], rs_recv.at[part], peer).wait_recv()
        projected = jnp.sum(rs_in[part].astype(F32), axis=0)
        stream = tokens[:, cols].astype(F32) + gate[:, cols] * (projected + out_bias[:, cols])
        rounded = stream.astype(BF16)
        block_out[:, cols] = rounded
        pieces.append(rounded.astype(F32))
    block_copy = pltpu.make_async_copy(block_out, block_hbm, out_sem.at[0])
    block_copy.start()

    normed_in = jnp.concatenate(pieces, axis=1)
    centered = normed_in - jnp.mean(normed_in, axis=1, keepdims=True)
    spread = jnp.mean(centered * centered, axis=1, keepdims=True)
    normed = centered * lax.rsqrt(spread + 1e-06)
    modulated = (normed * (1.0 + scale[...]) + shift[...]).astype(BF16)
    patches = (dot_nt(modulated, final_w[...]) + final_bias[...]) / LATENT_SCALE
    padded = jnp.concatenate([patches, jnp.zeros((TOK, HEAD_DIM - features), F32)], axis=1)
    lat[...] = padded.astype(BF16)

    for at, to in enumerate(halo_peers):
        remote(lat, halo.at[at], halo_send, halo_recv, to).start()
    tiles = {(0, 0): lat[...].astype(F32)}
    remote(halo, halo, halo_send, halo_recv, peer).wait_recv()
    for at, (dr, dc) in enumerate(halo_steps):
        tiles[(-dr, -dc)] = halo[at].astype(F32)

    def rolled(tile, by):
        return pltpu.roll(tile, by % HEAD_DIM, 1)

    top_edge, bottom_edge = s == 0, s == seqs - 1
    first_tile, last_tile = h == 0, h == heads - 1
    for dc in (-1, 0, 1):
        middle = tiles[(0, dc)]
        tiles[(-1, dc)] = jnp.where(top_edge, rolled(middle, 2), tiles[(-1, dc)])
        tiles[(1, dc)] = jnp.where(bottom_edge, rolled(middle, -2), tiles[(1, dc)])
    low = lax.broadcasted_iota(jnp.int32, (1, HEAD_DIM), 1) < features
    packed = {}
    for dr in (-1, 0, 1):
        middle = tiles[(dr, 0)]
        before = jnp.where(first_tile, rolled(middle, 1)[:1], tiles[(dr, -1)][TOK - 1 :])
        after = jnp.where(last_tile, rolled(middle, -1)[TOK - 1 :], tiles[(dr, 1)][:1])
        before = jnp.concatenate([before, middle[: TOK - 1]], axis=0)
        after = jnp.concatenate([middle[1:], after], axis=0)
        packed[(dr, 0)] = jnp.where(low, before, rolled(middle, features))
        packed[(dr, 1)] = jnp.where(low, middle, rolled(after, features))
    for parity in range(parities):
        up, side = parity // 2, parity % 2
        stacked = jnp.concatenate([packed[(up - 1, side)], packed[(up, side)]], axis=1)
        result = dot(stacked.astype(BF16), w_full[parity]) + conv_bias[...]
        for tile in range(pixels.shape[1]):
            pixels[up, tile, pl.ds(side, TOK, stride=2), :] = result[
                :, tile * HEAD_DIM : (tile + 1) * HEAD_DIM
            ]
    for tile in range(pixels.shape[1]):
        cols = slice(tile * HEAD_DIM, (tile + 1) * HEAD_DIM)
        decoded[:, :, cols] = pixels[:, tile].astype(BF16)
    decoded_copy = pltpu.make_async_copy(decoded, decoded_hbm, out_sem.at[1])
    decoded_copy.start()

    remote(kv_stage, kv_stage, kv_send, kv_recv, peer).wait_send()
    remote(q_stage, q_stage, q_a2a_send, q_a2a_recv, peer).wait_send()
    ring_all = kv.at[pl.ds(0, far - 1)]
    to_right(ring_all, ring_recv.at[0, 0, 0]).wait_send()
    to_left(ring_all, ring_recv.at[0, 0, 0]).wait_send()
    ring_half = kv.at[0, :, 0]
    to_right(ring_half, ring_recv.at[0, 0, 0], 1).wait_send()
    to_left(ring_half, ring_recv.at[0, 0, 0], 1).wait_send()
    three = qs.at[:, pl.ds(0, LAYER - 1)]
    remote(three, three, q_send, q_recv, peer).wait_send()
    three = o_stage.at[pl.ds(0, LAYER - 1)]
    remote(three, three, o_send, o_recv, peer).wait_send()
    three = mark_stage.at[pl.ds(0, LAYER - 1)]
    remote(three, three, mark_send, mark_recv, peer).wait_send()
    for part in range(rs_parts):
        whole = rs_stage.at[part]
        remote(whole, whole, rs_send.at[part], rs_recv.at[part], peer).wait_send()
    remote(halo, halo, halo_send, halo_recv, peer).wait_send()
    block_copy.wait()
    decoded_copy.wait()


def hand_over(block_in, decoded_in, block_to, decoded_to, block, decoded, sem):
    rooms = ((block_in, block, block_to), (decoded_in, decoded, decoded_to))
    loads = [pltpu.make_async_copy(a, b, sem.at[i]) for i, (a, b, _) in enumerate(rooms)]
    stores = [pltpu.make_async_copy(b, c, sem.at[2 + i]) for i, (_, b, c) in enumerate(rooms)]
    for load in loads:
        load.start()
    for load, store in zip(loads, stores):
        load.wait()
        store.start()
    for store in stores:
        store.wait()


def body(seqs, heads, *args):
    (
        queries,
        keys,
        values,
        text_keys,
        text_values,
        text_mask,
        tokens,
        out_weight,
        out_bias,
        gate,
        shift,
        scale,
        final_weight,
        final_bias,
        conv_weight,
        conv_bias,
    ) = args
    dim = queries.shape[3]
    width = GROUP * HEAD_DIM
    text = text_keys.shape[0]
    layers = seqs // LAYER
    far = layers // 2
    rows = heads * TOK
    features = final_weight.shape[1]
    taps = 9 * LAT_CH
    channels = conv_weight.shape[4]
    rs_parts = 2
    operands = (
        queries.reshape(TOK, dim),
        keys.reshape(TOK, dim),
        values.reshape(TOK, dim),
        text_keys,
        text_values,
        text_mask.reshape(1, text),
        tokens.reshape(TOK, dim),
        out_weight,
        out_bias.reshape(1, dim),
        gate.reshape(1, dim),
        shift.reshape(1, dim),
        scale.reshape(1, dim),
        final_weight.T,
        final_bias.reshape(1, features),
        conv_weight.reshape(3 * taps, channels),
        conv_bias.reshape(1, channels),
    )
    copied = [pltpu.VMEM(x.shape, x.dtype) for x in operands]
    dma = pltpu.SemaphoreType.DMA
    anywhere = pl.BlockSpec(memory_space=pl.ANY)
    results = (
        jax.ShapeDtypeStruct((TOK, dim), BF16),
        jax.ShapeDtypeStruct((2, 2 * TOK, channels), BF16),
    )
    block_out, decoded = pl.pallas_call(
        functools.partial(kernel, seqs, heads),
        out_shape=results,
        in_specs=[anywhere] * len(operands),
        out_specs=(anywhere, anywhere),
        scratch_shapes=copied
        + [
            pltpu.VMEM((heads, 2, TOK, width), BF16),
            pltpu.VMEM((heads, TOK, width), BF16),
            pltpu.VMEM((heads, 2, TOK, width), BF16),
            pltpu.VMEM((heads, TOK, width), BF16),
            pltpu.VMEM((layers, GROUP, 2, rows, HEAD_DIM), BF16),
            pltpu.VMEM((GROUP, LAYER, rows, HEAD_DIM), BF16),
            pltpu.VMEM((GROUP, HEAD_DIM, LAYER * rows), BF16),
            pltpu.VMEM((text, TOK), F32),
            pltpu.VMEM((GROUP, TOK, LAYER * rows), F32),
            pltpu.VMEM((GROUP, TOK, LAYER * rows), F32),
            pltpu.VMEM((GROUP, HEAD_DIM, LAYER * rows), F32),
            pltpu.VMEM((16, LAYER * rows), F32),
            pltpu.VMEM((LAYER, 16, min(HEAD_DIM, LAYER * rows)), BF16),
            pltpu.VMEM((LAYER, 16, min(HEAD_DIM, LAYER * rows)), BF16),
            pltpu.VMEM((16, min(HEAD_DIM, LAYER * rows)), F32),
            pltpu.VMEM((LAYER, GROUP, rows, HEAD_DIM), BF16),
            pltpu.VMEM((LAYER, GROUP, rows, HEAD_DIM), BF16),
            pltpu.VMEM((rs_parts, heads, TOK, dim // rs_parts), BF16),
            pltpu.VMEM((rs_parts, heads, TOK, dim // rs_parts), BF16),
            pltpu.VMEM((TOK, HEAD_DIM), BF16),
            pltpu.VMEM((8, TOK, HEAD_DIM), BF16),
            pltpu.VMEM((taps, channels), BF16),
            pltpu.VMEM((4, 4 * features, channels), BF16),
            pltpu.VMEM((2, channels // HEAD_DIM, 2 * TOK, HEAD_DIM), F32),
            pltpu.VMEM((TOK, dim), BF16),
            pltpu.VMEM((2, 2 * TOK, channels), BF16),
            dma((len(operands),)),
            dma((2,)),
            dma,
            dma,
            dma,
            dma,
            dma((2,)),
            dma((2,)),
            dma((layers, GROUP, 2)),
            dma,
            dma,
            dma,
            dma,
            dma,
            dma,
            dma((rs_parts,)),
            dma((rs_parts,)),
            dma,
            dma,
        ],
        compiler_params=pltpu.CompilerParams(
            collective_id=0, has_side_effects=True, vmem_limit_bytes=60 * 1024 * 1024
        ),
        cost_estimate=pl.CostEstimate(
            flops=1_200_000_000, bytes_accessed=5_000_000, transcendentals=1_000_000
        ),
    )(*operands)
    block_out, decoded = pl.pallas_call(
        hand_over,
        out_shape=results,
        in_specs=[anywhere] * 2,
        out_specs=(anywhere, anywhere),
        scratch_shapes=[pltpu.VMEM(x.shape, x.dtype) for x in results] + [dma((4,))],
        compiler_params=pltpu.CompilerParams(vmem_limit_bytes=60 * 1024 * 1024),
    )(block_out, decoded)
    return (
        block_out.reshape(1, TOK, 1, dim),
        decoded.reshape(1, 2, 2 * TOK, channels),
    )


def solution(mesh):
    seqs = mesh.shape["seq"]
    heads = mesh.shape["head"]
    spread = P("seq", "head", None, None)
    in_specs = (
        spread,
        spread,
        spread,
        P(None, "head"),
        P(None, "head"),
        P(),
        spread,
        P("head", None),
    ) + (P(),) * 8
    out_specs = (spread, P(None, "seq", "head", None))
    return jax.shard_map(
        functools.partial(body, seqs, heads),
        mesh=mesh,
        in_specs=in_specs,
        out_specs=out_specs,
        check_vma=False,
    )
```

```python
import functools

import jax
import jax.numpy as jnp
from jax import lax
from jax.experimental import pallas as pl
from jax.experimental.pallas import tpu as pltpu
from jax.sharding import PartitionSpec as P

HEAD_DIM = 128
GROUP = 3
LAT_CH = 16
TOK = 8
LAYER = 4
STRIDE = 3
LATENT_SCALE = 0.476986
NEG = -1e30
SCORE_SCALE = HEAD_DIM ** (-0.5)
LOG2E = 1.4426950408889634
BF16 = jnp.bfloat16
F32 = jnp.float32
MESH = pl.DeviceIdType.MESH


def dot(a, b):
    return jnp.dot(a, b, preferred_element_type=F32)


def dot_tn(a, b):
    return lax.dot_general(a, b, (((0,), (0,)), ((), ())), preferred_element_type=F32)


def dot_nt(a, b):
    return lax.dot_general(a, b, (((1,), (1,)), ((), ())), preferred_element_type=F32)


def kernel(
    seqs,
    heads,
    q_hbm,
    k_hbm,
    v_hbm,
    text_k_hbm,
    text_v_hbm,
    mask_hbm,
    tokens_hbm,
    out_w_hbm,
    out_bias_hbm,
    gate_hbm,
    shift_hbm,
    scale_hbm,
    final_w_hbm,
    final_bias_hbm,
    conv_w_hbm,
    conv_bias_hbm,
    block_hbm,
    decoded_hbm,
    queries,
    keys,
    values,
    text_k,
    text_v,
    mask,
    tokens,
    out_w,
    out_bias,
    gate,
    shift,
    scale,
    final_w,
    final_bias,
    conv_w,
    conv_bias,
    kv_stage,
    q_stage,
    kv_in,
    q_in,
    kv,
    qs,
    q_turned,
    mask_column,
    run_max,
    run_sum,
    run_acc,
    marks,
    mark_stage,
    mark_in,
    shares,
    o_stage,
    o_in,
    rs_stage,
    rs_in,
    lat,
    halo,
    w_sum,
    w_full,
    pixels,
    block_out,
    decoded,
    local_sem,
    out_sem,
    kv_send,
    kv_recv,
    q_a2a_send,
    q_a2a_recv,
    ring_send,
    half_send,
    long_send,
    ring_recv,
    q_send,
    q_recv,
    o_send,
    o_recv,
    mark_send,
    mark_recv,
    rs_send,
    rs_recv,
    halo_send,
    halo_recv,
):
    s = lax.axis_index("seq")
    h = lax.axis_index("head")
    layers = seqs // LAYER
    far = layers // 2
    z = s // LAYER
    j = lax.rem(s, LAYER)
    width = GROUP * HEAD_DIM
    dim = heads * width
    rows = heads * TOK
    rs_parts = rs_stage.shape[0]
    part_cols = dim // rs_parts

    def shifted(index, by, count):
        return lax.rem(index + (by % count), count)

    r = lax.rem(j + LAYER // 2, LAYER)

    def head_peer(i):
        return (z * LAYER + r, shifted(h, i, heads))

    def layer_peer(i):
        return (z * LAYER + shifted(j, i, LAYER), h)

    def slot_at(by):
        return lax.rem(z + by + layers, layers)

    def ring_peer(by):
        return (slot_at(by) * LAYER + j, h)

    right, left = ring_peer(1), ring_peer(-1)
    far_right, far_left = ring_peer(STRIDE), ring_peer(-STRIDE)

    def remote(src, dst, send, recv, device):
        return pltpu.make_async_remote_copy(
            src_ref=src,
            dst_ref=dst,
            send_sem=send,
            recv_sem=recv,
            device_id=device,
            device_id_type=MESH,
        )

    pairs = (
        (k_hbm, keys),
        (v_hbm, values),
        (q_hbm, queries),
        (conv_w_hbm, conv_w),
        (text_k_hbm, text_k),
        (text_v_hbm, text_v),
        (mask_hbm, mask),
        (tokens_hbm, tokens),
        (out_w_hbm, out_w),
        (out_bias_hbm, out_bias),
        (gate_hbm, gate),
        (shift_hbm, shift),
        (scale_hbm, scale),
        (final_w_hbm, final_w),
        (final_bias_hbm, final_bias),
        (conv_bias_hbm, conv_bias),
    )
    loads = [
        pltpu.make_async_copy(src, dst, local_sem.at[i]) for i, (src, dst) in enumerate(pairs)
    ]

    halo_steps = [(dr, dc) for dr in (-1, 0, 1) for dc in (-1, 0, 1) if (dr, dc) != (0, 0)]
    halo_peers = [(shifted(s, dr, seqs), shifted(h, dc, heads)) for dr, dc in halo_steps]
    partners = [head_peer(i) for i in range(heads)]
    partners += [layer_peer(i) for i in range(1, LAYER)]
    partners += [right, left, far_right, far_left]
    partners += halo_peers
    for load in loads[:3]:
        load.start()
    barrier = pltpu.get_barrier_semaphore()
    for partner in partners:
        pl.semaphore_signal(barrier, inc=1, device_id=partner, device_id_type=MESH)
    group_cols = [slice(g * width, (g + 1) * width) for g in range(heads)]
    for at, whole in enumerate((keys, values)):
        loads[at].wait()
        for g, cols in enumerate(group_cols):
            kv_stage[g, at] = whole[:, cols]
    pl.semaphore_wait(barrier, len(partners))

    def send_kv(i, carry):
        to = head_peer(i)
        remote(kv_stage.at[to[1]], kv_in.at[h], kv_send, kv_recv, to).start()
        return carry

    def send_q(i, carry):
        to = head_peer(i)
        remote(q_stage.at[to[1]], q_in.at[h], q_a2a_send, q_a2a_recv, to).start()
        return carry

    lax.fori_loop(0, heads, send_kv, 0)
    loads[2].wait()
    for g, cols in enumerate(group_cols):
        q_stage[g] = queries[:, cols]
    lax.fori_loop(0, heads, send_q, 0)
    for load in loads[3:7]:
        load.start()

    taps = w_sum.shape[0]
    parities = w_full.shape[0]
    features = final_w.shape[0]

    def sum_taps():
        conv_all = conv_w[...].astype(F32)
        total = conv_all[:taps] + conv_all[taps : 2 * taps] + conv_all[2 * taps :]
        w_sum[...] = total.astype(BF16)

    def conv_weights(parity):
        up = parity // 2
        side = lax.rem(parity, 2)
        depth = w_full.shape[1]
        row = lax.broadcasted_iota(jnp.int32, (depth, taps), 0)
        col = lax.broadcasted_iota(jnp.int32, (depth, taps), 1)
        tap_i = 2 * (row >> 7) + ((row >> 1) & 1) + up - 1
        tap_j = 2 * ((row >> 6) & 1) + (row & 1) + side - 1
        inside = (tap_i >= 0) & (tap_i <= 2) & (tap_j >= 0) & (tap_j <= 2)
        source = (tap_i * 3 + tap_j) * LAT_CH + ((row & 63) >> 2)
        pick = jnp.where(inside & (source == col), 1.0, 0.0).astype(BF16)
        w_full[parity] = dot(pick, w_sum[...]).astype(BF16)

    def rows_of(block):
        return block.astype(F32).reshape(rows, width).astype(BF16)

    peer = head_peer(0)
    remote(kv_in, kv_in, kv_send, kv_recv, peer).wait_recv()
    own_k = rows_of(kv_in[:, 0])
    own_v = rows_of(kv_in[:, 1])
    for n in range(GROUP):
        cols = slice(n * HEAD_DIM, (n + 1) * HEAD_DIM)
        kv[z, n, 0] = own_k[:, cols]
        kv[z, n, 1] = own_v[:, cols]

    def to_right(ref, recv, send=0):
        return remote(ref, ref, ring_send.at[0] if send == 0 else half_send.at[0], recv, right)

    def to_left(ref, recv, send=0):
        return remote(ref, ref, ring_send.at[1] if send == 0 else half_send.at[1], recv, left)

    pieces_of = [(n, part) for n in range(GROUP) for part in range(2)]

    for n, part in pieces_of:
        ref, recv = kv.at[z, n, part], ring_recv.at[z, n, part]
        remote(ref, ref, long_send.at[0], recv, far_right).start()
        remote(ref, ref, long_send.at[1], recv, far_left).start()
    for n, part in pieces_of:
        to_right(kv.at[z, n, part], ring_recv.at[z, n, part]).start()
        to_left(kv.at[z, n, part], ring_recv.at[z, n, part]).start()
    for load in loads[7:]:
        load.start()

    remote(q_in, q_in, q_a2a_send, q_a2a_recv, peer).wait_recv()
    own_q = rows_of(q_in[...])
    for n in range(GROUP):
        qs[n, r] = own_q[:, n * HEAD_DIM : (n + 1) * HEAD_DIM]
    for i in range(1, LAYER):
        remote(qs.at[:, r], qs.at[:, r], q_send, q_recv, layer_peer(i)).start()
    loads[3].wait()
    sum_taps()
    conv_weights(jnp.int32(0))
    made = 1

    def attend_text(n):
        share = text_k.shape[0] // LAYER
        mine = pl.ds(pl.multiple_of(j * share, share), share)
        cols = pl.ds(pl.multiple_of(n * HEAD_DIM, HEAD_DIM), HEAD_DIM)
        scores = dot(text_k[mine, cols], q_turned[n])
        real = jnp.broadcast_to(mask_column[mine, :1] == 1.0, scores.shape)
        scores = jnp.where(real, scores, NEG)
        top = jnp.max(scores, axis=0, keepdims=True)
        weights = jnp.where(real, jnp.exp2((scores - top) * (SCORE_SCALE * LOG2E)), 0.0)
        run_max[n, :1] = top
        run_sum[n, :1] = jnp.sum(weights, axis=0, keepdims=True)
        run_acc[n] = dot_tn(text_v[mine, cols], weights.astype(BF16))

    def absorb(n, one, other):
        keys_now = jnp.concatenate([kv[one, n, 0], kv[other, n, 0]], axis=0)
        values_now = jnp.concatenate([kv[one, n, 1], kv[other, n, 1]], axis=0)
        scores = dot(keys_now, q_turned[n])
        old = run_max[n, :1]
        top = jnp.maximum(old, jnp.max(scores, axis=0, keepdims=True))
        factor = jnp.exp2((old - top) * (SCORE_SCALE * LOG2E))
        weights = jnp.exp2((scores - top) * (SCORE_SCALE * LOG2E))
        total = run_sum[n, :1] * factor + jnp.sum(weights, axis=0, keepdims=True)
        acc = run_acc[n] * factor + dot_tn(values_now, weights.astype(BF16))
        return top, total, acc

    def pass_on(step, n):
        one = slot_at(-step)
        other = slot_at(step)
        for part in range(2):
            copy = to_right(kv.at[one, n, part], ring_recv.at[one, n, part])
            copy.wait_recv()
            copy.start()
            copy = to_left(kv.at[other, n, part], ring_recv.at[other, n, part])
            copy.wait_recv()
            copy.start()

    def pass_on_halves(step, n):
        one = slot_at(-step)
        other = slot_at(step)
        for part in range(2):
            copy = to_right(kv.at[one, n, part], ring_recv.at[one, n, part], 1)
            copy.wait_recv()
            if part == 0:
                copy.start()
            copy = to_left(kv.at[other, n, part], ring_recv.at[other, n, part], 1)
            copy.wait_recv()
            if part == 1:
                copy.start()

    def keep(step, n):
        one = slot_at(-step)
        other = slot_at(step)
        for part in range(2):
            to_right(kv.at[one, n, part], ring_recv.at[one, n, part]).wait_recv()
            to_left(kv.at[other, n, part], ring_recv.at[other, n, part]).wait_recv()

    def work_on(step, n):
        top, total, acc = absorb(n, slot_at(-step), slot_at(step))
        run_max[n, :1] = top
        run_sum[n, :1] = total
        run_acc[n] = acc

    def each_head(take, taken, worked):
        def one_head(n, carry):
            if take is not None:
                take(taken, n)
            if worked is not None:
                work_on(worked, n)
            return carry

        lax.fori_loop(0, GROUP, one_head, 0)

    each_head(pass_on, STRIDE, None)
    each_head(pass_on, 1, None)
    three = qs.at[:, pl.ds(0, LAYER - 1)]
    remote(three, three, q_send, q_recv, layer_peer(1)).wait_recv()
    for n in range(GROUP):
        q_turned[n] = qs[n].reshape(LAYER * rows, HEAD_DIM).T
    for load in loads[4:7]:
        load.wait()
    mask_column[...] = jnp.broadcast_to(mask[...].astype(F32), (TOK, mask.shape[1])).T

    def text_head(n, carry):
        attend_text(n)
        return carry

    lax.fori_loop(0, GROUP, text_head, 0)
    each_head(pass_on if far > 5 else pass_on_halves, 4, STRIDE)
    conv_weights(jnp.int32(1))
    made = 2
    each_head(keep, 2, 1)
    in_loop = min(parities - made, max(0, far - 5))

    def ring_step(step, carry):
        def one_head(n, inner):
            @pl.when(step < far - 1)
            def _():
                pass_on(step, n)

            @pl.when(step == far - 1)
            def _():
                pass_on_halves(step, n)

            work_on(step - 1, n)
            return inner

        lax.fori_loop(0, GROUP, one_head, 0)

        @pl.when(step - 5 < in_loop)
        def _():
            conv_weights(step - 5 + made)

        return carry

    if far > 5:
        lax.fori_loop(5, far, ring_step, 0)
    for parity in range(made + in_loop, parities):
        conv_weights(jnp.int32(parity))

    def last_two(i, carry):
        each_head(None, 0, 2 + i * (far - 3))
        return carry

    lax.fori_loop(0, 2, last_two, 0)

    opposite = slot_at(far)
    marks[...] = jnp.zeros_like(marks)

    def share_of(i):
        return shifted(r, i, LAYER)

    def last_step(n, carry):
        to_right(kv.at[opposite, n, 0], ring_recv.at[opposite, n, 0]).wait_recv()
        to_left(kv.at[opposite, n, 1], ring_recv.at[opposite, n, 1]).wait_recv()
        top, total, acc = absorb(n, z, opposite)
        share = (acc / total).T.astype(BF16)
        for i in range(LAYER):
            o_stage[i, n] = share[i * rows : (i + 1) * rows]
        for i in range(1, LAYER):
            remote(
                o_stage.at[share_of(i), n], o_in.at[j, n], o_send, o_recv, layer_peer(i)
            ).start()
        level = top * SCORE_SCALE + jnp.log(total)
        first = level.astype(BF16).astype(F32)
        second = (level - first).astype(BF16).astype(F32)
        marks[pl.ds(3 * n, 1)] = first
        marks[pl.ds(3 * n + 1, 1)] = second
        marks[pl.ds(3 * n + 2, 1)] = level - first - second
        return carry

    lax.fori_loop(0, GROUP, last_step, 0)
    level_rows = marks[...]
    lanes = mark_stage.shape[2]
    for i in range(LAYER):
        turned = level_rows if i == 0 else pltpu.roll(level_rows, (LAYER - i) * rows, 1)
        mark_stage[i] = turned[:, :lanes].astype(BF16)
    for i in range(1, LAYER):
        remote(
            mark_stage.at[share_of(i)], mark_in.at[j], mark_send, mark_recv, layer_peer(i)
        ).start()
    o_in[j] = o_stage[r]
    mark_in[j] = mark_stage[r]

    for load in loads[7:]:
        load.wait()
    three = o_in.at[pl.ds(0, LAYER - 1)]
    remote(three, three, o_send, o_recv, layer_peer(1)).wait_recv()
    three = mark_in.at[pl.ds(0, LAYER - 1)]
    remote(three, three, mark_send, mark_recv, layer_peer(1)).wait_recv()
    level_parts = [mark_in[i].astype(F32) for i in range(LAYER)]
    shares[...] = jnp.zeros_like(shares)
    for n in range(GROUP):
        levels = [
            part[3 * n : 3 * n + 1] + part[3 * n + 1 : 3 * n + 2] + part[3 * n + 2 : 3 * n + 3]
            for part in level_parts
        ]
        top = functools.reduce(jnp.maximum, levels)
        parts = [jnp.exp(level - top) for level in levels]
        total = functools.reduce(jnp.add, parts)
        for i, part in enumerate(parts):
            shares[n * LAYER + i : n * LAYER + i + 1] = part / total
    columns = shares[...].T[:rows]
    attended = []
    for n in range(GROUP):
        mixed = functools.reduce(
            jnp.add,
            [
                columns[:, n * LAYER + i : n * LAYER + i + 1] * o_in[i, n].astype(F32)
                for i in range(LAYER)
            ],
        )
        attended.append(mixed.astype(BF16))
    attended = jnp.concatenate(attended, axis=1)

    for part in range(rs_parts):
        product = dot(attended, out_w[:, part * part_cols : (part + 1) * part_cols])
        rs_stage[part] = product.reshape(heads, TOK, part_cols).astype(BF16)

        def send_part(i, carry, part=part):
            to = head_peer(i)
            remote(
                rs_stage.at[part, to[1]],
                rs_in.at[part, h],
                rs_send.at[part],
                rs_recv.at[part],
                to,
            ).start()
            return carry

        lax.fori_loop(0, heads, send_part, 0)
    pieces = []
    for part in range(rs_parts):
        cols = slice(part * part_cols, (part + 1) * part_cols)
        whole = rs_in.at[part]
        remote(whole, whole, rs_send.at[part], rs_recv.at[part], peer).wait_recv()
        projected = jnp.sum(rs_in[part].astype(F32), axis=0)
        stream = tokens[:, cols].astype(F32) + gate[:, cols] * (projected + out_bias[:, cols])
        rounded = stream.astype(BF16)
        block_out[:, cols] = rounded
        pieces.append(rounded.astype(F32))
    block_copy = pltpu.make_async_copy(block_out, block_hbm, out_sem.at[0])
    block_copy.start()

    normed_in = jnp.concatenate(pieces, axis=1)
    centered = normed_in - jnp.mean(normed_in, axis=1, keepdims=True)
    spread = jnp.mean(centered * centered, axis=1, keepdims=True)
    normed = centered * lax.rsqrt(spread + 1e-06)
    modulated = (normed * (1.0 + scale[...]) + shift[...]).astype(BF16)
    patches = (dot_nt(modulated, final_w[...]) + final_bias[...]) / LATENT_SCALE
    padded = jnp.concatenate([patches, jnp.zeros((TOK, HEAD_DIM - features), F32)], axis=1)
    lat[...] = padded.astype(BF16)

    for at, to in enumerate(halo_peers):
        remote(lat, halo.at[at], halo_send, halo_recv, to).start()
    tiles = {(0, 0): lat[...].astype(F32)}
    remote(halo, halo, halo_send, halo_recv, peer).wait_recv()
    for at, (dr, dc) in enumerate(halo_steps):
        tiles[(-dr, -dc)] = halo[at].astype(F32)

    def rolled(tile, by):
        return pltpu.roll(tile, by % HEAD_DIM, 1)

    top_edge, bottom_edge = s == 0, s == seqs - 1
    first_tile, last_tile = h == 0, h == heads - 1
    for dc in (-1, 0, 1):
        middle = tiles[(0, dc)]
        tiles[(-1, dc)] = jnp.where(top_edge, rolled(middle, 2), tiles[(-1, dc)])
        tiles[(1, dc)] = jnp.where(bottom_edge, rolled(middle, -2), tiles[(1, dc)])
    low = lax.broadcasted_iota(jnp.int32, (1, HEAD_DIM), 1) < features
    packed = {}
    for dr in (-1, 0, 1):
        middle = tiles[(dr, 0)]
        before = jnp.where(first_tile, rolled(middle, 1)[:1], tiles[(dr, -1)][TOK - 1 :])
        after = jnp.where(last_tile, rolled(middle, -1)[TOK - 1 :], tiles[(dr, 1)][:1])
        before = jnp.concatenate([before, middle[: TOK - 1]], axis=0)
        after = jnp.concatenate([middle[1:], after], axis=0)
        packed[(dr, 0)] = jnp.where(low, before, rolled(middle, features))
        packed[(dr, 1)] = jnp.where(low, middle, rolled(after, features))
    for parity in range(parities):
        up, side = parity // 2, parity % 2
        stacked = jnp.concatenate([packed[(up - 1, side)], packed[(up, side)]], axis=1)
        result = dot(stacked.astype(BF16), w_full[parity]) + conv_bias[...]
        for tile in range(pixels.shape[1]):
            pixels[up, tile, pl.ds(side, TOK, stride=2), :] = result[
                :, tile * HEAD_DIM : (tile + 1) * HEAD_DIM
            ]
    for tile in range(pixels.shape[1]):
        cols = slice(tile * HEAD_DIM, (tile + 1) * HEAD_DIM)
        decoded[:, :, cols] = pixels[:, tile].astype(BF16)
    decoded_copy = pltpu.make_async_copy(decoded, decoded_hbm, out_sem.at[1])
    decoded_copy.start()

    remote(kv_stage, kv_stage, kv_send, kv_recv, peer).wait_send()
    remote(q_stage, q_stage, q_a2a_send, q_a2a_recv, peer).wait_send()
    ring_one = kv.at[0]
    remote(ring_one, ring_one, long_send.at[0], ring_recv.at[0, 0, 0], far_right).wait_send()
    remote(ring_one, ring_one, long_send.at[1], ring_recv.at[0, 0, 0], far_left).wait_send()
    ring_all = kv.at[pl.ds(0, far - 2)]
    to_right(ring_all, ring_recv.at[0, 0, 0]).wait_send()
    to_left(ring_all, ring_recv.at[0, 0, 0]).wait_send()
    ring_half = kv.at[0, :, 0]
    to_right(ring_half, ring_recv.at[0, 0, 0], 1).wait_send()
    to_left(ring_half, ring_recv.at[0, 0, 0], 1).wait_send()
    three = qs.at[:, pl.ds(0, LAYER - 1)]
    remote(three, three, q_send, q_recv, peer).wait_send()
    three = o_stage.at[pl.ds(0, LAYER - 1)]
    remote(three, three, o_send, o_recv, peer).wait_send()
    three = mark_stage.at[pl.ds(0, LAYER - 1)]
    remote(three, three, mark_send, mark_recv, peer).wait_send()
    for part in range(rs_parts):
        whole = rs_stage.at[part]
        remote(whole, whole, rs_send.at[part], rs_recv.at[part], peer).wait_send()
    remote(halo, halo, halo_send, halo_recv, peer).wait_send()
    block_copy.wait()
    decoded_copy.wait()


def hand_over(block_in, decoded_in, block_to, decoded_to, block, decoded, sem):
    rooms = ((block_in, block, block_to), (decoded_in, decoded, decoded_to))
    loads = [pltpu.make_async_copy(a, b, sem.at[i]) for i, (a, b, _) in enumerate(rooms)]
    stores = [pltpu.make_async_copy(b, c, sem.at[2 + i]) for i, (_, b, c) in enumerate(rooms)]
    for load in loads:
        load.start()
    for load, store in zip(loads, stores):
        load.wait()
        store.start()
    for store in stores:
        store.wait()


def body(seqs, heads, *args):
    (
        queries,
        keys,
        values,
        text_keys,
        text_values,
        text_mask,
        tokens,
        out_weight,
        out_bias,
        gate,
        shift,
        scale,
        final_weight,
        final_bias,
        conv_weight,
        conv_bias,
    ) = args
    dim = queries.shape[3]
    width = GROUP * HEAD_DIM
    text = text_keys.shape[0]
    layers = seqs // LAYER
    far = layers // 2
    rows = heads * TOK
    features = final_weight.shape[1]
    taps = 9 * LAT_CH
    channels = conv_weight.shape[4]
    rs_parts = 2
    operands = (
        queries.reshape(TOK, dim),
        keys.reshape(TOK, dim),
        values.reshape(TOK, dim),
        text_keys,
        text_values,
        text_mask.reshape(1, text),
        tokens.reshape(TOK, dim),
        out_weight,
        out_bias.reshape(1, dim),
        gate.reshape(1, dim),
        shift.reshape(1, dim),
        scale.reshape(1, dim),
        final_weight.T,
        final_bias.reshape(1, features),
        conv_weight.reshape(3 * taps, channels),
        conv_bias.reshape(1, channels),
    )
    copied = [pltpu.VMEM(x.shape, x.dtype) for x in operands]
    dma = pltpu.SemaphoreType.DMA
    anywhere = pl.BlockSpec(memory_space=pl.ANY)
    results = (
        jax.ShapeDtypeStruct((TOK, dim), BF16),
        jax.ShapeDtypeStruct((2, 2 * TOK, channels), BF16),
    )
    block_out, decoded = pl.pallas_call(
        functools.partial(kernel, seqs, heads),
        out_shape=results,
        in_specs=[anywhere] * len(operands),
        out_specs=(anywhere, anywhere),
        scratch_shapes=copied
        + [
            pltpu.VMEM((heads, 2, TOK, width), BF16),
            pltpu.VMEM((heads, TOK, width), BF16),
            pltpu.VMEM((heads, 2, TOK, width), BF16),
            pltpu.VMEM((heads, TOK, width), BF16),
            pltpu.VMEM((layers, GROUP, 2, rows, HEAD_DIM), BF16),
            pltpu.VMEM((GROUP, LAYER, rows, HEAD_DIM), BF16),
            pltpu.VMEM((GROUP, HEAD_DIM, LAYER * rows), BF16),
            pltpu.VMEM((text, TOK), F32),
            pltpu.VMEM((GROUP, TOK, LAYER * rows), F32),
            pltpu.VMEM((GROUP, TOK, LAYER * rows), F32),
            pltpu.VMEM((GROUP, HEAD_DIM, LAYER * rows), F32),
            pltpu.VMEM((16, LAYER * rows), F32),
            pltpu.VMEM((LAYER, 16, min(HEAD_DIM, LAYER * rows)), BF16),
            pltpu.VMEM((LAYER, 16, min(HEAD_DIM, LAYER * rows)), BF16),
            pltpu.VMEM((16, min(HEAD_DIM, LAYER * rows)), F32),
            pltpu.VMEM((LAYER, GROUP, rows, HEAD_DIM), BF16),
            pltpu.VMEM((LAYER, GROUP, rows, HEAD_DIM), BF16),
            pltpu.VMEM((rs_parts, heads, TOK, dim // rs_parts), BF16),
            pltpu.VMEM((rs_parts, heads, TOK, dim // rs_parts), BF16),
            pltpu.VMEM((TOK, HEAD_DIM), BF16),
            pltpu.VMEM((8, TOK, HEAD_DIM), BF16),
            pltpu.VMEM((taps, channels), BF16),
            pltpu.VMEM((4, 4 * features, channels), BF16),
            pltpu.VMEM((2, channels // HEAD_DIM, 2 * TOK, HEAD_DIM), F32),
            pltpu.VMEM((TOK, dim), BF16),
            pltpu.VMEM((2, 2 * TOK, channels), BF16),
            dma((len(operands),)),
            dma((2,)),
            dma,
            dma,
            dma,
            dma,
            dma((2,)),
            dma((2,)),
            dma((2,)),
            dma((layers, GROUP, 2)),
            dma,
            dma,
            dma,
            dma,
            dma,
            dma,
            dma((rs_parts,)),
            dma((rs_parts,)),
            dma,
            dma,
        ],
        compiler_params=pltpu.CompilerParams(
            collective_id=0, has_side_effects=True, vmem_limit_bytes=60 * 1024 * 1024
        ),
        cost_estimate=pl.CostEstimate(
            flops=1_200_000_000, bytes_accessed=5_000_000, transcendentals=1_000_000
        ),
    )(*operands)
    block_out, decoded = pl.pallas_call(
        hand_over,
        out_shape=results,
        in_specs=[anywhere] * 2,
        out_specs=(anywhere, anywhere),
        scratch_shapes=[pltpu.VMEM(x.shape, x.dtype) for x in results] + [dma((4,))],
        compiler_params=pltpu.CompilerParams(vmem_limit_bytes=60 * 1024 * 1024),
    )(block_out, decoded)
    return (
        block_out.reshape(1, TOK, 1, dim),
        decoded.reshape(1, 2, 2 * TOK, channels),
    )


def solution(mesh):
    seqs = mesh.shape["seq"]
    heads = mesh.shape["head"]
    spread = P("seq", "head", None, None)
    in_specs = (
        spread,
        spread,
        spread,
        P(None, "head"),
        P(None, "head"),
        P(),
        spread,
        P("head", None),
    ) + (P(),) * 8
    out_specs = (spread, P(None, "seq", "head", None))
    return jax.shard_map(
        functools.partial(body, seqs, heads),
        mesh=mesh,
        in_specs=in_specs,
        out_specs=out_specs,
        check_vma=False,
    )
```

```python
import functools

import jax
import jax.numpy as jnp
from jax import lax
from jax.experimental import pallas as pl
from jax.experimental.pallas import tpu as pltpu
from jax.sharding import PartitionSpec as P

HEAD_DIM = 128
GROUP = 3
LAT_CH = 16
TOK = 8
LAYER = 4
LATENT_SCALE = 0.476986
NEG = -1e30
SCORE_SCALE = HEAD_DIM ** (-0.5)
LOG2E = 1.4426950408889634
BF16 = jnp.bfloat16
F32 = jnp.float32
MESH = pl.DeviceIdType.MESH


def dot(a, b):
    return jnp.dot(a, b, preferred_element_type=F32)


def dot_tn(a, b):
    return lax.dot_general(a, b, (((0,), (0,)), ((), ())), preferred_element_type=F32)


def dot_nt(a, b):
    return lax.dot_general(a, b, (((1,), (1,)), ((), ())), preferred_element_type=F32)


def kernel(
    seqs,
    heads,
    q_hbm,
    k_hbm,
    v_hbm,
    text_k_hbm,
    text_v_hbm,
    mask_hbm,
    tokens_hbm,
    out_w_hbm,
    out_bias_hbm,
    gate_hbm,
    shift_hbm,
    scale_hbm,
    final_w_hbm,
    final_bias_hbm,
    conv_w_hbm,
    conv_bias_hbm,
    block_hbm,
    decoded_hbm,
    queries,
    keys,
    values,
    text_k,
    text_v,
    mask,
    tokens,
    out_w,
    out_bias,
    gate,
    shift,
    scale,
    final_w,
    final_bias,
    conv_w,
    conv_bias,
    kv_stage,
    q_stage,
    kv_in,
    q_in,
    kv,
    qs,
    q_turned,
    mask_column,
    run_max,
    run_sum,
    run_acc,
    marks,
    mark_stage,
    mark_in,
    shares,
    o_stage,
    o_in,
    rs_stage,
    rs_in,
    lat,
    halo,
    w_sum,
    w_full,
    pixels,
    block_out,
    decoded,
    local_sem,
    out_sem,
    kv_send,
    kv_recv,
    q_a2a_send,
    q_a2a_recv,
    ring_send,
    half_send,
    ring_recv,
    q_send,
    q_recv,
    o_send,
    o_recv,
    mark_send,
    mark_recv,
    rs_send,
    rs_recv,
    halo_send,
    halo_recv,
):
    s = lax.axis_index("seq")
    h = lax.axis_index("head")
    layers = seqs // LAYER
    far = layers // 2
    z = s // LAYER
    j = lax.rem(s, LAYER)
    width = GROUP * HEAD_DIM
    dim = heads * width
    rows = heads * TOK
    rs_parts = rs_stage.shape[0]
    part_cols = dim // rs_parts

    def shifted(index, by, count):
        return lax.rem(index + (by % count), count)

    r = lax.rem(j + LAYER // 2, LAYER)

    def head_peer(i):
        return (z * LAYER + r, shifted(h, i, heads))

    def layer_peer(i):
        return (z * LAYER + shifted(j, i, LAYER), h)

    def slot_at(by):
        return lax.rem(z + by + layers, layers)

    def ring_peer(by):
        return (slot_at(by) * LAYER + j, h)

    right, left = ring_peer(1), ring_peer(-1)

    def remote(src, dst, send, recv, device):
        return pltpu.make_async_remote_copy(
            src_ref=src,
            dst_ref=dst,
            send_sem=send,
            recv_sem=recv,
            device_id=device,
            device_id_type=MESH,
        )

    pairs = (
        (k_hbm, keys),
        (v_hbm, values),
        (q_hbm, queries),
        (conv_w_hbm, conv_w),
        (text_k_hbm, text_k),
        (text_v_hbm, text_v),
        (mask_hbm, mask),
        (tokens_hbm, tokens),
        (out_w_hbm, out_w),
        (out_bias_hbm, out_bias),
        (gate_hbm, gate),
        (shift_hbm, shift),
        (scale_hbm, scale),
        (final_w_hbm, final_w),
        (final_bias_hbm, final_bias),
        (conv_bias_hbm, conv_bias),
    )
    loads = [
        pltpu.make_async_copy(src, dst, local_sem.at[i]) for i, (src, dst) in enumerate(pairs)
    ]

    halo_steps = [(dr, dc) for dr in (-1, 0, 1) for dc in (-1, 0, 1) if (dr, dc) != (0, 0)]
    halo_peers = [(shifted(s, dr, seqs), shifted(h, dc, heads)) for dr, dc in halo_steps]
    partners = [head_peer(i) for i in range(heads)]
    partners += [layer_peer(i) for i in range(1, LAYER)]
    partners += [right, left]
    partners += halo_peers
    for load in loads[:3]:
        load.start()
    barrier = pltpu.get_barrier_semaphore()
    for partner in partners:
        pl.semaphore_signal(barrier, inc=1, device_id=partner, device_id_type=MESH)
    group_cols = [slice(g * width, (g + 1) * width) for g in range(heads)]
    for at, whole in enumerate((keys, values)):
        loads[at].wait()
        for g, cols in enumerate(group_cols):
            kv_stage[g, at] = whole[:, cols]
    pl.semaphore_wait(barrier, len(partners))

    def send_kv(i, carry):
        to = head_peer(i)
        remote(kv_stage.at[to[1]], kv_in.at[h], kv_send, kv_recv, to).start()
        return carry

    def send_q(i, carry):
        to = head_peer(i)
        remote(q_stage.at[to[1]], q_in.at[h], q_a2a_send, q_a2a_recv, to).start()
        return carry

    lax.fori_loop(0, heads, send_kv, 0)
    loads[2].wait()
    for g, cols in enumerate(group_cols):
        q_stage[g] = queries[:, cols]
    lax.fori_loop(0, heads, send_q, 0)
    for load in loads[3:7]:
        load.start()

    taps = w_sum.shape[0]
    parities = w_full.shape[0]
    features = final_w.shape[0]

    def sum_taps():
        conv_all = conv_w[...].astype(F32)
        total = conv_all[:taps] + conv_all[taps : 2 * taps] + conv_all[2 * taps :]
        w_sum[...] = total.astype(BF16)

    def conv_weights(parity):
        up = parity // 2
        side = lax.rem(parity, 2)
        depth = w_full.shape[1]
        row = lax.broadcasted_iota(jnp.int32, (depth, taps), 0)
        col = lax.broadcasted_iota(jnp.int32, (depth, taps), 1)
        tap_i = 2 * (row >> 7) + ((row >> 1) & 1) + up - 1
        tap_j = 2 * ((row >> 6) & 1) + (row & 1) + side - 1
        inside = (tap_i >= 0) & (tap_i <= 2) & (tap_j >= 0) & (tap_j <= 2)
        source = (tap_i * 3 + tap_j) * LAT_CH + ((row & 63) >> 2)
        pick = jnp.where(inside & (source == col), 1.0, 0.0).astype(BF16)
        w_full[parity] = dot(pick, w_sum[...]).astype(BF16)

    def rows_of(block):
        return block.astype(F32).reshape(rows, width).astype(BF16)

    peer = head_peer(0)
    remote(kv_in, kv_in, kv_send, kv_recv, peer).wait_recv()
    own_k = rows_of(kv_in[:, 0])
    own_v = rows_of(kv_in[:, 1])
    for n in range(GROUP):
        cols = slice(n * HEAD_DIM, (n + 1) * HEAD_DIM)
        kv[z, n, 0] = own_k[:, cols]
        kv[z, n, 1] = own_v[:, cols]

    def to_right(ref, recv, send=0):
        return remote(ref, ref, ring_send.at[0] if send == 0 else half_send.at[0], recv, right)

    def to_left(ref, recv, send=0):
        return remote(ref, ref, ring_send.at[1] if send == 0 else half_send.at[1], recv, left)

    pieces_of = [(n, part) for n in range(GROUP) for part in range(2)]

    for n, part in pieces_of:
        to_right(kv.at[z, n, part], ring_recv.at[z, n, part]).start()
        to_left(kv.at[z, n, part], ring_recv.at[z, n, part]).start()
    for load in loads[7:]:
        load.start()

    remote(q_in, q_in, q_a2a_send, q_a2a_recv, peer).wait_recv()
    own_q = rows_of(q_in[...])
    for n in range(GROUP):
        qs[n, r] = own_q[:, n * HEAD_DIM : (n + 1) * HEAD_DIM]
    for i in range(1, LAYER):
        remote(qs.at[:, r], qs.at[:, r], q_send, q_recv, layer_peer(i)).start()
    def weigh(scores, top):
        return jnp.exp2((scores - top) * (SCORE_SCALE * LOG2E))

    def attend_first(n, carry):
        share = text_k.shape[0] // LAYER
        mine = pl.ds(pl.multiple_of(j * share, share), share)
        cols = pl.ds(pl.multiple_of(n * HEAD_DIM, HEAD_DIM), HEAD_DIM)
        keys_now = jnp.concatenate([text_k[mine, cols], kv[z, n, 0]], axis=0)
        values_now = jnp.concatenate([text_v[mine, cols], kv[z, n, 1]], axis=0)
        scores = dot(keys_now, q_turned[n])
        real = jnp.concatenate([mask_column[mine, :1], jnp.ones((rows, 1), F32)], axis=0) == 1.0
        real = jnp.broadcast_to(real, scores.shape)
        scores = jnp.where(real, scores, NEG)
        top = jnp.max(scores, axis=0, keepdims=True)
        weights = jnp.where(real, weigh(scores, top), 0.0)
        run_max[n, :1] = top
        run_sum[n, :1] = jnp.sum(weights, axis=0, keepdims=True)
        run_acc[n] = dot_tn(values_now, weights.astype(BF16))
        return carry

    def absorb(n, slots):
        keys_now = jnp.concatenate([kv[slot, n, 0] for slot in slots], axis=0)
        values_now = jnp.concatenate([kv[slot, n, 1] for slot in slots], axis=0)
        scores = dot(keys_now, q_turned[n])
        old = run_max[n, :1]
        top = jnp.maximum(old, jnp.max(scores, axis=0, keepdims=True))
        factor = weigh(old, top)
        weights = weigh(scores, top)
        total = run_sum[n, :1] * factor + jnp.sum(weights, axis=0, keepdims=True)
        acc = run_acc[n] * factor + dot_tn(values_now, weights.astype(BF16))
        return top, total, acc

    def work_on(n, steps):
        top, total, acc = absorb(n, [slot_at(by) for step in steps for by in (-step, step)])
        run_max[n, :1] = top
        run_sum[n, :1] = total
        run_acc[n] = acc

    def pass_on(step):
        one = slot_at(-step)
        other = slot_at(step)

        def one_head(n, carry):
            for part in range(2):
                copy = to_right(kv.at[one, n, part], ring_recv.at[one, n, part])
                copy.wait_recv()
                copy.start()
                copy = to_left(kv.at[other, n, part], ring_recv.at[other, n, part])
                copy.wait_recv()
                copy.start()
            return carry

        lax.fori_loop(0, GROUP, one_head, 0)

    def pass_on_halves(step):
        one = slot_at(-step)
        other = slot_at(step)

        def one_head(n, carry):
            for part in range(2):
                copy = to_right(kv.at[one, n, part], ring_recv.at[one, n, part], 1)
                copy.wait_recv()
                if part == 0:
                    copy.start()
                copy = to_left(kv.at[other, n, part], ring_recv.at[other, n, part], 1)
                copy.wait_recv()
                if part == 1:
                    copy.start()
            return carry

        lax.fori_loop(0, GROUP, one_head, 0)

    pass_on(1)
    three = qs.at[:, pl.ds(0, LAYER - 1)]
    remote(three, three, q_send, q_recv, layer_peer(1)).wait_recv()
    for n in range(GROUP):
        q_turned[n] = qs[n].reshape(LAYER * rows, HEAD_DIM).T
    for load in loads[3:7]:
        load.wait()
    mask_column[...] = jnp.broadcast_to(mask[...].astype(F32), (TOK, mask.shape[1])).T
    lax.fori_loop(0, GROUP, attend_first, 0)
    pass_on(2)
    sum_taps()

    def two_parities(first):
        def one_parity(parity, carry):
            conv_weights(parity)
            return carry

        lax.fori_loop(first, first + 2, one_parity, 0)

    two_parities(0)
    pass_on(3)
    two_parities(2)

    def middle_step(n, carry):
        @pl.when(n + 4 < far - 1)
        def _():
            pass_on(n + 4)

        work_on(n, range(1, far - 4))
        return carry

    lax.fori_loop(0, GROUP, middle_step, 0)
    pass_on_halves(far - 1)

    def late_step(n, carry):
        work_on(n, range(far - 4, far - 1))
        return carry

    lax.fori_loop(0, GROUP, late_step, 0)

    opposite = slot_at(far)
    marks[...] = jnp.zeros_like(marks)

    def share_of(i):
        return shifted(r, i, LAYER)

    def last_step(n, carry):
        to_right(kv.at[opposite, n, 0], ring_recv.at[opposite, n, 0]).wait_recv()
        to_left(kv.at[opposite, n, 1], ring_recv.at[opposite, n, 1]).wait_recv()
        top, total, acc = absorb(n, [slot_at(1 - far), slot_at(far - 1), opposite])
        share = (acc / total).T.astype(BF16)
        for i in range(LAYER):
            o_stage[i, n] = share[i * rows : (i + 1) * rows]
        for i in range(1, LAYER):
            remote(
                o_stage.at[share_of(i), n], o_in.at[j, n], o_send, o_recv, layer_peer(i)
            ).start()
        level = top * SCORE_SCALE + jnp.log(total)
        first = level.astype(BF16).astype(F32)
        second = (level - first).astype(BF16).astype(F32)
        marks[pl.ds(3 * n, 1)] = first
        marks[pl.ds(3 * n + 1, 1)] = second
        marks[pl.ds(3 * n + 2, 1)] = level - first - second
        return carry

    lax.fori_loop(0, GROUP, last_step, 0)
    level_rows = marks[...]
    lanes = mark_stage.shape[2]
    for i in range(LAYER):
        turned = level_rows if i == 0 else pltpu.roll(level_rows, (LAYER - i) * rows, 1)
        mark_stage[i] = turned[:, :lanes].astype(BF16)
    for i in range(1, LAYER):
        remote(
            mark_stage.at[share_of(i)], mark_in.at[j], mark_send, mark_recv, layer_peer(i)
        ).start()
    o_in[j] = o_stage[r]
    mark_in[j] = mark_stage[r]

    for load in loads[7:]:
        load.wait()
    three = o_in.at[pl.ds(0, LAYER - 1)]
    remote(three, three, o_send, o_recv, layer_peer(1)).wait_recv()
    three = mark_in.at[pl.ds(0, LAYER - 1)]
    remote(three, three, mark_send, mark_recv, layer_peer(1)).wait_recv()
    level_parts = [mark_in[i].astype(F32) for i in range(LAYER)]
    shares[...] = jnp.zeros_like(shares)
    for n in range(GROUP):
        levels = [
            part[3 * n : 3 * n + 1] + part[3 * n + 1 : 3 * n + 2] + part[3 * n + 2 : 3 * n + 3]
            for part in level_parts
        ]
        top = functools.reduce(jnp.maximum, levels)
        parts = [jnp.exp(level - top) for level in levels]
        total = functools.reduce(jnp.add, parts)
        for i, part in enumerate(parts):
            shares[n * LAYER + i : n * LAYER + i + 1] = part / total
    columns = shares[...].T[:rows]
    attended = []
    for n in range(GROUP):
        mixed = functools.reduce(
            jnp.add,
            [
                columns[:, n * LAYER + i : n * LAYER + i + 1] * o_in[i, n].astype(F32)
                for i in range(LAYER)
            ],
        )
        attended.append(mixed.astype(BF16))
    attended = jnp.concatenate(attended, axis=1)

    for part in range(rs_parts):
        product = dot(attended, out_w[:, part * part_cols : (part + 1) * part_cols])
        rs_stage[part] = product.reshape(heads, TOK, part_cols).astype(BF16)

        def send_part(i, carry, part=part):
            to = head_peer(i)
            remote(
                rs_stage.at[part, to[1]],
                rs_in.at[part, h],
                rs_send.at[part],
                rs_recv.at[part],
                to,
            ).start()
            return carry

        lax.fori_loop(0, heads, send_part, 0)
    pieces = []
    for part in range(rs_parts):
        cols = slice(part * part_cols, (part + 1) * part_cols)
        whole = rs_in.at[part]
        remote(whole, whole, rs_send.at[part], rs_recv.at[part], peer).wait_recv()
        projected = jnp.sum(rs_in[part].astype(F32), axis=0)
        stream = tokens[:, cols].astype(F32) + gate[:, cols] * (projected + out_bias[:, cols])
        rounded = stream.astype(BF16)
        block_out[:, cols] = rounded
        pieces.append(rounded.astype(F32))
    block_copy = pltpu.make_async_copy(block_out, block_hbm, out_sem.at[0])
    block_copy.start()

    normed_in = jnp.concatenate(pieces, axis=1)
    centered = normed_in - jnp.mean(normed_in, axis=1, keepdims=True)
    spread = jnp.mean(centered * centered, axis=1, keepdims=True)
    normed = centered * lax.rsqrt(spread + 1e-06)
    modulated = (normed * (1.0 + scale[...]) + shift[...]).astype(BF16)
    patches = (dot_nt(modulated, final_w[...]) + final_bias[...]) / LATENT_SCALE
    padded = jnp.concatenate([patches, jnp.zeros((TOK, HEAD_DIM - features), F32)], axis=1)
    lat[...] = padded.astype(BF16)

    for at, to in enumerate(halo_peers):
        remote(lat, halo.at[at], halo_send, halo_recv, to).start()
    tiles = {(0, 0): lat[...].astype(F32)}
    remote(halo, halo, halo_send, halo_recv, peer).wait_recv()
    for at, (dr, dc) in enumerate(halo_steps):
        tiles[(-dr, -dc)] = halo[at].astype(F32)

    def rolled(tile, by):
        return pltpu.roll(tile, by % HEAD_DIM, 1)

    top_edge, bottom_edge = s == 0, s == seqs - 1
    first_tile, last_tile = h == 0, h == heads - 1
    for dc in (-1, 0, 1):
        middle = tiles[(0, dc)]
        tiles[(-1, dc)] = jnp.where(top_edge, rolled(middle, 2), tiles[(-1, dc)])
        tiles[(1, dc)] = jnp.where(bottom_edge, rolled(middle, -2), tiles[(1, dc)])
    low = lax.broadcasted_iota(jnp.int32, (1, HEAD_DIM), 1) < features
    packed = {}
    for dr in (-1, 0, 1):
        middle = tiles[(dr, 0)]
        before = jnp.where(first_tile, rolled(middle, 1)[:1], tiles[(dr, -1)][TOK - 1 :])
        after = jnp.where(last_tile, rolled(middle, -1)[TOK - 1 :], tiles[(dr, 1)][:1])
        before = jnp.concatenate([before, middle[: TOK - 1]], axis=0)
        after = jnp.concatenate([middle[1:], after], axis=0)
        packed[(dr, 0)] = jnp.where(low, before, rolled(middle, features))
        packed[(dr, 1)] = jnp.where(low, middle, rolled(after, features))
    for parity in range(parities):
        up, side = parity // 2, parity % 2
        stacked = jnp.concatenate([packed[(up - 1, side)], packed[(up, side)]], axis=1)
        result = dot(stacked.astype(BF16), w_full[parity]) + conv_bias[...]
        for tile in range(pixels.shape[1]):
            pixels[up, tile, pl.ds(side, TOK, stride=2), :] = result[
                :, tile * HEAD_DIM : (tile + 1) * HEAD_DIM
            ]
    for tile in range(pixels.shape[1]):
        cols = slice(tile * HEAD_DIM, (tile + 1) * HEAD_DIM)
        decoded[:, :, cols] = pixels[:, tile].astype(BF16)
    decoded_copy = pltpu.make_async_copy(decoded, decoded_hbm, out_sem.at[1])
    decoded_copy.start()

    remote(kv_stage, kv_stage, kv_send, kv_recv, peer).wait_send()
    remote(q_stage, q_stage, q_a2a_send, q_a2a_recv, peer).wait_send()
    ring_all = kv.at[pl.ds(0, far - 1)]
    to_right(ring_all, ring_recv.at[0, 0, 0]).wait_send()
    to_left(ring_all, ring_recv.at[0, 0, 0]).wait_send()
    ring_half = kv.at[0, :, 0]
    to_right(ring_half, ring_recv.at[0, 0, 0], 1).wait_send()
    to_left(ring_half, ring_recv.at[0, 0, 0], 1).wait_send()
    three = qs.at[:, pl.ds(0, LAYER - 1)]
    remote(three, three, q_send, q_recv, peer).wait_send()
    three = o_stage.at[pl.ds(0, LAYER - 1)]
    remote(three, three, o_send, o_recv, peer).wait_send()
    three = mark_stage.at[pl.ds(0, LAYER - 1)]
    remote(three, three, mark_send, mark_recv, peer).wait_send()
    for part in range(rs_parts):
        whole = rs_stage.at[part]
        remote(whole, whole, rs_send.at[part], rs_recv.at[part], peer).wait_send()
    remote(halo, halo, halo_send, halo_recv, peer).wait_send()
    block_copy.wait()
    decoded_copy.wait()


def hand_over(block_in, decoded_in, block_to, decoded_to, block, decoded, sem):
    rooms = ((block_in, block, block_to), (decoded_in, decoded, decoded_to))
    loads = [pltpu.make_async_copy(a, b, sem.at[i]) for i, (a, b, _) in enumerate(rooms)]
    stores = [pltpu.make_async_copy(b, c, sem.at[2 + i]) for i, (_, b, c) in enumerate(rooms)]
    for load in loads:
        load.start()
    for load, store in zip(loads, stores):
        load.wait()
        store.start()
    for store in stores:
        store.wait()


def body(seqs, heads, *args):
    (
        queries,
        keys,
        values,
        text_keys,
        text_values,
        text_mask,
        tokens,
        out_weight,
        out_bias,
        gate,
        shift,
        scale,
        final_weight,
        final_bias,
        conv_weight,
        conv_bias,
    ) = args
    dim = queries.shape[3]
    width = GROUP * HEAD_DIM
    text = text_keys.shape[0]
    layers = seqs // LAYER
    far = layers // 2
    rows = heads * TOK
    features = final_weight.shape[1]
    taps = 9 * LAT_CH
    channels = conv_weight.shape[4]
    rs_parts = 2
    operands = (
        queries.reshape(TOK, dim),
        keys.reshape(TOK, dim),
        values.reshape(TOK, dim),
        text_keys,
        text_values,
        text_mask.reshape(1, text),
        tokens.reshape(TOK, dim),
        out_weight,
        out_bias.reshape(1, dim),
        gate.reshape(1, dim),
        shift.reshape(1, dim),
        scale.reshape(1, dim),
        final_weight.T,
        final_bias.reshape(1, features),
        conv_weight.reshape(3 * taps, channels),
        conv_bias.reshape(1, channels),
    )
    copied = [pltpu.VMEM(x.shape, x.dtype) for x in operands]
    dma = pltpu.SemaphoreType.DMA
    anywhere = pl.BlockSpec(memory_space=pl.ANY)
    results = (
        jax.ShapeDtypeStruct((TOK, dim), BF16),
        jax.ShapeDtypeStruct((2, 2 * TOK, channels), BF16),
    )
    block_out, decoded = pl.pallas_call(
        functools.partial(kernel, seqs, heads),
        out_shape=results,
        in_specs=[anywhere] * len(operands),
        out_specs=(anywhere, anywhere),
        scratch_shapes=copied
        + [
            pltpu.VMEM((heads, 2, TOK, width), BF16),
            pltpu.VMEM((heads, TOK, width), BF16),
            pltpu.VMEM((heads, 2, TOK, width), BF16),
            pltpu.VMEM((heads, TOK, width), BF16),
            pltpu.VMEM((layers, GROUP, 2, rows, HEAD_DIM), BF16),
            pltpu.VMEM((GROUP, LAYER, rows, HEAD_DIM), BF16),
            pltpu.VMEM((GROUP, HEAD_DIM, LAYER * rows), BF16),
            pltpu.VMEM((text, TOK), F32),
            pltpu.VMEM((GROUP, TOK, LAYER * rows), F32),
            pltpu.VMEM((GROUP, TOK, LAYER * rows), F32),
            pltpu.VMEM((GROUP, HEAD_DIM, LAYER * rows), F32),
            pltpu.VMEM((16, LAYER * rows), F32),
            pltpu.VMEM((LAYER, 16, min(HEAD_DIM, LAYER * rows)), BF16),
            pltpu.VMEM((LAYER, 16, min(HEAD_DIM, LAYER * rows)), BF16),
            pltpu.VMEM((16, min(HEAD_DIM, LAYER * rows)), F32),
            pltpu.VMEM((LAYER, GROUP, rows, HEAD_DIM), BF16),
            pltpu.VMEM((LAYER, GROUP, rows, HEAD_DIM), BF16),
            pltpu.VMEM((rs_parts, heads, TOK, dim // rs_parts), BF16),
            pltpu.VMEM((rs_parts, heads, TOK, dim // rs_parts), BF16),
            pltpu.VMEM((TOK, HEAD_DIM), BF16),
            pltpu.VMEM((8, TOK, HEAD_DIM), BF16),
            pltpu.VMEM((taps, channels), BF16),
            pltpu.VMEM((4, 4 * features, channels), BF16),
            pltpu.VMEM((2, channels // HEAD_DIM, 2 * TOK, HEAD_DIM), F32),
            pltpu.VMEM((TOK, dim), BF16),
            pltpu.VMEM((2, 2 * TOK, channels), BF16),
            dma((len(operands),)),
            dma((2,)),
            dma,
            dma,
            dma,
            dma,
            dma((2,)),
            dma((2,)),
            dma((layers, GROUP, 2)),
            dma,
            dma,
            dma,
            dma,
            dma,
            dma,
            dma((rs_parts,)),
            dma((rs_parts,)),
            dma,
            dma,
        ],
        compiler_params=pltpu.CompilerParams(
            collective_id=0, has_side_effects=True, vmem_limit_bytes=60 * 1024 * 1024
        ),
        cost_estimate=pl.CostEstimate(
            flops=1_200_000_000, bytes_accessed=5_000_000, transcendentals=1_000_000
        ),
    )(*operands)
    block_out, decoded = pl.pallas_call(
        hand_over,
        out_shape=results,
        in_specs=[anywhere] * 2,
        out_specs=(anywhere, anywhere),
        scratch_shapes=[pltpu.VMEM(x.shape, x.dtype) for x in results] + [dma((4,))],
        compiler_params=pltpu.CompilerParams(vmem_limit_bytes=60 * 1024 * 1024),
    )(block_out, decoded)
    return (
        block_out.reshape(1, TOK, 1, dim),
        decoded.reshape(1, 2, 2 * TOK, channels),
    )


def solution(mesh):
    seqs = mesh.shape["seq"]
    heads = mesh.shape["head"]
    spread = P("seq", "head", None, None)
    in_specs = (
        spread,
        spread,
        spread,
        P(None, "head"),
        P(None, "head"),
        P(),
        spread,
        P("head", None),
    ) + (P(),) * 8
    out_specs = (spread, P(None, "seq", "head", None))
    return jax.shard_map(
        functools.partial(body, seqs, heads),
        mesh=mesh,
        in_specs=in_specs,
        out_specs=out_specs,
        check_vma=False,
    )
```

```python
import functools

import jax
import jax.numpy as jnp
from jax import lax
from jax.experimental import pallas as pl
from jax.experimental.pallas import tpu as pltpu
from jax.sharding import PartitionSpec as P

HEAD_DIM = 128
GROUP = 3
LAT_CH = 16
TOK = 8
LAYER = 4
PAIR = 8
COLUMNS = 4
LATENT_SCALE = 0.476986
NEG = -1e30
SCORE_SCALE = HEAD_DIM ** (-0.5)
LOG2E = 1.4426950408889634
BF16 = jnp.bfloat16
F32 = jnp.float32
MESH = pl.DeviceIdType.MESH


def dot(a, b):
    return jnp.dot(a, b, preferred_element_type=F32)


def dot_tn(a, b):
    return lax.dot_general(a, b, (((0,), (0,)), ((), ())), preferred_element_type=F32)


def dot_nt(a, b):
    return lax.dot_general(a, b, (((1,), (1,)), ((), ())), preferred_element_type=F32)


def kernel(
    seqs,
    heads,
    q_hbm,
    k_hbm,
    v_hbm,
    text_k_hbm,
    text_v_hbm,
    mask_hbm,
    tokens_hbm,
    out_w_hbm,
    out_bias_hbm,
    gate_hbm,
    shift_hbm,
    scale_hbm,
    final_w_hbm,
    final_bias_hbm,
    conv_w_hbm,
    conv_bias_hbm,
    block_hbm,
    decoded_hbm,
    queries,
    keys,
    values,
    text_k,
    text_v,
    mask,
    tokens,
    out_w,
    out_bias,
    gate,
    shift,
    scale,
    final_w,
    final_bias,
    conv_w,
    conv_bias,
    kv_stage,
    q_stage,
    kv_in,
    q_in,
    kv,
    qs,
    q_turned,
    mask_column,
    run_max,
    run_sum,
    run_acc,
    marks,
    mark_stage,
    mark_in,
    shares,
    o_stage,
    o_in,
    rs_stage,
    rs_in,
    lat,
    halo,
    w_sum,
    w_full,
    pixels,
    block_out,
    decoded,
    local_sem,
    out_sem,
    kv_send,
    kv_recv,
    q_a2a_send,
    q_a2a_recv,
    ring_send,
    half_send,
    ring_recv,
    q_send,
    q_recv,
    o_send,
    o_recv,
    mark_send,
    mark_recv,
    rs_send,
    rs_recv,
    halo_send,
    halo_recv,
):
    s = lax.axis_index("seq")
    h = lax.axis_index("head")
    layers = seqs // PAIR
    far = layers // 2
    depth = s // LAYER
    j = lax.rem(s, LAYER)
    z = depth // 2
    parity_z = lax.rem(depth, 2)
    column = lax.rem(h, COLUMNS)
    y_high = h // COLUMNS
    part_of = y_high * LAYER + j
    place = parity_z * COLUMNS + column
    apart = lax.rem(y_high + parity_z, 2)
    width = GROUP * HEAD_DIM
    dim = heads * width
    rows = heads * TOK
    rs_parts = rs_stage.shape[0]
    part_cols = dim // rs_parts

    def shifted(index, by, count):
        return lax.rem(index + (by % count), count)

    r = lax.rem(j + LAYER // 2, LAYER)

    def head_peer(i):
        return (depth * LAYER + r, shifted(h, i, heads))

    def group_peer(i):
        at_depth = z * 2 + lax.rem(parity_z + i // COLUMNS, 2)
        at_column = lax.rem(column + lax.rem(i, COLUMNS), COLUMNS)
        group = lax.rem(at_depth, 2) * COLUMNS + at_column
        return (at_depth * LAYER + j, y_high * COLUMNS + at_column), group

    def part_peer(i):
        part = lax.rem(part_of + i, PAIR)
        return (depth * LAYER + lax.rem(part, LAYER), (part // LAYER) * COLUMNS + column)

    def row_peer(i):
        at_parity = lax.rem(parity_z + i // LAYER, 2)
        row = lax.rem(j + lax.rem(i, LAYER), LAYER)
        owner = lax.rem(row + LAYER // 2, LAYER)
        to = ((z * 2 + at_parity) * LAYER + owner, parity_z * COLUMNS + column)
        return to, at_parity * LAYER + row

    own_row = LAYER // 2

    def share_source(i):
        part = lax.rem(part_of + i, PAIR)
        at = (z * 2 + y_high) * LAYER + lax.rem(part, LAYER)
        return (at, (part // LAYER) * COLUMNS + column)

    def slot_at(by):
        return lax.rem(z + by + layers, layers)

    def ring_peer(by):
        return ((slot_at(by) * 2 + parity_z) * LAYER + j, h)

    right, left = ring_peer(1), ring_peer(-1)

    def remote(src, dst, send, recv, device):
        return pltpu.make_async_remote_copy(
            src_ref=src,
            dst_ref=dst,
            send_sem=send,
            recv_sem=recv,
            device_id=device,
            device_id_type=MESH,
        )

    pairs = (
        (k_hbm, keys),
        (v_hbm, values),
        (q_hbm, queries),
        (conv_w_hbm, conv_w),
        (text_k_hbm, text_k),
        (text_v_hbm, text_v),
        (mask_hbm, mask),
        (tokens_hbm, tokens),
        (out_w_hbm, out_w),
        (out_bias_hbm, out_bias),
        (gate_hbm, gate),
        (shift_hbm, shift),
        (scale_hbm, scale),
        (final_w_hbm, final_w),
        (final_bias_hbm, final_bias),
        (conv_bias_hbm, conv_bias),
    )
    loads = [
        pltpu.make_async_copy(src, dst, local_sem.at[i]) for i, (src, dst) in enumerate(pairs)
    ]

    halo_steps = [(dr, dc) for dr in (-1, 0, 1) for dc in (-1, 0, 1) if (dr, dc) != (0, 0)]
    halo_peers = [(shifted(s, dr, seqs), shifted(h, dc, heads)) for dr, dc in halo_steps]
    partners = [group_peer(i)[0] for i in range(1, heads)]
    partners += [right, left]
    partners += [part_peer(i) for i in range(1, PAIR)]
    partners += [share_source(i) for i in range(1, PAIR)]
    partners += [head_peer(i) for i in range(heads)]
    partners += halo_peers
    for load in loads[:3]:
        load.start()
    barrier = pltpu.get_barrier_semaphore()
    for partner in partners:
        pl.semaphore_signal(barrier, inc=1, device_id=partner, device_id_type=MESH)

    @pl.when(apart == 1)
    def _():
        pl.semaphore_signal(barrier, inc=1, device_id=share_source(0), device_id_type=MESH)

    group_cols = [slice(g * width, (g + 1) * width) for g in range(heads)]
    for at, whole in enumerate((keys, values)):
        loads[at].wait()
        for g, cols in enumerate(group_cols):
            kv_stage[g, at] = whole[:, cols]
    pl.semaphore_wait(barrier, len(partners) + apart)

    def send_kv(i, carry):
        to, group = group_peer(i)
        remote(kv_stage.at[group], kv_in.at[place], kv_send, kv_recv, to).start()
        return carry

    def send_q(i, carry):
        to, group = group_peer(i)
        remote(q_stage.at[group], q_in.at[place], q_a2a_send, q_a2a_recv, to).start()
        return carry

    lax.fori_loop(1, heads, send_kv, 0)
    kv_in[place] = kv_stage[place]
    loads[2].wait()
    for g, cols in enumerate(group_cols):
        q_stage[g] = queries[:, cols]
    lax.fori_loop(1, heads, send_q, 0)
    q_in[place] = q_stage[place]
    for load in loads[3:7]:
        load.start()

    taps = w_sum.shape[0]
    parities = w_full.shape[0]
    features = final_w.shape[0]

    def sum_taps():
        conv_all = conv_w[...].astype(F32)
        total = conv_all[:taps] + conv_all[taps : 2 * taps] + conv_all[2 * taps :]
        w_sum[...] = total.astype(BF16)

    def conv_weights(parity):
        up = parity // 2
        side = lax.rem(parity, 2)
        depth = w_full.shape[1]
        row = lax.broadcasted_iota(jnp.int32, (depth, taps), 0)
        col = lax.broadcasted_iota(jnp.int32, (depth, taps), 1)
        tap_i = 2 * (row >> 7) + ((row >> 1) & 1) + up - 1
        tap_j = 2 * ((row >> 6) & 1) + (row & 1) + side - 1
        inside = (tap_i >= 0) & (tap_i <= 2) & (tap_j >= 0) & (tap_j <= 2)
        source = (tap_i * 3 + tap_j) * LAT_CH + ((row & 63) >> 2)
        pick = jnp.where(inside & (source == col), 1.0, 0.0).astype(BF16)
        w_full[parity] = dot(pick, w_sum[...]).astype(BF16)

    def rows_of(block):
        return block.astype(F32).reshape(rows, width).astype(BF16)

    peer = head_peer(0)
    seven = kv_in.at[pl.ds(0, heads - 1)]
    remote(seven, seven, kv_send, kv_recv, peer).wait_recv()
    own_k = rows_of(kv_in[:, 0])
    own_v = rows_of(kv_in[:, 1])
    for n in range(GROUP):
        cols = slice(n * HEAD_DIM, (n + 1) * HEAD_DIM)
        kv[z, n, 0] = own_k[:, cols]
        kv[z, n, 1] = own_v[:, cols]

    def to_right(ref, recv, send=0):
        return remote(ref, ref, ring_send.at[0] if send == 0 else half_send.at[0], recv, right)

    def to_left(ref, recv, send=0):
        return remote(ref, ref, ring_send.at[1] if send == 0 else half_send.at[1], recv, left)

    pieces_of = [(n, part) for n in range(GROUP) for part in range(2)]

    for n, part in pieces_of:
        to_right(kv.at[z, n, part], ring_recv.at[z, n, part]).start()
        to_left(kv.at[z, n, part], ring_recv.at[z, n, part]).start()
    for load in loads[7:]:
        load.start()

    seven = q_in.at[pl.ds(0, heads - 1)]
    remote(seven, seven, q_a2a_send, q_a2a_recv, peer).wait_recv()
    own_q = rows_of(q_in[...])
    for n in range(GROUP):
        qs[part_of, n] = own_q[:, n * HEAD_DIM : (n + 1) * HEAD_DIM]

    def send_queries(i, carry):
        remote(qs.at[part_of], qs.at[part_of], q_send, q_recv, part_peer(i)).start()
        return carry

    lax.fori_loop(1, PAIR, send_queries, 0)

    def weigh(scores, top):
        return jnp.exp2((scores - top) * (SCORE_SCALE * LOG2E))

    def attend_first(n, carry):
        share = text_k.shape[0] // LAYER
        mine = pl.ds(pl.multiple_of(j * share, share), share)
        cols = pl.ds(pl.multiple_of(n * HEAD_DIM, HEAD_DIM), HEAD_DIM)
        keys_now = jnp.concatenate([text_k[mine, cols], kv[z, n, 0]], axis=0)
        values_now = jnp.concatenate([text_v[mine, cols], kv[z, n, 1]], axis=0)
        scores = dot(keys_now, q_turned[n])
        held = mask_column[mine, :1] * (1 - apart).astype(F32)
        real = jnp.concatenate([held, jnp.ones((rows, 1), F32)], axis=0) == 1.0
        real = jnp.broadcast_to(real, scores.shape)
        scores = jnp.where(real, scores, NEG)
        top = jnp.max(scores, axis=0, keepdims=True)
        weights = jnp.where(real, weigh(scores, top), 0.0)
        run_max[n, :1] = top
        run_sum[n, :1] = jnp.sum(weights, axis=0, keepdims=True)
        run_acc[n] = dot_tn(values_now, weights.astype(BF16))
        return carry

    def absorb(n, slots):
        keys_now = jnp.concatenate([kv[slot, n, 0] for slot in slots], axis=0)
        values_now = jnp.concatenate([kv[slot, n, 1] for slot in slots], axis=0)
        scores = dot(keys_now, q_turned[n])
        old = run_max[n, :1]
        top = jnp.maximum(old, jnp.max(scores, axis=0, keepdims=True))
        factor = weigh(old, top)
        weights = weigh(scores, top)
        total = run_sum[n, :1] * factor + jnp.sum(weights, axis=0, keepdims=True)
        acc = run_acc[n] * factor + dot_tn(values_now, weights.astype(BF16))
        return top, total, acc

    def work_on(n, steps):
        top, total, acc = absorb(n, [slot_at(by) for step in steps for by in (-step, step)])
        run_max[n, :1] = top
        run_sum[n, :1] = total
        run_acc[n] = acc

    def pass_on(step):
        one = slot_at(-step)
        other = slot_at(step)

        def one_head(n, carry):
            for part in range(2):
                copy = to_right(kv.at[one, n, part], ring_recv.at[one, n, part])
                copy.wait_recv()
                copy.start()
                copy = to_left(kv.at[other, n, part], ring_recv.at[other, n, part])
                copy.wait_recv()
                copy.start()
            return carry

        lax.fori_loop(0, GROUP, one_head, 0)

    def pass_on_halves(step):
        one = slot_at(-step)
        other = slot_at(step)

        def one_head(n, carry):
            for part in range(2):
                copy = to_right(kv.at[one, n, part], ring_recv.at[one, n, part], 1)
                copy.wait_recv()
                if part == 0:
                    copy.start()
                copy = to_left(kv.at[other, n, part], ring_recv.at[other, n, part], 1)
                copy.wait_recv()
                if part == 1:
                    copy.start()
            return carry

        lax.fori_loop(0, GROUP, one_head, 0)

    pass_on(1)
    seven = qs.at[pl.ds(0, PAIR - 1)]
    remote(seven, seven, q_send, q_recv, peer).wait_recv()
    half = rows // 2

    def turn_queries(n, carry):
        pieces = [
            qs[y * LAYER + row, n, at * half : (at + 1) * half]
            for at in range(2)
            for row in range(LAYER)
            for y in range(2)
        ]
        q_turned[n] = jnp.concatenate(pieces, axis=0).T
        return carry

    lax.fori_loop(0, GROUP, turn_queries, 0)
    for load in loads[3:7]:
        load.wait()
    mask_column[...] = jnp.broadcast_to(mask[...].astype(F32), (TOK, mask.shape[1])).T
    lax.fori_loop(0, GROUP, attend_first, 0)
    pass_on(2)
    sum_taps()

    def one_parity(parity, carry):
        conv_weights(parity)
        return carry

    lax.fori_loop(0, parities, one_parity, 0)
    pass_on_halves(3)

    def middle_step(n, carry):
        work_on(n, range(1, far - 1))
        return carry

    lax.fori_loop(0, GROUP, middle_step, 0)

    opposite = slot_at(far)
    marks[...] = jnp.zeros_like(marks)

    def last_step(n, carry):
        to_right(kv.at[opposite, n, 0], ring_recv.at[opposite, n, 0]).wait_recv()
        to_left(kv.at[opposite, n, 1], ring_recv.at[opposite, n, 1]).wait_recv()
        top, total, acc = absorb(n, [slot_at(1 - far), slot_at(far - 1), opposite])
        share = (acc / total).T.astype(BF16)
        for i in range(PAIR):
            o_stage[i, n] = share[i * rows : (i + 1) * rows]

        def send_share(i, inner):
            to, row = row_peer(i)

            @pl.when((i != own_row) | (apart == 1))
            def _():
                remote(o_stage.at[row, n], o_in.at[part_of, n], o_send, o_recv, to).start()

            return inner

        lax.fori_loop(0, PAIR, send_share, 0)
        level = top * SCORE_SCALE + jnp.log(total)
        first = level.astype(BF16).astype(F32)
        second = (level - first).astype(BF16).astype(F32)
        marks[pl.ds(3 * n, 1)] = first
        marks[pl.ds(3 * n + 1, 1)] = second
        marks[pl.ds(3 * n + 2, 1)] = level - first - second
        return carry

    lax.fori_loop(0, GROUP, last_step, 0)
    level_rows = marks[...]
    lanes = mark_stage.shape[2]
    for i in range(PAIR):
        turned = level_rows if i == 0 else pltpu.roll(level_rows, (PAIR - i) * rows, 1)
        mark_stage[i] = turned[:, :lanes].astype(BF16)

    def send_marks(i, carry):
        to, row = row_peer(i)

        @pl.when((i != own_row) | (apart == 1))
        def _():
            remote(mark_stage.at[row], mark_in.at[part_of], mark_send, mark_recv, to).start()

        return carry

    lax.fori_loop(0, PAIR, send_marks, 0)
    own_at = row_peer(own_row)[1]

    @pl.when(apart == 0)
    def _():
        o_in[part_of] = o_stage[own_at]
        mark_in[part_of] = mark_stage[own_at]

    for load in loads[7:]:
        load.wait()

    def await_shares(whole, send, recv, sent):
        def wait(ref):
            copy = remote(ref, ref, send, recv, peer)
            if sent:
                copy.wait_send()
            else:
                copy.wait_recv()

        @pl.when(apart == 1)
        def _():
            wait(whole)

        @pl.when(apart == 0)
        def _():
            wait(whole.at[pl.ds(0, PAIR - 1)])

    await_shares(o_in, o_send, o_recv, False)
    await_shares(mark_in, mark_send, mark_recv, False)
    level_parts = [mark_in[i].astype(F32) for i in range(PAIR)]
    shares[...] = jnp.zeros_like(shares)
    for n in range(GROUP):
        levels = [
            part[3 * n : 3 * n + 1] + part[3 * n + 1 : 3 * n + 2] + part[3 * n + 2 : 3 * n + 3]
            for part in level_parts
        ]
        top = functools.reduce(jnp.maximum, levels)
        parts = [jnp.exp(level - top) for level in levels]
        total = functools.reduce(jnp.add, parts)
        for i, part in enumerate(parts):
            shares[n * PAIR + i : n * PAIR + i + 1] = part / total
    columns = shares[...].T[:rows]
    attended = []
    for n in range(GROUP):
        mixed = functools.reduce(
            jnp.add,
            [
                columns[:, n * PAIR + i : n * PAIR + i + 1] * o_in[i, n].astype(F32)
                for i in range(PAIR)
            ],
        )
        attended.append(mixed.astype(BF16))
    attended = jnp.concatenate(attended, axis=1)

    for part in range(rs_parts):
        product = dot(attended, out_w[:, part * part_cols : (part + 1) * part_cols])
        rs_stage[part] = product.reshape(heads, TOK, part_cols).astype(BF16)

        def send_part(i, carry, part=part):
            to = head_peer(i)
            remote(
                rs_stage.at[part, to[1]],
                rs_in.at[part, h],
                rs_send.at[part],
                rs_recv.at[part],
                to,
            ).start()
            return carry

        lax.fori_loop(0, heads, send_part, 0)
    pieces = []
    for part in range(rs_parts):
        cols = slice(part * part_cols, (part + 1) * part_cols)
        whole = rs_in.at[part]
        remote(whole, whole, rs_send.at[part], rs_recv.at[part], peer).wait_recv()
        projected = jnp.sum(rs_in[part].astype(F32), axis=0)
        stream = tokens[:, cols].astype(F32) + gate[:, cols] * (projected + out_bias[:, cols])
        rounded = stream.astype(BF16)
        block_out[:, cols] = rounded
        pieces.append(rounded.astype(F32))
    block_copy = pltpu.make_async_copy(block_out, block_hbm, out_sem.at[0])
    block_copy.start()

    normed_in = jnp.concatenate(pieces, axis=1)
    centered = normed_in - jnp.mean(normed_in, axis=1, keepdims=True)
    spread = jnp.mean(centered * centered, axis=1, keepdims=True)
    normed = centered * lax.rsqrt(spread + 1e-06)
    modulated = (normed * (1.0 + scale[...]) + shift[...]).astype(BF16)
    patches = (dot_nt(modulated, final_w[...]) + final_bias[...]) / LATENT_SCALE
    padded = jnp.concatenate([patches, jnp.zeros((TOK, HEAD_DIM - features), F32)], axis=1)
    lat[...] = padded.astype(BF16)

    for at, to in enumerate(halo_peers):
        remote(lat, halo.at[at], halo_send, halo_recv, to).start()
    tiles = {(0, 0): lat[...].astype(F32)}
    remote(halo, halo, halo_send, halo_recv, peer).wait_recv()
    for at, (dr, dc) in enumerate(halo_steps):
        tiles[(-dr, -dc)] = halo[at].astype(F32)

    def rolled(tile, by):
        return pltpu.roll(tile, by % HEAD_DIM, 1)

    top_edge, bottom_edge = s == 0, s == seqs - 1
    first_tile, last_tile = h == 0, h == heads - 1
    for dc in (-1, 0, 1):
        middle = tiles[(0, dc)]
        tiles[(-1, dc)] = jnp.where(top_edge, rolled(middle, 2), tiles[(-1, dc)])
        tiles[(1, dc)] = jnp.where(bottom_edge, rolled(middle, -2), tiles[(1, dc)])
    low = lax.broadcasted_iota(jnp.int32, (1, HEAD_DIM), 1) < features
    packed = {}
    for dr in (-1, 0, 1):
        middle = tiles[(dr, 0)]
        before = jnp.where(first_tile, rolled(middle, 1)[:1], tiles[(dr, -1)][TOK - 1 :])
        after = jnp.where(last_tile, rolled(middle, -1)[TOK - 1 :], tiles[(dr, 1)][:1])
        before = jnp.concatenate([before, middle[: TOK - 1]], axis=0)
        after = jnp.concatenate([middle[1:], after], axis=0)
        packed[(dr, 0)] = jnp.where(low, before, rolled(middle, features))
        packed[(dr, 1)] = jnp.where(low, middle, rolled(after, features))
    for parity in range(parities):
        up, side = parity // 2, parity % 2
        stacked = jnp.concatenate([packed[(up - 1, side)], packed[(up, side)]], axis=1)
        result = dot(stacked.astype(BF16), w_full[parity]) + conv_bias[...]
        for tile in range(pixels.shape[1]):
            pixels[up, tile, pl.ds(side, TOK, stride=2), :] = result[
                :, tile * HEAD_DIM : (tile + 1) * HEAD_DIM
            ]
    for tile in range(pixels.shape[1]):
        cols = slice(tile * HEAD_DIM, (tile + 1) * HEAD_DIM)
        decoded[:, :, cols] = pixels[:, tile].astype(BF16)
    decoded_copy = pltpu.make_async_copy(decoded, decoded_hbm, out_sem.at[1])
    decoded_copy.start()

    seven = kv_stage.at[pl.ds(0, heads - 1)]
    remote(seven, seven, kv_send, kv_recv, peer).wait_send()
    seven = q_stage.at[pl.ds(0, heads - 1)]
    remote(seven, seven, q_a2a_send, q_a2a_recv, peer).wait_send()
    ring_all = kv.at[pl.ds(0, far - 1)]
    to_right(ring_all, ring_recv.at[0, 0, 0]).wait_send()
    to_left(ring_all, ring_recv.at[0, 0, 0]).wait_send()
    ring_half = kv.at[0, :, 0]
    to_right(ring_half, ring_recv.at[0, 0, 0], 1).wait_send()
    to_left(ring_half, ring_recv.at[0, 0, 0], 1).wait_send()
    seven = qs.at[pl.ds(0, PAIR - 1)]
    remote(seven, seven, q_send, q_recv, peer).wait_send()
    await_shares(o_stage, o_send, o_recv, True)
    await_shares(mark_stage, mark_send, mark_recv, True)
    for part in range(rs_parts):
        whole = rs_stage.at[part]
        remote(whole, whole, rs_send.at[part], rs_recv.at[part], peer).wait_send()
    remote(halo, halo, halo_send, halo_recv, peer).wait_send()
    block_copy.wait()
    decoded_copy.wait()


def hand_over(block_in, decoded_in, block_to, decoded_to, block, decoded, sem):
    rooms = ((block_in, block, block_to), (decoded_in, decoded, decoded_to))
    loads = [pltpu.make_async_copy(a, b, sem.at[i]) for i, (a, b, _) in enumerate(rooms)]
    stores = [pltpu.make_async_copy(b, c, sem.at[2 + i]) for i, (_, b, c) in enumerate(rooms)]
    for load in loads:
        load.start()
    for load, store in zip(loads, stores):
        load.wait()
        store.start()
    for store in stores:
        store.wait()


def body(seqs, heads, *args):
    (
        queries,
        keys,
        values,
        text_keys,
        text_values,
        text_mask,
        tokens,
        out_weight,
        out_bias,
        gate,
        shift,
        scale,
        final_weight,
        final_bias,
        conv_weight,
        conv_bias,
    ) = args
    dim = queries.shape[3]
    width = GROUP * HEAD_DIM
    text = text_keys.shape[0]
    layers = seqs // PAIR
    far = layers // 2
    rows = heads * TOK
    features = final_weight.shape[1]
    taps = 9 * LAT_CH
    channels = conv_weight.shape[4]
    rs_parts = 2
    operands = (
        queries.reshape(TOK, dim),
        keys.reshape(TOK, dim),
        values.reshape(TOK, dim),
        text_keys,
        text_values,
        text_mask.reshape(1, text),
        tokens.reshape(TOK, dim),
        out_weight,
        out_bias.reshape(1, dim),
        gate.reshape(1, dim),
        shift.reshape(1, dim),
        scale.reshape(1, dim),
        final_weight.T,
        final_bias.reshape(1, features),
        conv_weight.reshape(3 * taps, channels),
        conv_bias.reshape(1, channels),
    )
    copied = [pltpu.VMEM(x.shape, x.dtype) for x in operands]
    dma = pltpu.SemaphoreType.DMA
    anywhere = pl.BlockSpec(memory_space=pl.ANY)
    results = (
        jax.ShapeDtypeStruct((TOK, dim), BF16),
        jax.ShapeDtypeStruct((2, 2 * TOK, channels), BF16),
    )
    block_out, decoded = pl.pallas_call(
        functools.partial(kernel, seqs, heads),
        out_shape=results,
        in_specs=[anywhere] * len(operands),
        out_specs=(anywhere, anywhere),
        scratch_shapes=copied
        + [
            pltpu.VMEM((heads, 2, TOK, width), BF16),
            pltpu.VMEM((heads, TOK, width), BF16),
            pltpu.VMEM((heads, 2, TOK, width), BF16),
            pltpu.VMEM((heads, TOK, width), BF16),
            pltpu.VMEM((layers, GROUP, 2, rows, HEAD_DIM), BF16),
            pltpu.VMEM((PAIR, GROUP, rows, HEAD_DIM), BF16),
            pltpu.VMEM((GROUP, HEAD_DIM, PAIR * rows), BF16),
            pltpu.VMEM((text, TOK), F32),
            pltpu.VMEM((GROUP, TOK, PAIR * rows), F32),
            pltpu.VMEM((GROUP, TOK, PAIR * rows), F32),
            pltpu.VMEM((GROUP, HEAD_DIM, PAIR * rows), F32),
            pltpu.VMEM((16, PAIR * rows), F32),
            pltpu.VMEM((PAIR, 16, HEAD_DIM), BF16),
            pltpu.VMEM((PAIR, 16, HEAD_DIM), BF16),
            pltpu.VMEM((GROUP * PAIR, HEAD_DIM), F32),
            pltpu.VMEM((PAIR, GROUP, rows, HEAD_DIM), BF16),
            pltpu.VMEM((PAIR, GROUP, rows, HEAD_DIM), BF16),
            pltpu.VMEM((rs_parts, heads, TOK, dim // rs_parts), BF16),
            pltpu.VMEM((rs_parts, heads, TOK, dim // rs_parts), BF16),
            pltpu.VMEM((TOK, HEAD_DIM), BF16),
            pltpu.VMEM((8, TOK, HEAD_DIM), BF16),
            pltpu.VMEM((taps, channels), BF16),
            pltpu.VMEM((4, 4 * features, channels), BF16),
            pltpu.VMEM((2, channels // HEAD_DIM, 2 * TOK, HEAD_DIM), F32),
            pltpu.VMEM((TOK, dim), BF16),
            pltpu.VMEM((2, 2 * TOK, channels), BF16),
            dma((len(operands),)),
            dma((2,)),
            dma,
            dma,
            dma,
            dma,
            dma((2,)),
            dma((2,)),
            dma((layers, GROUP, 2)),
            dma,
            dma,
            dma,
            dma,
            dma,
            dma,
            dma((rs_parts,)),
            dma((rs_parts,)),
            dma,
            dma,
        ],
        compiler_params=pltpu.CompilerParams(
            collective_id=0, has_side_effects=True, vmem_limit_bytes=60 * 1024 * 1024
        ),
        cost_estimate=pl.CostEstimate(
            flops=1_200_000_000, bytes_accessed=5_000_000, transcendentals=1_000_000
        ),
    )(*operands)
    block_out, decoded = pl.pallas_call(
        hand_over,
        out_shape=results,
        in_specs=[anywhere] * 2,
        out_specs=(anywhere, anywhere),
        scratch_shapes=[pltpu.VMEM(x.shape, x.dtype) for x in results] + [dma((4,))],
        compiler_params=pltpu.CompilerParams(vmem_limit_bytes=60 * 1024 * 1024),
    )(block_out, decoded)
    return (
        block_out.reshape(1, TOK, 1, dim),
        decoded.reshape(1, 2, 2 * TOK, channels),
    )


def solution(mesh):
    seqs = mesh.shape["seq"]
    heads = mesh.shape["head"]
    spread = P("seq", "head", None, None)
    in_specs = (
        spread,
        spread,
        spread,
        P(None, "head"),
        P(None, "head"),
        P(),
        spread,
        P("head", None),
    ) + (P(),) * 8
    out_specs = (spread, P(None, "seq", "head", None))
    return jax.shard_map(
        functools.partial(body, seqs, heads),
        mesh=mesh,
        in_specs=in_specs,
        out_specs=out_specs,
        check_vma=False,
    )
```

```python
import functools

import jax
import jax.numpy as jnp
from jax import lax
from jax.experimental import pallas as pl
from jax.experimental.pallas import tpu as pltpu
from jax.sharding import PartitionSpec as P

HEAD_DIM = 128
GROUP = 3
LAT_CH = 16
TOK = 8
LAYER = 4
PAIR = 8
COLUMNS = 4
LATENT_SCALE = 0.476986
NEG = -1e30
SCORE_SCALE = HEAD_DIM ** (-0.5)
LOG2E = 1.4426950408889634
BF16 = jnp.bfloat16
F32 = jnp.float32
MESH = pl.DeviceIdType.MESH


def dot(a, b):
    return jnp.dot(a, b, preferred_element_type=F32)


def dot_tn(a, b):
    return lax.dot_general(a, b, (((0,), (0,)), ((), ())), preferred_element_type=F32)


def dot_nt(a, b):
    return lax.dot_general(a, b, (((1,), (1,)), ((), ())), preferred_element_type=F32)


def kernel(
    seqs,
    heads,
    q_hbm,
    k_hbm,
    v_hbm,
    text_k_hbm,
    text_v_hbm,
    mask_hbm,
    tokens_hbm,
    out_w_hbm,
    out_bias_hbm,
    gate_hbm,
    shift_hbm,
    scale_hbm,
    final_w_hbm,
    final_bias_hbm,
    conv_w_hbm,
    conv_bias_hbm,
    block_hbm,
    decoded_hbm,
    queries,
    keys,
    values,
    text_k,
    text_v,
    mask,
    tokens,
    out_w,
    out_bias,
    gate,
    shift,
    scale,
    final_w,
    final_bias,
    conv_w,
    conv_bias,
    kv_stage,
    q_stage,
    kv_in,
    q_in,
    kv,
    qs,
    q_turned,
    mask_column,
    run_max,
    run_sum,
    run_acc,
    marks,
    mark_stage,
    mark_in,
    shares,
    o_stage,
    o_in,
    rs_stage,
    rs_in,
    lat,
    halo,
    w_sum,
    w_full,
    pixels,
    block_out,
    decoded,
    local_sem,
    out_sem,
    kv_send,
    kv_recv,
    q_a2a_send,
    q_a2a_recv,
    ring_send,
    half_send,
    ring_recv,
    q_send,
    q_recv,
    o_send,
    o_recv,
    mark_send,
    mark_recv,
    rs_send,
    rs_recv,
    halo_send,
    halo_recv,
):
    s = lax.axis_index("seq")
    h = lax.axis_index("head")
    layers = seqs // PAIR
    far = layers // 2
    depth = s // LAYER
    j = lax.rem(s, LAYER)
    z = depth // 2
    parity_z = lax.rem(depth, 2)
    column = lax.rem(h, COLUMNS)
    y_high = h // COLUMNS
    part_of = y_high * LAYER + j
    place = parity_z * COLUMNS + column
    apart = lax.rem(y_high + parity_z, 2)
    width = GROUP * HEAD_DIM
    dim = heads * width
    rows = heads * TOK
    rs_parts = rs_stage.shape[0]
    part_cols = dim // rs_parts

    def shifted(index, by, count):
        return lax.rem(index + (by % count), count)

    r = lax.rem(j + LAYER // 2, LAYER)

    def head_peer(i):
        return (depth * LAYER + r, shifted(h, i, heads))

    def part_peer(i):
        part = lax.rem(part_of + i, PAIR)
        return (depth * LAYER + lax.rem(part, LAYER), (part // LAYER) * COLUMNS + column)

    def row_peer(i):
        at_parity = lax.rem(parity_z + i // LAYER, 2)
        row = lax.rem(j + lax.rem(i, LAYER), LAYER)
        owner = lax.rem(row + LAYER // 2, LAYER)
        to = ((z * 2 + at_parity) * LAYER + owner, parity_z * COLUMNS + column)
        return to, at_parity * LAYER + row

    own_row = LAYER // 2

    def share_source(i):
        part = lax.rem(part_of + i, PAIR)
        at = (z * 2 + y_high) * LAYER + lax.rem(part, LAYER)
        return (at, (part // LAYER) * COLUMNS + column)

    def slot_at(by):
        return lax.rem(z + by + layers, layers)

    def group_peer(i, by=0):
        at_depth = slot_at(by) * 2 + lax.rem(parity_z + i // COLUMNS, 2)
        at_column = lax.rem(column + lax.rem(i, COLUMNS), COLUMNS)
        group = lax.rem(at_depth, 2) * COLUMNS + at_column
        return (at_depth * LAYER + j, y_high * COLUMNS + at_column), group

    def ring_peer(by):
        return ((slot_at(by) * 2 + parity_z) * LAYER + j, h)

    right, left = ring_peer(1), ring_peer(-1)

    def remote(src, dst, send, recv, device):
        return pltpu.make_async_remote_copy(
            src_ref=src,
            dst_ref=dst,
            send_sem=send,
            recv_sem=recv,
            device_id=device,
            device_id_type=MESH,
        )

    pairs = (
        (k_hbm, keys),
        (v_hbm, values),
        (q_hbm, queries),
        (conv_w_hbm, conv_w),
        (text_k_hbm, text_k),
        (text_v_hbm, text_v),
        (mask_hbm, mask),
        (tokens_hbm, tokens),
        (out_w_hbm, out_w),
        (out_bias_hbm, out_bias),
        (gate_hbm, gate),
        (shift_hbm, shift),
        (scale_hbm, scale),
        (final_w_hbm, final_w),
        (final_bias_hbm, final_bias),
        (conv_bias_hbm, conv_bias),
    )
    loads = [
        pltpu.make_async_copy(src, dst, local_sem.at[i]) for i, (src, dst) in enumerate(pairs)
    ]

    halo_steps = [(dr, dc) for dr in (-1, 0, 1) for dc in (-1, 0, 1) if (dr, dc) != (0, 0)]
    halo_peers = [(shifted(s, dr, seqs), shifted(h, dc, heads)) for dr, dc in halo_steps]
    partners = [group_peer(i)[0] for i in range(1, heads)]
    partners += [group_peer(i, by)[0] for by in (1, -1) for i in range(heads)]
    partners += [part_peer(i) for i in range(1, PAIR)]
    partners += [share_source(i) for i in range(1, PAIR)]
    partners += [head_peer(i) for i in range(heads)]
    partners += halo_peers
    for load in loads[:3]:
        load.start()
    barrier = pltpu.get_barrier_semaphore()
    for partner in partners:
        pl.semaphore_signal(barrier, inc=1, device_id=partner, device_id_type=MESH)

    @pl.when(apart == 1)
    def _():
        pl.semaphore_signal(barrier, inc=1, device_id=share_source(0), device_id_type=MESH)

    group_cols = [slice(g * width, (g + 1) * width) for g in range(heads)]
    for at, whole in enumerate((keys, values)):
        loads[at].wait()
        for g, cols in enumerate(group_cols):
            kv_stage[g, at] = whole[:, cols]
    pl.semaphore_wait(barrier, len(partners) + apart)

    sides = ((1, 1), (2, -1), (0, 0))
    for at, by in sides:
        def send_kv(i, carry, at=at, by=by):
            to, group = group_peer(i, by)
            remote(
                kv_stage.at[group], kv_in.at[at, place], kv_send.at[at], kv_recv.at[at], to
            ).start()
            return carry

        lax.fori_loop(0 if by else 1, heads, send_kv, 0)
    kv_in[0, place] = kv_stage[place]

    def send_q(i, carry):
        to, group = group_peer(i)
        remote(q_stage.at[group], q_in.at[place], q_a2a_send, q_a2a_recv, to).start()
        return carry

    loads[2].wait()
    for g, cols in enumerate(group_cols):
        q_stage[g] = queries[:, cols]
    lax.fori_loop(1, heads, send_q, 0)
    q_in[place] = q_stage[place]
    for load in loads[3:7]:
        load.start()

    taps = w_sum.shape[0]
    parities = w_full.shape[0]
    features = final_w.shape[0]

    def sum_taps():
        conv_all = conv_w[...].astype(F32)
        total = conv_all[:taps] + conv_all[taps : 2 * taps] + conv_all[2 * taps :]
        w_sum[...] = total.astype(BF16)

    def conv_weights(parity):
        up = parity // 2
        side = lax.rem(parity, 2)
        depth = w_full.shape[1]
        row = lax.broadcasted_iota(jnp.int32, (depth, taps), 0)
        col = lax.broadcasted_iota(jnp.int32, (depth, taps), 1)
        tap_i = 2 * (row >> 7) + ((row >> 1) & 1) + up - 1
        tap_j = 2 * ((row >> 6) & 1) + (row & 1) + side - 1
        inside = (tap_i >= 0) & (tap_i <= 2) & (tap_j >= 0) & (tap_j <= 2)
        source = (tap_i * 3 + tap_j) * LAT_CH + ((row & 63) >> 2)
        pick = jnp.where(inside & (source == col), 1.0, 0.0).astype(BF16)
        w_full[parity] = dot(pick, w_sum[...]).astype(BF16)

    def rows_of(block):
        return block.astype(F32).reshape(rows, width).astype(BF16)

    peer = head_peer(0)

    def settle(at, by):
        came = kv_in.at[at] if by else kv_in.at[at, pl.ds(0, heads - 1)]
        remote(came, came, kv_send.at[at], kv_recv.at[at], peer).wait_recv()
        slot = slot_at(by)
        for part in range(2):
            whole = rows_of(kv_in[at, :, part])
            for n in range(GROUP):
                kv[slot, n, part] = whole[:, n * HEAD_DIM : (n + 1) * HEAD_DIM]

    def to_right(ref, recv, send=0):
        return remote(ref, ref, ring_send.at[0] if send == 0 else half_send.at[0], recv, right)

    def to_left(ref, recv, send=0):
        return remote(ref, ref, ring_send.at[1] if send == 0 else half_send.at[1], recv, left)

    pieces_of = [(n, part) for n in range(GROUP) for part in range(2)]

    settle(1, -1)
    for n, part in pieces_of:
        ref = kv.at[slot_at(-1), n, part]
        to_right(ref, ring_recv.at[slot_at(-1), n, part]).start()
    settle(2, 1)
    for n, part in pieces_of:
        ref = kv.at[slot_at(1), n, part]
        to_left(ref, ring_recv.at[slot_at(1), n, part]).start()
    settle(0, 0)
    for load in loads[7:]:
        load.start()

    seven = q_in.at[pl.ds(0, heads - 1)]
    remote(seven, seven, q_a2a_send, q_a2a_recv, peer).wait_recv()
    own_q = rows_of(q_in[...])
    for n in range(GROUP):
        qs[part_of, n] = own_q[:, n * HEAD_DIM : (n + 1) * HEAD_DIM]

    def send_queries(i, carry):
        remote(qs.at[part_of], qs.at[part_of], q_send, q_recv, part_peer(i)).start()
        return carry

    lax.fori_loop(1, PAIR, send_queries, 0)

    def weigh(scores, top):
        return jnp.exp2((scores - top) * (SCORE_SCALE * LOG2E))

    def attend_first(n, carry):
        share = text_k.shape[0] // LAYER
        mine = pl.ds(pl.multiple_of(j * share, share), share)
        cols = pl.ds(pl.multiple_of(n * HEAD_DIM, HEAD_DIM), HEAD_DIM)
        keys_now = jnp.concatenate([text_k[mine, cols], kv[z, n, 0]], axis=0)
        values_now = jnp.concatenate([text_v[mine, cols], kv[z, n, 1]], axis=0)
        scores = dot(keys_now, q_turned[n])
        held = mask_column[mine, :1] * (1 - apart).astype(F32)
        real = jnp.concatenate([held, jnp.ones((rows, 1), F32)], axis=0) == 1.0
        real = jnp.broadcast_to(real, scores.shape)
        scores = jnp.where(real, scores, NEG)
        top = jnp.max(scores, axis=0, keepdims=True)
        weights = jnp.where(real, weigh(scores, top), 0.0)
        run_max[n, :1] = top
        run_sum[n, :1] = jnp.sum(weights, axis=0, keepdims=True)
        run_acc[n] = dot_tn(values_now, weights.astype(BF16))
        return carry

    def absorb(n, slots):
        keys_now = jnp.concatenate([kv[slot, n, 0] for slot in slots], axis=0)
        values_now = jnp.concatenate([kv[slot, n, 1] for slot in slots], axis=0)
        scores = dot(keys_now, q_turned[n])
        old = run_max[n, :1]
        top = jnp.maximum(old, jnp.max(scores, axis=0, keepdims=True))
        factor = weigh(old, top)
        weights = weigh(scores, top)
        total = run_sum[n, :1] * factor + jnp.sum(weights, axis=0, keepdims=True)
        acc = run_acc[n] * factor + dot_tn(values_now, weights.astype(BF16))
        return top, total, acc

    def work_on(n, steps):
        top, total, acc = absorb(n, [slot_at(by) for step in steps for by in (-step, step)])
        run_max[n, :1] = top
        run_sum[n, :1] = total
        run_acc[n] = acc

    def pass_on(step):
        one = slot_at(-step)
        other = slot_at(step)

        def one_head(n, carry):
            for part in range(2):
                copy = to_right(kv.at[one, n, part], ring_recv.at[one, n, part])
                copy.wait_recv()
                copy.start()
                copy = to_left(kv.at[other, n, part], ring_recv.at[other, n, part])
                copy.wait_recv()
                copy.start()
            return carry

        lax.fori_loop(0, GROUP, one_head, 0)

    def pass_on_halves(step):
        one = slot_at(-step)
        other = slot_at(step)

        def one_head(n, carry):
            for part in range(2):
                copy = to_right(kv.at[one, n, part], ring_recv.at[one, n, part], 1)
                copy.wait_recv()
                if part == 0:
                    copy.start()
                copy = to_left(kv.at[other, n, part], ring_recv.at[other, n, part], 1)
                copy.wait_recv()
                if part == 1:
                    copy.start()
            return carry

        lax.fori_loop(0, GROUP, one_head, 0)

    seven = qs.at[pl.ds(0, PAIR - 1)]
    remote(seven, seven, q_send, q_recv, peer).wait_recv()
    half = rows // 2

    def turn_queries(n, carry):
        pieces = [
            qs[y * LAYER + row, n, at * half : (at + 1) * half]
            for at in range(2)
            for row in range(LAYER)
            for y in range(2)
        ]
        q_turned[n] = jnp.concatenate(pieces, axis=0).T
        return carry

    lax.fori_loop(0, GROUP, turn_queries, 0)
    for load in loads[3:7]:
        load.wait()
    mask_column[...] = jnp.broadcast_to(mask[...].astype(F32), (TOK, mask.shape[1])).T
    lax.fori_loop(0, GROUP, attend_first, 0)
    pass_on(2)
    sum_taps()

    def one_parity(parity, carry):
        conv_weights(parity)
        return carry

    lax.fori_loop(0, parities, one_parity, 0)
    pass_on_halves(3)

    def middle_step(n, carry):
        work_on(n, range(1, far - 1))
        return carry

    lax.fori_loop(0, GROUP, middle_step, 0)

    opposite = slot_at(far)
    marks[...] = jnp.zeros_like(marks)

    def last_step(n, carry):
        to_right(kv.at[opposite, n, 0], ring_recv.at[opposite, n, 0]).wait_recv()
        to_left(kv.at[opposite, n, 1], ring_recv.at[opposite, n, 1]).wait_recv()
        top, total, acc = absorb(n, [slot_at(1 - far), slot_at(far - 1), opposite])
        share = (acc / total).T.astype(BF16)
        for i in range(PAIR):
            o_stage[i, n] = share[i * rows : (i + 1) * rows]

        def send_share(i, inner):
            to, row = row_peer(i)

            @pl.when((i != own_row) | (apart == 1))
            def _():
                remote(o_stage.at[row, n], o_in.at[part_of, n], o_send, o_recv, to).start()

            return inner

        lax.fori_loop(0, PAIR, send_share, 0)
        level = top * SCORE_SCALE + jnp.log(total)
        first = level.astype(BF16).astype(F32)
        second = (level - first).astype(BF16).astype(F32)
        marks[pl.ds(3 * n, 1)] = first
        marks[pl.ds(3 * n + 1, 1)] = second
        marks[pl.ds(3 * n + 2, 1)] = level - first - second
        return carry

    lax.fori_loop(0, GROUP, last_step, 0)
    level_rows = marks[...]
    lanes = mark_stage.shape[2]
    for i in range(PAIR):
        turned = level_rows if i == 0 else pltpu.roll(level_rows, (PAIR - i) * rows, 1)
        mark_stage[i] = turned[:, :lanes].astype(BF16)

    def send_marks(i, carry):
        to, row = row_peer(i)

        @pl.when((i != own_row) | (apart == 1))
        def _():
            remote(mark_stage.at[row], mark_in.at[part_of], mark_send, mark_recv, to).start()

        return carry

    lax.fori_loop(0, PAIR, send_marks, 0)
    own_at = row_peer(own_row)[1]

    @pl.when(apart == 0)
    def _():
        o_in[part_of] = o_stage[own_at]
        mark_in[part_of] = mark_stage[own_at]

    for load in loads[7:]:
        load.wait()

    def await_shares(whole, send, recv, sent):
        def wait(ref):
            copy = remote(ref, ref, send, recv, peer)
            if sent:
                copy.wait_send()
            else:
                copy.wait_recv()

        @pl.when(apart == 1)
        def _():
            wait(whole)

        @pl.when(apart == 0)
        def _():
            wait(whole.at[pl.ds(0, PAIR - 1)])

    await_shares(o_in, o_send, o_recv, False)
    await_shares(mark_in, mark_send, mark_recv, False)
    level_parts = [mark_in[i].astype(F32) for i in range(PAIR)]
    shares[...] = jnp.zeros_like(shares)
    for n in range(GROUP):
        levels = [
            part[3 * n : 3 * n + 1] + part[3 * n + 1 : 3 * n + 2] + part[3 * n + 2 : 3 * n + 3]
            for part in level_parts
        ]
        top = functools.reduce(jnp.maximum, levels)
        parts = [jnp.exp(level - top) for level in levels]
        total = functools.reduce(jnp.add, parts)
        for i, part in enumerate(parts):
            shares[n * PAIR + i : n * PAIR + i + 1] = part / total
    columns = shares[...].T[:rows]
    attended = []
    for n in range(GROUP):
        mixed = functools.reduce(
            jnp.add,
            [
                columns[:, n * PAIR + i : n * PAIR + i + 1] * o_in[i, n].astype(F32)
                for i in range(PAIR)
            ],
        )
        attended.append(mixed.astype(BF16))
    attended = jnp.concatenate(attended, axis=1)

    for part in range(rs_parts):
        product = dot(attended, out_w[:, part * part_cols : (part + 1) * part_cols])
        rs_stage[part] = product.reshape(heads, TOK, part_cols).astype(BF16)

        def send_part(i, carry, part=part):
            to = head_peer(i)
            remote(
                rs_stage.at[part, to[1]],
                rs_in.at[part, h],
                rs_send.at[part],
                rs_recv.at[part],
                to,
            ).start()
            return carry

        lax.fori_loop(0, heads, send_part, 0)
    pieces = []
    for part in range(rs_parts):
        cols = slice(part * part_cols, (part + 1) * part_cols)
        whole = rs_in.at[part]
        remote(whole, whole, rs_send.at[part], rs_recv.at[part], peer).wait_recv()
        projected = jnp.sum(rs_in[part].astype(F32), axis=0)
        stream = tokens[:, cols].astype(F32) + gate[:, cols] * (projected + out_bias[:, cols])
        rounded = stream.astype(BF16)
        block_out[:, cols] = rounded
        pieces.append(rounded.astype(F32))
    block_copy = pltpu.make_async_copy(block_out, block_hbm, out_sem.at[0])
    block_copy.start()

    normed_in = jnp.concatenate(pieces, axis=1)
    centered = normed_in - jnp.mean(normed_in, axis=1, keepdims=True)
    spread = jnp.mean(centered * centered, axis=1, keepdims=True)
    normed = centered * lax.rsqrt(spread + 1e-06)
    modulated = (normed * (1.0 + scale[...]) + shift[...]).astype(BF16)
    patches = (dot_nt(modulated, final_w[...]) + final_bias[...]) / LATENT_SCALE
    padded = jnp.concatenate([patches, jnp.zeros((TOK, HEAD_DIM - features), F32)], axis=1)
    lat[...] = padded.astype(BF16)

    for at, to in enumerate(halo_peers):
        remote(lat, halo.at[at], halo_send, halo_recv, to).start()
    tiles = {(0, 0): lat[...].astype(F32)}
    remote(halo, halo, halo_send, halo_recv, peer).wait_recv()
    for at, (dr, dc) in enumerate(halo_steps):
        tiles[(-dr, -dc)] = halo[at].astype(F32)

    def rolled(tile, by):
        return pltpu.roll(tile, by % HEAD_DIM, 1)

    top_edge, bottom_edge = s == 0, s == seqs - 1
    first_tile, last_tile = h == 0, h == heads - 1
    for dc in (-1, 0, 1):
        middle = tiles[(0, dc)]
        tiles[(-1, dc)] = jnp.where(top_edge, rolled(middle, 2), tiles[(-1, dc)])
        tiles[(1, dc)] = jnp.where(bottom_edge, rolled(middle, -2), tiles[(1, dc)])
    low = lax.broadcasted_iota(jnp.int32, (1, HEAD_DIM), 1) < features
    packed = {}
    for dr in (-1, 0, 1):
        middle = tiles[(dr, 0)]
        before = jnp.where(first_tile, rolled(middle, 1)[:1], tiles[(dr, -1)][TOK - 1 :])
        after = jnp.where(last_tile, rolled(middle, -1)[TOK - 1 :], tiles[(dr, 1)][:1])
        before = jnp.concatenate([before, middle[: TOK - 1]], axis=0)
        after = jnp.concatenate([middle[1:], after], axis=0)
        packed[(dr, 0)] = jnp.where(low, before, rolled(middle, features))
        packed[(dr, 1)] = jnp.where(low, middle, rolled(after, features))
    for parity in range(parities):
        up, side = parity // 2, parity % 2
        stacked = jnp.concatenate([packed[(up - 1, side)], packed[(up, side)]], axis=1)
        result = dot(stacked.astype(BF16), w_full[parity]) + conv_bias[...]
        for tile in range(pixels.shape[1]):
            pixels[up, tile, pl.ds(side, TOK, stride=2), :] = result[
                :, tile * HEAD_DIM : (tile + 1) * HEAD_DIM
            ]
    for tile in range(pixels.shape[1]):
        cols = slice(tile * HEAD_DIM, (tile + 1) * HEAD_DIM)
        decoded[:, :, cols] = pixels[:, tile].astype(BF16)
    decoded_copy = pltpu.make_async_copy(decoded, decoded_hbm, out_sem.at[1])
    decoded_copy.start()

    for at, by in sides:
        gone = kv_stage if by else kv_stage.at[pl.ds(0, heads - 1)]
        remote(gone, gone, kv_send.at[at], kv_recv.at[at], peer).wait_send()
    seven = q_stage.at[pl.ds(0, heads - 1)]
    remote(seven, seven, q_a2a_send, q_a2a_recv, peer).wait_send()
    ring_all = kv.at[pl.ds(0, far - 2)]
    to_right(ring_all, ring_recv.at[0, 0, 0]).wait_send()
    to_left(ring_all, ring_recv.at[0, 0, 0]).wait_send()
    ring_half = kv.at[0, :, 0]
    to_right(ring_half, ring_recv.at[0, 0, 0], 1).wait_send()
    to_left(ring_half, ring_recv.at[0, 0, 0], 1).wait_send()
    seven = qs.at[pl.ds(0, PAIR - 1)]
    remote(seven, seven, q_send, q_recv, peer).wait_send()
    await_shares(o_stage, o_send, o_recv, True)
    await_shares(mark_stage, mark_send, mark_recv, True)
    for part in range(rs_parts):
        whole = rs_stage.at[part]
        remote(whole, whole, rs_send.at[part], rs_recv.at[part], peer).wait_send()
    remote(halo, halo, halo_send, halo_recv, peer).wait_send()
    block_copy.wait()
    decoded_copy.wait()


def hand_over(block_in, decoded_in, block_to, decoded_to, block, decoded, sem):
    rooms = ((block_in, block, block_to), (decoded_in, decoded, decoded_to))
    loads = [pltpu.make_async_copy(a, b, sem.at[i]) for i, (a, b, _) in enumerate(rooms)]
    stores = [pltpu.make_async_copy(b, c, sem.at[2 + i]) for i, (_, b, c) in enumerate(rooms)]
    for load in loads:
        load.start()
    for load, store in zip(loads, stores):
        load.wait()
        store.start()
    for store in stores:
        store.wait()


def body(seqs, heads, *args):
    (
        queries,
        keys,
        values,
        text_keys,
        text_values,
        text_mask,
        tokens,
        out_weight,
        out_bias,
        gate,
        shift,
        scale,
        final_weight,
        final_bias,
        conv_weight,
        conv_bias,
    ) = args
    dim = queries.shape[3]
    width = GROUP * HEAD_DIM
    text = text_keys.shape[0]
    layers = seqs // PAIR
    far = layers // 2
    rows = heads * TOK
    features = final_weight.shape[1]
    taps = 9 * LAT_CH
    channels = conv_weight.shape[4]
    rs_parts = 2
    operands = (
        queries.reshape(TOK, dim),
        keys.reshape(TOK, dim),
        values.reshape(TOK, dim),
        text_keys,
        text_values,
        text_mask.reshape(1, text),
        tokens.reshape(TOK, dim),
        out_weight,
        out_bias.reshape(1, dim),
        gate.reshape(1, dim),
        shift.reshape(1, dim),
        scale.reshape(1, dim),
        final_weight.T,
        final_bias.reshape(1, features),
        conv_weight.reshape(3 * taps, channels),
        conv_bias.reshape(1, channels),
    )
    copied = [pltpu.VMEM(x.shape, x.dtype) for x in operands]
    dma = pltpu.SemaphoreType.DMA
    anywhere = pl.BlockSpec(memory_space=pl.ANY)
    results = (
        jax.ShapeDtypeStruct((TOK, dim), BF16),
        jax.ShapeDtypeStruct((2, 2 * TOK, channels), BF16),
    )
    block_out, decoded = pl.pallas_call(
        functools.partial(kernel, seqs, heads),
        out_shape=results,
        in_specs=[anywhere] * len(operands),
        out_specs=(anywhere, anywhere),
        scratch_shapes=copied
        + [
            pltpu.VMEM((heads, 2, TOK, width), BF16),
            pltpu.VMEM((heads, TOK, width), BF16),
            pltpu.VMEM((3, heads, 2, TOK, width), BF16),
            pltpu.VMEM((heads, TOK, width), BF16),
            pltpu.VMEM((layers, GROUP, 2, rows, HEAD_DIM), BF16),
            pltpu.VMEM((PAIR, GROUP, rows, HEAD_DIM), BF16),
            pltpu.VMEM((GROUP, HEAD_DIM, PAIR * rows), BF16),
            pltpu.VMEM((text, TOK), F32),
            pltpu.VMEM((GROUP, TOK, PAIR * rows), F32),
            pltpu.VMEM((GROUP, TOK, PAIR * rows), F32),
            pltpu.VMEM((GROUP, HEAD_DIM, PAIR * rows), F32),
            pltpu.VMEM((16, PAIR * rows), F32),
            pltpu.VMEM((PAIR, 16, HEAD_DIM), BF16),
            pltpu.VMEM((PAIR, 16, HEAD_DIM), BF16),
            pltpu.VMEM((GROUP * PAIR, HEAD_DIM), F32),
            pltpu.VMEM((PAIR, GROUP, rows, HEAD_DIM), BF16),
            pltpu.VMEM((PAIR, GROUP, rows, HEAD_DIM), BF16),
            pltpu.VMEM((rs_parts, heads, TOK, dim // rs_parts), BF16),
            pltpu.VMEM((rs_parts, heads, TOK, dim // rs_parts), BF16),
            pltpu.VMEM((TOK, HEAD_DIM), BF16),
            pltpu.VMEM((8, TOK, HEAD_DIM), BF16),
            pltpu.VMEM((taps, channels), BF16),
            pltpu.VMEM((4, 4 * features, channels), BF16),
            pltpu.VMEM((2, channels // HEAD_DIM, 2 * TOK, HEAD_DIM), F32),
            pltpu.VMEM((TOK, dim), BF16),
            pltpu.VMEM((2, 2 * TOK, channels), BF16),
            dma((len(operands),)),
            dma((2,)),
            dma((3,)),
            dma((3,)),
            dma,
            dma,
            dma((2,)),
            dma((2,)),
            dma((layers, GROUP, 2)),
            dma,
            dma,
            dma,
            dma,
            dma,
            dma,
            dma((rs_parts,)),
            dma((rs_parts,)),
            dma,
            dma,
        ],
        compiler_params=pltpu.CompilerParams(
            collective_id=0, has_side_effects=True, vmem_limit_bytes=60 * 1024 * 1024
        ),
        cost_estimate=pl.CostEstimate(
            flops=1_200_000_000, bytes_accessed=5_000_000, transcendentals=1_000_000
        ),
    )(*operands)
    block_out, decoded = pl.pallas_call(
        hand_over,
        out_shape=results,
        in_specs=[anywhere] * 2,
        out_specs=(anywhere, anywhere),
        scratch_shapes=[pltpu.VMEM(x.shape, x.dtype) for x in results] + [dma((4,))],
        compiler_params=pltpu.CompilerParams(vmem_limit_bytes=60 * 1024 * 1024),
    )(block_out, decoded)
    return (
        block_out.reshape(1, TOK, 1, dim),
        decoded.reshape(1, 2, 2 * TOK, channels),
    )


def solution(mesh):
    seqs = mesh.shape["seq"]
    heads = mesh.shape["head"]
    spread = P("seq", "head", None, None)
    in_specs = (
        spread,
        spread,
        spread,
        P(None, "head"),
        P(None, "head"),
        P(),
        spread,
        P("head", None),
    ) + (P(),) * 8
    out_specs = (spread, P(None, "seq", "head", None))
    return jax.shard_map(
        functools.partial(body, seqs, heads),
        mesh=mesh,
        in_specs=in_specs,
        out_specs=out_specs,
        check_vma=False,
    )
```

```python
import functools

import jax
import jax.numpy as jnp
from jax import lax
from jax.experimental import pallas as pl
from jax.experimental.pallas import tpu as pltpu
from jax.sharding import PartitionSpec as P

HEAD_DIM = 128
GROUP = 3
LAT_CH = 16
TOK = 8
LAYER = 4
PAIR = 8
COLUMNS = 4
LATENT_SCALE = 0.476986
NEG = -1e30
SCORE_SCALE = HEAD_DIM ** (-0.5)
LOG2E = 1.4426950408889634
BF16 = jnp.bfloat16
F32 = jnp.float32
MESH = pl.DeviceIdType.MESH


def dot(a, b):
    return jnp.dot(a, b, preferred_element_type=F32)


def dot_tn(a, b):
    return lax.dot_general(a, b, (((0,), (0,)), ((), ())), preferred_element_type=F32)


def dot_nt(a, b):
    return lax.dot_general(a, b, (((1,), (1,)), ((), ())), preferred_element_type=F32)


def kernel(
    seqs,
    heads,
    q_hbm,
    k_hbm,
    v_hbm,
    text_k_hbm,
    text_v_hbm,
    mask_hbm,
    tokens_hbm,
    out_w_hbm,
    out_bias_hbm,
    gate_hbm,
    shift_hbm,
    scale_hbm,
    final_w_hbm,
    final_bias_hbm,
    conv_w_hbm,
    conv_bias_hbm,
    block_hbm,
    decoded_hbm,
    queries,
    keys,
    values,
    text_k,
    text_v,
    mask,
    tokens,
    out_w,
    out_bias,
    gate,
    shift,
    scale,
    final_w,
    final_bias,
    conv_w,
    conv_bias,
    kv_stage,
    q_stage,
    kv_in,
    q_in,
    kv,
    qs,
    q_turned,
    mask_column,
    run_max,
    run_sum,
    run_acc,
    marks,
    shares,
    o_stage,
    o_in,
    rs_stage,
    rs_in,
    lat,
    halo,
    w_sum,
    w_full,
    pixels,
    block_out,
    decoded,
    local_sem,
    out_sem,
    kv_send,
    kv_recv,
    q_a2a_send,
    q_a2a_recv,
    ring_send,
    half_send,
    ring_recv,
    q_send,
    q_recv,
    o_send,
    o_recv,
    rs_send,
    rs_recv,
    halo_send,
    halo_recv,
):
    s = lax.axis_index("seq")
    h = lax.axis_index("head")
    layers = seqs // PAIR
    far = layers // 2
    depth = s // LAYER
    j = lax.rem(s, LAYER)
    z = depth // 2
    parity_z = lax.rem(depth, 2)
    column = lax.rem(h, COLUMNS)
    y_high = h // COLUMNS
    part_of = y_high * LAYER + j
    place = parity_z * COLUMNS + column
    apart = lax.rem(y_high + parity_z, 2)
    width = GROUP * HEAD_DIM
    dim = heads * width
    rows = heads * TOK
    rs_parts = rs_stage.shape[0]
    part_cols = dim // rs_parts

    def shifted(index, by, count):
        return lax.rem(index + (by % count), count)

    r = lax.rem(j + LAYER // 2, LAYER)

    def head_peer(i):
        return (depth * LAYER + r, shifted(h, i, heads))

    def group_peer(i):
        at_depth = z * 2 + lax.rem(parity_z + i // COLUMNS, 2)
        at_column = lax.rem(column + lax.rem(i, COLUMNS), COLUMNS)
        group = lax.rem(at_depth, 2) * COLUMNS + at_column
        return (at_depth * LAYER + j, y_high * COLUMNS + at_column), group

    def part_peer(i):
        part = lax.rem(part_of + i, PAIR)
        return (depth * LAYER + lax.rem(part, LAYER), (part // LAYER) * COLUMNS + column)

    def row_peer(i):
        at_parity = lax.rem(parity_z + i // LAYER, 2)
        row = lax.rem(j + lax.rem(i, LAYER), LAYER)
        owner = lax.rem(row + LAYER // 2, LAYER)
        to = ((z * 2 + at_parity) * LAYER + owner, parity_z * COLUMNS + column)
        return to, at_parity * LAYER + row

    own_row = LAYER // 2

    def slot_at(by):
        return lax.rem(z + by + layers, layers)

    def ring_peer(by):
        return ((slot_at(by) * 2 + parity_z) * LAYER + j, h)

    right, left = ring_peer(1), ring_peer(-1)

    def remote(src, dst, send, recv, device):
        return pltpu.make_async_remote_copy(
            src_ref=src,
            dst_ref=dst,
            send_sem=send,
            recv_sem=recv,
            device_id=device,
            device_id_type=MESH,
        )

    pairs = (
        (k_hbm, keys),
        (v_hbm, values),
        (q_hbm, queries),
        (conv_w_hbm, conv_w),
        (text_k_hbm, text_k),
        (text_v_hbm, text_v),
        (mask_hbm, mask),
        (tokens_hbm, tokens),
        (out_w_hbm, out_w),
        (out_bias_hbm, out_bias),
        (gate_hbm, gate),
        (shift_hbm, shift),
        (scale_hbm, scale),
        (final_w_hbm, final_w),
        (final_bias_hbm, final_bias),
        (conv_bias_hbm, conv_bias),
    )
    loads = [
        pltpu.make_async_copy(src, dst, local_sem.at[i]) for i, (src, dst) in enumerate(pairs)
    ]

    halo_steps = [(dr, dc) for dr in (-1, 0, 1) for dc in (-1, 0, 1) if (dr, dc) != (0, 0)]
    halo_peers = [(shifted(s, dr, seqs), shifted(h, dc, heads)) for dr, dc in halo_steps]
    partners = [group_peer(i)[0] for i in range(1, heads)]
    partners += [right, left]
    partners += [part_peer(i) for i in range(1, PAIR)]
    partners += halo_peers
    for load in loads[:3]:
        load.start()
    barrier = pltpu.get_barrier_semaphore()
    for partner in partners:
        pl.semaphore_signal(barrier, inc=1, device_id=partner, device_id_type=MESH)

    group_cols = [slice(g * width, (g + 1) * width) for g in range(heads)]
    for at, whole in enumerate((keys, values)):
        loads[at].wait()
        for g, cols in enumerate(group_cols):
            kv_stage[g, at] = whole[:, cols]
    pl.semaphore_wait(barrier, len(partners))

    def send_kv(i, carry):
        to, group = group_peer(i)
        remote(kv_stage.at[group], kv_in.at[place], kv_send, kv_recv, to).start()
        return carry

    def send_q(i, carry):
        to, group = group_peer(i)
        remote(q_stage.at[group], q_in.at[place], q_a2a_send, q_a2a_recv, to).start()
        return carry

    lax.fori_loop(1, heads, send_kv, 0)
    kv_in[place] = kv_stage[place]
    loads[2].wait()
    for g, cols in enumerate(group_cols):
        q_stage[g] = queries[:, cols]
    lax.fori_loop(1, heads, send_q, 0)
    q_in[place] = q_stage[place]
    for load in loads[3:7]:
        load.start()

    taps = w_sum.shape[0]
    parities = w_full.shape[0]
    features = final_w.shape[0]

    def sum_taps():
        conv_all = conv_w[...].astype(F32)
        total = conv_all[:taps] + conv_all[taps : 2 * taps] + conv_all[2 * taps :]
        w_sum[...] = total.astype(BF16)

    def conv_weights(parity):
        up = parity // 2
        side = lax.rem(parity, 2)
        depth = w_full.shape[1]
        row = lax.broadcasted_iota(jnp.int32, (depth, taps), 0)
        col = lax.broadcasted_iota(jnp.int32, (depth, taps), 1)
        tap_i = 2 * (row >> 7) + ((row >> 1) & 1) + up - 1
        tap_j = 2 * ((row >> 6) & 1) + (row & 1) + side - 1
        inside = (tap_i >= 0) & (tap_i <= 2) & (tap_j >= 0) & (tap_j <= 2)
        source = (tap_i * 3 + tap_j) * LAT_CH + ((row & 63) >> 2)
        pick = jnp.where(inside & (source == col), 1.0, 0.0).astype(BF16)
        w_full[parity] = dot(pick, w_sum[...]).astype(BF16)

    def rows_of(block):
        return block.astype(F32).reshape(rows, width).astype(BF16)

    peer = head_peer(0)
    seven = kv_in.at[pl.ds(0, heads - 1)]
    remote(seven, seven, kv_send, kv_recv, peer).wait_recv()
    own_k = rows_of(kv_in[:, 0])
    own_v = rows_of(kv_in[:, 1])
    for n in range(GROUP):
        cols = slice(n * HEAD_DIM, (n + 1) * HEAD_DIM)
        kv[z, n, 0] = own_k[:, cols]
        kv[z, n, 1] = own_v[:, cols]

    def to_right(ref, recv, send=0):
        return remote(ref, ref, ring_send.at[0] if send == 0 else half_send.at[0], recv, right)

    def to_left(ref, recv, send=0):
        return remote(ref, ref, ring_send.at[1] if send == 0 else half_send.at[1], recv, left)

    for n in range(GROUP):
        to_right(kv.at[z, n], ring_recv.at[z, n, 0]).start()
        to_left(kv.at[z, n], ring_recv.at[z, n, 0]).start()
    for load in loads[7:]:
        load.start()

    seven = q_in.at[pl.ds(0, heads - 1)]
    remote(seven, seven, q_a2a_send, q_a2a_recv, peer).wait_recv()
    own_q = rows_of(q_in[...])
    for n in range(GROUP):
        qs[part_of, n] = own_q[:, n * HEAD_DIM : (n + 1) * HEAD_DIM]

    def send_queries(i, carry):
        remote(qs.at[part_of], qs.at[part_of], q_send, q_recv, part_peer(i)).start()
        return carry

    lax.fori_loop(1, PAIR, send_queries, 0)

    def weigh(scores, top):
        return jnp.exp2((scores - top) * (SCORE_SCALE * LOG2E))

    def attend_first(n, carry):
        share = text_k.shape[0] // LAYER
        mine = pl.ds(pl.multiple_of(j * share, share), share)
        cols = pl.ds(pl.multiple_of(n * HEAD_DIM, HEAD_DIM), HEAD_DIM)
        keys_now = jnp.concatenate([text_k[mine, cols], kv[z, n, 0]], axis=0)
        values_now = jnp.concatenate([text_v[mine, cols], kv[z, n, 1]], axis=0)
        scores = dot(keys_now, q_turned[n])
        held = mask_column[mine, :1] * (1 - apart).astype(F32)
        real = jnp.concatenate([held, jnp.ones((rows, 1), F32)], axis=0) == 1.0
        real = jnp.broadcast_to(real, scores.shape)
        scores = jnp.where(real, scores, NEG)
        top = jnp.max(scores, axis=0, keepdims=True)
        weights = jnp.where(real, weigh(scores, top), 0.0)
        run_max[n, :1] = top
        run_sum[n, :1] = jnp.sum(weights, axis=0, keepdims=True)
        run_acc[n] = dot_tn(values_now, weights.astype(BF16))
        return carry

    def absorb(n, slots):
        keys_now = jnp.concatenate([kv[slot, n, 0] for slot in slots], axis=0)
        values_now = jnp.concatenate([kv[slot, n, 1] for slot in slots], axis=0)
        scores = dot(keys_now, q_turned[n])
        old = run_max[n, :1]
        top = jnp.maximum(old, jnp.max(scores, axis=0, keepdims=True))
        factor = weigh(old, top)
        weights = weigh(scores, top)
        total = run_sum[n, :1] * factor + jnp.sum(weights, axis=0, keepdims=True)
        acc = run_acc[n] * factor + dot_tn(values_now, weights.astype(BF16))
        return top, total, acc

    def work_on(n, steps):
        top, total, acc = absorb(n, [slot_at(by) for step in steps for by in (-step, step)])
        run_max[n, :1] = top
        run_sum[n, :1] = total
        run_acc[n] = acc

    def pass_on(step):
        one = slot_at(-step)
        other = slot_at(step)

        def one_head(n, carry):
            copy = to_right(kv.at[one, n], ring_recv.at[one, n, 0])
            copy.wait_recv()
            copy.start()
            copy = to_left(kv.at[other, n], ring_recv.at[other, n, 0])
            copy.wait_recv()
            copy.start()
            return carry

        lax.fori_loop(0, GROUP, one_head, 0)

    def pass_on_halves(step):
        one = slot_at(-step)
        other = slot_at(step)

        def one_head(n, carry):
            to_right(kv.at[one, n], ring_recv.at[one, n, 0]).wait_recv()
            to_right(kv.at[one, n, 0], ring_recv.at[one, n, 0], 1).start()
            to_left(kv.at[other, n], ring_recv.at[other, n, 0]).wait_recv()
            to_left(kv.at[other, n, 1], ring_recv.at[other, n, 1], 1).start()
            return carry

        lax.fori_loop(0, GROUP, one_head, 0)

    pass_on(1)
    seven = qs.at[pl.ds(0, PAIR - 1)]
    remote(seven, seven, q_send, q_recv, peer).wait_recv()
    half = rows // 2

    def turn_queries(n, carry):
        pieces = [
            qs[y * LAYER + row, n, at * half : (at + 1) * half]
            for at in range(2)
            for row in range(LAYER)
            for y in range(2)
        ]
        q_turned[n] = jnp.concatenate(pieces, axis=0).T
        return carry

    lax.fori_loop(0, GROUP, turn_queries, 0)
    for load in loads[3:7]:
        load.wait()
    mask_column[...] = jnp.broadcast_to(mask[...].astype(F32), (TOK, mask.shape[1])).T
    lax.fori_loop(0, GROUP, attend_first, 0)
    pass_on(2)
    sum_taps()

    def one_parity(parity, carry):
        conv_weights(parity)
        return carry

    lax.fori_loop(0, parities, one_parity, 0)
    pass_on_halves(3)

    def middle_step(n, carry):
        work_on(n, range(1, far - 1))
        return carry

    lax.fori_loop(0, GROUP, middle_step, 0)

    opposite = slot_at(far)
    marks[...] = jnp.zeros_like(marks)

    def last_step(n, carry):
        to_right(kv.at[opposite, n, 0], ring_recv.at[opposite, n, 0]).wait_recv()
        to_left(kv.at[opposite, n, 1], ring_recv.at[opposite, n, 1]).wait_recv()
        top, total, acc = absorb(n, [slot_at(1 - far), slot_at(far - 1), opposite])
        share = (acc / total).T.astype(BF16)
        for i in range(PAIR):
            o_stage[i, pl.ds(pl.multiple_of(n * rows, rows), rows)] = share[
                i * rows : (i + 1) * rows
            ]
        level = top * SCORE_SCALE + jnp.log(total)
        first = level.astype(BF16).astype(F32)
        second = (level - first).astype(BF16).astype(F32)
        marks[pl.ds(3 * n, 1)] = first
        marks[pl.ds(3 * n + 1, 1)] = second
        marks[pl.ds(3 * n + 2, 1)] = level - first - second
        return carry

    lax.fori_loop(0, GROUP, last_step, 0)
    level_rows = marks[...]
    for i in range(PAIR):
        turned = level_rows if i == 0 else pltpu.roll(level_rows, (PAIR - i) * rows, 1)
        o_stage[i, GROUP * rows :] = turned[:, :HEAD_DIM].astype(BF16)

    def send_share(i, carry):
        to, row = row_peer(i)

        @pl.when((i != own_row) | (apart == 1))
        def _():
            remote(o_stage.at[row], o_in.at[part_of], o_send, o_recv, to).start()

        return carry

    lax.fori_loop(0, PAIR, send_share, 0)
    own_at = row_peer(own_row)[1]

    @pl.when(apart == 0)
    def _():
        o_in[part_of] = o_stage[own_at]

    for load in loads[7:]:
        load.wait()

    def await_shares(whole, send, recv, sent):
        def wait(ref):
            copy = remote(ref, ref, send, recv, peer)
            if sent:
                copy.wait_send()
            else:
                copy.wait_recv()

        @pl.when(apart == 1)
        def _():
            wait(whole)

        @pl.when(apart == 0)
        def _():
            wait(whole.at[pl.ds(0, PAIR - 1)])

    await_shares(o_in, o_send, o_recv, False)
    level_parts = [o_in[i, GROUP * rows :].astype(F32) for i in range(PAIR)]
    shares[...] = jnp.zeros_like(shares)
    for n in range(GROUP):
        levels = [
            part[3 * n : 3 * n + 1] + part[3 * n + 1 : 3 * n + 2] + part[3 * n + 2 : 3 * n + 3]
            for part in level_parts
        ]
        top = functools.reduce(jnp.maximum, levels)
        parts = [jnp.exp(level - top) for level in levels]
        total = functools.reduce(jnp.add, parts)
        for i, part in enumerate(parts):
            shares[n * PAIR + i : n * PAIR + i + 1] = part / total
    columns = shares[...].T[:rows]
    attended = []
    for n in range(GROUP):
        mixed = functools.reduce(
            jnp.add,
            [
                columns[:, n * PAIR + i : n * PAIR + i + 1] * o_in[i, n * rows : (n + 1) * rows].astype(F32)
                for i in range(PAIR)
            ],
        )
        attended.append(mixed.astype(BF16))
    attended = jnp.concatenate(attended, axis=1)

    for part in range(rs_parts):
        product = dot(attended, out_w[:, part * part_cols : (part + 1) * part_cols])
        rs_stage[part] = product.reshape(heads, TOK, part_cols).astype(BF16)

        def send_part(i, carry, part=part):
            to = head_peer(i)
            remote(
                rs_stage.at[part, to[1]],
                rs_in.at[part, h],
                rs_send.at[part],
                rs_recv.at[part],
                to,
            ).start()
            return carry

        lax.fori_loop(0, heads, send_part, 0)
    pieces = []
    for part in range(rs_parts):
        cols = slice(part * part_cols, (part + 1) * part_cols)
        whole = rs_in.at[part]
        remote(whole, whole, rs_send.at[part], rs_recv.at[part], peer).wait_recv()
        projected = jnp.sum(rs_in[part].astype(F32), axis=0)
        stream = tokens[:, cols].astype(F32) + gate[:, cols] * (projected + out_bias[:, cols])
        rounded = stream.astype(BF16)
        block_out[:, cols] = rounded
        pieces.append(rounded.astype(F32))
    block_copy = pltpu.make_async_copy(block_out, block_hbm, out_sem.at[0])
    block_copy.start()

    normed_in = jnp.concatenate(pieces, axis=1)
    centered = normed_in - jnp.mean(normed_in, axis=1, keepdims=True)
    spread = jnp.mean(centered * centered, axis=1, keepdims=True)
    normed = centered * lax.rsqrt(spread + 1e-06)
    modulated = (normed * (1.0 + scale[...]) + shift[...]).astype(BF16)
    patches = (dot_nt(modulated, final_w[...]) + final_bias[...]) / LATENT_SCALE
    padded = jnp.concatenate([patches, jnp.zeros((TOK, HEAD_DIM - features), F32)], axis=1)
    lat[...] = padded.astype(BF16)

    for at, to in enumerate(halo_peers):
        remote(lat, halo.at[at], halo_send, halo_recv, to).start()
    tiles = {(0, 0): lat[...].astype(F32)}
    remote(halo, halo, halo_send, halo_recv, peer).wait_recv()
    for at, (dr, dc) in enumerate(halo_steps):
        tiles[(-dr, -dc)] = halo[at].astype(F32)

    def rolled(tile, by):
        return pltpu.roll(tile, by % HEAD_DIM, 1)

    top_edge, bottom_edge = s == 0, s == seqs - 1
    first_tile, last_tile = h == 0, h == heads - 1
    for dc in (-1, 0, 1):
        middle = tiles[(0, dc)]
        tiles[(-1, dc)] = jnp.where(top_edge, rolled(middle, 2), tiles[(-1, dc)])
        tiles[(1, dc)] = jnp.where(bottom_edge, rolled(middle, -2), tiles[(1, dc)])
    low = lax.broadcasted_iota(jnp.int32, (1, HEAD_DIM), 1) < features
    packed = {}
    for dr in (-1, 0, 1):
        middle = tiles[(dr, 0)]
        before = jnp.where(first_tile, rolled(middle, 1)[:1], tiles[(dr, -1)][TOK - 1 :])
        after = jnp.where(last_tile, rolled(middle, -1)[TOK - 1 :], tiles[(dr, 1)][:1])
        before = jnp.concatenate([before, middle[: TOK - 1]], axis=0)
        after = jnp.concatenate([middle[1:], after], axis=0)
        packed[(dr, 0)] = jnp.where(low, before, rolled(middle, features))
        packed[(dr, 1)] = jnp.where(low, middle, rolled(after, features))
    for parity in range(parities):
        up, side = parity // 2, parity % 2
        stacked = jnp.concatenate([packed[(up - 1, side)], packed[(up, side)]], axis=1)
        result = dot(stacked.astype(BF16), w_full[parity]) + conv_bias[...]
        for tile in range(pixels.shape[1]):
            pixels[up, tile, pl.ds(side, TOK, stride=2), :] = result[
                :, tile * HEAD_DIM : (tile + 1) * HEAD_DIM
            ]
    for tile in range(pixels.shape[1]):
        cols = slice(tile * HEAD_DIM, (tile + 1) * HEAD_DIM)
        decoded[:, :, cols] = pixels[:, tile].astype(BF16)
    decoded_copy = pltpu.make_async_copy(decoded, decoded_hbm, out_sem.at[1])
    decoded_copy.start()

    seven = kv_stage.at[pl.ds(0, heads - 1)]
    remote(seven, seven, kv_send, kv_recv, peer).wait_send()
    seven = q_stage.at[pl.ds(0, heads - 1)]
    remote(seven, seven, q_a2a_send, q_a2a_recv, peer).wait_send()
    ring_all = kv.at[pl.ds(0, far - 1)]
    to_right(ring_all, ring_recv.at[0, 0, 0]).wait_send()
    to_left(ring_all, ring_recv.at[0, 0, 0]).wait_send()
    ring_half = kv.at[0, :, 0]
    to_right(ring_half, ring_recv.at[0, 0, 0], 1).wait_send()
    to_left(ring_half, ring_recv.at[0, 0, 0], 1).wait_send()
    seven = qs.at[pl.ds(0, PAIR - 1)]
    remote(seven, seven, q_send, q_recv, peer).wait_send()
    await_shares(o_stage, o_send, o_recv, True)
    for part in range(rs_parts):
        whole = rs_stage.at[part]
        remote(whole, whole, rs_send.at[part], rs_recv.at[part], peer).wait_send()
    remote(halo, halo, halo_send, halo_recv, peer).wait_send()
    block_copy.wait()
    decoded_copy.wait()


def hand_over(block_in, decoded_in, block_to, decoded_to, block, decoded, sem):
    rooms = ((block_in, block, block_to), (decoded_in, decoded, decoded_to))
    loads = [pltpu.make_async_copy(a, b, sem.at[i]) for i, (a, b, _) in enumerate(rooms)]
    stores = [pltpu.make_async_copy(b, c, sem.at[2 + i]) for i, (_, b, c) in enumerate(rooms)]
    for load in loads:
        load.start()
    for load, store in zip(loads, stores):
        load.wait()
        store.start()
    for store in stores:
        store.wait()


def body(seqs, heads, *args):
    (
        queries,
        keys,
        values,
        text_keys,
        text_values,
        text_mask,
        tokens,
        out_weight,
        out_bias,
        gate,
        shift,
        scale,
        final_weight,
        final_bias,
        conv_weight,
        conv_bias,
    ) = args
    dim = queries.shape[3]
    width = GROUP * HEAD_DIM
    text = text_keys.shape[0]
    layers = seqs // PAIR
    far = layers // 2
    rows = heads * TOK
    features = final_weight.shape[1]
    taps = 9 * LAT_CH
    channels = conv_weight.shape[4]
    rs_parts = 1
    operands = (
        queries.reshape(TOK, dim),
        keys.reshape(TOK, dim),
        values.reshape(TOK, dim),
        text_keys,
        text_values,
        text_mask.reshape(1, text),
        tokens.reshape(TOK, dim),
        out_weight,
        out_bias.reshape(1, dim),
        gate.reshape(1, dim),
        shift.reshape(1, dim),
        scale.reshape(1, dim),
        final_weight.T,
        final_bias.reshape(1, features),
        conv_weight.reshape(3 * taps, channels),
        conv_bias.reshape(1, channels),
    )
    copied = [pltpu.VMEM(x.shape, x.dtype) for x in operands]
    dma = pltpu.SemaphoreType.DMA
    anywhere = pl.BlockSpec(memory_space=pl.ANY)
    results = (
        jax.ShapeDtypeStruct((TOK, dim), BF16),
        jax.ShapeDtypeStruct((2, 2 * TOK, channels), BF16),
    )
    block_out, decoded = pl.pallas_call(
        functools.partial(kernel, seqs, heads),
        out_shape=results,
        in_specs=[anywhere] * len(operands),
        out_specs=(anywhere, anywhere),
        scratch_shapes=copied
        + [
            pltpu.VMEM((heads, 2, TOK, width), BF16),
            pltpu.VMEM((heads, TOK, width), BF16),
            pltpu.VMEM((heads, 2, TOK, width), BF16),
            pltpu.VMEM((heads, TOK, width), BF16),
            pltpu.VMEM((layers, GROUP, 2, rows, HEAD_DIM), BF16),
            pltpu.VMEM((PAIR, GROUP, rows, HEAD_DIM), BF16),
            pltpu.VMEM((GROUP, HEAD_DIM, PAIR * rows), BF16),
            pltpu.VMEM((text, TOK), F32),
            pltpu.VMEM((GROUP, TOK, PAIR * rows), F32),
            pltpu.VMEM((GROUP, TOK, PAIR * rows), F32),
            pltpu.VMEM((GROUP, HEAD_DIM, PAIR * rows), F32),
            pltpu.VMEM((16, PAIR * rows), F32),
            pltpu.VMEM((GROUP * PAIR, HEAD_DIM), F32),
            pltpu.VMEM((PAIR, GROUP * rows + 16, HEAD_DIM), BF16),
            pltpu.VMEM((PAIR, GROUP * rows + 16, HEAD_DIM), BF16),
            pltpu.VMEM((rs_parts, heads, TOK, dim // rs_parts), BF16),
            pltpu.VMEM((rs_parts, heads, TOK, dim // rs_parts), BF16),
            pltpu.VMEM((TOK, HEAD_DIM), BF16),
            pltpu.VMEM((8, TOK, HEAD_DIM), BF16),
            pltpu.VMEM((taps, channels), BF16),
            pltpu.VMEM((4, 4 * features, channels), BF16),
            pltpu.VMEM((2, channels // HEAD_DIM, 2 * TOK, HEAD_DIM), F32),
            pltpu.VMEM((TOK, dim), BF16),
            pltpu.VMEM((2, 2 * TOK, channels), BF16),
            dma((len(operands),)),
            dma((2,)),
            dma,
            dma,
            dma,
            dma,
            dma((2,)),
            dma((2,)),
            dma((layers, GROUP, 2)),
            dma,
            dma,
            dma,
            dma,
            dma((rs_parts,)),
            dma((rs_parts,)),
            dma,
            dma,
        ],
        compiler_params=pltpu.CompilerParams(
            collective_id=0, has_side_effects=True, vmem_limit_bytes=60 * 1024 * 1024
        ),
        cost_estimate=pl.CostEstimate(
            flops=1_200_000_000, bytes_accessed=5_000_000, transcendentals=1_000_000
        ),
    )(*operands)
    block_out, decoded = pl.pallas_call(
        hand_over,
        out_shape=results,
        in_specs=[anywhere] * 2,
        out_specs=(anywhere, anywhere),
        scratch_shapes=[pltpu.VMEM(x.shape, x.dtype) for x in results] + [dma((4,))],
        compiler_params=pltpu.CompilerParams(vmem_limit_bytes=60 * 1024 * 1024),
    )(block_out, decoded)
    return (
        block_out.reshape(1, TOK, 1, dim),
        decoded.reshape(1, 2, 2 * TOK, channels),
    )


def solution(mesh):
    seqs = mesh.shape["seq"]
    heads = mesh.shape["head"]
    spread = P("seq", "head", None, None)
    in_specs = (
        spread,
        spread,
        spread,
        P(None, "head"),
        P(None, "head"),
        P(),
        spread,
        P("head", None),
    ) + (P(),) * 8
    out_specs = (spread, P(None, "seq", "head", None))
    return jax.shard_map(
        functools.partial(body, seqs, heads),
        mesh=mesh,
        in_specs=in_specs,
        out_specs=out_specs,
        check_vma=False,
    )
```

```python
import functools

import jax
import jax.numpy as jnp
from jax import lax
from jax.experimental import pallas as pl
from jax.experimental.pallas import tpu as pltpu
from jax.sharding import PartitionSpec as P

HEAD_DIM = 128
GROUP = 3
LAT_CH = 16
TOK = 8
LAYER = 4
PAIR = 8
COLUMNS = 4
LATENT_SCALE = 0.476986
NEG = -1e30
SCORE_SCALE = HEAD_DIM ** (-0.5)
LOG2E = 1.4426950408889634
BF16 = jnp.bfloat16
F32 = jnp.float32
MESH = pl.DeviceIdType.MESH


def dot(a, b):
    return jnp.dot(a, b, preferred_element_type=F32)


def dot_tn(a, b):
    return lax.dot_general(a, b, (((0,), (0,)), ((), ())), preferred_element_type=F32)


def dot_nt(a, b):
    return lax.dot_general(a, b, (((1,), (1,)), ((), ())), preferred_element_type=F32)


def kernel(
    seqs,
    heads,
    q_hbm,
    k_hbm,
    v_hbm,
    text_k_hbm,
    text_v_hbm,
    mask_hbm,
    tokens_hbm,
    out_w_hbm,
    out_bias_hbm,
    gate_hbm,
    shift_hbm,
    scale_hbm,
    final_w_hbm,
    final_bias_hbm,
    conv_w_hbm,
    conv_bias_hbm,
    block_hbm,
    decoded_hbm,
    queries,
    keys,
    values,
    text_k,
    text_v,
    mask,
    tokens,
    out_w,
    out_bias,
    gate,
    shift,
    scale,
    final_w,
    final_bias,
    conv_w,
    conv_bias,
    kv_stage,
    q_stage,
    kv_in,
    q_in,
    kv,
    qs,
    q_turned,
    mask_column,
    run_max,
    run_sum,
    run_acc,
    marks,
    mark_stage,
    mark_in,
    shares,
    o_stage,
    o_in,
    rs_stage,
    rs_in,
    lat,
    halo,
    w_sum,
    w_full,
    pixels,
    block_out,
    decoded,
    local_sem,
    out_sem,
    kv_send,
    kv_recv,
    q_a2a_send,
    q_a2a_recv,
    ring_send,
    half_send,
    ring_recv,
    q_send,
    q_recv,
    o_send,
    o_recv,
    mark_send,
    mark_recv,
    rs_send,
    rs_recv,
    halo_send,
    halo_recv,
):
    s = lax.axis_index("seq")
    h = lax.axis_index("head")
    layers = seqs // PAIR
    far = layers // 2
    depth = s // LAYER
    j = lax.rem(s, LAYER)
    z = depth // 2
    parity_z = lax.rem(depth, 2)
    column = lax.rem(h, COLUMNS)
    y_high = h // COLUMNS
    part_of = y_high * LAYER + j
    place = parity_z * COLUMNS + column
    apart = lax.rem(y_high + parity_z, 2)
    width = GROUP * HEAD_DIM
    dim = heads * width
    rows = heads * TOK
    rs_parts = rs_stage.shape[0]
    part_cols = dim // rs_parts

    def shifted(index, by, count):
        return lax.rem(index + (by % count), count)

    r = lax.rem(j + LAYER // 2, LAYER)

    def head_peer(i):
        return (depth * LAYER + r, shifted(h, i, heads))

    def group_peer(i):
        at_depth = z * 2 + lax.rem(parity_z + i // COLUMNS, 2)
        at_column = lax.rem(column + lax.rem(i, COLUMNS), COLUMNS)
        group = lax.rem(at_depth, 2) * COLUMNS + at_column
        return (at_depth * LAYER + j, y_high * COLUMNS + at_column), group

    def part_peer(i):
        part = lax.rem(part_of + i, PAIR)
        return (depth * LAYER + lax.rem(part, LAYER), (part // LAYER) * COLUMNS + column)

    def row_peer(i):
        at_parity = lax.rem(parity_z + i // LAYER, 2)
        row = lax.rem(j + lax.rem(i, LAYER), LAYER)
        owner = lax.rem(row + LAYER // 2, LAYER)
        to = ((z * 2 + at_parity) * LAYER + owner, parity_z * COLUMNS + column)
        return to, at_parity * LAYER + row

    own_row = LAYER // 2

    def slot_at(by):
        return lax.rem(z + by + layers, layers)

    def ring_peer(by):
        return ((slot_at(by) * 2 + parity_z) * LAYER + j, h)

    right, left = ring_peer(1), ring_peer(-1)

    def remote(src, dst, send, recv, device):
        return pltpu.make_async_remote_copy(
            src_ref=src,
            dst_ref=dst,
            send_sem=send,
            recv_sem=recv,
            device_id=device,
            device_id_type=MESH,
        )

    pairs = (
        (k_hbm, keys),
        (v_hbm, values),
        (q_hbm, queries),
        (conv_w_hbm, conv_w),
        (text_k_hbm, text_k),
        (text_v_hbm, text_v),
        (mask_hbm, mask),
        (tokens_hbm, tokens),
        (out_w_hbm, out_w),
        (out_bias_hbm, out_bias),
        (gate_hbm, gate),
        (shift_hbm, shift),
        (scale_hbm, scale),
        (final_w_hbm, final_w),
        (final_bias_hbm, final_bias),
        (conv_bias_hbm, conv_bias),
    )
    loads = [
        pltpu.make_async_copy(src, dst, local_sem.at[i]) for i, (src, dst) in enumerate(pairs)
    ]

    halo_steps = [(dr, dc) for dr in (-1, 0, 1) for dc in (-1, 0, 1) if (dr, dc) != (0, 0)]
    halo_peers = [(shifted(s, dr, seqs), shifted(h, dc, heads)) for dr, dc in halo_steps]
    partners = [group_peer(i)[0] for i in range(1, heads)]
    partners += [right, left]
    partners += [part_peer(i) for i in range(1, PAIR)]
    partners += halo_peers
    for load in loads[:3]:
        load.start()
    barrier = pltpu.get_barrier_semaphore()
    for partner in partners:
        pl.semaphore_signal(barrier, inc=1, device_id=partner, device_id_type=MESH)

    group_cols = [slice(g * width, (g + 1) * width) for g in range(heads)]
    for at, whole in enumerate((keys, values)):
        loads[at].wait()
        for g, cols in enumerate(group_cols):
            kv_stage[g, at] = whole[:, cols]
    pl.semaphore_wait(barrier, len(partners))

    def send_kv(i, carry):
        to, group = group_peer(i)
        remote(kv_stage.at[group], kv_in.at[place], kv_send, kv_recv, to).start()
        return carry

    def send_q(i, carry):
        to, group = group_peer(i)
        remote(q_stage.at[group], q_in.at[place], q_a2a_send, q_a2a_recv, to).start()
        return carry

    lax.fori_loop(1, heads, send_kv, 0)
    kv_in[place] = kv_stage[place]
    loads[2].wait()
    for g, cols in enumerate(group_cols):
        q_stage[g] = queries[:, cols]
    lax.fori_loop(1, heads, send_q, 0)
    q_in[place] = q_stage[place]
    for load in loads[3:7]:
        load.start()

    taps = w_sum.shape[0]
    parities = w_full.shape[0]
    features = final_w.shape[0]

    def sum_taps():
        conv_all = conv_w[...].astype(F32)
        total = conv_all[:taps] + conv_all[taps : 2 * taps] + conv_all[2 * taps :]
        w_sum[...] = total.astype(BF16)

    def conv_weights(parity):
        up = parity // 2
        side = lax.rem(parity, 2)
        depth = w_full.shape[1]
        row = lax.broadcasted_iota(jnp.int32, (depth, taps), 0)
        col = lax.broadcasted_iota(jnp.int32, (depth, taps), 1)
        tap_i = 2 * (row >> 7) + ((row >> 1) & 1) + up - 1
        tap_j = 2 * ((row >> 6) & 1) + (row & 1) + side - 1
        inside = (tap_i >= 0) & (tap_i <= 2) & (tap_j >= 0) & (tap_j <= 2)
        source = (tap_i * 3 + tap_j) * LAT_CH + ((row & 63) >> 2)
        pick = jnp.where(inside & (source == col), 1.0, 0.0).astype(BF16)
        w_full[parity] = dot(pick, w_sum[...]).astype(BF16)

    def rows_of(block):
        return block.astype(F32).reshape(rows, width).astype(BF16)

    peer = head_peer(0)
    seven = kv_in.at[pl.ds(0, heads - 1)]
    remote(seven, seven, kv_send, kv_recv, peer).wait_recv()
    own_k = rows_of(kv_in[:, 0])
    own_v = rows_of(kv_in[:, 1])
    for n in range(GROUP):
        cols = slice(n * HEAD_DIM, (n + 1) * HEAD_DIM)
        kv[z, n, 0] = own_k[:, cols]
        kv[z, n, 1] = own_v[:, cols]

    def to_right(ref, recv, send=0):
        return remote(ref, ref, ring_send.at[0] if send == 0 else half_send.at[0], recv, right)

    def to_left(ref, recv, send=0):
        return remote(ref, ref, ring_send.at[1] if send == 0 else half_send.at[1], recv, left)

    pieces_of = [(n, part) for n in range(GROUP) for part in range(2)]

    for n, part in pieces_of:
        to_right(kv.at[z, n, part], ring_recv.at[z, n, part]).start()
        to_left(kv.at[z, n, part], ring_recv.at[z, n, part]).start()
    for load in loads[7:]:
        load.start()

    seven = q_in.at[pl.ds(0, heads - 1)]
    remote(seven, seven, q_a2a_send, q_a2a_recv, peer).wait_recv()
    own_q = rows_of(q_in[...])
    for n in range(GROUP):
        qs[part_of, n] = own_q[:, n * HEAD_DIM : (n + 1) * HEAD_DIM]

    def send_queries(i, carry):
        remote(qs.at[part_of], qs.at[part_of], q_send, q_recv, part_peer(i)).start()
        return carry

    lax.fori_loop(1, PAIR, send_queries, 0)

    def weigh(scores, top):
        return jnp.exp2((scores - top) * (SCORE_SCALE * LOG2E))

    def attend_first(n, carry):
        share = text_k.shape[0] // LAYER
        mine = pl.ds(pl.multiple_of(j * share, share), share)
        cols = pl.ds(pl.multiple_of(n * HEAD_DIM, HEAD_DIM), HEAD_DIM)
        keys_now = jnp.concatenate([text_k[mine, cols], kv[z, n, 0]], axis=0)
        values_now = jnp.concatenate([text_v[mine, cols], kv[z, n, 1]], axis=0)
        scores = dot(keys_now, q_turned[n])
        held = mask_column[mine, :1] * (1 - apart).astype(F32)
        real = jnp.concatenate([held, jnp.ones((rows, 1), F32)], axis=0) == 1.0
        real = jnp.broadcast_to(real, scores.shape)
        scores = jnp.where(real, scores, NEG)
        top = jnp.max(scores, axis=0, keepdims=True)
        weights = jnp.where(real, weigh(scores, top), 0.0)
        run_max[n, :1] = top
        run_sum[n, :1] = jnp.sum(weights, axis=0, keepdims=True)
        run_acc[n] = dot_tn(values_now, weights.astype(BF16))
        return carry

    def absorb(n, slots):
        keys_now = jnp.concatenate([kv[slot, n, 0] for slot in slots], axis=0)
        values_now = jnp.concatenate([kv[slot, n, 1] for slot in slots], axis=0)
        scores = dot(keys_now, q_turned[n])
        old = run_max[n, :1]
        top = jnp.maximum(old, jnp.max(scores, axis=0, keepdims=True))
        factor = weigh(old, top)
        weights = weigh(scores, top)
        total = run_sum[n, :1] * factor + jnp.sum(weights, axis=0, keepdims=True)
        acc = run_acc[n] * factor + dot_tn(values_now, weights.astype(BF16))
        return top, total, acc

    def work_on(n, steps):
        top, total, acc = absorb(n, [slot_at(by) for step in steps for by in (-step, step)])
        run_max[n, :1] = top
        run_sum[n, :1] = total
        run_acc[n] = acc

    def pass_on(step):
        one = slot_at(-step)
        other = slot_at(step)

        def one_head(n, carry):
            for part in range(2):
                copy = to_right(kv.at[one, n, part], ring_recv.at[one, n, part])
                copy.wait_recv()
                copy.start()
                copy = to_left(kv.at[other, n, part], ring_recv.at[other, n, part])
                copy.wait_recv()
                copy.start()
            return carry

        lax.fori_loop(0, GROUP, one_head, 0)

    def pass_on_halves(step):
        one = slot_at(-step)
        other = slot_at(step)

        def one_head(n, carry):
            for part in range(2):
                copy = to_right(kv.at[one, n, part], ring_recv.at[one, n, part], 1)
                copy.wait_recv()
                if part == 0:
                    copy.start()
                copy = to_left(kv.at[other, n, part], ring_recv.at[other, n, part], 1)
                copy.wait_recv()
                if part == 1:
                    copy.start()
            return carry

        lax.fori_loop(0, GROUP, one_head, 0)

    pass_on(1)
    seven = qs.at[pl.ds(0, PAIR - 1)]
    remote(seven, seven, q_send, q_recv, peer).wait_recv()
    half = rows // 2

    def turn_queries(n, carry):
        pieces = [
            qs[y * LAYER + row, n, at * half : (at + 1) * half]
            for at in range(2)
            for row in range(LAYER)
            for y in range(2)
        ]
        q_turned[n] = jnp.concatenate(pieces, axis=0).T
        return carry

    lax.fori_loop(0, GROUP, turn_queries, 0)
    for load in loads[3:7]:
        load.wait()
    mask_column[...] = jnp.broadcast_to(mask[...].astype(F32), (TOK, mask.shape[1])).T
    lax.fori_loop(0, GROUP, attend_first, 0)
    pass_on(2)
    sum_taps()

    def one_parity(parity, carry):
        conv_weights(parity)
        return carry

    lax.fori_loop(0, parities, one_parity, 0)
    pass_on_halves(3)

    def middle_step(n, carry):
        work_on(n, range(1, far - 1))
        return carry

    lax.fori_loop(0, GROUP, middle_step, 0)

    opposite = slot_at(far)
    marks[...] = jnp.zeros_like(marks)

    def last_step(n, carry):
        to_right(kv.at[opposite, n, 0], ring_recv.at[opposite, n, 0]).wait_recv()
        to_left(kv.at[opposite, n, 1], ring_recv.at[opposite, n, 1]).wait_recv()
        top, total, acc = absorb(n, [slot_at(1 - far), slot_at(far - 1), opposite])
        share = (acc / total).T.astype(BF16)
        for i in range(PAIR):
            o_stage[i, n] = share[i * rows : (i + 1) * rows]

        def send_share(i, inner):
            to, row = row_peer(i)

            @pl.when((i != own_row) | (apart == 1))
            def _():
                remote(o_stage.at[row, n], o_in.at[part_of, n], o_send, o_recv, to).start()

            return inner

        lax.fori_loop(0, PAIR, send_share, 0)
        level = top * SCORE_SCALE + jnp.log(total)
        first = level.astype(BF16).astype(F32)
        second = (level - first).astype(BF16).astype(F32)
        marks[pl.ds(3 * n, 1)] = first
        marks[pl.ds(3 * n + 1, 1)] = second
        marks[pl.ds(3 * n + 2, 1)] = level - first - second
        return carry

    lax.fori_loop(0, GROUP, last_step, 0)
    level_rows = marks[...]
    lanes = mark_stage.shape[2]
    for i in range(PAIR):
        turned = level_rows if i == 0 else pltpu.roll(level_rows, (PAIR - i) * rows, 1)
        mark_stage[i] = turned[:, :lanes].astype(BF16)

    def send_marks(i, carry):
        to, row = row_peer(i)

        @pl.when((i != own_row) | (apart == 1))
        def _():
            remote(mark_stage.at[row], mark_in.at[part_of], mark_send, mark_recv, to).start()

        return carry

    lax.fori_loop(0, PAIR, send_marks, 0)
    own_at = row_peer(own_row)[1]

    @pl.when(apart == 0)
    def _():
        o_in[part_of] = o_stage[own_at]
        mark_in[part_of] = mark_stage[own_at]

    for load in loads[7:]:
        load.wait()

    def await_shares(whole, send, recv, sent):
        def wait(ref):
            copy = remote(ref, ref, send, recv, peer)
            if sent:
                copy.wait_send()
            else:
                copy.wait_recv()

        @pl.when(apart == 1)
        def _():
            wait(whole)

        @pl.when(apart == 0)
        def _():
            wait(whole.at[pl.ds(0, PAIR - 1)])

    await_shares(o_in, o_send, o_recv, False)
    await_shares(mark_in, mark_send, mark_recv, False)
    level_parts = [mark_in[i].astype(F32) for i in range(PAIR)]
    shares[...] = jnp.zeros_like(shares)
    for n in range(GROUP):
        levels = [
            part[3 * n : 3 * n + 1] + part[3 * n + 1 : 3 * n + 2] + part[3 * n + 2 : 3 * n + 3]
            for part in level_parts
        ]
        top = functools.reduce(jnp.maximum, levels)
        parts = [jnp.exp(level - top) for level in levels]
        total = functools.reduce(jnp.add, parts)
        for i, part in enumerate(parts):
            shares[n * PAIR + i : n * PAIR + i + 1] = part / total
    columns = shares[...].T[:rows]
    attended = []
    for n in range(GROUP):
        mixed = functools.reduce(
            jnp.add,
            [
                columns[:, n * PAIR + i : n * PAIR + i + 1] * o_in[i, n].astype(F32)
                for i in range(PAIR)
            ],
        )
        attended.append(mixed.astype(BF16))
    attended = jnp.concatenate(attended, axis=1)

    for part in range(rs_parts):
        product = dot(attended, out_w[:, part * part_cols : (part + 1) * part_cols])
        rs_stage[part] = product.reshape(heads, TOK, part_cols).astype(BF16)

        def send_part(i, carry, part=part):
            to = head_peer(i)
            remote(
                rs_stage.at[part, to[1]],
                rs_in.at[part, h],
                rs_send.at[part],
                rs_recv.at[part],
                to,
            ).start()
            return carry

        lax.fori_loop(0, heads, send_part, 0)
    pieces = []
    for part in range(rs_parts):
        cols = slice(part * part_cols, (part + 1) * part_cols)
        whole = rs_in.at[part]
        remote(whole, whole, rs_send.at[part], rs_recv.at[part], peer).wait_recv()
        projected = jnp.sum(rs_in[part].astype(F32), axis=0)
        stream = tokens[:, cols].astype(F32) + gate[:, cols] * (projected + out_bias[:, cols])
        rounded = stream.astype(BF16)
        block_out[:, cols] = rounded
        pieces.append(rounded.astype(F32))
    block_copy = pltpu.make_async_copy(block_out, block_hbm, out_sem.at[0])
    block_copy.start()

    normed_in = jnp.concatenate(pieces, axis=1)
    centered = normed_in - jnp.mean(normed_in, axis=1, keepdims=True)
    spread = jnp.mean(centered * centered, axis=1, keepdims=True)
    normed = centered * lax.rsqrt(spread + 1e-06)
    modulated = (normed * (1.0 + scale[...]) + shift[...]).astype(BF16)
    patches = (dot_nt(modulated, final_w[...]) + final_bias[...]) / LATENT_SCALE
    padded = jnp.concatenate([patches, jnp.zeros((TOK, HEAD_DIM - features), F32)], axis=1)
    lat[...] = padded.astype(BF16)

    for at, to in enumerate(halo_peers):
        remote(lat, halo.at[at], halo_send, halo_recv, to).start()
    tiles = {(0, 0): lat[...].astype(F32)}
    remote(halo, halo, halo_send, halo_recv, peer).wait_recv()
    for at, (dr, dc) in enumerate(halo_steps):
        tiles[(-dr, -dc)] = halo[at].astype(F32)

    def rolled(tile, by):
        return pltpu.roll(tile, by % HEAD_DIM, 1)

    top_edge, bottom_edge = s == 0, s == seqs - 1
    first_tile, last_tile = h == 0, h == heads - 1
    for dc in (-1, 0, 1):
        middle = tiles[(0, dc)]
        tiles[(-1, dc)] = jnp.where(top_edge, rolled(middle, 2), tiles[(-1, dc)])
        tiles[(1, dc)] = jnp.where(bottom_edge, rolled(middle, -2), tiles[(1, dc)])
    low = lax.broadcasted_iota(jnp.int32, (1, HEAD_DIM), 1) < features
    packed = {}
    for dr in (-1, 0, 1):
        middle = tiles[(dr, 0)]
        before = jnp.where(first_tile, rolled(middle, 1)[:1], tiles[(dr, -1)][TOK - 1 :])
        after = jnp.where(last_tile, rolled(middle, -1)[TOK - 1 :], tiles[(dr, 1)][:1])
        before = jnp.concatenate([before, middle[: TOK - 1]], axis=0)
        after = jnp.concatenate([middle[1:], after], axis=0)
        packed[(dr, 0)] = jnp.where(low, before, rolled(middle, features))
        packed[(dr, 1)] = jnp.where(low, middle, rolled(after, features))
    for parity in range(parities):
        up, side = parity // 2, parity % 2
        stacked = jnp.concatenate([packed[(up - 1, side)], packed[(up, side)]], axis=1)
        result = dot(stacked.astype(BF16), w_full[parity]) + conv_bias[...]
        for tile in range(pixels.shape[1]):
            pixels[up, tile, pl.ds(side, TOK, stride=2), :] = result[
                :, tile * HEAD_DIM : (tile + 1) * HEAD_DIM
            ]
    for tile in range(pixels.shape[1]):
        cols = slice(tile * HEAD_DIM, (tile + 1) * HEAD_DIM)
        decoded[:, :, cols] = pixels[:, tile].astype(BF16)
    decoded_copy = pltpu.make_async_copy(decoded, decoded_hbm, out_sem.at[1])
    decoded_copy.start()

    seven = kv_stage.at[pl.ds(0, heads - 1)]
    remote(seven, seven, kv_send, kv_recv, peer).wait_send()
    seven = q_stage.at[pl.ds(0, heads - 1)]
    remote(seven, seven, q_a2a_send, q_a2a_recv, peer).wait_send()
    ring_all = kv.at[pl.ds(0, far - 1)]
    to_right(ring_all, ring_recv.at[0, 0, 0]).wait_send()
    to_left(ring_all, ring_recv.at[0, 0, 0]).wait_send()
    ring_half = kv.at[0, :, 0]
    to_right(ring_half, ring_recv.at[0, 0, 0], 1).wait_send()
    to_left(ring_half, ring_recv.at[0, 0, 0], 1).wait_send()
    seven = qs.at[pl.ds(0, PAIR - 1)]
    remote(seven, seven, q_send, q_recv, peer).wait_send()
    await_shares(o_stage, o_send, o_recv, True)
    await_shares(mark_stage, mark_send, mark_recv, True)
    for part in range(rs_parts):
        whole = rs_stage.at[part]
        remote(whole, whole, rs_send.at[part], rs_recv.at[part], peer).wait_send()
    remote(halo, halo, halo_send, halo_recv, peer).wait_send()
    block_copy.wait()
    decoded_copy.wait()


def hand_over(block_in, decoded_in, block_to, decoded_to, block, decoded, sem):
    rooms = ((block_in, block, block_to), (decoded_in, decoded, decoded_to))
    loads = [pltpu.make_async_copy(a, b, sem.at[i]) for i, (a, b, _) in enumerate(rooms)]
    stores = [pltpu.make_async_copy(b, c, sem.at[2 + i]) for i, (_, b, c) in enumerate(rooms)]
    for load in loads:
        load.start()
    for load, store in zip(loads, stores):
        load.wait()
        store.start()
    for store in stores:
        store.wait()


def body(seqs, heads, *args):
    (
        queries,
        keys,
        values,
        text_keys,
        text_values,
        text_mask,
        tokens,
        out_weight,
        out_bias,
        gate,
        shift,
        scale,
        final_weight,
        final_bias,
        conv_weight,
        conv_bias,
    ) = args
    dim = queries.shape[3]
    width = GROUP * HEAD_DIM
    text = text_keys.shape[0]
    layers = seqs // PAIR
    far = layers // 2
    rows = heads * TOK
    features = final_weight.shape[1]
    taps = 9 * LAT_CH
    channels = conv_weight.shape[4]
    rs_parts = 4
    operands = (
        queries.reshape(TOK, dim),
        keys.reshape(TOK, dim),
        values.reshape(TOK, dim),
        text_keys,
        text_values,
        text_mask.reshape(1, text),
        tokens.reshape(TOK, dim),
        out_weight,
        out_bias.reshape(1, dim),
        gate.reshape(1, dim),
        shift.reshape(1, dim),
        scale.reshape(1, dim),
        final_weight.T,
        final_bias.reshape(1, features),
        conv_weight.reshape(3 * taps, channels),
        conv_bias.reshape(1, channels),
    )
    copied = [pltpu.VMEM(x.shape, x.dtype) for x in operands]
    dma = pltpu.SemaphoreType.DMA
    anywhere = pl.BlockSpec(memory_space=pl.ANY)
    results = (
        jax.ShapeDtypeStruct((TOK, dim), BF16),
        jax.ShapeDtypeStruct((2, 2 * TOK, channels), BF16),
    )
    block_out, decoded = pl.pallas_call(
        functools.partial(kernel, seqs, heads),
        out_shape=results,
        in_specs=[anywhere] * len(operands),
        out_specs=(anywhere, anywhere),
        scratch_shapes=copied
        + [
            pltpu.VMEM((heads, 2, TOK, width), BF16),
            pltpu.VMEM((heads, TOK, width), BF16),
            pltpu.VMEM((heads, 2, TOK, width), BF16),
            pltpu.VMEM((heads, TOK, width), BF16),
            pltpu.VMEM((layers, GROUP, 2, rows, HEAD_DIM), BF16),
            pltpu.VMEM((PAIR, GROUP, rows, HEAD_DIM), BF16),
            pltpu.VMEM((GROUP, HEAD_DIM, PAIR * rows), BF16),
            pltpu.VMEM((text, TOK), F32),
            pltpu.VMEM((GROUP, TOK, PAIR * rows), F32),
            pltpu.VMEM((GROUP, TOK, PAIR * rows), F32),
            pltpu.VMEM((GROUP, HEAD_DIM, PAIR * rows), F32),
            pltpu.VMEM((16, PAIR * rows), F32),
            pltpu.VMEM((PAIR, 16, HEAD_DIM), BF16),
            pltpu.VMEM((PAIR, 16, HEAD_DIM), BF16),
            pltpu.VMEM((GROUP * PAIR, HEAD_DIM), F32),
            pltpu.VMEM((PAIR, GROUP, rows, HEAD_DIM), BF16),
            pltpu.VMEM((PAIR, GROUP, rows, HEAD_DIM), BF16),
            pltpu.VMEM((rs_parts, heads, TOK, dim // rs_parts), BF16),
            pltpu.VMEM((rs_parts, heads, TOK, dim // rs_parts), BF16),
            pltpu.VMEM((TOK, HEAD_DIM), BF16),
            pltpu.VMEM((8, TOK, HEAD_DIM), BF16),
            pltpu.VMEM((taps, channels), BF16),
            pltpu.VMEM((4, 4 * features, channels), BF16),
            pltpu.VMEM((2, channels // HEAD_DIM, 2 * TOK, HEAD_DIM), F32),
            pltpu.VMEM((TOK, dim), BF16),
            pltpu.VMEM((2, 2 * TOK, channels), BF16),
            dma((len(operands),)),
            dma((2,)),
            dma,
            dma,
            dma,
            dma,
            dma((2,)),
            dma((2,)),
            dma((layers, GROUP, 2)),
            dma,
            dma,
            dma,
            dma,
            dma,
            dma,
            dma((rs_parts,)),
            dma((rs_parts,)),
            dma,
            dma,
        ],
        compiler_params=pltpu.CompilerParams(
            collective_id=0, has_side_effects=True, vmem_limit_bytes=60 * 1024 * 1024
        ),
        cost_estimate=pl.CostEstimate(
            flops=1_200_000_000, bytes_accessed=5_000_000, transcendentals=1_000_000
        ),
    )(*operands)
    block_out, decoded = pl.pallas_call(
        hand_over,
        out_shape=results,
        in_specs=[anywhere] * 2,
        out_specs=(anywhere, anywhere),
        scratch_shapes=[pltpu.VMEM(x.shape, x.dtype) for x in results] + [dma((4,))],
        compiler_params=pltpu.CompilerParams(vmem_limit_bytes=60 * 1024 * 1024),
    )(block_out, decoded)
    return (
        block_out.reshape(1, TOK, 1, dim),
        decoded.reshape(1, 2, 2 * TOK, channels),
    )


def solution(mesh):
    seqs = mesh.shape["seq"]
    heads = mesh.shape["head"]
    spread = P("seq", "head", None, None)
    in_specs = (
        spread,
        spread,
        spread,
        P(None, "head"),
        P(None, "head"),
        P(),
        spread,
        P("head", None),
    ) + (P(),) * 8
    out_specs = (spread, P(None, "seq", "head", None))
    return jax.shard_map(
        functools.partial(body, seqs, heads),
        mesh=mesh,
        in_specs=in_specs,
        out_specs=out_specs,
        check_vma=False,
    )
```

```python
import functools

import jax
import jax.numpy as jnp
from jax import lax
from jax.experimental import pallas as pl
from jax.experimental.pallas import tpu as pltpu
from jax.sharding import PartitionSpec as P

HEAD_DIM = 128
GROUP = 3
LAT_CH = 16
TOK = 8
LAYER = 4
PAIR = 8
COLUMNS = 4
LATENT_SCALE = 0.476986
NEG = -1e30
SCORE_SCALE = HEAD_DIM ** (-0.5)
LOG2E = 1.4426950408889634
BF16 = jnp.bfloat16
F32 = jnp.float32
MESH = pl.DeviceIdType.MESH


def dot(a, b):
    return jnp.dot(a, b, preferred_element_type=F32)


def dot_tn(a, b):
    return lax.dot_general(a, b, (((0,), (0,)), ((), ())), preferred_element_type=F32)


def dot_nt(a, b):
    return lax.dot_general(a, b, (((1,), (1,)), ((), ())), preferred_element_type=F32)


def kernel(
    seqs,
    heads,
    q_hbm,
    k_hbm,
    v_hbm,
    text_k_hbm,
    text_v_hbm,
    mask_hbm,
    tokens_hbm,
    out_w_hbm,
    out_bias_hbm,
    gate_hbm,
    shift_hbm,
    scale_hbm,
    final_w_hbm,
    final_bias_hbm,
    conv_w_hbm,
    conv_bias_hbm,
    block_out,
    decoded,
    queries,
    keys,
    values,
    text_k,
    text_v,
    mask,
    tokens,
    out_w,
    out_bias,
    gate,
    shift,
    scale,
    final_w,
    final_bias,
    conv_w,
    conv_bias,
    kv_stage,
    q_stage,
    kv_in,
    q_in,
    kv,
    qs,
    q_turned,
    mask_column,
    run_max,
    run_sum,
    run_acc,
    marks,
    mark_stage,
    mark_in,
    shares,
    o_stage,
    o_in,
    rs_stage,
    rs_in,
    lat,
    halo,
    w_sum,
    w_full,
    pixels,
    local_sem,
    kv_send,
    kv_recv,
    q_a2a_send,
    q_a2a_recv,
    ring_send,
    half_send,
    ring_recv,
    q_send,
    q_recv,
    o_send,
    o_recv,
    mark_send,
    mark_recv,
    rs_send,
    rs_recv,
    halo_send,
    halo_recv,
):
    s = lax.axis_index("seq")
    h = lax.axis_index("head")
    layers = seqs // PAIR
    far = layers // 2
    depth = s // LAYER
    j = lax.rem(s, LAYER)
    z = depth // 2
    parity_z = lax.rem(depth, 2)
    column = lax.rem(h, COLUMNS)
    y_high = h // COLUMNS
    part_of = y_high * LAYER + j
    place = parity_z * COLUMNS + column
    apart = lax.rem(y_high + parity_z, 2)
    width = GROUP * HEAD_DIM
    dim = heads * width
    rows = heads * TOK
    rs_parts = rs_stage.shape[0]
    part_cols = dim // rs_parts

    def shifted(index, by, count):
        return lax.rem(index + (by % count), count)

    r = lax.rem(j + LAYER // 2, LAYER)

    def head_peer(i):
        return (depth * LAYER + r, shifted(h, i, heads))

    def group_peer(i):
        at_depth = z * 2 + lax.rem(parity_z + i // COLUMNS, 2)
        at_column = lax.rem(column + lax.rem(i, COLUMNS), COLUMNS)
        group = lax.rem(at_depth, 2) * COLUMNS + at_column
        return (at_depth * LAYER + j, y_high * COLUMNS + at_column), group

    def part_peer(i):
        part = lax.rem(part_of + i, PAIR)
        return (depth * LAYER + lax.rem(part, LAYER), (part // LAYER) * COLUMNS + column)

    def row_peer(i):
        at_parity = lax.rem(parity_z + i // LAYER, 2)
        row = lax.rem(j + lax.rem(i, LAYER), LAYER)
        owner = lax.rem(row + LAYER // 2, LAYER)
        to = ((z * 2 + at_parity) * LAYER + owner, parity_z * COLUMNS + column)
        return to, at_parity * LAYER + row

    own_row = LAYER // 2

    def slot_at(by):
        return lax.rem(z + by + layers, layers)

    def ring_peer(by):
        return ((slot_at(by) * 2 + parity_z) * LAYER + j, h)

    right, left = ring_peer(1), ring_peer(-1)

    def remote(src, dst, send, recv, device):
        return pltpu.make_async_remote_copy(
            src_ref=src,
            dst_ref=dst,
            send_sem=send,
            recv_sem=recv,
            device_id=device,
            device_id_type=MESH,
        )

    pairs = (
        (k_hbm, keys),
        (v_hbm, values),
        (q_hbm, queries),
        (conv_w_hbm, conv_w),
        (text_k_hbm, text_k),
        (text_v_hbm, text_v),
        (mask_hbm, mask),
        (tokens_hbm, tokens),
        (out_w_hbm, out_w),
        (out_bias_hbm, out_bias),
        (gate_hbm, gate),
        (shift_hbm, shift),
        (scale_hbm, scale),
        (final_w_hbm, final_w),
        (final_bias_hbm, final_bias),
        (conv_bias_hbm, conv_bias),
    )
    loads = [
        pltpu.make_async_copy(src, dst, local_sem.at[i]) for i, (src, dst) in enumerate(pairs)
    ]

    halo_steps = [(dr, dc) for dr in (-1, 0, 1) for dc in (-1, 0, 1) if (dr, dc) != (0, 0)]
    halo_peers = [(shifted(s, dr, seqs), shifted(h, dc, heads)) for dr, dc in halo_steps]
    partners = [group_peer(i)[0] for i in range(1, heads)]
    partners += [right, left]
    partners += [part_peer(i) for i in range(1, PAIR)]
    partners += halo_peers
    for load in loads[:3]:
        load.start()
    barrier = pltpu.get_barrier_semaphore()
    for partner in partners:
        pl.semaphore_signal(barrier, inc=1, device_id=partner, device_id_type=MESH)

    group_cols = [slice(g * width, (g + 1) * width) for g in range(heads)]
    for at, whole in enumerate((keys, values)):
        loads[at].wait()
        for g, cols in enumerate(group_cols):
            kv_stage[g, at] = whole[:, cols]
    pl.semaphore_wait(barrier, len(partners))

    def send_kv(i, carry):
        to, group = group_peer(i)
        remote(kv_stage.at[group], kv_in.at[place], kv_send, kv_recv, to).start()
        return carry

    def send_q(i, carry):
        to, group = group_peer(i)
        remote(q_stage.at[group], q_in.at[place], q_a2a_send, q_a2a_recv, to).start()
        return carry

    lax.fori_loop(1, heads, send_kv, 0)
    kv_in[place] = kv_stage[place]
    loads[2].wait()
    for g, cols in enumerate(group_cols):
        q_stage[g] = queries[:, cols]
    lax.fori_loop(1, heads, send_q, 0)
    q_in[place] = q_stage[place]
    for load in loads[3:7]:
        load.start()

    taps = w_sum.shape[0]
    parities = w_full.shape[0]
    features = final_w.shape[0]

    def sum_taps():
        conv_all = conv_w[...].astype(F32)
        total = conv_all[:taps] + conv_all[taps : 2 * taps] + conv_all[2 * taps :]
        w_sum[...] = total.astype(BF16)

    def conv_weights(parity):
        up = parity // 2
        side = lax.rem(parity, 2)
        depth = w_full.shape[1]
        row = lax.broadcasted_iota(jnp.int32, (depth, taps), 0)
        col = lax.broadcasted_iota(jnp.int32, (depth, taps), 1)
        tap_i = 2 * (row >> 7) + ((row >> 1) & 1) + up - 1
        tap_j = 2 * ((row >> 6) & 1) + (row & 1) + side - 1
        inside = (tap_i >= 0) & (tap_i <= 2) & (tap_j >= 0) & (tap_j <= 2)
        source = (tap_i * 3 + tap_j) * LAT_CH + ((row & 63) >> 2)
        pick = jnp.where(inside & (source == col), 1.0, 0.0).astype(BF16)
        w_full[parity] = dot(pick, w_sum[...]).astype(BF16)

    def rows_of(block):
        return block.astype(F32).reshape(rows, width).astype(BF16)

    peer = head_peer(0)
    seven = kv_in.at[pl.ds(0, heads - 1)]
    remote(seven, seven, kv_send, kv_recv, peer).wait_recv()
    own_k = rows_of(kv_in[:, 0])
    own_v = rows_of(kv_in[:, 1])
    for n in range(GROUP):
        cols = slice(n * HEAD_DIM, (n + 1) * HEAD_DIM)
        kv[z, n, 0] = own_k[:, cols]
        kv[z, n, 1] = own_v[:, cols]

    def to_right(ref, recv, send=0):
        return remote(ref, ref, ring_send.at[0] if send == 0 else half_send.at[0], recv, right)

    def to_left(ref, recv, send=0):
        return remote(ref, ref, ring_send.at[1] if send == 0 else half_send.at[1], recv, left)

    pieces_of = [(n, part) for n in range(GROUP) for part in range(2)]

    for n, part in pieces_of:
        to_right(kv.at[z, n, part], ring_recv.at[z, n, part]).start()
        to_left(kv.at[z, n, part], ring_recv.at[z, n, part]).start()
    for load in loads[7:]:
        load.start()

    seven = q_in.at[pl.ds(0, heads - 1)]
    remote(seven, seven, q_a2a_send, q_a2a_recv, peer).wait_recv()
    own_q = rows_of(q_in[...])
    for n in range(GROUP):
        qs[part_of, n] = own_q[:, n * HEAD_DIM : (n + 1) * HEAD_DIM]

    def send_queries(i, carry):
        remote(qs.at[part_of], qs.at[part_of], q_send, q_recv, part_peer(i)).start()
        return carry

    lax.fori_loop(1, PAIR, send_queries, 0)

    def weigh(scores, top):
        return jnp.exp2((scores - top) * (SCORE_SCALE * LOG2E))

    def attend_first(n, carry):
        share = text_k.shape[0] // LAYER
        mine = pl.ds(pl.multiple_of(j * share, share), share)
        cols = pl.ds(pl.multiple_of(n * HEAD_DIM, HEAD_DIM), HEAD_DIM)
        keys_now = jnp.concatenate([text_k[mine, cols], kv[z, n, 0]], axis=0)
        values_now = jnp.concatenate([text_v[mine, cols], kv[z, n, 1]], axis=0)
        scores = dot(keys_now, q_turned[n])
        held = mask_column[mine, :1] * (1 - apart).astype(F32)
        real = jnp.concatenate([held, jnp.ones((rows, 1), F32)], axis=0) == 1.0
        real = jnp.broadcast_to(real, scores.shape)
        scores = jnp.where(real, scores, NEG)
        top = jnp.max(scores, axis=0, keepdims=True)
        weights = jnp.where(real, weigh(scores, top), 0.0)
        run_max[n, :1] = top
        run_sum[n, :1] = jnp.sum(weights, axis=0, keepdims=True)
        run_acc[n] = dot_tn(values_now, weights.astype(BF16))
        return carry

    def absorb(n, slots):
        keys_now = jnp.concatenate([kv[slot, n, 0] for slot in slots], axis=0)
        values_now = jnp.concatenate([kv[slot, n, 1] for slot in slots], axis=0)
        scores = dot(keys_now, q_turned[n])
        old = run_max[n, :1]
        top = jnp.maximum(old, jnp.max(scores, axis=0, keepdims=True))
        factor = weigh(old, top)
        weights = weigh(scores, top)
        total = run_sum[n, :1] * factor + jnp.sum(weights, axis=0, keepdims=True)
        acc = run_acc[n] * factor + dot_tn(values_now, weights.astype(BF16))
        return top, total, acc

    def work_on(n, steps):
        top, total, acc = absorb(n, [slot_at(by) for step in steps for by in (-step, step)])
        run_max[n, :1] = top
        run_sum[n, :1] = total
        run_acc[n] = acc

    def pass_on(step):
        one = slot_at(-step)
        other = slot_at(step)

        def one_head(n, carry):
            for part in range(2):
                copy = to_right(kv.at[one, n, part], ring_recv.at[one, n, part])
                copy.wait_recv()
                copy.start()
                copy = to_left(kv.at[other, n, part], ring_recv.at[other, n, part])
                copy.wait_recv()
                copy.start()
            return carry

        lax.fori_loop(0, GROUP, one_head, 0)

    def pass_on_halves(step):
        one = slot_at(-step)
        other = slot_at(step)

        def one_head(n, carry):
            for part in range(2):
                copy = to_right(kv.at[one, n, part], ring_recv.at[one, n, part], 1)
                copy.wait_recv()
                if part == 0:
                    copy.start()
                copy = to_left(kv.at[other, n, part], ring_recv.at[other, n, part], 1)
                copy.wait_recv()
                if part == 1:
                    copy.start()
            return carry

        lax.fori_loop(0, GROUP, one_head, 0)

    pass_on(1)
    seven = qs.at[pl.ds(0, PAIR - 1)]
    remote(seven, seven, q_send, q_recv, peer).wait_recv()
    half = rows // 2

    def turn_queries(n, carry):
        pieces = [
            qs[y * LAYER + row, n, at * half : (at + 1) * half]
            for at in range(2)
            for row in range(LAYER)
            for y in range(2)
        ]
        q_turned[n] = jnp.concatenate(pieces, axis=0).T
        return carry

    lax.fori_loop(0, GROUP, turn_queries, 0)
    for load in loads[3:7]:
        load.wait()
    mask_column[...] = jnp.broadcast_to(mask[...].astype(F32), (TOK, mask.shape[1])).T
    lax.fori_loop(0, GROUP, attend_first, 0)
    pass_on(2)
    sum_taps()

    def one_parity(parity, carry):
        conv_weights(parity)
        return carry

    lax.fori_loop(0, parities, one_parity, 0)
    pass_on_halves(3)

    def middle_step(n, carry):
        work_on(n, range(1, far - 1))
        return carry

    lax.fori_loop(0, GROUP, middle_step, 0)

    opposite = slot_at(far)
    marks[...] = jnp.zeros_like(marks)

    def last_step(n, carry):
        to_right(kv.at[opposite, n, 0], ring_recv.at[opposite, n, 0]).wait_recv()
        to_left(kv.at[opposite, n, 1], ring_recv.at[opposite, n, 1]).wait_recv()
        top, total, acc = absorb(n, [slot_at(1 - far), slot_at(far - 1), opposite])
        share = (acc / total).T.astype(BF16)
        for i in range(PAIR):
            o_stage[i, n] = share[i * rows : (i + 1) * rows]

        def send_share(i, inner):
            to, row = row_peer(i)

            @pl.when((i != own_row) | (apart == 1))
            def _():
                remote(o_stage.at[row, n], o_in.at[part_of, n], o_send, o_recv, to).start()

            return inner

        lax.fori_loop(0, PAIR, send_share, 0)
        level = top * SCORE_SCALE + jnp.log(total)
        first = level.astype(BF16).astype(F32)
        second = (level - first).astype(BF16).astype(F32)
        marks[pl.ds(3 * n, 1)] = first
        marks[pl.ds(3 * n + 1, 1)] = second
        marks[pl.ds(3 * n + 2, 1)] = level - first - second
        return carry

    lax.fori_loop(0, GROUP, last_step, 0)
    level_rows = marks[...]
    lanes = mark_stage.shape[2]
    for i in range(PAIR):
        turned = level_rows if i == 0 else pltpu.roll(level_rows, (PAIR - i) * rows, 1)
        mark_stage[i] = turned[:, :lanes].astype(BF16)

    def send_marks(i, carry):
        to, row = row_peer(i)

        @pl.when((i != own_row) | (apart == 1))
        def _():
            remote(mark_stage.at[row], mark_in.at[part_of], mark_send, mark_recv, to).start()

        return carry

    lax.fori_loop(0, PAIR, send_marks, 0)
    own_at = row_peer(own_row)[1]

    @pl.when(apart == 0)
    def _():
        o_in[part_of] = o_stage[own_at]
        mark_in[part_of] = mark_stage[own_at]

    for load in loads[7:]:
        load.wait()

    def await_shares(whole, send, recv, sent):
        def wait(ref):
            copy = remote(ref, ref, send, recv, peer)
            if sent:
                copy.wait_send()
            else:
                copy.wait_recv()

        @pl.when(apart == 1)
        def _():
            wait(whole)

        @pl.when(apart == 0)
        def _():
            wait(whole.at[pl.ds(0, PAIR - 1)])

    await_shares(o_in, o_send, o_recv, False)
    await_shares(mark_in, mark_send, mark_recv, False)
    level_parts = [mark_in[i].astype(F32) for i in range(PAIR)]
    shares[...] = jnp.zeros_like(shares)
    for n in range(GROUP):
        levels = [
            part[3 * n : 3 * n + 1] + part[3 * n + 1 : 3 * n + 2] + part[3 * n + 2 : 3 * n + 3]
            for part in level_parts
        ]
        top = functools.reduce(jnp.maximum, levels)
        parts = [jnp.exp(level - top) for level in levels]
        total = functools.reduce(jnp.add, parts)
        for i, part in enumerate(parts):
            shares[n * PAIR + i : n * PAIR + i + 1] = part / total
    columns = shares[...].T[:rows]
    attended = []
    for n in range(GROUP):
        mixed = functools.reduce(
            jnp.add,
            [
                columns[:, n * PAIR + i : n * PAIR + i + 1] * o_in[i, n].astype(F32)
                for i in range(PAIR)
            ],
        )
        attended.append(mixed.astype(BF16))
    attended = jnp.concatenate(attended, axis=1)

    for part in range(rs_parts):
        product = dot(attended, out_w[:, part * part_cols : (part + 1) * part_cols])
        rs_stage[part] = product.reshape(heads, TOK, part_cols).astype(BF16)

        def send_part(i, carry, part=part):
            to = head_peer(i)
            remote(
                rs_stage.at[part, to[1]],
                rs_in.at[part, h],
                rs_send.at[part],
                rs_recv.at[part],
                to,
            ).start()
            return carry

        lax.fori_loop(0, heads, send_part, 0)
    pieces = []
    for part in range(rs_parts):
        cols = slice(part * part_cols, (part + 1) * part_cols)
        whole = rs_in.at[part]
        remote(whole, whole, rs_send.at[part], rs_recv.at[part], peer).wait_recv()
        projected = jnp.sum(rs_in[part].astype(F32), axis=0)
        stream = tokens[:, cols].astype(F32) + gate[:, cols] * (projected + out_bias[:, cols])
        rounded = stream.astype(BF16)
        block_out[:, cols] = rounded
        pieces.append(rounded.astype(F32))

    normed_in = jnp.concatenate(pieces, axis=1)
    centered = normed_in - jnp.mean(normed_in, axis=1, keepdims=True)
    spread = jnp.mean(centered * centered, axis=1, keepdims=True)
    normed = centered * lax.rsqrt(spread + 1e-06)
    modulated = (normed * (1.0 + scale[...]) + shift[...]).astype(BF16)
    patches = (dot_nt(modulated, final_w[...]) + final_bias[...]) / LATENT_SCALE
    padded = jnp.concatenate([patches, jnp.zeros((TOK, HEAD_DIM - features), F32)], axis=1)
    lat[...] = padded.astype(BF16)

    for at, to in enumerate(halo_peers):
        remote(lat, halo.at[at], halo_send, halo_recv, to).start()
    tiles = {(0, 0): lat[...].astype(F32)}
    remote(halo, halo, halo_send, halo_recv, peer).wait_recv()
    for at, (dr, dc) in enumerate(halo_steps):
        tiles[(-dr, -dc)] = halo[at].astype(F32)

    def rolled(tile, by):
        return pltpu.roll(tile, by % HEAD_DIM, 1)

    top_edge, bottom_edge = s == 0, s == seqs - 1
    first_tile, last_tile = h == 0, h == heads - 1
    for dc in (-1, 0, 1):
        middle = tiles[(0, dc)]
        tiles[(-1, dc)] = jnp.where(top_edge, rolled(middle, 2), tiles[(-1, dc)])
        tiles[(1, dc)] = jnp.where(bottom_edge, rolled(middle, -2), tiles[(1, dc)])
    low = lax.broadcasted_iota(jnp.int32, (1, HEAD_DIM), 1) < features
    packed = {}
    for dr in (-1, 0, 1):
        middle = tiles[(dr, 0)]
        before = jnp.where(first_tile, rolled(middle, 1)[:1], tiles[(dr, -1)][TOK - 1 :])
        after = jnp.where(last_tile, rolled(middle, -1)[TOK - 1 :], tiles[(dr, 1)][:1])
        before = jnp.concatenate([before, middle[: TOK - 1]], axis=0)
        after = jnp.concatenate([middle[1:], after], axis=0)
        packed[(dr, 0)] = jnp.where(low, before, rolled(middle, features))
        packed[(dr, 1)] = jnp.where(low, middle, rolled(after, features))
    for parity in range(parities):
        up, side = parity // 2, parity % 2
        stacked = jnp.concatenate([packed[(up - 1, side)], packed[(up, side)]], axis=1)
        result = dot(stacked.astype(BF16), w_full[parity]) + conv_bias[...]
        for tile in range(pixels.shape[1]):
            pixels[up, tile, pl.ds(side, TOK, stride=2), :] = result[
                :, tile * HEAD_DIM : (tile + 1) * HEAD_DIM
            ]
    for tile in range(pixels.shape[1]):
        cols = slice(tile * HEAD_DIM, (tile + 1) * HEAD_DIM)
        decoded[:, :, cols] = pixels[:, tile].astype(BF16)

    seven = kv_stage.at[pl.ds(0, heads - 1)]
    remote(seven, seven, kv_send, kv_recv, peer).wait_send()
    seven = q_stage.at[pl.ds(0, heads - 1)]
    remote(seven, seven, q_a2a_send, q_a2a_recv, peer).wait_send()
    ring_all = kv.at[pl.ds(0, far - 1)]
    to_right(ring_all, ring_recv.at[0, 0, 0]).wait_send()
    to_left(ring_all, ring_recv.at[0, 0, 0]).wait_send()
    ring_half = kv.at[0, :, 0]
    to_right(ring_half, ring_recv.at[0, 0, 0], 1).wait_send()
    to_left(ring_half, ring_recv.at[0, 0, 0], 1).wait_send()
    seven = qs.at[pl.ds(0, PAIR - 1)]
    remote(seven, seven, q_send, q_recv, peer).wait_send()
    await_shares(o_stage, o_send, o_recv, True)
    await_shares(mark_stage, mark_send, mark_recv, True)
    for part in range(rs_parts):
        whole = rs_stage.at[part]
        remote(whole, whole, rs_send.at[part], rs_recv.at[part], peer).wait_send()
    remote(halo, halo, halo_send, halo_recv, peer).wait_send()


def hand_over(block_in, decoded_in, block_to, decoded_to, sem):
    copies = [
        pltpu.make_async_copy(block_in, block_to, sem.at[0]),
        pltpu.make_async_copy(decoded_in, decoded_to, sem.at[1]),
    ]
    for copy in copies:
        copy.start()
    for copy in copies:
        copy.wait()


def body(seqs, heads, *args):
    (
        queries,
        keys,
        values,
        text_keys,
        text_values,
        text_mask,
        tokens,
        out_weight,
        out_bias,
        gate,
        shift,
        scale,
        final_weight,
        final_bias,
        conv_weight,
        conv_bias,
    ) = args
    dim = queries.shape[3]
    width = GROUP * HEAD_DIM
    text = text_keys.shape[0]
    layers = seqs // PAIR
    far = layers // 2
    rows = heads * TOK
    features = final_weight.shape[1]
    taps = 9 * LAT_CH
    channels = conv_weight.shape[4]
    rs_parts = 4
    operands = (
        queries.reshape(TOK, dim),
        keys.reshape(TOK, dim),
        values.reshape(TOK, dim),
        text_keys,
        text_values,
        text_mask.reshape(1, text),
        tokens.reshape(TOK, dim),
        out_weight,
        out_bias.reshape(1, dim),
        gate.reshape(1, dim),
        shift.reshape(1, dim),
        scale.reshape(1, dim),
        final_weight.T,
        final_bias.reshape(1, features),
        conv_weight.reshape(3 * taps, channels),
        conv_bias.reshape(1, channels),
    )
    copied = [pltpu.VMEM(x.shape, x.dtype) for x in operands]
    dma = pltpu.SemaphoreType.DMA
    anywhere = pl.BlockSpec(memory_space=pl.ANY)
    results = (
        jax.ShapeDtypeStruct((TOK, dim), BF16),
        jax.ShapeDtypeStruct((2, 2 * TOK, channels), BF16),
    )
    held = pl.BlockSpec(memory_space=pltpu.VMEM)
    block_out, decoded = pl.pallas_call(
        functools.partial(kernel, seqs, heads),
        out_shape=tuple(pltpu.VMEM(x.shape, x.dtype) for x in results),
        in_specs=[anywhere] * len(operands),
        out_specs=(held, held),
        scratch_shapes=copied
        + [
            pltpu.VMEM((heads, 2, TOK, width), BF16),
            pltpu.VMEM((heads, TOK, width), BF16),
            pltpu.VMEM((heads, 2, TOK, width), BF16),
            pltpu.VMEM((heads, TOK, width), BF16),
            pltpu.VMEM((layers, GROUP, 2, rows, HEAD_DIM), BF16),
            pltpu.VMEM((PAIR, GROUP, rows, HEAD_DIM), BF16),
            pltpu.VMEM((GROUP, HEAD_DIM, PAIR * rows), BF16),
            pltpu.VMEM((text, TOK), F32),
            pltpu.VMEM((GROUP, TOK, PAIR * rows), F32),
            pltpu.VMEM((GROUP, TOK, PAIR * rows), F32),
            pltpu.VMEM((GROUP, HEAD_DIM, PAIR * rows), F32),
            pltpu.VMEM((16, PAIR * rows), F32),
            pltpu.VMEM((PAIR, 16, HEAD_DIM), BF16),
            pltpu.VMEM((PAIR, 16, HEAD_DIM), BF16),
            pltpu.VMEM((GROUP * PAIR, HEAD_DIM), F32),
            pltpu.VMEM((PAIR, GROUP, rows, HEAD_DIM), BF16),
            pltpu.VMEM((PAIR, GROUP, rows, HEAD_DIM), BF16),
            pltpu.VMEM((rs_parts, heads, TOK, dim // rs_parts), BF16),
            pltpu.VMEM((rs_parts, heads, TOK, dim // rs_parts), BF16),
            pltpu.VMEM((TOK, HEAD_DIM), BF16),
            pltpu.VMEM((8, TOK, HEAD_DIM), BF16),
            pltpu.VMEM((taps, channels), BF16),
            pltpu.VMEM((4, 4 * features, channels), BF16),
            pltpu.VMEM((2, channels // HEAD_DIM, 2 * TOK, HEAD_DIM), F32),
            dma((len(operands),)),
            dma,
            dma,
            dma,
            dma,
            dma((2,)),
            dma((2,)),
            dma((layers, GROUP, 2)),
            dma,
            dma,
            dma,
            dma,
            dma,
            dma,
            dma((rs_parts,)),
            dma((rs_parts,)),
            dma,
            dma,
        ],
        compiler_params=pltpu.CompilerParams(
            collective_id=0, has_side_effects=True, vmem_limit_bytes=60 * 1024 * 1024
        ),
        cost_estimate=pl.CostEstimate(
            flops=1_200_000_000, bytes_accessed=5_000_000, transcendentals=1_000_000
        ),
    )(*operands)
    block_out, decoded = pl.pallas_call(
        hand_over,
        out_shape=results,
        in_specs=(anywhere, anywhere),
        out_specs=(anywhere, anywhere),
        scratch_shapes=[dma((2,))],
        compiler_params=pltpu.CompilerParams(vmem_limit_bytes=2 * 1024 * 1024),
    )(block_out, decoded)
    return (
        block_out.reshape(1, TOK, 1, dim),
        decoded.reshape(1, 2, 2 * TOK, channels),
    )


def solution(mesh):
    seqs = mesh.shape["seq"]
    heads = mesh.shape["head"]
    spread = P("seq", "head", None, None)
    in_specs = (
        spread,
        spread,
        spread,
        P(None, "head"),
        P(None, "head"),
        P(),
        spread,
        P("head", None),
    ) + (P(),) * 8
    out_specs = (spread, P(None, "seq", "head", None))
    return jax.shard_map(
        functools.partial(body, seqs, heads),
        mesh=mesh,
        in_specs=in_specs,
        out_specs=out_specs,
        check_vma=False,
    )
```

```python
import functools

import jax
import jax.numpy as jnp
from jax import lax
from jax.experimental import pallas as pl
from jax.experimental.pallas import tpu as pltpu
from jax.sharding import PartitionSpec as P

HEAD_DIM = 128
GROUP = 3
LAT_CH = 16
TOK = 8
LAYER = 4
PAIR = 8
COLUMNS = 4
LATENT_SCALE = 0.476986
NEG = -1e30
SCORE_SCALE = HEAD_DIM ** (-0.5)
LOG2E = 1.4426950408889634
BF16 = jnp.bfloat16
F32 = jnp.float32
MESH = pl.DeviceIdType.MESH


def dot(a, b):
    return jnp.dot(a, b, preferred_element_type=F32)


def dot_tn(a, b):
    return lax.dot_general(a, b, (((0,), (0,)), ((), ())), preferred_element_type=F32)


def dot_nt(a, b):
    return lax.dot_general(a, b, (((1,), (1,)), ((), ())), preferred_element_type=F32)


def kernel(
    seqs,
    heads,
    q_hbm,
    k_hbm,
    v_hbm,
    text_k_hbm,
    text_v_hbm,
    mask_hbm,
    tokens_hbm,
    out_w_hbm,
    out_bias_hbm,
    gate_hbm,
    shift_hbm,
    scale_hbm,
    final_w_hbm,
    final_bias_hbm,
    conv_w_hbm,
    conv_bias_hbm,
    block_out,
    decoded,
    queries,
    keys,
    values,
    text_k,
    text_v,
    mask,
    tokens,
    out_w,
    out_bias,
    gate,
    shift,
    scale,
    final_w,
    final_bias,
    conv_w,
    conv_bias,
    kv_stage,
    q_stage,
    kv_in,
    q_in,
    kv,
    qs,
    q_turned,
    mask_column,
    run_max,
    run_sum,
    run_acc,
    marks,
    mark_stage,
    mark_in,
    shares,
    o_stage,
    o_in,
    rs_stage,
    rs_in,
    lat,
    halo,
    w_sum,
    w_full,
    pixels,
    local_sem,
    kv_send,
    kv_recv,
    q_a2a_send,
    q_a2a_recv,
    ring_send,
    half_send,
    ring_recv,
    q_send,
    q_recv,
    o_send,
    o_recv,
    mark_send,
    mark_recv,
    rs_send,
    rs_recv,
    halo_send,
    halo_recv,
):
    s = lax.axis_index("seq")
    h = lax.axis_index("head")
    layers = seqs // PAIR
    far = layers // 2
    depth = s // LAYER
    j = lax.rem(s, LAYER)
    z = depth // 2
    parity_z = lax.rem(depth, 2)
    column = lax.rem(h, COLUMNS)
    y_high = h // COLUMNS
    part_of = y_high * LAYER + j
    place = parity_z * COLUMNS + column
    apart = lax.rem(y_high + parity_z, 2)
    width = GROUP * HEAD_DIM
    dim = heads * width
    rows = heads * TOK
    rs_parts = rs_stage.shape[0]
    part_cols = dim // rs_parts

    def shifted(index, by, count):
        return lax.rem(index + (by % count), count)

    r = lax.rem(j + LAYER // 2, LAYER)

    def head_peer(i):
        return (depth * LAYER + r, shifted(h, i, heads))

    def group_peer(i):
        at_depth = z * 2 + lax.rem(parity_z + i // COLUMNS, 2)
        at_column = lax.rem(column + lax.rem(i, COLUMNS), COLUMNS)
        group = lax.rem(at_depth, 2) * COLUMNS + at_column
        return (at_depth * LAYER + j, y_high * COLUMNS + at_column), group

    def part_peer(i):
        part = lax.rem(part_of + i, PAIR)
        return (depth * LAYER + lax.rem(part, LAYER), (part // LAYER) * COLUMNS + column)

    def row_peer(i):
        at_parity = lax.rem(parity_z + i // LAYER, 2)
        row = lax.rem(j + lax.rem(i, LAYER), LAYER)
        owner = lax.rem(row + LAYER // 2, LAYER)
        to = ((z * 2 + at_parity) * LAYER + owner, parity_z * COLUMNS + column)
        return to, at_parity * LAYER + row

    own_row = LAYER // 2

    def slot_at(by):
        return lax.rem(z + by + layers, layers)

    def ring_peer(by):
        return ((slot_at(by) * 2 + parity_z) * LAYER + j, h)

    right, left = ring_peer(1), ring_peer(-1)

    def remote(src, dst, send, recv, device):
        return pltpu.make_async_remote_copy(
            src_ref=src,
            dst_ref=dst,
            send_sem=send,
            recv_sem=recv,
            device_id=device,
            device_id_type=MESH,
        )

    pairs = (
        (k_hbm, keys),
        (v_hbm, values),
        (q_hbm, queries),
        (conv_w_hbm, conv_w),
        (text_k_hbm, text_k),
        (text_v_hbm, text_v),
        (mask_hbm, mask),
        (tokens_hbm, tokens),
        (out_w_hbm, out_w),
        (out_bias_hbm, out_bias),
        (gate_hbm, gate),
        (shift_hbm, shift),
        (scale_hbm, scale),
        (final_w_hbm, final_w),
        (final_bias_hbm, final_bias),
        (conv_bias_hbm, conv_bias),
    )
    loads = [
        pltpu.make_async_copy(src, dst, local_sem.at[i]) for i, (src, dst) in enumerate(pairs)
    ]

    halo_steps = [(dr, dc) for dr in (-1, 0, 1) for dc in (-1, 0, 1) if (dr, dc) != (0, 0)]
    halo_peers = [(shifted(s, dr, seqs), shifted(h, dc, heads)) for dr, dc in halo_steps]
    partners = [group_peer(i)[0] for i in range(1, heads)]
    partners += [right, left]
    partners += [part_peer(i) for i in range(1, PAIR)]
    for load in loads[:3]:
        load.start()
    barrier = pltpu.get_barrier_semaphore()
    for partner in partners:
        pl.semaphore_signal(barrier, inc=1, device_id=partner, device_id_type=MESH)

    group_cols = [slice(g * width, (g + 1) * width) for g in range(heads)]
    for at, whole in enumerate((keys, values)):
        loads[at].wait()
        for g, cols in enumerate(group_cols):
            kv_stage[g, at] = whole[:, cols]
    pl.semaphore_wait(barrier, len(partners))

    def send_kv(i, carry):
        to, group = group_peer(i)
        remote(kv_stage.at[group], kv_in.at[place], kv_send, kv_recv, to).start()
        return carry

    def send_q(i, carry):
        to, group = group_peer(i)
        remote(q_stage.at[group], q_in.at[place], q_a2a_send, q_a2a_recv, to).start()
        return carry

    lax.fori_loop(1, heads, send_kv, 0)
    kv_in[place] = kv_stage[place]
    loads[2].wait()
    for g, cols in enumerate(group_cols):
        q_stage[g] = queries[:, cols]
    lax.fori_loop(1, heads, send_q, 0)
    q_in[place] = q_stage[place]
    for load in loads[3:7]:
        load.start()

    taps = w_sum.shape[0]
    parities = w_full.shape[0]
    features = final_w.shape[0]

    def sum_taps():
        conv_all = conv_w[...].astype(F32)
        total = conv_all[:taps] + conv_all[taps : 2 * taps] + conv_all[2 * taps :]
        w_sum[...] = total.astype(BF16)

    def conv_weights(parity):
        up = parity // 2
        side = lax.rem(parity, 2)
        depth = w_full.shape[1]
        row = lax.broadcasted_iota(jnp.int32, (depth, taps), 0)
        col = lax.broadcasted_iota(jnp.int32, (depth, taps), 1)
        tap_i = 2 * (row >> 7) + ((row >> 1) & 1) + up - 1
        tap_j = 2 * ((row >> 6) & 1) + (row & 1) + side - 1
        inside = (tap_i >= 0) & (tap_i <= 2) & (tap_j >= 0) & (tap_j <= 2)
        source = (tap_i * 3 + tap_j) * LAT_CH + ((row & 63) >> 2)
        pick = jnp.where(inside & (source == col), 1.0, 0.0).astype(BF16)
        w_full[parity] = dot(pick, w_sum[...]).astype(BF16)

    def rows_of(block):
        return block.astype(F32).reshape(rows, width).astype(BF16)

    peer = head_peer(0)
    seven = kv_in.at[pl.ds(0, heads - 1)]
    remote(seven, seven, kv_send, kv_recv, peer).wait_recv()
    own_k = rows_of(kv_in[:, 0])
    own_v = rows_of(kv_in[:, 1])
    for n in range(GROUP):
        cols = slice(n * HEAD_DIM, (n + 1) * HEAD_DIM)
        kv[z, n, 0] = own_k[:, cols]
        kv[z, n, 1] = own_v[:, cols]

    def to_right(ref, recv, send=0):
        return remote(ref, ref, ring_send.at[0] if send == 0 else half_send.at[0], recv, right)

    def to_left(ref, recv, send=0):
        return remote(ref, ref, ring_send.at[1] if send == 0 else half_send.at[1], recv, left)

    pieces_of = [(n, part) for n in range(GROUP) for part in range(2)]

    for n, part in pieces_of:
        to_right(kv.at[z, n, part], ring_recv.at[z, n, part]).start()
        to_left(kv.at[z, n, part], ring_recv.at[z, n, part]).start()
    for load in loads[7:]:
        load.start()

    seven = q_in.at[pl.ds(0, heads - 1)]
    remote(seven, seven, q_a2a_send, q_a2a_recv, peer).wait_recv()
    own_q = rows_of(q_in[...])
    for n in range(GROUP):
        qs[part_of, n] = own_q[:, n * HEAD_DIM : (n + 1) * HEAD_DIM]

    def send_queries(i, carry):
        remote(qs.at[part_of], qs.at[part_of], q_send, q_recv, part_peer(i)).start()
        return carry

    lax.fori_loop(1, PAIR, send_queries, 0)

    def weigh(scores, top):
        return jnp.exp2((scores - top) * (SCORE_SCALE * LOG2E))

    def attend_first(n, carry):
        share = text_k.shape[0] // LAYER
        mine = pl.ds(pl.multiple_of(j * share, share), share)
        cols = pl.ds(pl.multiple_of(n * HEAD_DIM, HEAD_DIM), HEAD_DIM)
        keys_now = jnp.concatenate([text_k[mine, cols], kv[z, n, 0]], axis=0)
        values_now = jnp.concatenate([text_v[mine, cols], kv[z, n, 1]], axis=0)
        scores = dot(keys_now, q_turned[n])
        held = mask_column[mine, :1] * (1 - apart).astype(F32)
        real = jnp.concatenate([held, jnp.ones((rows, 1), F32)], axis=0) == 1.0
        real = jnp.broadcast_to(real, scores.shape)
        scores = jnp.where(real, scores, NEG)
        top = jnp.max(scores, axis=0, keepdims=True)
        weights = jnp.where(real, weigh(scores, top), 0.0)
        run_max[n, :1] = top
        run_sum[n, :1] = jnp.sum(weights, axis=0, keepdims=True)
        run_acc[n] = dot_tn(values_now, weights.astype(BF16))
        return carry

    def absorb(n, slots):
        keys_now = jnp.concatenate([kv[slot, n, 0] for slot in slots], axis=0)
        values_now = jnp.concatenate([kv[slot, n, 1] for slot in slots], axis=0)
        scores = dot(keys_now, q_turned[n])
        old = run_max[n, :1]
        top = jnp.maximum(old, jnp.max(scores, axis=0, keepdims=True))
        factor = weigh(old, top)
        weights = weigh(scores, top)
        total = run_sum[n, :1] * factor + jnp.sum(weights, axis=0, keepdims=True)
        acc = run_acc[n] * factor + dot_tn(values_now, weights.astype(BF16))
        return top, total, acc

    def work_on(n, steps):
        top, total, acc = absorb(n, [slot_at(by) for step in steps for by in (-step, step)])
        run_max[n, :1] = top
        run_sum[n, :1] = total
        run_acc[n] = acc

    def pass_on(step):
        one = slot_at(-step)
        other = slot_at(step)

        def one_head(n, carry):
            for part in range(2):
                copy = to_right(kv.at[one, n, part], ring_recv.at[one, n, part])
                copy.wait_recv()
                copy.start()
                copy = to_left(kv.at[other, n, part], ring_recv.at[other, n, part])
                copy.wait_recv()
                copy.start()
            return carry

        lax.fori_loop(0, GROUP, one_head, 0)

    def pass_on_halves(step):
        one = slot_at(-step)
        other = slot_at(step)

        def one_head(n, carry):
            for part in range(2):
                copy = to_right(kv.at[one, n, part], ring_recv.at[one, n, part], 1)
                copy.wait_recv()
                if part == 0:
                    copy.start()
                copy = to_left(kv.at[other, n, part], ring_recv.at[other, n, part], 1)
                copy.wait_recv()
                if part == 1:
                    copy.start()
            return carry

        lax.fori_loop(0, GROUP, one_head, 0)

    pass_on(1)
    seven = qs.at[pl.ds(0, PAIR - 1)]
    remote(seven, seven, q_send, q_recv, peer).wait_recv()
    half = rows // 2

    def turn_queries(n, carry):
        pieces = [
            qs[y * LAYER + row, n, at * half : (at + 1) * half]
            for at in range(2)
            for row in range(LAYER)
            for y in range(2)
        ]
        q_turned[n] = jnp.concatenate(pieces, axis=0).T
        return carry

    lax.fori_loop(0, GROUP, turn_queries, 0)
    for load in loads[3:7]:
        load.wait()
    mask_column[...] = jnp.broadcast_to(mask[...].astype(F32), (TOK, mask.shape[1])).T
    lax.fori_loop(0, GROUP, attend_first, 0)
    pass_on(2)
    sum_taps()

    def one_parity(parity, carry):
        conv_weights(parity)
        return carry

    lax.fori_loop(0, parities, one_parity, 0)
    pass_on_halves(3)

    def middle_step(n, carry):
        work_on(n, range(1, far))
        return carry

    lax.fori_loop(0, GROUP, middle_step, 0)

    opposite = slot_at(far)
    marks[...] = jnp.zeros_like(marks)

    def last_step(n, carry):
        to_right(kv.at[opposite, n, 0], ring_recv.at[opposite, n, 0]).wait_recv()
        to_left(kv.at[opposite, n, 1], ring_recv.at[opposite, n, 1]).wait_recv()
        top, total, acc = absorb(n, [opposite])
        share = (acc / total).T.astype(BF16)
        for i in range(PAIR):
            o_stage[i, n] = share[i * rows : (i + 1) * rows]

        def send_share(i, inner):
            to, row = row_peer(i)

            @pl.when((i != own_row) | (apart == 1))
            def _():
                remote(o_stage.at[row, n], o_in.at[part_of, n], o_send, o_recv, to).start()

            return inner

        lax.fori_loop(0, PAIR, send_share, 0)
        level = top * SCORE_SCALE + jnp.log(total)
        first = level.astype(BF16).astype(F32)
        second = (level - first).astype(BF16).astype(F32)
        marks[pl.ds(3 * n, 1)] = first
        marks[pl.ds(3 * n + 1, 1)] = second
        marks[pl.ds(3 * n + 2, 1)] = level - first - second
        return carry

    lax.fori_loop(0, GROUP, last_step, 0)
    level_rows = marks[...]
    lanes = mark_stage.shape[2]
    for i in range(PAIR):
        turned = level_rows if i == 0 else pltpu.roll(level_rows, (PAIR - i) * rows, 1)
        mark_stage[i] = turned[:, :lanes].astype(BF16)

    def send_marks(i, carry):
        to, row = row_peer(i)

        @pl.when((i != own_row) | (apart == 1))
        def _():
            remote(mark_stage.at[row], mark_in.at[part_of], mark_send, mark_recv, to).start()

        return carry

    lax.fori_loop(0, PAIR, send_marks, 0)
    own_at = row_peer(own_row)[1]

    @pl.when(apart == 0)
    def _():
        o_in[part_of] = o_stage[own_at]
        mark_in[part_of] = mark_stage[own_at]

    for load in loads[7:]:
        load.wait()

    def await_shares(whole, send, recv, sent):
        def wait(ref):
            copy = remote(ref, ref, send, recv, peer)
            if sent:
                copy.wait_send()
            else:
                copy.wait_recv()

        @pl.when(apart == 1)
        def _():
            wait(whole)

        @pl.when(apart == 0)
        def _():
            wait(whole.at[pl.ds(0, PAIR - 1)])

    await_shares(o_in, o_send, o_recv, False)
    await_shares(mark_in, mark_send, mark_recv, False)
    level_parts = [mark_in[i].astype(F32) for i in range(PAIR)]
    shares[...] = jnp.zeros_like(shares)
    for n in range(GROUP):
        levels = [
            part[3 * n : 3 * n + 1] + part[3 * n + 1 : 3 * n + 2] + part[3 * n + 2 : 3 * n + 3]
            for part in level_parts
        ]
        top = functools.reduce(jnp.maximum, levels)
        parts = [jnp.exp(level - top) for level in levels]
        total = functools.reduce(jnp.add, parts)
        for i, part in enumerate(parts):
            shares[n * PAIR + i : n * PAIR + i + 1] = part / total
    columns = shares[...].T[:rows]
    attended = []
    for n in range(GROUP):
        mixed = functools.reduce(
            jnp.add,
            [
                columns[:, n * PAIR + i : n * PAIR + i + 1] * o_in[i, n].astype(F32)
                for i in range(PAIR)
            ],
        )
        attended.append(mixed.astype(BF16))
    attended = jnp.concatenate(attended, axis=1)

    for part in range(rs_parts):
        product = dot(attended, out_w[:, part * part_cols : (part + 1) * part_cols])
        rs_stage[part] = product.reshape(heads, TOK, part_cols).astype(BF16)

        def send_part(i, carry, part=part):
            to = head_peer(i)
            remote(
                rs_stage.at[part, to[1]],
                rs_in.at[part, h],
                rs_send.at[part],
                rs_recv.at[part],
                to,
            ).start()
            return carry

        lax.fori_loop(0, heads, send_part, 0)
    pieces = []
    for part in range(rs_parts):
        cols = slice(part * part_cols, (part + 1) * part_cols)
        whole = rs_in.at[part]
        remote(whole, whole, rs_send.at[part], rs_recv.at[part], peer).wait_recv()
        projected = jnp.sum(rs_in[part].astype(F32), axis=0)
        stream = tokens[:, cols].astype(F32) + gate[:, cols] * (projected + out_bias[:, cols])
        rounded = stream.astype(BF16)
        block_out[:, cols] = rounded
        pieces.append(rounded.astype(F32))

    normed_in = jnp.concatenate(pieces, axis=1)
    centered = normed_in - jnp.mean(normed_in, axis=1, keepdims=True)
    spread = jnp.mean(centered * centered, axis=1, keepdims=True)
    normed = centered * lax.rsqrt(spread + 1e-06)
    modulated = (normed * (1.0 + scale[...]) + shift[...]).astype(BF16)
    patches = (dot_nt(modulated, final_w[...]) + final_bias[...]) / LATENT_SCALE
    padded = jnp.concatenate([patches, jnp.zeros((TOK, HEAD_DIM - features), F32)], axis=1)
    lat[...] = padded.astype(BF16)

    for at, to in enumerate(halo_peers):
        remote(lat, halo.at[at], halo_send, halo_recv, to).start()
    tiles = {(0, 0): lat[...].astype(F32)}
    remote(halo, halo, halo_send, halo_recv, peer).wait_recv()
    for at, (dr, dc) in enumerate(halo_steps):
        tiles[(-dr, -dc)] = halo[at].astype(F32)

    def rolled(tile, by):
        return pltpu.roll(tile, by % HEAD_DIM, 1)

    top_edge, bottom_edge = s == 0, s == seqs - 1
    first_tile, last_tile = h == 0, h == heads - 1
    for dc in (-1, 0, 1):
        middle = tiles[(0, dc)]
        tiles[(-1, dc)] = jnp.where(top_edge, rolled(middle, 2), tiles[(-1, dc)])
        tiles[(1, dc)] = jnp.where(bottom_edge, rolled(middle, -2), tiles[(1, dc)])
    low = lax.broadcasted_iota(jnp.int32, (1, HEAD_DIM), 1) < features
    packed = {}
    for dr in (-1, 0, 1):
        middle = tiles[(dr, 0)]
        before = jnp.where(first_tile, rolled(middle, 1)[:1], tiles[(dr, -1)][TOK - 1 :])
        after = jnp.where(last_tile, rolled(middle, -1)[TOK - 1 :], tiles[(dr, 1)][:1])
        before = jnp.concatenate([before, middle[: TOK - 1]], axis=0)
        after = jnp.concatenate([middle[1:], after], axis=0)
        packed[(dr, 0)] = jnp.where(low, before, rolled(middle, features))
        packed[(dr, 1)] = jnp.where(low, middle, rolled(after, features))
    for parity in range(parities):
        up, side = parity // 2, parity % 2
        stacked = jnp.concatenate([packed[(up - 1, side)], packed[(up, side)]], axis=1)
        result = dot(stacked.astype(BF16), w_full[parity]) + conv_bias[...]
        for tile in range(pixels.shape[1]):
            pixels[up, tile, pl.ds(side, TOK, stride=2), :] = result[
                :, tile * HEAD_DIM : (tile + 1) * HEAD_DIM
            ]
    for tile in range(pixels.shape[1]):
        cols = slice(tile * HEAD_DIM, (tile + 1) * HEAD_DIM)
        decoded[:, :, cols] = pixels[:, tile].astype(BF16)

    seven = kv_stage.at[pl.ds(0, heads - 1)]
    remote(seven, seven, kv_send, kv_recv, peer).wait_send()
    seven = q_stage.at[pl.ds(0, heads - 1)]
    remote(seven, seven, q_a2a_send, q_a2a_recv, peer).wait_send()
    ring_all = kv.at[pl.ds(0, far - 1)]
    to_right(ring_all, ring_recv.at[0, 0, 0]).wait_send()
    to_left(ring_all, ring_recv.at[0, 0, 0]).wait_send()
    ring_half = kv.at[0, :, 0]
    to_right(ring_half, ring_recv.at[0, 0, 0], 1).wait_send()
    to_left(ring_half, ring_recv.at[0, 0, 0], 1).wait_send()
    seven = qs.at[pl.ds(0, PAIR - 1)]
    remote(seven, seven, q_send, q_recv, peer).wait_send()
    await_shares(o_stage, o_send, o_recv, True)
    await_shares(mark_stage, mark_send, mark_recv, True)
    for part in range(rs_parts):
        whole = rs_stage.at[part]
        remote(whole, whole, rs_send.at[part], rs_recv.at[part], peer).wait_send()
    remote(halo, halo, halo_send, halo_recv, peer).wait_send()


def hand_over(block_in, decoded_in, block_to, decoded_to, sem):
    copies = [
        pltpu.make_async_copy(block_in, block_to, sem.at[0]),
        pltpu.make_async_copy(decoded_in, decoded_to, sem.at[1]),
    ]
    for copy in copies:
        copy.start()
    for copy in copies:
        copy.wait()


def body(seqs, heads, *args):
    (
        queries,
        keys,
        values,
        text_keys,
        text_values,
        text_mask,
        tokens,
        out_weight,
        out_bias,
        gate,
        shift,
        scale,
        final_weight,
        final_bias,
        conv_weight,
        conv_bias,
    ) = args
    dim = queries.shape[3]
    width = GROUP * HEAD_DIM
    text = text_keys.shape[0]
    layers = seqs // PAIR
    far = layers // 2
    rows = heads * TOK
    features = final_weight.shape[1]
    taps = 9 * LAT_CH
    channels = conv_weight.shape[4]
    rs_parts = 4
    operands = (
        queries.reshape(TOK, dim),
        keys.reshape(TOK, dim),
        values.reshape(TOK, dim),
        text_keys,
        text_values,
        text_mask.reshape(1, text),
        tokens.reshape(TOK, dim),
        out_weight,
        out_bias.reshape(1, dim),
        gate.reshape(1, dim),
        shift.reshape(1, dim),
        scale.reshape(1, dim),
        final_weight.T,
        final_bias.reshape(1, features),
        conv_weight.reshape(3 * taps, channels),
        conv_bias.reshape(1, channels),
    )
    copied = [pltpu.VMEM(x.shape, x.dtype) for x in operands]
    dma = pltpu.SemaphoreType.DMA
    anywhere = pl.BlockSpec(memory_space=pl.ANY)
    results = (
        jax.ShapeDtypeStruct((TOK, dim), BF16),
        jax.ShapeDtypeStruct((2, 2 * TOK, channels), BF16),
    )
    held = pl.BlockSpec(memory_space=pltpu.VMEM)
    block_out, decoded = pl.pallas_call(
        functools.partial(kernel, seqs, heads),
        out_shape=tuple(pltpu.VMEM(x.shape, x.dtype) for x in results),
        in_specs=[anywhere] * len(operands),
        out_specs=(held, held),
        scratch_shapes=copied
        + [
            pltpu.VMEM((heads, 2, TOK, width), BF16),
            pltpu.VMEM((heads, TOK, width), BF16),
            pltpu.VMEM((heads, 2, TOK, width), BF16),
            pltpu.VMEM((heads, TOK, width), BF16),
            pltpu.VMEM((layers, GROUP, 2, rows, HEAD_DIM), BF16),
            pltpu.VMEM((PAIR, GROUP, rows, HEAD_DIM), BF16),
            pltpu.VMEM((GROUP, HEAD_DIM, PAIR * rows), BF16),
            pltpu.VMEM((text, TOK), F32),
            pltpu.VMEM((GROUP, TOK, PAIR * rows), F32),
            pltpu.VMEM((GROUP, TOK, PAIR * rows), F32),
            pltpu.VMEM((GROUP, HEAD_DIM, PAIR * rows), F32),
            pltpu.VMEM((16, PAIR * rows), F32),
            pltpu.VMEM((PAIR, 16, HEAD_DIM), BF16),
            pltpu.VMEM((PAIR, 16, HEAD_DIM), BF16),
            pltpu.VMEM((GROUP * PAIR, HEAD_DIM), F32),
            pltpu.VMEM((PAIR, GROUP, rows, HEAD_DIM), BF16),
            pltpu.VMEM((PAIR, GROUP, rows, HEAD_DIM), BF16),
            pltpu.VMEM((rs_parts, heads, TOK, dim // rs_parts), BF16),
            pltpu.VMEM((rs_parts, heads, TOK, dim // rs_parts), BF16),
            pltpu.VMEM((TOK, HEAD_DIM), BF16),
            pltpu.VMEM((8, TOK, HEAD_DIM), BF16),
            pltpu.VMEM((taps, channels), BF16),
            pltpu.VMEM((4, 4 * features, channels), BF16),
            pltpu.VMEM((2, channels // HEAD_DIM, 2 * TOK, HEAD_DIM), F32),
            dma((len(operands),)),
            dma,
            dma,
            dma,
            dma,
            dma((2,)),
            dma((2,)),
            dma((layers, GROUP, 2)),
            dma,
            dma,
            dma,
            dma,
            dma,
            dma,
            dma((rs_parts,)),
            dma((rs_parts,)),
            dma,
            dma,
        ],
        compiler_params=pltpu.CompilerParams(
            collective_id=0, has_side_effects=True, vmem_limit_bytes=60 * 1024 * 1024
        ),
        cost_estimate=pl.CostEstimate(
            flops=1_200_000_000, bytes_accessed=5_000_000, transcendentals=1_000_000
        ),
    )(*operands)
    block_out, decoded = pl.pallas_call(
        hand_over,
        out_shape=results,
        in_specs=(anywhere, anywhere),
        out_specs=(anywhere, anywhere),
        scratch_shapes=[dma((2,))],
        compiler_params=pltpu.CompilerParams(vmem_limit_bytes=2 * 1024 * 1024),
    )(block_out, decoded)
    return (
        block_out.reshape(1, TOK, 1, dim),
        decoded.reshape(1, 2, 2 * TOK, channels),
    )


def solution(mesh):
    seqs = mesh.shape["seq"]
    heads = mesh.shape["head"]
    spread = P("seq", "head", None, None)
    in_specs = (
        spread,
        spread,
        spread,
        P(None, "head"),
        P(None, "head"),
        P(),
        spread,
        P("head", None),
    ) + (P(),) * 8
    out_specs = (spread, P(None, "seq", "head", None))
    return jax.shard_map(
        functools.partial(body, seqs, heads),
        mesh=mesh,
        in_specs=in_specs,
        out_specs=out_specs,
        check_vma=False,
    )
```

```python
import functools

import jax
import jax.numpy as jnp
from jax import lax
from jax.experimental import pallas as pl
from jax.experimental.pallas import tpu as pltpu
from jax.sharding import PartitionSpec as P

HEAD_DIM = 128
GROUP = 3
LAT_CH = 16
TOK = 8
LAYER = 4
PAIR = 8
COLUMNS = 4
LATENT_SCALE = 0.476986
NEG = -1e30
SCORE_SCALE = HEAD_DIM ** (-0.5)
LOG2E = 1.4426950408889634
BF16 = jnp.bfloat16
F32 = jnp.float32
MESH = pl.DeviceIdType.MESH


def dot(a, b):
    return jnp.dot(a, b, preferred_element_type=F32)


def dot_tn(a, b):
    return lax.dot_general(a, b, (((0,), (0,)), ((), ())), preferred_element_type=F32)


def dot_nt(a, b):
    return lax.dot_general(a, b, (((1,), (1,)), ((), ())), preferred_element_type=F32)


def kernel(
    seqs,
    heads,
    q_hbm,
    k_hbm,
    v_hbm,
    text_k_hbm,
    text_v_hbm,
    mask_hbm,
    tokens_hbm,
    out_w_hbm,
    out_bias_hbm,
    gate_hbm,
    shift_hbm,
    scale_hbm,
    final_w_hbm,
    final_bias_hbm,
    conv_w_hbm,
    conv_bias_hbm,
    block_out,
    decoded,
    queries,
    keys,
    values,
    text_k,
    text_v,
    mask,
    tokens,
    out_w,
    out_bias,
    gate,
    shift,
    scale,
    final_w,
    final_bias,
    conv_w,
    conv_bias,
    kv_stage,
    q_stage,
    kv_in,
    q_in,
    kv,
    qs,
    q_turned,
    mask_column,
    run_max,
    run_sum,
    run_acc,
    marks,
    mark_stage,
    mark_in,
    shares,
    o_stage,
    o_in,
    rs_stage,
    rs_in,
    lat,
    halo,
    w_sum,
    w_full,
    pixels,
    local_sem,
    kv_send,
    kv_recv,
    q_a2a_send,
    q_a2a_recv,
    ring_send,
    half_send,
    ring_recv,
    q_send,
    q_recv,
    o_send,
    o_recv,
    mark_send,
    mark_recv,
    rs_send,
    rs_recv,
    halo_send,
    halo_recv,
):
    s = lax.axis_index("seq")
    h = lax.axis_index("head")
    layers = seqs // PAIR
    far = layers // 2
    depth = s // LAYER
    j = lax.rem(s, LAYER)
    z = depth // 2
    parity_z = lax.rem(depth, 2)
    column = lax.rem(h, COLUMNS)
    y_high = h // COLUMNS
    part_of = y_high * LAYER + j
    place = parity_z * COLUMNS + column
    apart = lax.rem(y_high + parity_z, 2)
    width = GROUP * HEAD_DIM
    dim = heads * width
    rows = heads * TOK
    rs_parts = rs_stage.shape[0]
    part_cols = dim // rs_parts

    def shifted(index, by, count):
        return lax.rem(index + (by % count), count)

    r = lax.rem(j + LAYER // 2, LAYER)

    def head_peer(i):
        return (depth * LAYER + r, shifted(h, i, heads))

    def group_peer(i):
        at_depth = z * 2 + lax.rem(parity_z + i // COLUMNS, 2)
        at_column = lax.rem(column + lax.rem(i, COLUMNS), COLUMNS)
        group = lax.rem(at_depth, 2) * COLUMNS + at_column
        return (at_depth * LAYER + j, y_high * COLUMNS + at_column), group

    def part_peer(i):
        part = lax.rem(part_of + i, PAIR)
        return (depth * LAYER + lax.rem(part, LAYER), (part // LAYER) * COLUMNS + column)

    def row_peer(i):
        at_parity = lax.rem(parity_z + i // LAYER, 2)
        row = lax.rem(j + lax.rem(i, LAYER), LAYER)
        owner = lax.rem(row + LAYER // 2, LAYER)
        to = ((z * 2 + at_parity) * LAYER + owner, parity_z * COLUMNS + column)
        return to, at_parity * LAYER + row

    own_row = LAYER // 2

    def slot_at(by):
        return lax.rem(z + by + layers, layers)

    def ring_peer(by):
        return ((slot_at(by) * 2 + parity_z) * LAYER + j, h)

    right, left = ring_peer(1), ring_peer(-1)

    def remote(src, dst, send, recv, device):
        return pltpu.make_async_remote_copy(
            src_ref=src,
            dst_ref=dst,
            send_sem=send,
            recv_sem=recv,
            device_id=device,
            device_id_type=MESH,
        )

    pairs = (
        (k_hbm, keys),
        (v_hbm, values),
        (q_hbm, queries),
        (conv_w_hbm, conv_w),
        (text_k_hbm, text_k),
        (text_v_hbm, text_v),
        (mask_hbm, mask),
        (tokens_hbm, tokens),
        (out_w_hbm, out_w),
        (out_bias_hbm, out_bias),
        (gate_hbm, gate),
        (shift_hbm, shift),
        (scale_hbm, scale),
        (final_w_hbm, final_w),
        (final_bias_hbm, final_bias),
        (conv_bias_hbm, conv_bias),
    )
    loads = [
        pltpu.make_async_copy(src, dst, local_sem.at[i]) for i, (src, dst) in enumerate(pairs)
    ]

    halo_steps = [(dr, dc) for dr in (-1, 0, 1) for dc in (-1, 0, 1) if (dr, dc) != (0, 0)]
    halo_peers = [(shifted(s, dr, seqs), shifted(h, dc, heads)) for dr, dc in halo_steps]
    partners = [group_peer(i)[0] for i in range(1, heads)]
    partners += [right, left]
    partners += [part_peer(i) for i in range(1, PAIR)]
    for load in loads[:3]:
        load.start()
    barrier = pltpu.get_barrier_semaphore()
    for partner in partners:
        pl.semaphore_signal(barrier, inc=1, device_id=partner, device_id_type=MESH)

    group_cols = [slice(g * width, (g + 1) * width) for g in range(heads)]
    for at, whole in enumerate((keys, values)):
        loads[at].wait()
        for g, cols in enumerate(group_cols):
            kv_stage[g, at] = whole[:, cols]
    pl.semaphore_wait(barrier, len(partners))

    def send_kv(i, carry):
        to, group = group_peer(i)
        remote(kv_stage.at[group], kv_in.at[place], kv_send, kv_recv, to).start()
        return carry

    def send_q(i, carry):
        to, group = group_peer(i)
        remote(q_stage.at[group], q_in.at[place], q_a2a_send, q_a2a_recv, to).start()
        return carry

    lax.fori_loop(1, heads, send_kv, 0)
    kv_in[place] = kv_stage[place]
    loads[2].wait()
    for g, cols in enumerate(group_cols):
        q_stage[g] = queries[:, cols]
    lax.fori_loop(1, heads, send_q, 0)
    q_in[place] = q_stage[place]
    for load in loads[3:7]:
        load.start()

    taps = w_sum.shape[0]
    parities = w_full.shape[0]
    features = final_w.shape[0]

    def sum_taps():
        conv_all = conv_w[...].astype(F32)
        total = conv_all[:taps] + conv_all[taps : 2 * taps] + conv_all[2 * taps :]
        w_sum[...] = total.astype(BF16)

    def conv_weights(parity):
        up = parity // 2
        side = lax.rem(parity, 2)
        depth = w_full.shape[1]
        row = lax.broadcasted_iota(jnp.int32, (depth, taps), 0)
        col = lax.broadcasted_iota(jnp.int32, (depth, taps), 1)
        tap_i = 2 * (row >> 7) + ((row >> 1) & 1) + up - 1
        tap_j = 2 * ((row >> 6) & 1) + (row & 1) + side - 1
        inside = (tap_i >= 0) & (tap_i <= 2) & (tap_j >= 0) & (tap_j <= 2)
        source = (tap_i * 3 + tap_j) * LAT_CH + ((row & 63) >> 2)
        pick = jnp.where(inside & (source == col), 1.0, 0.0).astype(BF16)
        w_full[parity] = dot(pick, w_sum[...]).astype(BF16)

    def rows_of(block):
        return block.astype(F32).reshape(rows, width).astype(BF16)

    peer = head_peer(0)
    seven = kv_in.at[pl.ds(0, heads - 1)]
    remote(seven, seven, kv_send, kv_recv, peer).wait_recv()
    own_k = rows_of(kv_in[:, 0])
    own_v = rows_of(kv_in[:, 1])
    for n in range(GROUP):
        cols = slice(n * HEAD_DIM, (n + 1) * HEAD_DIM)
        kv[z, n, 0] = own_k[:, cols]
        kv[z, n, 1] = own_v[:, cols]

    def to_right(ref, recv, send=0):
        return remote(ref, ref, ring_send.at[0] if send == 0 else half_send.at[0], recv, right)

    def to_left(ref, recv, send=0):
        return remote(ref, ref, ring_send.at[1] if send == 0 else half_send.at[1], recv, left)

    pieces_of = [(n, part) for n in range(GROUP) for part in range(2)]

    for n, part in pieces_of:
        to_right(kv.at[z, n, part], ring_recv.at[z, n, part]).start()
        to_left(kv.at[z, n, part], ring_recv.at[z, n, part]).start()
    for load in loads[7:]:
        load.start()

    seven = q_in.at[pl.ds(0, heads - 1)]
    remote(seven, seven, q_a2a_send, q_a2a_recv, peer).wait_recv()
    own_q = rows_of(q_in[...])
    for n in range(GROUP):
        qs[part_of, n] = own_q[:, n * HEAD_DIM : (n + 1) * HEAD_DIM]

    def send_queries(i, carry):
        remote(qs.at[part_of], qs.at[part_of], q_send, q_recv, part_peer(i)).start()
        return carry

    lax.fori_loop(1, PAIR, send_queries, 0)

    def weigh(scores, top):
        return jnp.exp2((scores - top) * (SCORE_SCALE * LOG2E))

    def attend_first(n, carry):
        share = text_k.shape[0] // LAYER
        mine = pl.ds(pl.multiple_of(j * share, share), share)
        cols = pl.ds(pl.multiple_of(n * HEAD_DIM, HEAD_DIM), HEAD_DIM)
        keys_now = jnp.concatenate([text_k[mine, cols], kv[z, n, 0]], axis=0)
        values_now = jnp.concatenate([text_v[mine, cols], kv[z, n, 1]], axis=0)
        scores = dot(keys_now, q_turned[n])
        held = mask_column[mine, :1] * (1 - apart).astype(F32)
        real = jnp.concatenate([held, jnp.ones((rows, 1), F32)], axis=0) == 1.0
        real = jnp.broadcast_to(real, scores.shape)
        scores = jnp.where(real, scores, NEG)
        top = jnp.max(scores, axis=0, keepdims=True)
        weights = jnp.where(real, weigh(scores, top), 0.0)
        run_max[n, :1] = top
        run_sum[n, :1] = jnp.sum(weights, axis=0, keepdims=True)
        run_acc[n] = dot_tn(values_now, weights.astype(BF16))
        return carry

    def absorb(n, slots):
        keys_now = jnp.concatenate([kv[slot, n, 0] for slot in slots], axis=0)
        values_now = jnp.concatenate([kv[slot, n, 1] for slot in slots], axis=0)
        scores = dot(keys_now, q_turned[n])
        old = run_max[n, :1]
        top = jnp.maximum(old, jnp.max(scores, axis=0, keepdims=True))
        factor = weigh(old, top)
        weights = weigh(scores, top)
        total = run_sum[n, :1] * factor + jnp.sum(weights, axis=0, keepdims=True)
        acc = run_acc[n] * factor + dot_tn(values_now, weights.astype(BF16))
        return top, total, acc

    def work_on(n, steps):
        top, total, acc = absorb(n, [slot_at(by) for step in steps for by in (-step, step)])
        run_max[n, :1] = top
        run_sum[n, :1] = total
        run_acc[n] = acc

    def pass_on(step):
        one = slot_at(-step)
        other = slot_at(step)

        def one_head(n, carry):
            for part in range(2):
                copy = to_right(kv.at[one, n, part], ring_recv.at[one, n, part])
                copy.wait_recv()
                copy.start()
                copy = to_left(kv.at[other, n, part], ring_recv.at[other, n, part])
                copy.wait_recv()
                copy.start()
            return carry

        lax.fori_loop(0, GROUP, one_head, 0)

    def pass_on_halves(step):
        one = slot_at(-step)
        other = slot_at(step)

        def one_head(n, carry):
            for part in range(2):
                copy = to_right(kv.at[one, n, part], ring_recv.at[one, n, part], 1)
                copy.wait_recv()
                if part == 0:
                    copy.start()
                copy = to_left(kv.at[other, n, part], ring_recv.at[other, n, part], 1)
                copy.wait_recv()
                if part == 1:
                    copy.start()
            return carry

        lax.fori_loop(0, GROUP, one_head, 0)

    pass_on(1)
    seven = qs.at[pl.ds(0, PAIR - 1)]
    remote(seven, seven, q_send, q_recv, peer).wait_recv()
    half = rows // 2

    def turn_queries(n, carry):
        pieces = [
            qs[y * LAYER + row, n, at * half : (at + 1) * half]
            for at in range(2)
            for row in range(LAYER)
            for y in range(2)
        ]
        q_turned[n] = jnp.concatenate(pieces, axis=0).T
        return carry

    lax.fori_loop(0, GROUP, turn_queries, 0)
    for load in loads[3:7]:
        load.wait()
    mask_column[...] = jnp.broadcast_to(mask[...].astype(F32), (TOK, mask.shape[1])).T
    lax.fori_loop(0, GROUP, attend_first, 0)
    pass_on(2)
    sum_taps()

    def one_parity(parity, carry):
        conv_weights(parity)
        return carry

    lax.fori_loop(0, parities, one_parity, 0)
    pass_on_halves(3)

    def middle_step(n, carry):
        work_on(n, range(1, far))
        return carry

    lax.fori_loop(0, GROUP, middle_step, 0)

    opposite = slot_at(far)
    marks[...] = jnp.zeros_like(marks)

    def last_step(n, carry):
        to_right(kv.at[opposite, n, 0], ring_recv.at[opposite, n, 0]).wait_recv()
        to_left(kv.at[opposite, n, 1], ring_recv.at[opposite, n, 1]).wait_recv()
        top, total, acc = absorb(n, [opposite])
        share = (acc / total).T.astype(BF16)
        for i in range(PAIR):
            o_stage[i, n] = share[i * rows : (i + 1) * rows]

        def send_share(i, inner):
            to, row = row_peer(i)

            @pl.when((i != own_row) | (apart == 1))
            def _():
                remote(o_stage.at[row, n], o_in.at[part_of, n], o_send, o_recv, to).start()

            return inner

        lax.fori_loop(0, PAIR, send_share, 0)
        level = top * SCORE_SCALE + jnp.log(total)
        first = level.astype(BF16).astype(F32)
        second = (level - first).astype(BF16).astype(F32)
        marks[pl.ds(3 * n, 1)] = first
        marks[pl.ds(3 * n + 1, 1)] = second
        marks[pl.ds(3 * n + 2, 1)] = level - first - second
        return carry

    lax.fori_loop(0, GROUP, last_step, 0)
    level_rows = marks[...]
    lanes = mark_stage.shape[2]
    for i in range(PAIR):
        turned = level_rows if i == 0 else pltpu.roll(level_rows, (PAIR - i) * rows, 1)
        mark_stage[i] = turned[:, :lanes].astype(BF16)

    def send_marks(i, carry):
        to, row = row_peer(i)

        @pl.when((i != own_row) | (apart == 1))
        def _():
            remote(mark_stage.at[row], mark_in.at[part_of], mark_send, mark_recv, to).start()

        return carry

    lax.fori_loop(0, PAIR, send_marks, 0)
    own_at = row_peer(own_row)[1]

    @pl.when(apart == 0)
    def _():
        o_in[part_of] = o_stage[own_at]
        mark_in[part_of] = mark_stage[own_at]

    for load in loads[7:]:
        load.wait()

    def await_shares(whole, send, recv, sent):
        def wait(ref):
            copy = remote(ref, ref, send, recv, peer)
            if sent:
                copy.wait_send()
            else:
                copy.wait_recv()

        @pl.when(apart == 1)
        def _():
            wait(whole)

        @pl.when(apart == 0)
        def _():
            wait(whole.at[pl.ds(0, PAIR - 1)])

    await_shares(o_in, o_send, o_recv, False)
    await_shares(mark_in, mark_send, mark_recv, False)
    level_parts = [mark_in[i].astype(F32) for i in range(PAIR)]
    shares[...] = jnp.zeros_like(shares)
    for n in range(GROUP):
        levels = [
            part[3 * n : 3 * n + 1] + part[3 * n + 1 : 3 * n + 2] + part[3 * n + 2 : 3 * n + 3]
            for part in level_parts
        ]
        top = functools.reduce(jnp.maximum, levels)
        parts = [jnp.exp(level - top) for level in levels]
        total = functools.reduce(jnp.add, parts)
        for i, part in enumerate(parts):
            shares[n * PAIR + i : n * PAIR + i + 1] = part / total
    columns = shares[...].T[:rows]
    attended = []
    for n in range(GROUP):
        mixed = functools.reduce(
            jnp.add,
            [
                columns[:, n * PAIR + i : n * PAIR + i + 1] * o_in[i, n].astype(F32)
                for i in range(PAIR)
            ],
        )
        attended.append(mixed.astype(BF16))
    attended = jnp.concatenate(attended, axis=1)

    for part in range(rs_parts):
        product = dot(attended, out_w[:, part * part_cols : (part + 1) * part_cols])
        rs_stage[part] = product.reshape(heads, TOK, part_cols).astype(BF16)

        def send_part(i, carry, part=part):
            to = head_peer(i)
            remote(
                rs_stage.at[part, to[1]],
                rs_in.at[part, h],
                rs_send.at[part],
                rs_recv.at[part],
                to,
            ).start()
            return carry

        lax.fori_loop(0, heads, send_part, 0)
    pieces = []
    for part in range(rs_parts):
        cols = slice(part * part_cols, (part + 1) * part_cols)
        whole = rs_in.at[part]
        remote(whole, whole, rs_send.at[part], rs_recv.at[part], peer).wait_recv()
        projected = jnp.sum(rs_in[part].astype(F32), axis=0)
        stream = tokens[:, cols].astype(F32) + gate[:, cols] * (projected + out_bias[:, cols])
        rounded = stream.astype(BF16)
        block_out[:, cols] = rounded
        pieces.append(rounded.astype(F32))

    normed_in = jnp.concatenate(pieces, axis=1)
    centered = normed_in - jnp.mean(normed_in, axis=1, keepdims=True)
    spread = jnp.mean(centered * centered, axis=1, keepdims=True)
    normed = centered * lax.rsqrt(spread + 1e-06)
    modulated = (normed * (1.0 + scale[...]) + shift[...]).astype(BF16)
    patches = (dot_nt(modulated, final_w[...]) + final_bias[...]) / LATENT_SCALE
    padded = jnp.concatenate([patches, jnp.zeros((TOK, HEAD_DIM - features), F32)], axis=1)
    lat[...] = padded.astype(BF16)

    for at, to in enumerate(halo_peers):
        remote(lat, halo.at[at], halo_send, halo_recv, to).start()
    tiles = {(0, 0): lat[...].astype(F32)}
    seven = kv_stage.at[pl.ds(0, heads - 1)]
    remote(seven, seven, kv_send, kv_recv, peer).wait_send()
    seven = q_stage.at[pl.ds(0, heads - 1)]
    remote(seven, seven, q_a2a_send, q_a2a_recv, peer).wait_send()
    ring_all = kv.at[pl.ds(0, far - 1)]
    to_right(ring_all, ring_recv.at[0, 0, 0]).wait_send()
    to_left(ring_all, ring_recv.at[0, 0, 0]).wait_send()
    ring_half = kv.at[0, :, 0]
    to_right(ring_half, ring_recv.at[0, 0, 0], 1).wait_send()
    to_left(ring_half, ring_recv.at[0, 0, 0], 1).wait_send()
    seven = qs.at[pl.ds(0, PAIR - 1)]
    remote(seven, seven, q_send, q_recv, peer).wait_send()
    await_shares(o_stage, o_send, o_recv, True)
    await_shares(mark_stage, mark_send, mark_recv, True)
    for part in range(rs_parts):
        whole = rs_stage.at[part]
        remote(whole, whole, rs_send.at[part], rs_recv.at[part], peer).wait_send()
    remote(halo, halo, halo_send, halo_recv, peer).wait_recv()
    for at, (dr, dc) in enumerate(halo_steps):
        tiles[(-dr, -dc)] = halo[at].astype(F32)

    def rolled(tile, by):
        return pltpu.roll(tile, by % HEAD_DIM, 1)

    top_edge, bottom_edge = s == 0, s == seqs - 1
    first_tile, last_tile = h == 0, h == heads - 1
    for dc in (-1, 0, 1):
        middle = tiles[(0, dc)]
        tiles[(-1, dc)] = jnp.where(top_edge, rolled(middle, 2), tiles[(-1, dc)])
        tiles[(1, dc)] = jnp.where(bottom_edge, rolled(middle, -2), tiles[(1, dc)])
    low = lax.broadcasted_iota(jnp.int32, (1, HEAD_DIM), 1) < features
    packed = {}
    for dr in (-1, 0, 1):
        middle = tiles[(dr, 0)]
        before = jnp.where(first_tile, rolled(middle, 1)[:1], tiles[(dr, -1)][TOK - 1 :])
        after = jnp.where(last_tile, rolled(middle, -1)[TOK - 1 :], tiles[(dr, 1)][:1])
        before = jnp.concatenate([before, middle[: TOK - 1]], axis=0)
        after = jnp.concatenate([middle[1:], after], axis=0)
        packed[(dr, 0)] = jnp.where(low, before, rolled(middle, features))
        packed[(dr, 1)] = jnp.where(low, middle, rolled(after, features))
    for parity in range(parities):
        up, side = parity // 2, parity % 2
        stacked = jnp.concatenate([packed[(up - 1, side)], packed[(up, side)]], axis=1)
        result = dot(stacked.astype(BF16), w_full[parity]) + conv_bias[...]
        for tile in range(pixels.shape[1]):
            pixels[up, tile, pl.ds(side, TOK, stride=2), :] = result[
                :, tile * HEAD_DIM : (tile + 1) * HEAD_DIM
            ]
    for tile in range(pixels.shape[1]):
        cols = slice(tile * HEAD_DIM, (tile + 1) * HEAD_DIM)
        decoded[:, :, cols] = pixels[:, tile].astype(BF16)

    remote(halo, halo, halo_send, halo_recv, peer).wait_send()


def hand_over(block_in, decoded_in, block_to, decoded_to, sem):
    copies = [
        pltpu.make_async_copy(block_in, block_to, sem.at[0]),
        pltpu.make_async_copy(decoded_in, decoded_to, sem.at[1]),
    ]
    for copy in copies:
        copy.start()
    for copy in copies:
        copy.wait()


def body(seqs, heads, *args):
    (
        queries,
        keys,
        values,
        text_keys,
        text_values,
        text_mask,
        tokens,
        out_weight,
        out_bias,
        gate,
        shift,
        scale,
        final_weight,
        final_bias,
        conv_weight,
        conv_bias,
    ) = args
    dim = queries.shape[3]
    width = GROUP * HEAD_DIM
    text = text_keys.shape[0]
    layers = seqs // PAIR
    far = layers // 2
    rows = heads * TOK
    features = final_weight.shape[1]
    taps = 9 * LAT_CH
    channels = conv_weight.shape[4]
    rs_parts = 4
    operands = (
        queries.reshape(TOK, dim),
        keys.reshape(TOK, dim),
        values.reshape(TOK, dim),
        text_keys,
        text_values,
        text_mask.reshape(1, text),
        tokens.reshape(TOK, dim),
        out_weight,
        out_bias.reshape(1, dim),
        gate.reshape(1, dim),
        shift.reshape(1, dim),
        scale.reshape(1, dim),
        final_weight.T,
        final_bias.reshape(1, features),
        conv_weight.reshape(3 * taps, channels),
        conv_bias.reshape(1, channels),
    )
    copied = [pltpu.VMEM(x.shape, x.dtype) for x in operands]
    dma = pltpu.SemaphoreType.DMA
    anywhere = pl.BlockSpec(memory_space=pl.ANY)
    results = (
        jax.ShapeDtypeStruct((TOK, dim), BF16),
        jax.ShapeDtypeStruct((2, 2 * TOK, channels), BF16),
    )
    held = pl.BlockSpec(memory_space=pltpu.VMEM)
    block_out, decoded = pl.pallas_call(
        functools.partial(kernel, seqs, heads),
        out_shape=tuple(pltpu.VMEM(x.shape, x.dtype) for x in results),
        in_specs=[anywhere] * len(operands),
        out_specs=(held, held),
        scratch_shapes=copied
        + [
            pltpu.VMEM((heads, 2, TOK, width), BF16),
            pltpu.VMEM((heads, TOK, width), BF16),
            pltpu.VMEM((heads, 2, TOK, width), BF16),
            pltpu.VMEM((heads, TOK, width), BF16),
            pltpu.VMEM((layers, GROUP, 2, rows, HEAD_DIM), BF16),
            pltpu.VMEM((PAIR, GROUP, rows, HEAD_DIM), BF16),
            pltpu.VMEM((GROUP, HEAD_DIM, PAIR * rows), BF16),
            pltpu.VMEM((text, TOK), F32),
            pltpu.VMEM((GROUP, TOK, PAIR * rows), F32),
            pltpu.VMEM((GROUP, TOK, PAIR * rows), F32),
            pltpu.VMEM((GROUP, HEAD_DIM, PAIR * rows), F32),
            pltpu.VMEM((16, PAIR * rows), F32),
            pltpu.VMEM((PAIR, 16, HEAD_DIM), BF16),
            pltpu.VMEM((PAIR, 16, HEAD_DIM), BF16),
            pltpu.VMEM((GROUP * PAIR, HEAD_DIM), F32),
            pltpu.VMEM((PAIR, GROUP, rows, HEAD_DIM), BF16),
            pltpu.VMEM((PAIR, GROUP, rows, HEAD_DIM), BF16),
            pltpu.VMEM((rs_parts, heads, TOK, dim // rs_parts), BF16),
            pltpu.VMEM((rs_parts, heads, TOK, dim // rs_parts), BF16),
            pltpu.VMEM((TOK, HEAD_DIM), BF16),
            pltpu.VMEM((8, TOK, HEAD_DIM), BF16),
            pltpu.VMEM((taps, channels), BF16),
            pltpu.VMEM((4, 4 * features, channels), BF16),
            pltpu.VMEM((2, channels // HEAD_DIM, 2 * TOK, HEAD_DIM), F32),
            dma((len(operands),)),
            dma,
            dma,
            dma,
            dma,
            dma((2,)),
            dma((2,)),
            dma((layers, GROUP, 2)),
            dma,
            dma,
            dma,
            dma,
            dma,
            dma,
            dma((rs_parts,)),
            dma((rs_parts,)),
            dma,
            dma,
        ],
        compiler_params=pltpu.CompilerParams(
            collective_id=0, has_side_effects=True, vmem_limit_bytes=60 * 1024 * 1024
        ),
        cost_estimate=pl.CostEstimate(
            flops=1_200_000_000, bytes_accessed=5_000_000, transcendentals=1_000_000
        ),
    )(*operands)
    block_out, decoded = pl.pallas_call(
        hand_over,
        out_shape=results,
        in_specs=(anywhere, anywhere),
        out_specs=(anywhere, anywhere),
        scratch_shapes=[dma((2,))],
        compiler_params=pltpu.CompilerParams(vmem_limit_bytes=2 * 1024 * 1024),
    )(block_out, decoded)
    return (
        block_out.reshape(1, TOK, 1, dim),
        decoded.reshape(1, 2, 2 * TOK, channels),
    )


def solution(mesh):
    seqs = mesh.shape["seq"]
    heads = mesh.shape["head"]
    spread = P("seq", "head", None, None)
    in_specs = (
        spread,
        spread,
        spread,
        P(None, "head"),
        P(None, "head"),
        P(),
        spread,
        P("head", None),
    ) + (P(),) * 8
    out_specs = (spread, P(None, "seq", "head", None))
    return jax.shard_map(
        functools.partial(body, seqs, heads),
        mesh=mesh,
        in_specs=in_specs,
        out_specs=out_specs,
        check_vma=False,
    )
```

```python
import functools

import jax
import jax.numpy as jnp
from jax import lax
from jax.experimental import pallas as pl
from jax.experimental.pallas import tpu as pltpu
from jax.sharding import PartitionSpec as P

HEAD_DIM = 128
GROUP = 3
LAT_CH = 16
TOK = 8
LAYER = 4
PAIR = 8
COLUMNS = 4
LATENT_SCALE = 0.476986
NEG = -1e30
SCORE_SCALE = HEAD_DIM ** (-0.5)
LOG2E = 1.4426950408889634
BF16 = jnp.bfloat16
F32 = jnp.float32
MESH = pl.DeviceIdType.MESH


def dot(a, b):
    return jnp.dot(a, b, preferred_element_type=F32)


def dot_tn(a, b):
    return lax.dot_general(a, b, (((0,), (0,)), ((), ())), preferred_element_type=F32)


def dot_nt(a, b):
    return lax.dot_general(a, b, (((1,), (1,)), ((), ())), preferred_element_type=F32)


def kernel(
    seqs,
    heads,
    q_hbm,
    k_hbm,
    v_hbm,
    text_k_hbm,
    text_v_hbm,
    mask_hbm,
    tokens_hbm,
    out_w_hbm,
    out_bias_hbm,
    gate_hbm,
    shift_hbm,
    scale_hbm,
    final_w_hbm,
    final_bias_hbm,
    conv_w_hbm,
    conv_bias_hbm,
    block_out,
    decoded,
    queries,
    keys,
    values,
    text_k,
    text_v,
    mask,
    tokens,
    out_w,
    out_bias,
    gate,
    shift,
    scale,
    final_w,
    final_bias,
    conv_w,
    conv_bias,
    kv_stage,
    q_stage,
    kv_in,
    q_in,
    kv,
    qs,
    q_turned,
    mask_column,
    run_max,
    run_sum,
    run_acc,
    marks,
    mark_stage,
    mark_in,
    shares,
    o_stage,
    o_in,
    rs_stage,
    rs_in,
    lat,
    halo,
    w_sum,
    w_full,
    pixels,
    local_sem,
    kv_send,
    kv_recv,
    q_a2a_send,
    q_a2a_recv,
    ring_send,
    half_send,
    ring_recv,
    q_send,
    q_recv,
    o_send,
    o_recv,
    mark_send,
    mark_recv,
    rs_send,
    rs_recv,
    halo_send,
    halo_recv,
):
    s = lax.axis_index("seq")
    h = lax.axis_index("head")
    layers = seqs // PAIR
    far = layers // 2
    depth = s // LAYER
    j = lax.rem(s, LAYER)
    z = depth // 2
    parity_z = lax.rem(depth, 2)
    column = lax.rem(h, COLUMNS)
    y_high = h // COLUMNS
    part_of = y_high * LAYER + j
    place = parity_z * COLUMNS + column
    apart = lax.rem(y_high + parity_z, 2)
    width = GROUP * HEAD_DIM
    dim = heads * width
    rows = heads * TOK
    rs_parts = rs_stage.shape[0]
    part_cols = dim // rs_parts

    def shifted(index, by, count):
        return lax.rem(index + (by % count), count)

    r = lax.rem(j + LAYER // 2, LAYER)

    def head_peer(i):
        return (depth * LAYER + r, shifted(h, i, heads))

    def group_peer(i):
        at_depth = z * 2 + lax.rem(parity_z + i // COLUMNS, 2)
        at_column = lax.rem(column + lax.rem(i, COLUMNS), COLUMNS)
        group = lax.rem(at_depth, 2) * COLUMNS + at_column
        return (at_depth * LAYER + j, y_high * COLUMNS + at_column), group

    def part_peer(i):
        part = lax.rem(part_of + i, PAIR)
        return (depth * LAYER + lax.rem(part, LAYER), (part // LAYER) * COLUMNS + column)

    def row_peer(i):
        at_parity = lax.rem(parity_z + i // LAYER, 2)
        row = lax.rem(j + lax.rem(i, LAYER), LAYER)
        owner = lax.rem(row + LAYER // 2, LAYER)
        to = ((z * 2 + at_parity) * LAYER + owner, parity_z * COLUMNS + column)
        return to, at_parity * LAYER + row

    own_row = LAYER // 2

    def slot_at(by):
        return lax.rem(z + by + layers, layers)

    def ring_peer(by):
        return ((slot_at(by) * 2 + parity_z) * LAYER + j, h)

    right, left = ring_peer(1), ring_peer(-1)

    def remote(src, dst, send, recv, device):
        return pltpu.make_async_remote_copy(
            src_ref=src,
            dst_ref=dst,
            send_sem=send,
            recv_sem=recv,
            device_id=device,
            device_id_type=MESH,
        )

    pairs = (
        (k_hbm, keys),
        (v_hbm, values),
        (q_hbm, queries),
        (conv_w_hbm, conv_w),
        (text_k_hbm, text_k),
        (text_v_hbm, text_v),
        (mask_hbm, mask),
        (tokens_hbm, tokens),
        (out_w_hbm, out_w),
        (out_bias_hbm, out_bias),
        (gate_hbm, gate),
        (shift_hbm, shift),
        (scale_hbm, scale),
        (final_w_hbm, final_w),
        (final_bias_hbm, final_bias),
        (conv_bias_hbm, conv_bias),
    )
    loads = [
        pltpu.make_async_copy(src, dst, local_sem.at[i]) for i, (src, dst) in enumerate(pairs)
    ]

    halo_steps = [(dr, dc) for dr in (-1, 0, 1) for dc in (-1, 0, 1) if (dr, dc) != (0, 0)]
    halo_peers = [(shifted(s, dr, seqs), shifted(h, dc, heads)) for dr, dc in halo_steps]
    partners = [group_peer(i)[0] for i in range(1, heads)]
    partners += [right, left]
    partners += [part_peer(i) for i in range(1, PAIR)]
    for load in loads[:3]:
        load.start()
    barrier = pltpu.get_barrier_semaphore()
    for partner in partners:
        pl.semaphore_signal(barrier, inc=1, device_id=partner, device_id_type=MESH)

    group_cols = [slice(g * width, (g + 1) * width) for g in range(heads)]
    for at, whole in enumerate((keys, values)):
        loads[at].wait()
        for g, cols in enumerate(group_cols):
            kv_stage[g, at] = whole[:, cols]
    pl.semaphore_wait(barrier, len(partners))

    def send_kv(i, carry):
        to, group = group_peer(i)
        remote(kv_stage.at[group], kv_in.at[place], kv_send, kv_recv, to).start()
        return carry

    def send_q(i, carry):
        to, group = group_peer(i)
        remote(q_stage.at[group], q_in.at[place], q_a2a_send, q_a2a_recv, to).start()
        return carry

    lax.fori_loop(1, heads, send_kv, 0)
    kv_in[place] = kv_stage[place]
    loads[2].wait()
    for g, cols in enumerate(group_cols):
        q_stage[g] = queries[:, cols]
    lax.fori_loop(1, heads, send_q, 0)
    q_in[place] = q_stage[place]
    for load in loads[3:7]:
        load.start()

    taps = w_sum.shape[0]
    parities = w_full.shape[0]
    features = final_w.shape[0]

    def sum_taps():
        conv_all = conv_w[...].astype(F32)
        total = conv_all[:taps] + conv_all[taps : 2 * taps] + conv_all[2 * taps :]
        w_sum[...] = total.astype(BF16)

    def conv_weights(parity):
        up = parity // 2
        side = lax.rem(parity, 2)
        depth = w_full.shape[1]
        row = lax.broadcasted_iota(jnp.int32, (depth, taps), 0)
        col = lax.broadcasted_iota(jnp.int32, (depth, taps), 1)
        tap_i = 2 * (row >> 7) + ((row >> 1) & 1) + up - 1
        tap_j = 2 * ((row >> 6) & 1) + (row & 1) + side - 1
        inside = (tap_i >= 0) & (tap_i <= 2) & (tap_j >= 0) & (tap_j <= 2)
        source = (tap_i * 3 + tap_j) * LAT_CH + ((row & 63) >> 2)
        pick = jnp.where(inside & (source == col), 1.0, 0.0).astype(BF16)
        w_full[parity] = dot(pick, w_sum[...]).astype(BF16)

    def rows_of(block):
        return block.astype(F32).reshape(rows, width).astype(BF16)

    peer = head_peer(0)
    seven = kv_in.at[pl.ds(0, heads - 1)]
    remote(seven, seven, kv_send, kv_recv, peer).wait_recv()
    own_k = rows_of(kv_in[:, 0])
    own_v = rows_of(kv_in[:, 1])
    for n in range(GROUP):
        cols = slice(n * HEAD_DIM, (n + 1) * HEAD_DIM)
        kv[z, n, 0] = own_k[:, cols]
        kv[z, n, 1] = own_v[:, cols]

    def to_right(ref, recv, send=0):
        return remote(ref, ref, ring_send.at[0] if send == 0 else half_send.at[0], recv, right)

    def to_left(ref, recv, send=0):
        return remote(ref, ref, ring_send.at[1] if send == 0 else half_send.at[1], recv, left)

    def piece(slot, n, part):
        return kv.at[slot, n, part // 2, pl.ds(part % 2 * (rows // 2), rows // 2)]

    pieces_of = [(n, part) for n in range(GROUP) for part in range(4)]

    for n, part in pieces_of:
        to_right(piece(z, n, part), ring_recv.at[z, n, part]).start()
        to_left(piece(z, n, part), ring_recv.at[z, n, part]).start()
    for load in loads[7:]:
        load.start()

    seven = q_in.at[pl.ds(0, heads - 1)]
    remote(seven, seven, q_a2a_send, q_a2a_recv, peer).wait_recv()
    own_q = rows_of(q_in[...])
    for n in range(GROUP):
        qs[part_of, n] = own_q[:, n * HEAD_DIM : (n + 1) * HEAD_DIM]

    def send_queries(i, carry):
        remote(qs.at[part_of], qs.at[part_of], q_send, q_recv, part_peer(i)).start()
        return carry

    lax.fori_loop(1, PAIR, send_queries, 0)

    def weigh(scores, top):
        return jnp.exp2((scores - top) * (SCORE_SCALE * LOG2E))

    def attend_first(n, carry):
        share = text_k.shape[0] // LAYER
        mine = pl.ds(pl.multiple_of(j * share, share), share)
        cols = pl.ds(pl.multiple_of(n * HEAD_DIM, HEAD_DIM), HEAD_DIM)
        keys_now = jnp.concatenate([text_k[mine, cols], kv[z, n, 0]], axis=0)
        values_now = jnp.concatenate([text_v[mine, cols], kv[z, n, 1]], axis=0)
        scores = dot(keys_now, q_turned[n])
        held = mask_column[mine, :1] * (1 - apart).astype(F32)
        real = jnp.concatenate([held, jnp.ones((rows, 1), F32)], axis=0) == 1.0
        real = jnp.broadcast_to(real, scores.shape)
        scores = jnp.where(real, scores, NEG)
        top = jnp.max(scores, axis=0, keepdims=True)
        weights = jnp.where(real, weigh(scores, top), 0.0)
        run_max[n, :1] = top
        run_sum[n, :1] = jnp.sum(weights, axis=0, keepdims=True)
        run_acc[n] = dot_tn(values_now, weights.astype(BF16))
        return carry

    def absorb(n, slots):
        keys_now = jnp.concatenate([kv[slot, n, 0] for slot in slots], axis=0)
        values_now = jnp.concatenate([kv[slot, n, 1] for slot in slots], axis=0)
        scores = dot(keys_now, q_turned[n])
        old = run_max[n, :1]
        top = jnp.maximum(old, jnp.max(scores, axis=0, keepdims=True))
        factor = weigh(old, top)
        weights = weigh(scores, top)
        total = run_sum[n, :1] * factor + jnp.sum(weights, axis=0, keepdims=True)
        acc = run_acc[n] * factor + dot_tn(values_now, weights.astype(BF16))
        return top, total, acc

    def work_on(n, steps):
        top, total, acc = absorb(n, [slot_at(by) for step in steps for by in (-step, step)])
        run_max[n, :1] = top
        run_sum[n, :1] = total
        run_acc[n] = acc

    def pass_on(step):
        one = slot_at(-step)
        other = slot_at(step)

        def one_head(n, carry):
            for part in range(4):
                copy = to_right(piece(one, n, part), ring_recv.at[one, n, part])
                copy.wait_recv()
                copy.start()
                copy = to_left(piece(other, n, part), ring_recv.at[other, n, part])
                copy.wait_recv()
                copy.start()
            return carry

        lax.fori_loop(0, GROUP, one_head, 0)

    def pass_on_halves(step):
        one = slot_at(-step)
        other = slot_at(step)

        def one_head(n, carry):
            for part in range(4):
                copy = to_right(piece(one, n, part), ring_recv.at[one, n, part], 1)
                copy.wait_recv()
                if part < 2:
                    copy.start()
                copy = to_left(piece(other, n, part), ring_recv.at[other, n, part], 1)
                copy.wait_recv()
                if part >= 2:
                    copy.start()
            return carry

        lax.fori_loop(0, GROUP, one_head, 0)

    pass_on(1)
    seven = qs.at[pl.ds(0, PAIR - 1)]
    remote(seven, seven, q_send, q_recv, peer).wait_recv()
    half = rows // 2

    def turn_queries(n, carry):
        pieces = [
            qs[y * LAYER + row, n, at * half : (at + 1) * half]
            for at in range(2)
            for row in range(LAYER)
            for y in range(2)
        ]
        q_turned[n] = jnp.concatenate(pieces, axis=0).T
        return carry

    lax.fori_loop(0, GROUP, turn_queries, 0)
    for load in loads[3:7]:
        load.wait()
    mask_column[...] = jnp.broadcast_to(mask[...].astype(F32), (TOK, mask.shape[1])).T
    lax.fori_loop(0, GROUP, attend_first, 0)
    pass_on(2)
    sum_taps()

    def one_parity(parity, carry):
        conv_weights(parity)
        return carry

    lax.fori_loop(0, parities, one_parity, 0)
    pass_on_halves(3)

    def middle_step(n, carry):
        work_on(n, range(1, far))
        return carry

    lax.fori_loop(0, GROUP, middle_step, 0)

    opposite = slot_at(far)
    marks[...] = jnp.zeros_like(marks)

    def last_step(n, carry):
        for part in range(2):
            to_right(piece(opposite, n, part), ring_recv.at[opposite, n, part]).wait_recv()
        for part in range(2, 4):
            to_left(piece(opposite, n, part), ring_recv.at[opposite, n, part]).wait_recv()
        top, total, acc = absorb(n, [opposite])
        share = (acc / total).T.astype(BF16)
        for i in range(PAIR):
            o_stage[i, n] = share[i * rows : (i + 1) * rows]

        def send_share(i, inner):
            to, row = row_peer(i)

            @pl.when((i != own_row) | (apart == 1))
            def _():
                remote(o_stage.at[row, n], o_in.at[part_of, n], o_send, o_recv, to).start()

            return inner

        lax.fori_loop(0, PAIR, send_share, 0)
        level = top * SCORE_SCALE + jnp.log(total)
        first = level.astype(BF16).astype(F32)
        second = (level - first).astype(BF16).astype(F32)
        marks[pl.ds(3 * n, 1)] = first
        marks[pl.ds(3 * n + 1, 1)] = second
        marks[pl.ds(3 * n + 2, 1)] = level - first - second
        return carry

    lax.fori_loop(0, GROUP, last_step, 0)
    level_rows = marks[...]
    lanes = mark_stage.shape[2]
    for i in range(PAIR):
        turned = level_rows if i == 0 else pltpu.roll(level_rows, (PAIR - i) * rows, 1)
        mark_stage[i] = turned[:, :lanes].astype(BF16)

    def send_marks(i, carry):
        to, row = row_peer(i)

        @pl.when((i != own_row) | (apart == 1))
        def _():
            remote(mark_stage.at[row], mark_in.at[part_of], mark_send, mark_recv, to).start()

        return carry

    lax.fori_loop(0, PAIR, send_marks, 0)
    own_at = row_peer(own_row)[1]

    @pl.when(apart == 0)
    def _():
        o_in[part_of] = o_stage[own_at]
        mark_in[part_of] = mark_stage[own_at]

    for load in loads[7:]:
        load.wait()

    def await_shares(whole, send, recv, sent):
        def wait(ref):
            copy = remote(ref, ref, send, recv, peer)
            if sent:
                copy.wait_send()
            else:
                copy.wait_recv()

        @pl.when(apart == 1)
        def _():
            wait(whole)

        @pl.when(apart == 0)
        def _():
            wait(whole.at[pl.ds(0, PAIR - 1)])

    await_shares(o_in, o_send, o_recv, False)
    await_shares(mark_in, mark_send, mark_recv, False)
    level_parts = [mark_in[i].astype(F32) for i in range(PAIR)]
    shares[...] = jnp.zeros_like(shares)
    for n in range(GROUP):
        levels = [
            part[3 * n : 3 * n + 1] + part[3 * n + 1 : 3 * n + 2] + part[3 * n + 2 : 3 * n + 3]
            for part in level_parts
        ]
        top = functools.reduce(jnp.maximum, levels)
        parts = [jnp.exp(level - top) for level in levels]
        total = functools.reduce(jnp.add, parts)
        for i, part in enumerate(parts):
            shares[n * PAIR + i : n * PAIR + i + 1] = part / total
    columns = shares[...].T[:rows]
    attended = []
    for n in range(GROUP):
        mixed = functools.reduce(
            jnp.add,
            [
                columns[:, n * PAIR + i : n * PAIR + i + 1] * o_in[i, n].astype(F32)
                for i in range(PAIR)
            ],
        )
        attended.append(mixed.astype(BF16))
    attended = jnp.concatenate(attended, axis=1)

    for part in range(rs_parts):
        product = dot(attended, out_w[:, part * part_cols : (part + 1) * part_cols])
        rs_stage[part] = product.reshape(heads, TOK, part_cols).astype(BF16)

        def send_part(i, carry, part=part):
            to = head_peer(i)
            remote(
                rs_stage.at[part, to[1]],
                rs_in.at[part, h],
                rs_send.at[part],
                rs_recv.at[part],
                to,
            ).start()
            return carry

        lax.fori_loop(0, heads, send_part, 0)
    pieces = []
    for part in range(rs_parts):
        cols = slice(part * part_cols, (part + 1) * part_cols)
        whole = rs_in.at[part]
        remote(whole, whole, rs_send.at[part], rs_recv.at[part], peer).wait_recv()
        projected = jnp.sum(rs_in[part].astype(F32), axis=0)
        stream = tokens[:, cols].astype(F32) + gate[:, cols] * (projected + out_bias[:, cols])
        rounded = stream.astype(BF16)
        block_out[:, cols] = rounded
        pieces.append(rounded.astype(F32))

    normed_in = jnp.concatenate(pieces, axis=1)
    centered = normed_in - jnp.mean(normed_in, axis=1, keepdims=True)
    spread = jnp.mean(centered * centered, axis=1, keepdims=True)
    normed = centered * lax.rsqrt(spread + 1e-06)
    modulated = (normed * (1.0 + scale[...]) + shift[...]).astype(BF16)
    patches = (dot_nt(modulated, final_w[...]) + final_bias[...]) / LATENT_SCALE
    padded = jnp.concatenate([patches, jnp.zeros((TOK, HEAD_DIM - features), F32)], axis=1)
    lat[...] = padded.astype(BF16)

    for at, to in enumerate(halo_peers):
        remote(lat, halo.at[at], halo_send, halo_recv, to).start()
    tiles = {(0, 0): lat[...].astype(F32)}
    seven = kv_stage.at[pl.ds(0, heads - 1)]
    remote(seven, seven, kv_send, kv_recv, peer).wait_send()
    seven = q_stage.at[pl.ds(0, heads - 1)]
    remote(seven, seven, q_a2a_send, q_a2a_recv, peer).wait_send()
    ring_all = kv.at[pl.ds(0, far - 1)]
    to_right(ring_all, ring_recv.at[0, 0, 0]).wait_send()
    to_left(ring_all, ring_recv.at[0, 0, 0]).wait_send()
    ring_half = kv.at[0, :, 0]
    to_right(ring_half, ring_recv.at[0, 0, 0], 1).wait_send()
    to_left(ring_half, ring_recv.at[0, 0, 0], 1).wait_send()
    seven = qs.at[pl.ds(0, PAIR - 1)]
    remote(seven, seven, q_send, q_recv, peer).wait_send()
    await_shares(o_stage, o_send, o_recv, True)
    await_shares(mark_stage, mark_send, mark_recv, True)
    for part in range(rs_parts):
        whole = rs_stage.at[part]
        remote(whole, whole, rs_send.at[part], rs_recv.at[part], peer).wait_send()
    remote(halo, halo, halo_send, halo_recv, peer).wait_recv()
    for at, (dr, dc) in enumerate(halo_steps):
        tiles[(-dr, -dc)] = halo[at].astype(F32)

    def rolled(tile, by):
        return pltpu.roll(tile, by % HEAD_DIM, 1)

    top_edge, bottom_edge = s == 0, s == seqs - 1
    first_tile, last_tile = h == 0, h == heads - 1
    for dc in (-1, 0, 1):
        middle = tiles[(0, dc)]
        tiles[(-1, dc)] = jnp.where(top_edge, rolled(middle, 2), tiles[(-1, dc)])
        tiles[(1, dc)] = jnp.where(bottom_edge, rolled(middle, -2), tiles[(1, dc)])
    low = lax.broadcasted_iota(jnp.int32, (1, HEAD_DIM), 1) < features
    packed = {}
    for dr in (-1, 0, 1):
        middle = tiles[(dr, 0)]
        before = jnp.where(first_tile, rolled(middle, 1)[:1], tiles[(dr, -1)][TOK - 1 :])
        after = jnp.where(last_tile, rolled(middle, -1)[TOK - 1 :], tiles[(dr, 1)][:1])
        before = jnp.concatenate([before, middle[: TOK - 1]], axis=0)
        after = jnp.concatenate([middle[1:], after], axis=0)
        packed[(dr, 0)] = jnp.where(low, before, rolled(middle, features))
        packed[(dr, 1)] = jnp.where(low, middle, rolled(after, features))
    for parity in range(parities):
        up, side = parity // 2, parity % 2
        stacked = jnp.concatenate([packed[(up - 1, side)], packed[(up, side)]], axis=1)
        result = dot(stacked.astype(BF16), w_full[parity]) + conv_bias[...]
        for tile in range(pixels.shape[1]):
            pixels[up, tile, pl.ds(side, TOK, stride=2), :] = result[
                :, tile * HEAD_DIM : (tile + 1) * HEAD_DIM
            ]
    for tile in range(pixels.shape[1]):
        cols = slice(tile * HEAD_DIM, (tile + 1) * HEAD_DIM)
        decoded[:, :, cols] = pixels[:, tile].astype(BF16)

    remote(halo, halo, halo_send, halo_recv, peer).wait_send()


def hand_over(block_in, decoded_in, block_to, decoded_to, sem):
    copies = [
        pltpu.make_async_copy(block_in, block_to, sem.at[0]),
        pltpu.make_async_copy(decoded_in, decoded_to, sem.at[1]),
    ]
    for copy in copies:
        copy.start()
    for copy in copies:
        copy.wait()


def body(seqs, heads, *args):
    (
        queries,
        keys,
        values,
        text_keys,
        text_values,
        text_mask,
        tokens,
        out_weight,
        out_bias,
        gate,
        shift,
        scale,
        final_weight,
        final_bias,
        conv_weight,
        conv_bias,
    ) = args
    dim = queries.shape[3]
    width = GROUP * HEAD_DIM
    text = text_keys.shape[0]
    layers = seqs // PAIR
    far = layers // 2
    rows = heads * TOK
    features = final_weight.shape[1]
    taps = 9 * LAT_CH
    channels = conv_weight.shape[4]
    rs_parts = 4
    operands = (
        queries.reshape(TOK, dim),
        keys.reshape(TOK, dim),
        values.reshape(TOK, dim),
        text_keys,
        text_values,
        text_mask.reshape(1, text),
        tokens.reshape(TOK, dim),
        out_weight,
        out_bias.reshape(1, dim),
        gate.reshape(1, dim),
        shift.reshape(1, dim),
        scale.reshape(1, dim),
        final_weight.T,
        final_bias.reshape(1, features),
        conv_weight.reshape(3 * taps, channels),
        conv_bias.reshape(1, channels),
    )
    copied = [pltpu.VMEM(x.shape, x.dtype) for x in operands]
    dma = pltpu.SemaphoreType.DMA
    anywhere = pl.BlockSpec(memory_space=pl.ANY)
    results = (
        jax.ShapeDtypeStruct((TOK, dim), BF16),
        jax.ShapeDtypeStruct((2, 2 * TOK, channels), BF16),
    )
    held = pl.BlockSpec(memory_space=pltpu.VMEM)
    block_out, decoded = pl.pallas_call(
        functools.partial(kernel, seqs, heads),
        out_shape=tuple(pltpu.VMEM(x.shape, x.dtype) for x in results),
        in_specs=[anywhere] * len(operands),
        out_specs=(held, held),
        scratch_shapes=copied
        + [
            pltpu.VMEM((heads, 2, TOK, width), BF16),
            pltpu.VMEM((heads, TOK, width), BF16),
            pltpu.VMEM((heads, 2, TOK, width), BF16),
            pltpu.VMEM((heads, TOK, width), BF16),
            pltpu.VMEM((layers, GROUP, 2, rows, HEAD_DIM), BF16),
            pltpu.VMEM((PAIR, GROUP, rows, HEAD_DIM), BF16),
            pltpu.VMEM((GROUP, HEAD_DIM, PAIR * rows), BF16),
            pltpu.VMEM((text, TOK), F32),
            pltpu.VMEM((GROUP, TOK, PAIR * rows), F32),
            pltpu.VMEM((GROUP, TOK, PAIR * rows), F32),
            pltpu.VMEM((GROUP, HEAD_DIM, PAIR * rows), F32),
            pltpu.VMEM((16, PAIR * rows), F32),
            pltpu.VMEM((PAIR, 16, HEAD_DIM), BF16),
            pltpu.VMEM((PAIR, 16, HEAD_DIM), BF16),
            pltpu.VMEM((GROUP * PAIR, HEAD_DIM), F32),
            pltpu.VMEM((PAIR, GROUP, rows, HEAD_DIM), BF16),
            pltpu.VMEM((PAIR, GROUP, rows, HEAD_DIM), BF16),
            pltpu.VMEM((rs_parts, heads, TOK, dim // rs_parts), BF16),
            pltpu.VMEM((rs_parts, heads, TOK, dim // rs_parts), BF16),
            pltpu.VMEM((TOK, HEAD_DIM), BF16),
            pltpu.VMEM((8, TOK, HEAD_DIM), BF16),
            pltpu.VMEM((taps, channels), BF16),
            pltpu.VMEM((4, 4 * features, channels), BF16),
            pltpu.VMEM((2, channels // HEAD_DIM, 2 * TOK, HEAD_DIM), F32),
            dma((len(operands),)),
            dma,
            dma,
            dma,
            dma,
            dma((2,)),
            dma((2,)),
            dma((layers, GROUP, 4)),
            dma,
            dma,
            dma,
            dma,
            dma,
            dma,
            dma((rs_parts,)),
            dma((rs_parts,)),
            dma,
            dma,
        ],
        compiler_params=pltpu.CompilerParams(
            collective_id=0, has_side_effects=True, vmem_limit_bytes=60 * 1024 * 1024
        ),
        cost_estimate=pl.CostEstimate(
            flops=1_200_000_000, bytes_accessed=5_000_000, transcendentals=1_000_000
        ),
    )(*operands)
    block_out, decoded = pl.pallas_call(
        hand_over,
        out_shape=results,
        in_specs=(anywhere, anywhere),
        out_specs=(anywhere, anywhere),
        scratch_shapes=[dma((2,))],
        compiler_params=pltpu.CompilerParams(vmem_limit_bytes=2 * 1024 * 1024),
    )(block_out, decoded)
    return (
        block_out.reshape(1, TOK, 1, dim),
        decoded.reshape(1, 2, 2 * TOK, channels),
    )


def solution(mesh):
    seqs = mesh.shape["seq"]
    heads = mesh.shape["head"]
    spread = P("seq", "head", None, None)
    in_specs = (
        spread,
        spread,
        spread,
        P(None, "head"),
        P(None, "head"),
        P(),
        spread,
        P("head", None),
    ) + (P(),) * 8
    out_specs = (spread, P(None, "seq", "head", None))
    return jax.shard_map(
        functools.partial(body, seqs, heads),
        mesh=mesh,
        in_specs=in_specs,
        out_specs=out_specs,
        check_vma=False,
    )
```
